32 devices in a mesh: pb: 8 (over y, x, core), mem: 4 (over z).
Axes of the slice: x: 2, y: 2, z: 4, core: 2. Of those that a mesh axis runs over, the one named last changes fastest.
Arguments:
- hidden_in: bfloat16 [16, 1024, 1024], P('pb', 'mem'), may hold values from -6 to 6
- encoder_rows: bfloat16 [8, 12, 256, 1024], P('pb', 'mem'), may hold values from -6 to 6
- passage_map: int32 [16, 8], P('pb'), may hold values from 0 to 11, as said below
- self_qkv: bfloat16 [3, 1024, 1024], P(None, 'mem'), may hold values from -0.1875 to 0.1875
- self_out: bfloat16 [1024, 1024], P('mem'), may hold values from -0.75 to 0.75
- cross_qkv: bfloat16 [3, 1024, 1024], P(None, 'mem'), may hold values from -0.1875 to 0.1875
- cross_out: bfloat16 [1024, 1024], P('mem'), may hold values from -0.75 to 0.75
- ffn_in: bfloat16 [1024, 4096], P('mem'), may hold values from -0.1875 to 0.1875
- ffn_out: bfloat16 [4096, 1024], P('mem'), may hold values from -0.09375 to 0.09375
- ffn_in_bias: bfloat16 [4096], P('mem'), may hold values from -3 to 3
- biases: bfloat16 [10, 1024], P(None, 'mem'), may hold values from -3 to 3
- gains: bfloat16 [3, 1024], P(None, 'mem'), may hold values from 0.5 to 1.5
- cotangent: bfloat16 [16, 1024, 1024], P('pb', 'mem'), may hold values from -6 to 6
Outputs:
- layer_out: bfloat16 [16, 1024, 1024], P('pb', 'mem')
- grad_in: float32 [16, 1024, 1024], P('pb', 'mem')
- grad_encoder: float32 [8, 12, 256, 1024], P('pb', 'mem')
- grad_self_qkv: float32 [3, 1024, 1024], P(None, 'mem')
- grad_self_out: float32 [1024, 1024], P('mem')
- grad_cross_qkv: float32 [3, 1024, 1024], P(None, 'mem')
- grad_cross_out: float32 [1024, 1024], P('mem')
- grad_ffn_in: float32 [1024, 4096], P('mem')
- grad_ffn_out: float32 [4096, 1024], P('mem')
- grad_ffn_in_bias: float32 [4096], P('mem')
- grad_biases: float32 [10, 1024], P(None, 'mem')
- grad_gains: float32 [3, 1024], P(None, 'mem')
The draws below stay inside these ranges and needn't reach their ends.
Inputs may be any that keep to these rules, and one draw needn't show every extreme that they name: `passage_map`: each question names 8 different passages of its own pb index, numbered within that index; every passage of an index is named by some question.
All inputs are finite; a program needn't handle non-finite values.
Results may differ from the reference program's by a relative error of at most 0.025.
Values may be sent and summed in bfloat16 or wider, within the bound.
A program may use at most 320 MiB of HBM per device.

```python
import jax
import jax.numpy as jnp
from jax import lax

D = 1024
H = 16
HD = 64
FF = 4096
LEN = 1024
QPG = 2
PLEN = 256
NPASS = 8
U_GRP = 12
QUEST = 16
N_PB = 8


def draw_passage_map(key, part):
    key = jax.random.fold_in(key, 7)
    starts = jnp.arange(QPG, dtype=jnp.int32) * (U_GRP - NPASS) // max(QPG - 1, 1)

    def one_group(group_key):
        order_key, slot_key = jax.random.split(group_key)
        order = jax.random.permutation(order_key, U_GRP)
        slots = jax.vmap(lambda inner_key: jax.random.permutation(inner_key, NPASS))(jax.random.split(slot_key, QPG))
        return order[starts[:, None] + slots]
    picked = jax.vmap(one_group)(jax.random.split(key, N_PB))
    return picked.reshape(N_PB * QPG, NPASS).astype(jnp.int32)


def steps_of(rng, extent, cuts, least, high):
    level = 1.0
    for axis_at, shards_of in cuts:
        heights = jax.random.uniform(jax.random.fold_in(jax.random.fold_in(rng, 6), axis_at), (shards_of,), jnp.float32, least / len(cuts), high / len(cuts))
        level = level * jnp.repeat(jnp.exp(heights), extent[axis_at] // shards_of).reshape((-1,) + (1,) * (len(extent) - 1 - axis_at))
    return level


def bell_draw(stream_key, dims, scale, limit, shards=(), held_as=jnp.bfloat16):
    values = jax.random.normal(stream_key, dims, jnp.float32) * scale
    if len(shards) > 0:
        values = steps_of(stream_key, dims, shards, -0.22, 0.18) * values
    return jnp.clip(values, min=-limit, max=limit).astype(held_as)


def setup_inputs(seed: int = 0) -> dict:
    key_list = jax.random.split(jax.random.key(seed), 14)
    return {
        "hidden_in": bell_draw(key_list[0], (QUEST, LEN, D), 1.0, 6.0, ((0, 8), (1, 4))),
        "encoder_rows": bell_draw(key_list[1], (N_PB, U_GRP, PLEN, D), 1.0, 6.0, ((0, 8), (1, 4))),
        "passage_map": draw_passage_map(jax.random.fold_in(key_list[13], 71), 0),
        "self_qkv": bell_draw(key_list[3], (3, D, D), D ** -0.5, 0.1875, ((1, 4),)),
        "self_out": bell_draw(key_list[4], (D, D), (D // 16) ** -0.5, 0.75, ((0, 4),)),
        "cross_qkv": bell_draw(key_list[5], (3, D, D), D ** -0.5, 0.1875, ((1, 4),)),
        "cross_out": bell_draw(key_list[6], (D, D), (D // 16) ** -0.5, 0.75, ((0, 4),)),
        "ffn_in": bell_draw(key_list[7], (D, FF), D ** -0.5, 0.1875, ((0, 4),)),
        "ffn_out": bell_draw(key_list[8], (FF, D), FF ** -0.5, 0.09375, ((0, 4),)),
        "ffn_in_bias": bell_draw(key_list[9], (FF,), 0.3, 3.0, ((0, 4),)),
        "biases": bell_draw(key_list[10], (10, D), 0.3, 3.0, ((1, 4),)),
        "gains": jnp.clip(1.0 + 0.1 * jax.random.normal(key_list[11], (3, D), jnp.float32), 0.5, 1.5).astype(jnp.bfloat16),
        "cotangent": bell_draw(key_list[12], (QUEST, LEN, D), 1.0, 6.0, ((0, 8), (1, 4))),
    }


@jax.custom_vjp
def low(v):
    return lax.optimization_barrier(v.astype(jnp.bfloat16)).astype(jnp.float32)

@jax.custom_vjp
def low_back(v):
    return v

def low_keep(v):
    return (low(v), None)

def low_pass(kept, grad):
    return (grad,)

def back_keep(v):
    return (v, None)

def back_low(kept, grad):
    return (low(grad),)
low.defvjp(low_keep, low_pass)
low_back.defvjp(back_keep, back_low)
highest = lax.Precision.HIGHEST

def matmul(left, right):
    return jnp.dot(left, right, precision=highest)

def both_ways(value):
    return low_back(low(value))

def layer_norm(values, gain, shift):
    centre = values - lax.optimization_barrier(jnp.mean(values, axis=-1, keepdims=True))
    spread = lax.optimization_barrier(jnp.mean(centre * centre, axis=-1, keepdims=True))
    return centre * lax.rsqrt(spread + 1e-05) * gain + shift

def attention(queries, key_rows, value_rows, allowed):
    scores = jnp.einsum('qhe,khe->hqk', queries, key_rows, precision=highest)
    scores = low_back(jnp.where(allowed[None], scores, -1000000000.0))
    largest = lax.optimization_barrier(jnp.max(scores, axis=-1, keepdims=True))
    expo = jnp.exp(scores - largest)
    probs = low(expo / lax.optimization_barrier(jnp.sum(expo, axis=-1, keepdims=True)))
    return jnp.einsum('hqk,khe->qhe', probs, value_rows, precision=highest)

def group_layer(params, tokens, memory, allowed_rows):
    self_qkv, self_out, cross_qkv, cross_out, ffn_in, ffn_out, ffn_in_bias, biases, gains = params
    flat = tokens.reshape(QPG * LEN, D)
    projected = jnp.einsum('te,ieo->tio', flat, self_qkv, precision=highest)
    queries = both_ways((projected[:, 0] + biases[0]) * 0.125)
    key_rows = both_ways(projected[:, 1])
    value_rows = both_ways(projected[:, 2] + biases[1])
    causal = jnp.arange(LEN)[None, :] <= jnp.arange(LEN)[:, None]

    def self_block(inputs):
        return attention(inputs[0], inputs[1], inputs[2], causal)
    mixed = lax.map(jax.checkpoint(self_block), (queries.reshape(QPG, LEN, H, HD), key_rows.reshape(QPG, LEN, H, HD), value_rows.reshape(QPG, LEN, H, HD)))
    attended = both_ways(mixed.reshape(QPG * LEN, D))
    self_branch = low_back(matmul(attended, self_out) + biases[2])
    first = layer_norm(flat + self_branch, gains[0], biases[6])
    first_low = low(first)
    cross_queries = both_ways((matmul(first_low, cross_qkv[0]) + biases[3]) * 0.125)
    memory_proj = jnp.einsum('te,ieo->tio', memory, cross_qkv[1:3], precision=highest)
    memory_keys = both_ways(memory_proj[:, 0]).reshape(U_GRP * PLEN, H, HD)
    memory_values = both_ways(memory_proj[:, 1] + biases[4]).reshape(U_GRP * PLEN, H, HD)

    def cross_block(inputs):
        return attention(inputs[0], memory_keys, memory_values, inputs[1][None, :])
    cross_mixed = lax.map(jax.checkpoint(cross_block), (cross_queries.reshape(QPG, LEN, H, HD), allowed_rows))
    cross_attended = both_ways(cross_mixed.reshape(QPG * LEN, D))
    cross_branch = low_back(matmul(cross_attended, cross_out) + biases[5])
    second = layer_norm(first + cross_branch, gains[1], biases[7])
    second_low = low(second)
    hidden = low_back(matmul(second_low, ffn_in) + ffn_in_bias)
    activated = low(jax.nn.gelu(hidden, approximate=False))
    ffn_branch = low_back(matmul(activated, ffn_out) + biases[9])
    result = layer_norm(second + ffn_branch, gains[2], biases[8])
    return result.reshape(QPG, LEN, D)

def reference(hidden_in, encoder_rows, passage_map, self_qkv, self_out, cross_qkv, cross_out, ffn_in, ffn_out, ffn_in_bias, biases, gains, cotangent):
    params = (self_qkv.astype(jnp.float32), self_out.astype(jnp.float32), cross_qkv.astype(jnp.float32), cross_out.astype(jnp.float32), ffn_in.astype(jnp.float32), ffn_out.astype(jnp.float32), ffn_in_bias.astype(jnp.float32), biases.astype(jnp.float32), gains.astype(jnp.float32))
    tokens = hidden_in.astype(jnp.float32)
    memory = encoder_rows.astype(jnp.float32)
    grouped_map = passage_map.reshape(N_PB, QPG, NPASS)
    member = jnp.any(grouped_map[:, :, :, None] == jnp.arange(U_GRP, dtype=jnp.int32)[None, None, None, :], axis=2)
    allowed = jnp.repeat(member, PLEN, axis=2)

    def whole(params_in, tokens_in, memory_in):

        def one_group(inputs):
            return group_layer(params_in, inputs[0], inputs[1], inputs[2])
        result = lax.map(jax.checkpoint(one_group), (tokens_in.reshape(N_PB, QPG, LEN, D), memory_in.reshape(N_PB, U_GRP * PLEN, D), allowed))
        return result.reshape(QUEST, LEN, D)
    output, pullback = jax.vjp(whole, params, tokens, memory)
    grad_params, grad_tokens, grad_memory = pullback(cotangent.astype(jnp.float32))
    return (output.astype(jnp.bfloat16), grad_tokens, grad_memory, grad_params[0], grad_params[1], grad_params[2], grad_params[3], grad_params[4], grad_params[5], grad_params[6], grad_params[7], grad_params[8])
```

```python
import functools

import jax
import jax.numpy as jnp
from jax import lax
from jax.experimental import pallas as pl
from jax.experimental.pallas import tpu as pltpu
from jax.sharding import PartitionSpec as P

HD = 64
PLEN = 256
BLK = 256
F32 = jnp.float32
BF16 = jnp.bfloat16

NN = (((1,), (0,)), ((), ()))
NT = (((1,), (1,)), ((), ()))


def mm(a, b, dims=NN):
    return lax.dot_general(a, b, dims, preferred_element_type=F32)


def head_mask_rows(block, head):
    rows = lax.broadcasted_iota(jnp.int32, block.shape, 0)
    return jnp.where((rows // HD) == head, block, jnp.zeros_like(block))


def head_rows(block, head, extra=None):
    block = block.astype(F32)
    rows = lax.broadcasted_iota(jnp.int32, block.shape, 0)
    out = jnp.where((rows // HD) == head, block, 0.0)
    if extra is not None:
        rest = -extra
        for i in range(3):
            term = rest.astype(BF16).astype(F32)
            rest = rest - term
            out = jnp.where(rows == (1 - head) * HD + i, term, out)
    return out.astype(BF16)


def ones_in(block, head):
    lanes = lax.broadcasted_iota(jnp.int32, block.shape, 1)
    first = (1 - head) * HD
    return jnp.where((lanes >= first) & (lanes < first + 3), jnp.ones_like(block), block)


def pick_heads(first, second):
    lanes = lax.broadcasted_iota(jnp.int32, first.shape, 1)
    return jnp.where(lanes < HD, first, second)


MESH = pl.DeviceIdType.MESH
ANY = pl.BlockSpec(memory_space=pl.ANY)
VMEM = pl.BlockSpec(memory_space=pltpu.VMEM)
PLANE = 4


def flip(index, bits):
    bit = 1
    while bit <= bits:
        if bits & bit:
            unit = jnp.int32(bit)
            index = index + unit - 2 * unit * lax.rem(lax.div(index, unit), jnp.int32(2))
        bit *= 2
    return index


class Place:
    def __init__(self, plane, planes=1):
        self.pb = lax.axis_index("pb")
        self.mem = lax.axis_index("mem")
        two = jnp.int32(2)
        self.core = lax.rem(self.pb, two)
        self.quarter = lax.rem(lax.div(self.pb, two), jnp.int32(plane))
        self.parity = lax.rem(self.mem, two)
        self.half = lax.div(self.mem, two)
        self.plane = plane
        self.planes = planes

    def near(self, t):
        return (flip(self.pb, 2 * t), self.mem)

    def far(self, r):
        return (flip(self.pb, 2 * self.plane * r), self.mem)

    def line(self, s):
        return (self.pb, flip(self.mem, s))

    def twin(self):
        return (flip(self.pb, 1), self.mem)

    def pair(self):
        return (self.pb, flip(self.mem, 1))

    def worker(self, k):
        return (self.pb - self.core + self.half, 2 * self.core + flip(self.parity, k))

    def at_home(self):
        return self.half == self.core

    def meet(self, peers):
        barrier = pltpu.get_barrier_semaphore()
        for pb_bits, mem_bits in peers:
            pl.semaphore_signal(
                barrier,
                inc=1,
                device_id=(flip(self.pb, pb_bits), flip(self.mem, mem_bits)),
                device_id_type=MESH,
            )
        pl.semaphore_wait(barrier, len(peers))


def column_peers(n_mem):
    return [(a, b) for a in range(2) for b in range(n_mem) if (a, b) != (0, 0)]


def plane_peers(plane):
    return [(2 * t, 0) for t in range(1, plane)]


class Sems:
    def __init__(self, ref):
        self.ref = ref
        self.used = 0

    def take(self, count):
        first = self.used
        self.used += count
        return [self.ref.at[first + i] for i in range(count)]


def remote(src, dst, send_sem, recv_sem, device):
    return pltpu.make_async_remote_copy(
        src_ref=src,
        dst_ref=dst,
        send_sem=send_sem,
        recv_sem=recv_sem,
        device_id=device,
        device_id_type=MESH,
    )


class Spread:
    def __init__(self, place, sems, src, dst, kinds=(0, 1)):
        self.place, self.src, self.dst, self.kinds = place, src, dst, kinds
        self.send = sems.take(2)
        self.recv = sems.take(2)

    def copy(self, k):
        return remote(self.src(k), self.dst(k), self.send[k], self.recv[k], self.place.worker(k))

    def start(self):
        for k in self.kinds:
            if k == 0:
                home = self.place.at_home()

                @pl.when(home)
                def _():
                    pltpu.make_async_copy(self.src(0), self.dst(0), self.recv[0]).start()

                @pl.when(jnp.logical_not(home))
                def _():
                    self.copy(0).start()
            else:
                self.copy(k).start()

    def wait_recv(self, k):
        if k == 0:
            home = self.place.at_home()

            @pl.when(home)
            def _():
                pltpu.make_async_copy(self.src(0), self.dst(0), self.recv[0]).wait()

            @pl.when(jnp.logical_not(home))
            def _():
                self.copy(0).wait_recv()
        else:
            self.copy(k).wait_recv()

    def wait_send(self):
        for k in self.kinds:
            if k == 0:

                @pl.when(jnp.logical_not(self.place.at_home()))
                def _():
                    self.copy(0).wait_send()
            else:
                self.copy(k).wait_send()


class Own:
    def __init__(self, place, sems, shard, full, columns, n_mem):
        self.copies = []
        mem, core = place.mem, place.core
        if columns:
            unit = full.shape[-1] // n_mem
            for b, sem in zip(range(n_mem), sems.take(n_mem)):
                start = pl.multiple_of(2 * unit * b + unit * core, unit)
                src = shard.at[:, :, :, pl.ds(start, unit)]
                dst = full.at[:, mem, :, :, pl.ds(unit * b, unit)]
                self.copies.append(pltpu.make_async_copy(src, dst, sem))
        else:
            (sem,) = sems.take(1)
            self.copies.append(pltpu.make_async_copy(shard.at[core], full.at[0, mem], sem))

    def start(self):
        for copy in self.copies:
            copy.start()

    def wait(self):
        for copy in self.copies:
            copy.wait()


class Line:
    def __init__(self, place, sems, src, dst, n_mem):
        send, recv = sems.take(n_mem - 1), sems.take(n_mem - 1)
        self.copies = [
            remote(src(s), dst(s), send[s - 1], recv[s - 1], place.line(s)) for s in range(1, n_mem)
        ]

    def start(self):
        for copy in self.copies:
            copy.start()

    def wait_recv(self, s):
        self.copies[s - 1].wait_recv()

    def wait_send(self):
        for copy in self.copies:
            copy.wait_send()


class Share:
    def __init__(self, place, sems, src, block):
        send, recv = sems.take(4), sems.take(4)
        rows = src.shape[-2]
        half = rows // 2

        def part(ref, i):
            return ref.at[:, pl.ds(i * half, half)]

        self.first = [
            remote(src, block(0), send[t - 1], recv[t - 1], place.near(t)) for t in (1, 2)
        ]
        self.second = [
            remote(part(block(t), t - 1), part(block(t), t - 1), send[t + 1], recv[t + 1], place.near(3 - t))
            for t in (1, 2)
        ]

    def start(self):
        for copy in self.first:
            copy.start()

    def forward(self):
        for direct, onward in zip(self.first, self.second):
            direct.wait_recv()
            onward.start()

    def wait(self):
        for copy in self.first:
            copy.wait_send()
        for copy in self.second:
            copy.wait()


class Chain:
    def __init__(self, place, sems, block, n_mem):
        self.place, self.block, self.n = place, block, n_mem
        self.sems = {way: (sems.take(n_mem - 1), sems.take(n_mem - 1)) for way in (1, -1)}

    def copy(self, way, hops):
        mem = self.place.mem
        source = lax.rem(mem + jnp.int32(self.n - way * hops), jnp.int32(self.n))
        target = lax.rem(mem + jnp.int32(self.n + way), jnp.int32(self.n))
        send, recv = self.sems[way]
        piece = self.block(source)
        return remote(piece, piece, send[hops], recv[hops], (self.place.pb, target))

    def comes(self, way, hops):
        mem = self.place.mem
        return mem >= hops if way == 1 else mem + hops < self.n

    def goes(self, way, hops):
        mem = self.place.mem
        ahead = mem + 1 < self.n if way == 1 else mem >= 1
        return jnp.logical_and(ahead, self.comes(way, hops))

    def start(self):
        for way in (1, -1):

            @pl.when(self.goes(way, 0))
            def _():
                self.copy(way, 0).start()

    def relay(self, hops, arrived):
        for way in (1, -1):

            @pl.when(self.comes(way, hops))
            def _():
                self.copy(way, hops - 1).wait_recv()
                if hops < self.n - 1:

                    @pl.when(self.goes(way, hops))
                    def _():
                        self.copy(way, hops).start()

                arrived(hops if way == 1 else self.n - hops)

    def wait_send(self):
        for hops in range(self.n - 1):
            for way in (1, -1):

                @pl.when(self.goes(way, hops))
                def _():
                    self.copy(way, hops).wait_send()


class Gather:
    def __init__(self, place, sems, shard, full, columns, n_mem, in_plane=True):
        mem, quarter = place.mem, place.quarter
        self.n_mem = n_mem
        self.in_plane = in_plane
        self.own = Own(place, sems, shard, full, columns, n_mem)
        self.chain = Chain(place, sems, lambda i: full.at[:, i, quarter], n_mem)
        self.shares = {}
        for d in range(1, n_mem if in_plane else 1):
            source = lax.rem(mem + jnp.int32(n_mem - d), jnp.int32(n_mem))

            def block(t, source=source):
                return full.at[:, source, flip(quarter, t)]

            self.shares[d] = Share(place, sems, block(0), block)

    def begin(self):
        self.own.wait()
        self.chain.start()

    def share(self, hops):
        self.chain.relay(hops, lambda d: self.shares[d].start() if self.in_plane else None)

    def forward(self, hops):
        for way, d in ((1, hops), (-1, self.n_mem - hops)):

            @pl.when(self.chain.comes(way, hops))
            def _():
                self.shares[d].forward()

    def finish(self):
        self.chain.wait_send()
        for share in self.shares.values():
            share.wait()


GATHER_SEMS = 44


def half_views(shard, columns, n_mem, plane):
    if columns:
        lead, depth, hidden = shard.shape
        part = depth // plane
        return shard.reshape(lead, plane, part, hidden), (lead, n_mem, plane, part, hidden // 2)
    depth, width = shard.shape
    part = depth // 2 // plane
    return shard.reshape(2, plane, part, width), (1, n_mem, plane, part, width)


class Walk:
    def __init__(self, refs):
        self.refs = list(refs)

    def take(self, count):
        out, self.refs = self.refs[:count], self.refs[count:]
        return out

    def one(self):
        return self.take(1)[0]


def softmax_units(units, finish, serve=None):
    def scores_of(unit, j):
        return unit[0][j]()

    ready = [scores_of(units[0], j) for j in range(len(units[0][0]))]
    for n, (_, values, tag) in enumerate(units):
        if serve is not None:
            serve(n)
        coming = list(range(len(units[n + 1][0]))) if n + 1 < len(units) else []
        following = []
        top = functools.reduce(
            jnp.maximum, [jnp.max(tile, axis=0, keepdims=True) for tile in ready]
        )
        total = jnp.zeros_like(top)
        acc = None
        share = -(-len(coming) // len(ready))
        for j, tile in enumerate(ready):
            for i in coming[j * share : (j + 1) * share]:
                following.append(scores_of(units[n + 1], i))
            probs = jnp.exp(tile - top)
            total += jnp.sum(probs, axis=0, keepdims=True)
            part = mm(values[j](), probs.astype(BF16))
            acc = part if acc is None else acc + part
        finish(tag, acc / total, top + jnp.log(total))
        ready = following


def self_attend(place, pair, q_vm, k_vm, v_vm, o_vm, lse_vm, v_t, o_t):
    base = 2 * place.core + place.parity
    count = q_vm.shape[0] // BLK
    lanes = pl.ds(pl.multiple_of(pair * 2 * HD, 2 * HD), 2 * HD)

    def rows(i):
        return pl.ds(pl.multiple_of(flip(base, i) * BLK, BLK), BLK)

    for j in range(count):
        v_t[:, j * BLK : (j + 1) * BLK] = v_vm[rows(j), lanes].T
    key_pos = lax.broadcasted_iota(jnp.int32, (BLK, BLK), 0)
    query_pos = lax.broadcasted_iota(jnp.int32, (BLK, BLK), 1)
    units = []
    for i in range(count):
        q_t = q_vm[rows(i), lanes].T
        for head in range(2):
            q_head = head_rows(q_t, head)

            def score(j, i=i, q_head=q_head):
                tile = mm(k_vm[rows(j), lanes], q_head)
                return jnp.where(key_pos <= query_pos, tile, -1000000000.0) if j == i else tile

            def value(j, head=head):
                return v_t[head * HD : (head + 1) * HD, j * BLK : (j + 1) * BLK]

            units.append(
                (
                    [functools.partial(score, j) for j in range(i + 1)],
                    [functools.partial(value, j) for j in range(i + 1)],
                    (i, head),
                )
            )

    def finish(tag, mixed, lse):
        i, head = tag
        span = slice(i * BLK, (i + 1) * BLK)
        o_t[head * HD : (head + 1) * HD, span] = mixed
        lse_vm[pair, head : head + 1, span] = lse

    softmax_units(units, finish)
    for i in range(count):
        o_vm[rows(i), lanes] = o_t[:, i * BLK : (i + 1) * BLK].T.astype(BF16)


def tiles(rows, step):
    def run(i, carry):
        step(pl.ds(pl.multiple_of(i * BLK, BLK), BLK))
        return carry

    lax.fori_loop(0, rows // BLK, run, 0)


def front_kernel(n_mem, plane, kinds, places, x_ref, enc_ref, map_ref, small_ref, *refs):
    refs = Walk(refs)
    count = len(kinds)
    shards = refs.take(count)
    x_out, enc_out, index_out, small_out = refs.take(4)
    halves = refs.take(count)
    kept = refs.take(11)
    x_vm, w_vm, so_vm, cq_w, small_vm = refs.take(5)
    q_vm, k_vm, v_vm, sa_vm, lse_vm, h1_vm, unit_vm, scale_vm, cq_vm = refs.take(9)
    k_all, v_all, v_t, o_t, part_vm, twin_vm, kv_w, enc_vm, map_in = refs.take(9)
    sems = Sems(refs.one())
    place = Place(plane)
    n_bias, n_gain = places
    rows = x_ref.shape[1]
    gathers = [
        Gather(place, sems, shard, half, columns, n_mem)
        for shard, half, columns in zip(shards, halves, kinds)
    ]
    spread = Spread(
        place,
        sems,
        lambda k: x_ref.at[flip(place.parity, k)],
        lambda k: x_out.at[pl.ds(rows * k, rows)],
    )
    twin_send, twin_recv = sems.take(2), sems.take(2)
    twin = [
        remote(
            x_out.at[pl.ds(rows * k, rows)],
            x_out.at[pl.ds(rows * (k + 2), rows)],
            twin_send[k],
            twin_recv[k],
            place.twin(),
        )
        for k in range(2)
    ]
    map_sems = sems.take(2)
    map_copy = remote(map_ref, map_in, map_sems[0], map_sems[1], place.twin())
    (small_sem,) = sems.take(1)
    small_own = pltpu.make_async_copy(small_ref, small_out.at[place.mem], small_sem)
    small_line = Line(
        place, sems, lambda s: small_ref, lambda s: small_out.at[place.mem], n_mem
    )
    units = enc_vm.shape[1]
    encs, enc_twins, enc_pairs, enc_onwards, enc_ends = [], [], [], [], []
    for u in range(units):
        encs.append(
            Spread(
                place, sems, lambda k, u=u: enc_ref.at[u], lambda k, u=u: enc_vm.at[0, u], kinds=(0,)
            )
        )
        pair_sems, twin_sems, end_sems = sems.take(2), sems.take(2), sems.take(2)
        enc_pairs.append(remote(enc_ref.at[u], enc_vm.at[1, u], *pair_sems, place.pair()))
        enc_onwards.append(remote(enc_vm.at[0, u], enc_vm.at[1, u], *pair_sems, place.pair()))
        enc_twins.append(remote(enc_vm.at[0, u], enc_vm.at[2, u], *twin_sems, place.twin()))
        enc_ends.append(remote(enc_vm.at[1, u], enc_vm.at[3, u], *end_sems, place.twin()))
    enc_keeps = [
        pltpu.make_async_copy(enc_vm.at[i], enc_out.at[i], sem) for i, sem in enumerate(sems.take(4))
    ]
    home = place.at_home()
    away = jnp.logical_not(home)
    loads = [
        pltpu.make_async_copy(src, dst, sem)
        for src, dst, sem in zip(
            (x_out, halves[0], halves[1], halves[2].at[0], small_out, halves[2].at[pl.ds(1, 2)]),
            (x_vm, w_vm, so_vm, cq_w, small_vm, kv_w),
            sems.take(6),
        )
    ]
    keeps = [
        pltpu.make_async_copy(src, dst, sem)
        for src, dst, sem in zip(
            (q_vm, k_vm, v_vm, sa_vm, lse_vm, h1_vm, unit_vm, scale_vm, cq_vm, k_all, v_all),
            kept,
            sems.take(11),
        )
    ]
    swap_sems = sems.take(4)
    own = 2 * rows
    swap_part = remote(part_vm, twin_vm, swap_sems[0], swap_sems[1], place.twin())
    swap_h1 = remote(
        h1_vm.at[pl.ds(0, own)], h1_vm.at[pl.ds(own, own)], swap_sems[2], swap_sems[3], place.twin()
    )

    for gather in gathers:
        gather.own.start()
    small_own.start()
    place.meet(column_peers(n_mem) + plane_peers(plane))
    for gather in gathers:
        gather.begin()
    small_line.start()
    map_copy.start()
    spread.start()
    for gather in gathers:
        gather.share(1)
    for gather in gathers:
        gather.share(2)
    gathers[0].forward(1)
    for k in range(2):
        spread.wait_recv(k)
        twin[k].start()
    for gather in gathers:
        gather.share(3)
    for u in range(units):
        encs[u].start()

        @pl.when(home)
        def _():
            enc_pairs[u].start()

    def first_arrival(u):
        encs[u].wait_recv(0)

        @pl.when(away)
        def _():
            enc_onwards[u].start()

        enc_twins[u].start()

    def second_arrival(u):
        @pl.when(home)
        def _():
            enc_pairs[u].wait()

        @pl.when(away)
        def _():
            enc_onwards[u].wait()

        enc_ends[u].start()

    for hops in (2, 3):
        gathers[0].forward(hops)
    for hops in (1, 2, 3):
        for gather in gathers[1:]:
            gather.forward(hops)
    for copy in twin:
        copy.wait_recv()
    small_own.wait()
    for s in range(1, n_mem):
        small_line.wait_recv(s)
    gathers[0].finish()
    for copy in (loads[0], loads[1], loads[4]):
        copy.start()
    for copy in (loads[0], loads[1], loads[4]):
        copy.wait()

    def half_row(row):
        lanes = pl.ds(pl.multiple_of(place.core * 2 * HD, 2 * HD), 2 * HD)
        return jnp.concatenate(
            [small_vm[b, :, lanes].astype(F32)[row : row + 1] for b in range(n_mem)], axis=1
        )

    def full_row(row):
        return jnp.concatenate(
            [small_vm[b].astype(F32)[row : row + 1] for b in range(n_mem)], axis=1
        )

    bias_q, bias_v = half_row(0), half_row(1)
    depth = x_vm.shape[1]

    def weight(ref):
        return ref[...].reshape(-1, ref.shape[-1])

    def project(span):
        x_tile = x_vm[span, :]
        q_vm[span, :] = ((mm(x_tile, weight(w_vm.at[0])) + bias_q) * 0.125).astype(BF16)
        k_vm[span, :] = mm(x_tile, weight(w_vm.at[1])).astype(BF16)
        v_vm[span, :] = (mm(x_tile, weight(w_vm.at[2])) + bias_v).astype(BF16)

    tiles(x_vm.shape[0], project)
    for copy in keeps[:3]:
        copy.start()
    pairs = q_vm.shape[1] // (2 * HD)
    for pair in range(pairs):
        self_attend(place, pair, q_vm, k_vm, v_vm, sa_vm, lse_vm, v_t, o_t)
        if pair in (0, pairs // 2):
            first_arrival(min(pair, 1))
    for copy in keeps[3:5]:
        copy.start()
    for gather in gathers[1:]:
        gather.finish()
    for copy in (loads[2], loads[3], loads[5]):
        copy.start()
    for copy in (loads[2], loads[3], loads[5]):
        copy.wait()

    def other_part(span):
        part_vm[span, :] = mm(
            sa_vm[pl.ds(pl.multiple_of(span.start + own, BLK), BLK), :], weight(so_vm)
        ).astype(BF16)

    tiles(own, other_part)
    swap_part.start()

    def own_part(span):
        unit_vm[span, :] = mm(sa_vm[span, :], weight(so_vm)) + x_vm[span, :].astype(F32)

    tiles(own, own_part)
    for u in range(2, units):
        first_arrival(u)
    bias_out = full_row(2)
    gain, shift = full_row(n_bias), full_row(6)
    swap_part.wait()

    def normalise(span):
        values = unit_vm[span, :] + twin_vm[span, :].astype(F32) + bias_out
        centre = values - jnp.mean(values, axis=-1, keepdims=True)
        scale = lax.rsqrt(jnp.mean(centre * centre, axis=-1, keepdims=True) + 1e-05)
        unit = centre * scale
        unit_vm[span, :] = unit
        scale_vm[span, :] = jnp.broadcast_to(scale, (BLK, scale_vm.shape[1]))
        h1_vm[span, :] = (unit * gain + shift).astype(BF16)

    tiles(own, normalise)
    swap_h1.start()
    for copy in keeps[6:8]:
        copy.start()
    bias_cq = half_row(3)

    def queries(span):
        cq_vm[span, :] = ((mm(h1_vm[span, :], weight(cq_w)) + bias_cq) * 0.125).astype(BF16)

    tiles(own, queries)
    swap_h1.wait()
    keeps[5].start()

    def other_queries(span):
        queries(pl.ds(pl.multiple_of(span.start + own, BLK), BLK))

    tiles(own, other_queries)
    keeps[8].start()

    map_copy.wait()
    near_map, far_map = map_ref[...], map_in[...]
    both_maps = jnp.where(home, near_map, far_map)
    mine = jnp.where(place.parity == 0, both_maps[:1], both_maps[1:])
    group = lax.div(mine, jnp.full_like(mine, units))
    index_out[...] = (group ^ (2 * place.core + place.parity)) * units + lax.rem(
        mine, jnp.full_like(mine, units)
    )

    bias_cv = half_row(4)

    def memory(block, u):
        rows_here = enc_vm[block, u]
        k_all[block * units + u] = mm(rows_here, weight(kv_w.at[0])).astype(BF16)
        v_all[block * units + u] = (mm(rows_here, weight(kv_w.at[1])) + bias_cv).astype(BF16)

    for u in range(units):
        second_arrival(u)
        memory(0, u)
    enc_keeps[0].start()
    enc_keeps[1].start()
    for block, copies in ((2, enc_twins), (1, None), (3, enc_ends)):
        for u in range(units):
            if copies is not None:
                copies[u].wait_recv()
            memory(block, u)
    enc_keeps[2].start()
    enc_keeps[3].start()
    for copy in keeps[9:]:
        copy.start()
    spread.wait_send()
    for copy in twin:
        copy.wait_send()
    small_line.wait_send()
    for item in encs:
        item.wait_send()
    for copy in enc_twins + enc_ends:
        copy.wait_send()
    for copy in keeps + enc_keeps:
        copy.wait()


def front(n_mem, plane, places, hidden_in, enc, passage_map, small, params):
    kinds = tuple(columns for _, columns in params)
    views = [half_views(shard, columns, n_mem, plane) for shard, columns in params]
    seg, width = hidden_in.shape[1:]
    rows, own = 4 * seg, 2 * seg
    part = width // 2
    pairs = part // (2 * HD)
    passages = 4 * enc.shape[0]
    shapes = (
        [((rows, width), BF16), ((4,) + enc.shape, BF16), ((1, passage_map.shape[1]), jnp.int32)]
        + [((n_mem,) + small.shape, BF16)]
        + [(full, BF16) for _, full in views]
    )
    kept = [
        ((rows, part), BF16),
        ((rows, part), BF16),
        ((rows, part), BF16),
        ((rows, part), BF16),
        ((pairs, 2, rows), F32),
        ((rows, width), BF16),
        ((own, width), F32),
        ((own, 2 * HD), F32),
        ((rows, part), BF16),
        ((passages, PLEN, part), BF16),
        ((passages, PLEN, part), BF16),
    ]
    scratch = [
        ((rows, width), BF16),
        (views[0][1], BF16),
        (views[1][1][1:], BF16),
        (views[2][1][1:], BF16),
        ((n_mem,) + small.shape, BF16),
    ] + kept + [
        ((2 * HD, rows), BF16),
        ((2 * HD, rows), F32),
        ((own, width), BF16),
        ((own, width), BF16),
        ((2,) + views[2][1][1:], BF16),
        ((4,) + enc.shape, BF16),
        (passage_map.shape, jnp.int32),
    ]
    scratch[2] = (views[1][1], BF16)
    outs = pl.pallas_call(
        functools.partial(front_kernel, n_mem, plane, kinds, places),
        in_specs=[VMEM] * (4 + len(params)),
        out_specs=[ANY, ANY, VMEM] + [ANY] * (len(shapes) + len(kept) - 3),
        out_shape=[jax.ShapeDtypeStruct(*item) for item in shapes + kept],
        scratch_shapes=[pltpu.VMEM(*item) for item in scratch]
        + [pltpu.SemaphoreType.DMA((90 + GATHER_SEMS * len(params),))],
        compiler_params=pltpu.CompilerParams(
            collective_id=0, has_side_effects=True, vmem_limit_bytes=60 * 2**20
        ),
        cost_estimate=pl.CostEstimate(
            flops=rows * width * part * 10, bytes_accessed=40 * 2**20, transcendentals=rows * rows * 8
        ),
        name="front",
    )(hidden_in, enc, passage_map, small, *[view for view, _ in views])
    count = 4 + len(params)
    return outs[:4], outs[4:count], outs[count:]


class PlaneSum:
    def __init__(self, place, sems, grad, own, bufs, rows, lanes=None):
        self.own = own
        self.from_near, self.via, self.add = bufs
        quarter = place.quarter
        first, count = rows
        half = count // 2
        self.lead, self.n_mem = own.shape[:2]
        lanes = pl.ds(*(lanes or (0, grad.shape[-1])))

        def piece(t, lo, size):
            return grad.at[:, :, flip(quarter, t), pl.ds(first + lo, size), lanes]

        loads = sems.take(3)
        self.loads = [pltpu.make_async_copy(piece(0, 0, count), own, loads[0])]
        send, recv = sems.take(6), sems.take(6)
        self.onward, self.direct, self.summed = [], [], []
        for t in (1, 2):
            lo = (t - 1) * half
            self.onward.append(
                remote(piece(3, lo, half), self.via.at[t - 1], send[t - 1], recv[t - 1], place.near(t))
            )
            self.direct.append(
                remote(
                    piece(t, lo, half),
                    self.from_near.at[t - 1, :, :, pl.ds(lo, half)],
                    send[t + 1],
                    recv[t + 1],
                    place.near(t),
                )
            )
            other = half - lo
            self.loads.append(
                pltpu.make_async_copy(piece(t, other, half), self.add.at[t - 1], loads[t])
            )
            self.summed.append(
                remote(
                    self.add.at[t - 1],
                    self.from_near.at[t - 1, :, :, pl.ds(other, half)],
                    send[t + 3],
                    recv[t + 3],
                    place.near(t),
                )
            )

    def start(self):
        for copy in self.onward + self.loads + self.direct:
            copy.start()

    def each(self, step):
        def run(i, carry):
            step(lax.div(i, jnp.int32(self.n_mem)), lax.rem(i, jnp.int32(self.n_mem)))
            return carry

        lax.fori_loop(0, self.lead * self.n_mem, run, 0)

    def middle(self):
        for copy in self.loads:
            copy.wait()
        for t in (1, 2):
            self.onward[2 - t].wait_recv()

            def add(l, m, t=t):
                total = self.add[t - 1, l, m].astype(F32) + self.via[2 - t, l, m].astype(F32)
                self.add[t - 1, l, m] = total.astype(BF16)

            self.each(add)
            self.summed[t - 1].start()

    def end(self):
        for copy in self.direct + self.summed:
            copy.wait_recv()

        def add(l, m):
            total = self.own[l, m].astype(F32)
            for t in range(2):
                total += self.from_near[t, l, m].astype(F32)
            self.own[l, m] = total.astype(BF16)

        self.each(add)

    def wait_send(self):
        for copy in self.onward + self.direct + self.summed:
            copy.wait_send()


class Settle:
    def __init__(self, place, sems, own, out, bufs, columns, n_mem, rows, lane=0):
        self.place, self.n_mem, self.columns, self.rows = place, n_mem, columns, rows
        self.lane = lane
        self.own, self.out = own, out
        self.line_in, self.far_in, self.slots = bufs
        quarter, mem, core = place.quarter, place.mem, place.core
        slots = self.slots

        def slot(t):
            return slots.at[flip(quarter, t), core]

        self.line = Line(
            place, sems, lambda s: own.at[:, flip(mem, s)], lambda s: self.line_in.at[s - 1], n_mem
        )
        others = place.planes - 1
        far_send, far_recv = sems.take(others), sems.take(others)
        self.far = [
            remote(slot(0), self.far_in.at[r - 1], far_send[r - 1], far_recv[r - 1], place.far(r))
            for r in range(1, place.planes)
        ]
        self.share = Share(place, sems, slot(0), slot)
        twin_send, twin_recv = sems.take(place.plane), sems.take(place.plane)
        self.twin = [
            remote(slot(t), slot(t), twin_send[t], twin_recv[t], place.twin())
            for t in range(place.plane)
        ]

    def start(self):
        self.line.start()

    def middle(self):
        for s in range(1, self.n_mem):
            self.line.wait_recv(s)
        quarter, core, mem = self.place.quarter, self.place.core, self.place.mem
        lead = self.own.shape[0]
        for l in range(lead):
            total = self.own[l, mem].astype(F32)
            for s in range(self.n_mem - 1):
                total += self.line_in[s, l].astype(F32)
            self.slots[quarter, core, l] = total.astype(BF16)
        if self.far:
            for copy in self.far:
                copy.start()
            for copy in self.far:
                copy.wait()
            for l in range(lead):
                total = self.slots[quarter, core, l].astype(F32)
                for r in range(len(self.far)):
                    total += self.far_in[r, l].astype(F32)
                self.slots[quarter, core, l] = total.astype(BF16)
        self.share.start()
        self.twin[0].start()

    def forward(self):
        self.share.forward()
        self.twin[1].start()
        self.twin[2].start()

    def end(self):
        self.share.wait()
        self.twin[3].start()
        for copy in self.twin:
            copy.wait()
        self.line.wait_send()
        lead = self.own.shape[0]
        wide = self.slots.shape[-1]
        first, count = self.rows
        for q in range(self.place.plane):
            for c in range(2):
                for l in range(lead):
                    if self.columns:
                        unit = self.out.shape[-1] // (2 * self.n_mem)
                        for b in range(wide // unit):
                            start = unit * (2 * (self.lane // unit + b) + c)
                            self.out[l, q, first : first + count, start : start + unit] = self.slots[
                                q, c, l, :, b * unit : (b + 1) * unit
                            ]
                    else:
                        self.out[c, q, first : first + count] = self.slots[q, c, l]


PLANE_SUM_SEMS = 15


def settle_sems(n_mem, plane, planes):
    return 2 * (n_mem - 1) + 2 * (planes - 1) + 8 + 2 * plane


def plane_sum_scratch(grad_shape, n_mem, count, cols=None):
    lead, cols = grad_shape[0], cols or grad_shape[-1]
    return [
        pltpu.VMEM((2, lead, n_mem, count, cols), BF16),
        pltpu.VMEM((2, lead, n_mem, count // 2, cols), BF16),
        pltpu.VMEM((2, lead, n_mem, count // 2, cols), BF16),
    ]


def settle_scratch(grad_shape, n_mem, plane, planes, count, cols=None):
    lead, cols = grad_shape[0], cols or grad_shape[-1]
    return [
        pltpu.VMEM((n_mem - 1, lead, count, cols), BF16),
        pltpu.VMEM((max(planes - 1, 1), lead, count, cols), BF16),
        pltpu.VMEM((plane, 2, lead, count, cols), BF16),
    ]


def sum_shape(grad_shape):
    lead, n_mem, _, rows, cols = grad_shape
    return jax.ShapeDtypeStruct((lead, n_mem, rows, cols), BF16)


def reduce_out(grad_shape, columns, plane):
    lead, _, _, rows, cols = grad_shape
    shape = (lead, plane, rows, 2 * cols) if columns else (2, plane, rows, cols)
    return jax.ShapeDtypeStruct(shape, BF16)


def reduce_peers(n_mem, plane, planes):
    return (
        [(1, 0)]
        + [(0, s) for s in range(1, n_mem)]
        + plane_peers(plane)
        + [(2 * plane * r, 0) for r in range(1, planes)]
    )


def whole(shape):
    return pl.BlockSpec(shape, lambda *grid: (0,) * len(shape))


class Fetch:
    def __init__(self, sems, src, dst):
        self.copy = pltpu.make_async_copy(src, dst, sems.take(1)[0])
        self.dst = dst
        self.here = False

    def start(self):
        self.copy.start()

    def get(self):
        if not self.here:
            self.copy.wait()
            self.here = True
        return self.dst


def unit_norm(values):
    centre = values - jnp.mean(values, axis=-1, keepdims=True)
    scale = lax.rsqrt(jnp.mean(centre * centre, axis=-1, keepdims=True) + 1e-05)
    return centre * scale, scale


def unit_norm_back(grad, unit, scale, gain):
    inner = grad * gain
    return (
        inner
        - jnp.mean(inner, axis=-1, keepdims=True)
        - unit * jnp.mean(inner * unit, axis=-1, keepdims=True)
    ) * scale


def feed_kernel(n_mem, plane, cot_ref, rows_ref, bias_ref, *refs):
    refs = Walk(refs)
    fetched = refs.take(4)
    out_part = refs.one()
    final_out, dca_ref, dz2_ref, sums_ref, bias_sum, own_out, dw_in, dw_co = refs.take(8)
    kept = refs.take(4)
    out_w = refs.one()
    cot_vm, h2_vm, unit_vm, scale_vm, act_vm, slope_vm, p_vm, part_vm, twin_vm = refs.take(9)
    final_vm, df_vm, dco_vm, dw_out = refs.take(4)
    bufs = refs.take(3)
    sems = Sems(refs.one())
    place = Place(plane)
    ca, unit1, w_co, w_in = [Fetch(sems, src, dst) for src, dst in zip(fetched, kept)]
    mem, quarter = place.mem, place.quarter
    pieces = [Fetch(sems, out_part.at[0, mem], out_w.at[0, mem])]
    shares = []
    for d in range(1, n_mem):
        source = lax.rem(mem + jnp.int32(n_mem - d), jnp.int32(n_mem))

        def place_of(t, source=source):
            return out_w.at[:, source, flip(quarter, t)]

        pieces.append(Fetch(sems, out_part.at[:, source, quarter], place_of(0)))
        shares.append(Share(place, sems, place_of(0), place_of))
    rows = h2_vm.shape[0]
    own = rows // 2
    seg = own // 2
    hidden = act_vm.shape[1]
    block = hidden // n_mem
    out_sum = PlaneSum(place, sems, dw_out, own_out, bufs, (0, dw_out.shape[3]))
    spread_cot = Spread(
        place,
        sems,
        lambda k: cot_ref.at[flip(place.parity, k)],
        lambda k: cot_vm.at[pl.ds(seg * k, seg)],
    )
    spread_final = Spread(
        place,
        sems,
        lambda k: final_vm.at[pl.ds(seg * k, seg)],
        lambda k: final_out.at[place.parity],
    )

    def swap(src, dst):
        send, recv = sems.take(2)
        return remote(src, dst, send, recv, place.twin())

    def half_lanes(ref, i):
        wide = ref.shape[1] // 2
        return ref.at[:, pl.ds(i * wide, wide)]

    swap_co = swap(part_vm, twin_vm)
    swap_h2 = swap(h2_vm.at[pl.ds(0, own)], h2_vm.at[pl.ds(own, own)])
    swap_ffn = [swap(half_lanes(part_vm, i), half_lanes(twin_vm, i)) for i in range(2)]
    swap_df = swap(df_vm.at[pl.ds(0, own)], df_vm.at[pl.ds(own, own)])
    swap_dh2 = [swap(half_lanes(part_vm, i), half_lanes(twin_vm, i)) for i in range(2)]
    swap_dco = swap(dco_vm.at[pl.ds(0, own)], dco_vm.at[pl.ds(own, own)])

    for item in [ca, w_co] + pieces + [unit1, w_in]:
        item.start()
    place.meet(column_peers(n_mem) + plane_peers(plane))
    spread_cot.start()
    for item in pieces:
        item.get()
    for share in shares:
        share.start()
    row = {name: rows_ref[i : i + 1, :] for i, name in enumerate(("g0", "b6", "b5", "g1", "b7", "b9", "g2", "b8"))}
    sums_ref[...] = jnp.zeros_like(sums_ref)
    bias_sum[...] = jnp.zeros_like(bias_sum)

    def after(span):
        return pl.ds(pl.multiple_of(span.start + own, BLK), BLK)

    ca, w_co = ca.get(), w_co.get()

    def co_other(span):
        part_vm[span, :] = mm(ca[after(span), :], w_co[...]).astype(BF16)

    tiles(own, co_other)
    swap_co.start()
    unit1 = unit1.get()

    def co_own(span):
        p_vm[span, :] = unit1[span, :] * row["g0"] + row["b6"] + mm(ca[span, :], w_co[...])

    tiles(own, co_own)
    swap_co.wait()

    def second_norm(span):
        values = p_vm[span, :] + twin_vm[span, :].astype(F32) + row["b5"]
        unit, scale = unit_norm(values)
        unit_vm[span, :] = unit
        scale_vm[span, :] = jnp.broadcast_to(scale, (BLK, scale_vm.shape[1]))
        h2_vm[span, :] = (unit * row["g1"] + row["b7"]).astype(BF16)

    tiles(own, second_norm)
    swap_h2.start()
    w_in = w_in.get()

    def forward(span):
        def part(i, carry):
            lanes = pl.ds(pl.multiple_of(i * block, block), block)
            pre = mm(h2_vm[span, :], w_in[:, lanes]) + bias_ref[:, lanes]
            cdf = 0.5 * (1.0 + lax.erf(pre * 0.7071067811865476))
            act_vm[span, lanes] = (pre * cdf).astype(BF16)
            density = jnp.exp(-0.5 * pre * pre) * 0.3989422804014327
            slope_vm[span, lanes] = (cdf + pre * density).astype(BF16)
            return carry

        lax.fori_loop(0, n_mem, part, 0)

    ours, others = pl.ds(0, own), pl.ds(own, own)
    width = h2_vm.shape[1]
    column = width // 2
    forward(ours)
    for share in shares:
        share.forward()
    swap_h2.wait()
    forward(others)
    for share in shares:
        share.wait()
    for i in range(2):
        lanes = slice(i * column, (i + 1) * column)
        weights = out_w[0, :, :, :, lanes].reshape(hidden, column)
        part_vm[:, lanes] = mm(act_vm[others, :], weights).astype(BF16)
        swap_ffn[i].start()
    p_vm[...] = mm(act_vm[ours, :], out_w[0].reshape(hidden, width))
    for k in range(2):
        spread_cot.wait_recv(k)
    for copy in swap_ffn:
        copy.wait()

    def third_norm(span):
        values = (
            unit_vm[span, :] * row["g1"]
            + row["b7"]
            + p_vm[span, :]
            + twin_vm[span, :].astype(F32)
            + row["b9"]
        )
        unit, scale = unit_norm(values)
        final_vm[span, :] = (unit * row["g2"] + row["b8"]).astype(BF16)
        grad = cot_vm[span, :].astype(F32)
        out = unit_norm_back(grad, unit, scale, row["g2"])
        dz2_ref[span, :] = out
        low = out.astype(BF16)
        df_vm[span, :] = low
        sums_ref[0:1, :] += jnp.sum(grad * unit, axis=0, keepdims=True)
        sums_ref[1:2, :] += jnp.sum(grad, axis=0, keepdims=True)
        sums_ref[2:3, :] += jnp.sum(low.astype(F32), axis=0, keepdims=True)

    tiles(own, third_norm)
    swap_df.start()
    spread_final.start()
    swap_df.wait()

    def out_weights(m, carry):
        lanes = pl.ds(pl.multiple_of(m * block, block), block)
        dw_out[0, m] = mm(act_vm[:, lanes].T, df_vm[...]).astype(BF16).reshape(dw_out.shape[2:])
        return carry

    lax.fori_loop(0, n_mem, out_weights, 0)
    out_sum.start()

    def hidden_grad(i, carry):
        lanes = pl.ds(pl.multiple_of(i * block, block), block)
        weights = out_w[0, i].reshape(block, width)
        grad = mm(df_vm[...], weights, NT) * slope_vm[:, lanes].astype(F32)
        low = grad.astype(BF16)
        slope_vm[:, lanes] = low
        bias_sum[:, lanes] = jnp.sum(low.astype(F32), axis=0, keepdims=True)
        return carry

    lax.fori_loop(0, n_mem, hidden_grad, 0)
    narrow = width // 4
    for i in range(2):
        for j in (2 * i, 2 * i + 1):
            lanes = slice(j * narrow, (j + 1) * narrow)
            grad = mm(slope_vm[...], w_in[lanes, :], NT)
            part_vm[:, lanes] = grad[own:].astype(BF16)
            dz2_ref[:, lanes] += grad[:own]
        swap_dh2[i].start()
    out_sum.middle()
    for copy in swap_dh2:
        copy.wait()

    def second_back(span):
        grad = dz2_ref[span, :] + twin_vm[span, :].astype(F32)
        unit = unit_vm[span, :]
        out = unit_norm_back(grad, unit, scale_vm[span, :1], row["g1"])
        dz2_ref[span, :] = out
        low = out.astype(BF16)
        dco_vm[span, :] = low
        sums_ref[3:4, :] += jnp.sum(grad * unit, axis=0, keepdims=True)
        sums_ref[4:5, :] += jnp.sum(grad, axis=0, keepdims=True)
        sums_ref[5:6, :] += jnp.sum(low.astype(F32), axis=0, keepdims=True)

    tiles(own, second_back)
    swap_dco.start()
    depth = h2_vm.shape[1] // n_mem

    def in_weights(m, carry):
        lanes = pl.ds(pl.multiple_of(m * depth, depth), depth)
        dw_in[0, m] = mm(h2_vm[:, lanes].T, slope_vm[...]).astype(BF16).reshape(dw_in.shape[2:])
        return carry

    lax.fori_loop(0, n_mem, in_weights, 0)
    swap_dco.wait()

    dca_ref[...] = mm(dco_vm[...], w_co[...], NT).astype(BF16)
    heads = ca.shape[1] // n_mem

    def co_weights(m, carry):
        lanes = pl.ds(pl.multiple_of(m * heads, heads), heads)
        dw_co[0, m] = mm(ca[:, lanes].T, dco_vm[...]).astype(BF16).reshape(dw_co.shape[2:])
        return carry

    lax.fori_loop(0, n_mem, co_weights, 0)
    out_sum.end()
    out_sum.wait_send()
    spread_cot.wait_send()
    for k in range(2):
        spread_final.wait_recv(k)
    spread_final.wait_send()


def feed(n_mem, plane, cotangent, vectors, bias, ca, unit1, w_co, w_in, w_out):
    rows, part = ca.shape
    width, hidden = w_in.shape
    own = rows // 2

    def grad_shape(depth, cols):
        return (1, n_mem, plane, depth // (n_mem * plane), cols)

    out_shape, in_shape = grad_shape(hidden, width), grad_shape(width, hidden)
    shapes = [
        jax.ShapeDtypeStruct((2, own // 2, width), BF16),
        jax.ShapeDtypeStruct((rows, part), BF16),
        jax.ShapeDtypeStruct((own, width), F32),
        jax.ShapeDtypeStruct((8, width), F32),
        jax.ShapeDtypeStruct((1, hidden), F32),
        sum_shape(out_shape),
        jax.ShapeDtypeStruct(in_shape, BF16),
        jax.ShapeDtypeStruct(grad_shape(part, width), BF16),
    ]
    fetched = [ca, unit1, w_co, w_in, w_out]
    scratch = [pltpu.VMEM(item.shape, item.dtype) for item in fetched] + [
        pltpu.VMEM((own, width), BF16),
        pltpu.VMEM((rows, width), BF16),
        pltpu.VMEM((own, width), F32),
        pltpu.VMEM((own, 2 * HD), F32),
        pltpu.VMEM((rows, hidden), BF16),
        pltpu.VMEM((rows, hidden), BF16),
        pltpu.VMEM((own, width), F32),
        pltpu.VMEM((own, width), BF16),
        pltpu.VMEM((own, width), BF16),
        pltpu.VMEM((own, width), BF16),
        pltpu.VMEM((rows, width), BF16),
        pltpu.VMEM((rows, width), BF16),
        pltpu.VMEM(out_shape, BF16),
    ]
    scratch += plane_sum_scratch(out_shape, n_mem, out_shape[3])
    scratch += [pltpu.SemaphoreType.DMA((PLANE_SUM_SEMS + 60,))]
    return pl.pallas_call(
        functools.partial(feed_kernel, n_mem, plane),
        in_specs=[VMEM] * 3 + [ANY] * len(fetched),
        out_specs=[ANY] + [VMEM] * (len(shapes) - 1),
        out_shape=shapes,
        scratch_shapes=scratch,
        compiler_params=pltpu.CompilerParams(
            vmem_limit_bytes=60 * 2**20, collective_id=1, has_side_effects=True
        ),
        cost_estimate=pl.CostEstimate(
            flops=rows * width * hidden * 12, bytes_accessed=40 * 2**20, transcendentals=rows * hidden * 2
        ),
        name="feed",
    )(cotangent, vectors, bias, *fetched)


def middle_kernel(n_mem, plane, planes, settled, slot_ref, member_ref, index_ref, *refs):
    refs = Walk(refs)
    dq_ref, dk_ref, dv_ref, wc_ref, scale_ref, gain_ref = refs.take(6)
    fetched = refs.take(6)
    ready = refs.take(len(settled))
    dsa_ref, dz1_ref, sums_ref, enc_out, own_cross, own_so = refs.take(6)
    outs = refs.take(len(settled))
    kept = refs.take(6)
    wk_t, wv_t, named_ref = refs.take(3)
    theirs, mine, twin_in, pair_in, dw_cross, dw_so, part_vm, twin_vm, dso_vm = refs.take(9)
    cross_bufs, so_bufs = refs.take(3), refs.take(3)
    settle_bufs = [refs.take(3) for _ in settled]
    sems = Sems(refs.one())
    place = Place(plane, planes)
    fetches = [Fetch(sems, src, dst) for src, dst in zip(fetched, kept)]
    h1_ref, enc_ref, dz2_ref, unit_ref, so_ref, sa_ref = kept
    settles = [
        Settle(
            place, sems, ready[i], outs[i], settle_bufs[i], columns, n_mem, (0, ready[i].shape[2])
        )
        for i, columns in enumerate(settled)
    ]
    cross_sum = PlaneSum(place, sems, dw_cross, own_cross, cross_bufs, (0, dw_cross.shape[3]))
    so_sum = PlaneSum(place, sems, dw_so, own_so, so_bufs, (0, dw_so.shape[3]))
    passages = mine.shape[0]
    units = passages // 2
    twin_sems = sems.take(2 * passages)
    twins = [
        remote(theirs.at[u], twin_in.at[u], twin_sems[2 * u], twin_sems[2 * u + 1], place.twin())
        for u in range(passages)
    ]
    pair_sems = sems.take(2 * units)
    pairs = [
        remote(
            mine.at[units + u], pair_in.at[u], pair_sems[2 * u], pair_sems[2 * u + 1], place.pair()
        )
        for u in range(units)
    ]
    homes = [
        Spread(place, sems, lambda k, u=u: mine.at[u], lambda k, u=u: enc_out.at[u], kinds=(0,))
        for u in range(units)
    ]
    swap_sems = sems.take(4)
    own = dz2_ref.shape[0]
    swap_part = remote(part_vm, twin_vm, swap_sems[0], swap_sems[1], place.twin())
    swap_dso = remote(
        dso_vm.at[pl.ds(0, own)], dso_vm.at[pl.ds(own, own)], swap_sems[2], swap_sems[3], place.twin()
    )

    for item in fetches:
        item.start()
    wk_t[...] = wc_ref[1].T
    wv_t[...] = wc_ref[2].T
    place.meet(
        column_peers(n_mem) + plane_peers(plane) + [(2 * plane * r, 0) for r in range(1, planes)]
    )
    for item in settles:
        item.start()

    def passage_grad(u):
        slot = slot_ref[u]
        value = mm(dk_ref[slot], wk_t[...]) + mm(dv_ref[slot], wv_t[...])
        return (value * member_ref[u]).astype(BF16)

    def add_twin(u):
        twins[u].wait_recv()

        def add(i, carry):
            span = pl.ds(pl.multiple_of(i * 64, 64), 64)
            total = mine[u, span, :].astype(F32) + twin_in[u, span, :].astype(F32)
            mine[u, span, :] = total.astype(BF16)
            return carry

        lax.fori_loop(0, PLEN // 64, add, 0)

    def send_home(u):
        add_twin(u)
        pairs[u].wait_recv()

        def add(i, carry):
            span = pl.ds(pl.multiple_of(i * 64, 64), 64)
            total = mine[u, span, :].astype(F32) + pair_in[u, span, :].astype(F32)
            mine[u, span, :] = total.astype(BF16)
            return carry

        lax.fori_loop(0, PLEN // 64, add, 0)
        homes[u].start()

    for group in (range(units, passages), range(units)):
        for u in group:
            theirs[u] = passage_grad(passages + u)
            twins[u].start()
        for u in group:
            mine[u] = passage_grad(u)
        if group.start:
            for u in group:
                add_twin(u)
                pairs[u - units].start()

    for item in fetches:
        item.get()
    for j in range(index_ref.shape[0]):
        named_ref[j * PLEN : (j + 1) * PLEN, :] = enc_ref[index_ref[j]]

    part = dw_cross.shape[-1]
    depth = h1_ref.shape[1] // n_mem

    def stacked(ref):
        return ref[...].reshape(-1, ref.shape[-1])

    def cross_weights(m, carry):
        lanes = pl.ds(pl.multiple_of(m * depth, depth), depth)
        split = dw_cross.shape[2:]
        dw_cross[0, m] = (
            (mm(h1_ref[:, lanes].T, dq_ref[...]) * 0.125).astype(BF16).reshape(split)
        )
        named_t = named_ref[:, lanes].T
        dw_cross[1, m] = mm(named_t, stacked(dk_ref)).astype(BF16).reshape(split)
        dw_cross[2, m] = mm(named_t, stacked(dv_ref)).astype(BF16).reshape(split)
        return carry

    lax.fori_loop(0, n_mem // 2, cross_weights, 0)
    send_home(0)
    lax.fori_loop(n_mem // 2, n_mem, cross_weights, 0)
    cross_sum.start()

    part_vm[...] = (mm(dq_ref[own:, :], wc_ref[0], NT) * 0.125).astype(BF16)
    swap_part.start()
    dz1_ref[...] = dz2_ref[...] + mm(dq_ref[:own, :], wc_ref[0], NT) * 0.125
    sums_ref[...] = jnp.zeros_like(sums_ref)
    sums_ref[3:4, :part] = 0.125 * jnp.sum(dq_ref[...].astype(F32), axis=0, keepdims=True)
    sums_ref[4:5, :part] = jnp.sum(stacked(dv_ref).astype(F32), axis=0, keepdims=True)
    send_home(1)
    swap_part.wait()
    gain = gain_ref[...]

    def norm(span):
        grad = dz1_ref[span, :] + twin_vm[span, :].astype(F32)
        unit = unit_ref[span, :]
        inner = grad * gain
        out = (
            inner
            - jnp.mean(inner, axis=-1, keepdims=True)
            - unit * jnp.mean(inner * unit, axis=-1, keepdims=True)
        ) * scale_ref[span, :1]
        dz1_ref[span, :] = out
        low = out.astype(BF16)
        dso_vm[span, :] = low
        sums_ref[0:1, :] += jnp.sum(grad * unit, axis=0, keepdims=True)
        sums_ref[1:2, :] += jnp.sum(grad, axis=0, keepdims=True)
        sums_ref[2:3, :] += jnp.sum(low.astype(F32), axis=0, keepdims=True)

    tiles(own, norm)
    swap_dso.start()
    cross_sum.middle()

    dsa_ref[:own, :] = mm(dso_vm[:own, :], so_ref[...], NT).astype(BF16)
    for u in range(2, units):
        send_home(u)
    swap_dso.wait()
    dsa_ref[own:, :] = mm(dso_vm[own:, :], so_ref[...], NT).astype(BF16)
    block = sa_ref.shape[1] // n_mem

    def so_weights(m, carry):
        lanes = pl.ds(pl.multiple_of(m * block, block), block)
        dw_so[0, m] = (
            mm(sa_ref[:, lanes].T, dso_vm[...]).astype(BF16).reshape(dw_so.shape[2:])
        )
        return carry

    lax.fori_loop(0, n_mem, so_weights, 0)
    so_sum.start()
    for item in settles:
        item.middle()
    cross_sum.end()
    for item in settles:
        item.forward()
    so_sum.middle()
    for item in settles:
        item.end()
    so_sum.end()
    cross_sum.wait_send()
    so_sum.wait_send()
    for copy in twins + pairs:
        copy.wait_send()
    for item in homes:
        item.wait_recv(0)
        item.wait_send()


def middle(
    n_mem, plane, planes, slot, member, index, dq, dk, dv, wc, so, sa, h1, enc, dz2, unit, scale, gain, ready
):
    rows, part = dq.shape
    width = h1.shape[1]
    own = rows // 2
    passages = slot.shape[0] // 2
    settled = tuple(columns for _, columns in ready)
    settled_shapes = [item.shape[:2] + (plane,) + item.shape[2:] for item, _ in ready]
    cross_shape = (3, n_mem, plane, width // (n_mem * plane), part)
    so_shape = (1, n_mem, plane, part // (n_mem * plane), width)
    shapes = [
        jax.ShapeDtypeStruct((rows, part), BF16),
        jax.ShapeDtypeStruct((own, width), F32),
        jax.ShapeDtypeStruct((8, width), F32),
        jax.ShapeDtypeStruct((passages // 2, PLEN, width), BF16),
        sum_shape(cross_shape),
        sum_shape(so_shape),
    ] + [reduce_out(shape, columns, plane) for shape, columns in zip(settled_shapes, settled)]
    fetched = [h1, enc, dz2, unit, so, sa]
    scratch = [pltpu.VMEM(item.shape, item.dtype) for item in fetched] + [
        pltpu.VMEM((part, width), BF16),
        pltpu.VMEM((part, width), BF16),
        pltpu.VMEM(dk.shape[:1] + (width,), BF16),
        pltpu.VMEM((passages, PLEN, width), BF16),
        pltpu.VMEM((passages, PLEN, width), BF16),
        pltpu.VMEM((passages, PLEN, width), BF16),
        pltpu.VMEM((passages // 2, PLEN, width), BF16),
        pltpu.VMEM(cross_shape, BF16),
        pltpu.VMEM(so_shape, BF16),
        pltpu.VMEM((own, width), BF16),
        pltpu.VMEM((own, width), BF16),
        pltpu.VMEM((rows, width), BF16),
    ]
    scratch += plane_sum_scratch(cross_shape, n_mem, cross_shape[3])
    scratch += plane_sum_scratch(so_shape, n_mem, so_shape[3])
    for shape in settled_shapes:
        scratch += settle_scratch(shape, n_mem, plane, planes, shape[3])
    count = (
        len(ready) * settle_sems(n_mem, plane, planes) + 2 * PLANE_SUM_SEMS + 2 * passages
        + passages + 4 * passages // 2 + 4 + 6
    )
    smem = pl.BlockSpec(memory_space=pltpu.SMEM)
    outs = pl.pallas_call(
        functools.partial(middle_kernel, n_mem, plane, planes, settled),
        in_specs=[smem, smem, smem] + [VMEM] * 6 + [ANY] * 6 + [VMEM] * len(ready),
        out_specs=[VMEM] * 3 + [ANY] + [VMEM] * (2 + len(ready)),
        out_shape=shapes,
        scratch_shapes=scratch + [pltpu.SemaphoreType.DMA((count,))],
        compiler_params=pltpu.CompilerParams(
            vmem_limit_bytes=60 * 2**20, collective_id=3, has_side_effects=True
        ),
        cost_estimate=pl.CostEstimate(
            flops=rows * part * width * 30, bytes_accessed=40 * 2**20, transcendentals=0
        ),
        name="middle",
    )(
        slot,
        member,
        index,
        dq,
        dk.reshape(-1, PLEN, part),
        dv.reshape(-1, PLEN, part),
        wc,
        scale,
        gain,
        *fetched,
        *[item for item, _ in ready],
    )
    return outs[:4], outs[4:6], outs[6:]


def self_attend_back(place, pair, q_vm, k_vm, v_vm, o_vm, do_vm, lse_vm, outs, scratch):
    dq_vm, dk_vm, dv_vm = outs
    q_a, do_a, k_t, q_h, do_h, p_vm, ds_vm = scratch
    base = 2 * place.core + place.parity
    count = q_vm.shape[0] // BLK
    lanes = pl.ds(pl.multiple_of(pair * 2 * HD, 2 * HD), 2 * HD)

    def rows(i):
        return pl.ds(pl.multiple_of(flip(base, i) * BLK, BLK), BLK)

    for i in range(count):
        span = slice(i * BLK, (i + 1) * BLK)
        q_a[span, :] = q_vm[rows(i), lanes]
        do_a[span, :] = do_vm[rows(i), lanes]
        k_t[:, span] = k_vm[rows(i), lanes].T
        q_t = q_a[span, :].T
        do_t = do_a[span, :].T
        prod = (do_a[span, :].astype(F32) * o_vm[rows(i), lanes].astype(F32)).T
        for head in range(2):
            delta = jnp.sum(prod[head * HD : (head + 1) * HD, :], axis=0, keepdims=True)
            q_h[head, :, span] = head_rows(q_t, head, lse_vm[pair, head : head + 1, span])
            do_h[head, :, span] = head_rows(do_t, head, delta)
    key_pos = lax.broadcasted_iota(jnp.int32, (BLK, BLK), 0)
    query_pos = lax.broadcasted_iota(jnp.int32, (BLK, BLK), 1)
    units = [(j, i, head) for j in range(count) for head in range(2) for i in range(j, count)]

    def products(unit):
        j, i, head = unit
        span = slice(i * BLK, (i + 1) * BLK)
        return (
            mm(ones_in(k_vm[rows(j), lanes], head), q_h[head, :, span]),
            mm(ones_in(v_vm[rows(j), lanes], head), do_h[head, :, span]),
        )

    ready = products(units[0])
    halves = {}
    for n, (j, i, head) in enumerate(units):
        coming = products(units[n + 1]) if n + 1 < len(units) else None
        scores, dprobs = ready
        probs = jnp.exp(scores)
        if i == j:
            probs = jnp.where(key_pos <= query_pos, probs, 0.0)
        keys, span = slice(j * BLK, (j + 1) * BLK), slice(i * BLK, (i + 1) * BLK)
        p_vm[head, keys, span] = probs.astype(BF16)
        ds_vm[head, keys, span] = (probs * dprobs).astype(BF16)
        if i == count - 1:
            late = slice(j * BLK, count * BLK)
            halves[head] = (
                mm(p_vm[head, keys, late], do_a[late, :]),
                mm(ds_vm[head, keys, late], q_a[late, :]),
            )
            if head == 1:
                dv_vm[rows(j), lanes] = pick_heads(halves[0][0], halves[1][0]).astype(BF16)
                dk_vm[rows(j), lanes] = pick_heads(halves[0][1], halves[1][1]).astype(BF16)
        ready = coming
    for i in range(count):
        span, keys = slice(i * BLK, (i + 1) * BLK), slice(0, (i + 1) * BLK)
        dq_t = jnp.concatenate(
            [
                mm(k_t[head * HD : (head + 1) * HD, keys], ds_vm[head, keys, span])
                for head in range(2)
            ],
            axis=0,
        )
        dq_vm[rows(i), lanes] = dq_t.T.astype(BF16) * BF16(0.125)


def last_kernel(n_mem, plane, planes, settled, chunks, *refs):
    refs = Walk(refs)
    q_ref, k_ref, v_ref, o_ref, do_ref, lse_ref, feed_ref, hidden_ref, middle_ref = refs.take(9)
    fetched = refs.take(3)
    ready = refs.take(len(settled))
    small_out, dx_out, self_out = refs.take(3)
    outs = refs.take(len(settled))
    x_ref, w_ref, dz1_ref = kept = refs.take(3)
    dq_vm, dk_vm, dv_vm = refs.take(3)
    attend_scratch = refs.take(7)
    x_t, dw_vm = refs.take(2)
    part_vm, twin_vm, dx_vm = refs.take(3)
    chunk_own = [refs.one() for _ in range(chunks)]
    chunk_bufs = [refs.take(3) for _ in range(chunks)]
    chunk_settle = [refs.take(3) for _ in range(chunks)]
    settle_bufs = [refs.take(3) for _ in settled]
    small_near, small_line, small_twin, small_far, small_sum, sem_ref = refs.take(6)
    sems = Sems(sem_ref)
    place = Place(plane, planes)
    fetches = [Fetch(sems, src, dst) for src, dst in zip(fetched, kept)]
    settles = [
        Settle(
            place, sems, ready[i], outs[i], settle_bufs[i], columns, n_mem, (0, ready[i].shape[2])
        )
        for i, columns in enumerate(settled)
    ]
    rows, part = q_ref.shape
    lanes = part // chunks
    depth = dw_vm.shape[3]
    sums = [
        PlaneSum(
            place, sems, dw_vm, chunk_own[c], chunk_bufs[c], (0, depth), (c * lanes, lanes)
        )
        for c in range(chunks)
    ]
    ends = [
        Settle(
            place, sems, chunk_own[c], self_out, chunk_settle[c], True, n_mem, (0, depth), c * lanes
        )
        for c in range(chunks)
    ]
    near_sems = sems.take(6)
    near = [
        remote(
            small_sum, small_near.at[t - 1], near_sems[2 * t - 2], near_sems[2 * t - 1], place.near(t)
        )
        for t in range(1, plane)
    ]
    line = Line(
        place, sems, lambda s: small_sum.at[flip(place.mem, s)], lambda s: small_line.at[s - 1], n_mem
    )
    twin_sems = sems.take(2)
    twin = remote(small_sum.at[place.mem], small_twin, twin_sems[0], twin_sems[1], place.twin())
    far_sems = sems.take(2 * (planes - 1))
    far = [
        remote(
            small_sum.at[place.mem],
            small_far.at[r - 1],
            far_sems[2 * r - 2],
            far_sems[2 * r - 1],
            place.far(r),
        )
        for r in range(1, planes)
    ]
    seg = dx_out.shape[1]
    own = 2 * seg
    spread = Spread(
        place,
        sems,
        lambda k: dx_vm.at[pl.ds(seg * k, seg)],
        lambda k: dx_out.at[place.parity],
    )
    swap_sems = sems.take(2)
    swap_part = remote(part_vm, twin_vm, swap_sems[0], swap_sems[1], place.twin())

    for item in fetches:
        item.start()
    place.meet(
        column_peers(n_mem) + plane_peers(plane) + [(2 * plane * r, 0) for r in range(1, planes)]
    )
    for item in settles:
        item.start()
    block = x_ref.shape[1] // n_mem

    def input_part(span):
        return (
            mm(dq_vm[span, :], w_ref[0], NT)
            + mm(dk_vm[span, :], w_ref[1], NT)
            + mm(dv_vm[span, :], w_ref[2], NT)
        )

    pairs = part // (2 * HD)
    late = []
    for c in range(chunks):
        for pair in range(c * pairs // chunks, (c + 1) * pairs // chunks):
            self_attend_back(
                place,
                pair,
                q_ref,
                k_ref,
                v_ref,
                o_ref,
                do_ref,
                lse_ref,
                (dq_vm, dk_vm, dv_vm),
                attend_scratch,
            )
        if c == 0:
            for item in fetches:
                item.get()
            for m in range(n_mem):
                x_t[m] = x_ref[:, m * block : (m + 1) * block].T
        span = slice(c * lanes, (c + 1) * lanes)

        def weights(m, carry, span=span):
            for i, grad in enumerate((dq_vm, dk_vm, dv_vm)):
                dw_vm[i, m, :, :, span] = (
                    mm(x_t[m], grad[:, span]).astype(BF16).reshape(plane, depth, lanes)
                )
            return carry

        if c < chunks - 2:
            lax.fori_loop(0, n_mem, weights, 0)
            sums[c].start()
        if c == 1:
            sums[0].middle()
        if c == 2:
            for item in settles:
                item.middle()
            sums[0].end()
            ends[0].start()
            sums[1].middle()
        late.append(weights)
    part_vm[...] = input_part(slice(own, 2 * own)).astype(BF16)
    swap_part.start()
    lax.fori_loop(0, n_mem, late[-2], 0)
    sums[-2].start()
    swap_part.wait()
    total = dz1_ref[...] + input_part(slice(0, own)) + twin_vm[...].astype(F32)
    dx_vm[...] = total.astype(BF16)
    spread.start()
    lax.fori_loop(0, n_mem, late[-1], 0)
    sums[-1].start()
    sums[1].end()
    ends[1].start()
    for item in settles:
        item.forward()
    sums[-2].middle()

    small_sum[...] = jnp.zeros_like(small_sum)
    wide = small_sum.shape[2]
    unit = wide // 2
    first = place.core == 0
    for row, ref, at in (
        (2, middle_ref, 2),
        (5, feed_ref, 5),
        (6, middle_ref, 1),
        (7, feed_ref, 4),
        (8, feed_ref, 1),
        (9, feed_ref, 2),
        (10, middle_ref, 0),
        (11, feed_ref, 3),
        (12, feed_ref, 0),
    ):
        for b in range(n_mem):
            small_sum[b, row : row + 1, :] = ref[at : at + 1, b * wide : (b + 1) * wide]
    for row, value in (
        (0, jnp.sum(dq_vm[...].astype(F32), axis=0, keepdims=True)),
        (1, jnp.sum(dv_vm[...].astype(F32), axis=0, keepdims=True)),
        (3, middle_ref[3:4, :part]),
        (4, middle_ref[4:5, :part]),
    ):
        for b in range(n_mem):
            side = value[:, b * unit : (b + 1) * unit]
            none = jnp.zeros_like(side)
            small_sum[b, row : row + 1, :unit] = jnp.where(first, side, none)
            small_sum[b, row : row + 1, unit:] = jnp.where(first, none, side)
    count = hidden_ref.shape[1] // (n_mem * wide)
    for b in range(n_mem):
        for i in range(count):
            at = (b * count + i) * wide
            side = hidden_ref[:, at : at + wide]
            none = jnp.zeros_like(side)
            row = 13 + i
            small_sum[b, row : row + 1, :] = jnp.where(first, side, none)
            small_sum[b, row + count : row + count + 1, :] = jnp.where(first, none, side)
    for copy in near:
        copy.start()
    sums[-1].middle()
    sums[-2].end()
    ends[-2].start()
    ends[0].middle()
    for copy in near:
        copy.wait()
    total = small_sum[...]
    for t in range(plane - 1):
        total += small_near[t]
    small_sum[...] = total
    line.start()
    sums[-1].end()
    ends[-1].start()
    ends[1].middle()
    ends[0].forward()
    for item in settles:
        item.end()
    ends[-2].middle()
    ends[1].forward()
    for s in range(1, n_mem):
        line.wait_recv(s)
    line.wait_send()
    value = small_sum[place.mem]
    for s in range(n_mem - 1):
        value += small_line[s]
    small_sum[place.mem] = value
    twin.start()
    ends[-1].middle()
    ends[-2].forward()
    for item in ends[:-2]:
        item.end()
    twin.wait()
    value = small_sum[place.mem] + small_twin[...]
    if far:
        small_sum[place.mem] = value
        for copy in far:
            copy.start()
        for copy in far:
            copy.wait()
        for r in range(planes - 1):
            value += small_far[r]
    small_out[...] = value
    ends[-1].forward()
    ends[-2].end()
    ends[-1].end()
    for item in sums:
        item.wait_send()
    for k in range(2):
        spread.wait_recv(k)
    spread.wait_send()


def last(n_mem, plane, planes, q, k, v, o, do, lse, x, w, dz1, sums, small_shape, ready):
    rows, part = q.shape
    chunks = part // (2 * HD)
    width = x.shape[1]
    own = rows // 2
    settled = tuple(columns for _, columns in ready)
    settled_shapes = [item.shape[:2] + (plane,) + item.shape[2:] for item, _ in ready]
    grad_shape = (3, n_mem, plane, width // (n_mem * plane), part)
    depth, lanes = grad_shape[3], part // chunks
    small_part = small_shape[1:]
    shapes = [
        jax.ShapeDtypeStruct(small_part, F32),
        jax.ShapeDtypeStruct((2, own // 2, width), BF16),
        reduce_out(grad_shape, True, plane),
    ] + [reduce_out(shape, columns, plane) for shape, columns in zip(settled_shapes, settled)]
    fetched = [x, w, dz1]
    scratch = (
        [pltpu.VMEM(item.shape, item.dtype) for item in fetched]
        + [pltpu.VMEM((rows, part), BF16)] * 3
        + [
            pltpu.VMEM((rows, 2 * HD), BF16),
            pltpu.VMEM((rows, 2 * HD), BF16),
            pltpu.VMEM((2 * HD, rows), BF16),
            pltpu.VMEM((2, 2 * HD, rows), BF16),
            pltpu.VMEM((2, 2 * HD, rows), BF16),
            pltpu.VMEM((2, rows, rows), BF16),
            pltpu.VMEM((2, rows, rows), BF16),
            pltpu.VMEM((n_mem, width // n_mem, rows), BF16),
            pltpu.VMEM(grad_shape, BF16),
        ]
        + [pltpu.VMEM((own, width), BF16)] * 3
        + [pltpu.VMEM((3, n_mem, depth, lanes), BF16)] * chunks
    )
    for _ in range(chunks):
        scratch += plane_sum_scratch(grad_shape, n_mem, depth, lanes)
    for _ in range(chunks):
        scratch += settle_scratch(grad_shape, n_mem, plane, planes, depth, lanes)
    for shape in settled_shapes:
        scratch += settle_scratch(shape, n_mem, plane, planes, shape[3])
    scratch += [
        pltpu.VMEM((plane - 1,) + small_shape, F32),
        pltpu.VMEM((n_mem - 1,) + small_part, F32),
        pltpu.VMEM(small_part, F32),
        pltpu.VMEM((max(planes - 1, 1),) + small_part, F32),
        pltpu.VMEM(small_shape, F32),
        pltpu.SemaphoreType.DMA(
            (
                (len(ready) + chunks) * settle_sems(n_mem, plane, planes)
                + chunks * PLANE_SUM_SEMS
                + 24
                + 2 * planes,
            )
        ),
    ]
    outs = pl.pallas_call(
        functools.partial(last_kernel, n_mem, plane, planes, settled, chunks),
        in_specs=[VMEM] * 9 + [ANY] * 3 + [VMEM] * len(ready),
        out_specs=[VMEM, ANY, VMEM] + [VMEM] * len(ready),
        out_shape=shapes,
        scratch_shapes=scratch,
        compiler_params=pltpu.CompilerParams(
            vmem_limit_bytes=60 * 2**20, collective_id=4, has_side_effects=True
        ),
        cost_estimate=pl.CostEstimate(
            flops=rows * rows * width * 40, bytes_accessed=40 * 2**20, transcendentals=rows * rows * 8
        ),
        name="last",
    )(q, k, v, o, do, lse, *sums, *fetched, *[item for item, _ in ready])
    return outs[0], outs[1], outs[2:]


def cross_forward_kernel(n_mem, plane, kinds, index_ref, q_ref, k_ref, v_ref, *refs):
    refs = Walk(refs)
    count_w = len(kinds)
    shards = refs.take(count_w)
    o_ref, lse_ref = refs.take(2)
    halves = refs.take(count_w)
    v_t, o_t, sem_ref = refs.take(3)
    sems = Sems(sem_ref)
    place = Place(plane)
    step = pl.program_id(0) * pl.num_programs(1) + pl.program_id(1)
    last = pl.num_programs(0) * pl.num_programs(1) - 1
    gathers = [
        Gather(place, sems, shard, half, columns, n_mem, i != 1)
        for i, (shard, half, columns) in enumerate(zip(shards, halves, kinds))
    ]
    @pl.when(step == 0)
    def _():
        for gather in gathers:
            gather.own.start()
        place.meet(column_peers(n_mem) + plane_peers(plane))
        for gather in gathers:
            gather.begin()

    rows = q_ref.shape[0]
    count = index_ref.shape[0]

    @pl.when(pl.program_id(1) == 0)
    def _():
        for j in range(count):
            v_t[:, j * BLK : (j + 1) * BLK] = v_ref[index_ref[j]].T

    units = []
    for i in range(rows // BLK):
        q_t = q_ref[i * BLK : (i + 1) * BLK, :].T
        for head in range(2):
            q_head = head_rows(q_t, head)

            def score(j, q_head=q_head):
                return mm(k_ref[index_ref[j]], q_head)

            def value(j, head=head):
                return v_t[head * HD : (head + 1) * HD, j * BLK : (j + 1) * BLK]

            units.append(
                (
                    [functools.partial(score, j) for j in range(count)],
                    [functools.partial(value, j) for j in range(count)],
                    (i, head),
                )
            )

    def finish(tag, mixed, lse):
        i, head = tag
        span = slice(i * BLK, (i + 1) * BLK)
        o_t[head * HD : (head + 1) * HD, span] = mixed
        lse_ref[0, head : head + 1, span] = lse

    whole_one, line_one, small_one = gathers
    plan = {
        4: [(whole_one.share, 1), (small_one.share, 1)],
        6: [(line_one.share, 1)],
        10: [(whole_one.share, 2), (small_one.share, 2)],
        12: [(line_one.share, 2), (whole_one.forward, 1), (small_one.forward, 1)],
        17: [(whole_one.share, 3), (small_one.share, 3)],
        19: [(line_one.share, 3), (whole_one.forward, 2), (small_one.forward, 2)],
        24: [(whole_one.forward, 3), (small_one.forward, 3)],
    }

    def serve(n):
        for when, calls in plan.items():
            if when % len(units) == n:

                @pl.when(step == when // len(units))
                def _():
                    for call, hops in calls:
                        call(hops)

    softmax_units(units, finish, serve)
    o_ref[...] = o_t[...].T.astype(BF16)

    @pl.when(step == last)
    def _():
        for gather in gathers:
            gather.finish()


def cross_forward(n_mem, plane, index, q, k, v, params):
    rows, width = q.shape
    pairs = width // (2 * HD)
    keys = index.shape[0] * PLEN
    block = 2 * BLK
    question = pl.BlockSpec((block, 2 * HD), lambda h, i: (i, h))
    memory = pl.BlockSpec(k.shape[:2] + (2 * HD,), lambda h, i: (0, 0, h))
    kinds = tuple(columns for _, columns in params)
    views = [half_views(shard, columns, n_mem, plane) for shard, columns in params]
    outs = pl.pallas_call(
        functools.partial(cross_forward_kernel, n_mem, plane, kinds),
        grid=(pairs, rows // block),
        in_specs=[pl.BlockSpec(memory_space=pltpu.SMEM), question, memory, memory]
        + [whole(view.shape) for view, _ in views],
        out_specs=[question, pl.BlockSpec((1, 2, block), lambda h, i: (h, 0, i))]
        + [ANY] * len(params),
        out_shape=[
            jax.ShapeDtypeStruct((rows, width), BF16),
            jax.ShapeDtypeStruct((pairs, 2, rows), F32),
        ]
        + [jax.ShapeDtypeStruct(full, BF16) for _, full in views],
        scratch_shapes=[
            pltpu.VMEM((2 * HD, keys), BF16),
            pltpu.VMEM((2 * HD, block), F32),
            pltpu.SemaphoreType.DMA((4 + GATHER_SEMS * len(params),)),
        ],
        compiler_params=pltpu.CompilerParams(
            vmem_limit_bytes=60 * 2**20, collective_id=2, has_side_effects=True
        ),
        cost_estimate=pl.CostEstimate(
            flops=rows * keys * width * 16,
            bytes_accessed=rows * width * 4 + k.size * 4,
            transcendentals=rows * keys * pairs * 2,
        ),
        name="cross_forward",
    )(index, q, k, v, *[view for view, _ in views])
    return outs[:2], outs[2:]


def cross_backward_kernel(
    n_mem, plane, planes, chunks, settled, index_ref, q_ref, k_ref, v_ref, o_ref, do_ref, lse_ref, *refs
):
    refs = Walk(refs)
    kinds = {which: columns for which, columns, _ in chunks}
    grads = refs.take(len(kinds))
    ready = refs.take(len(settled))
    dq_ref, dk_ref, dv_ref = refs.take(3)
    outs = refs.take(len(kinds))
    ready_outs = refs.take(len(settled))
    q_h, do_h, dq_t, p_vm, ds_vm = refs.take(5)
    sems = Sems(refs.refs[-1])
    place = Place(plane, planes)
    sums, settles = [], []
    for which, columns, rows_of in chunks:
        own = refs.one()
        sums.append(PlaneSum(place, sems, grads[which], own, refs.take(3), rows_of))
        settles.append(
            Settle(place, sems, own, outs[which], refs.take(3), columns, n_mem, rows_of)
        )
    first = [
        Settle(
            place, sems, ready[i], ready_outs[i], refs.take(3), columns, n_mem, (0, ready[i].shape[2])
        )
        for i, columns in enumerate(settled)
    ]
    passage = pl.program_id(1)
    step = pl.program_id(0) * pl.num_programs(1) + passage
    steps = pl.num_programs(0) * pl.num_programs(1)
    rows = q_ref.shape[0]
    count = rows // BLK

    @pl.when(step == 0)
    def _():
        place.meet(
            column_peers(n_mem) + plane_peers(plane) + [(2 * plane * r, 0) for r in range(1, planes)]
        )
        for item in first:
            item.start()

    def at(when, *calls):
        @pl.when(step == when)
        def _():
            for call in calls:
                call()

    for i, (plane_sum, settle) in enumerate(zip(sums, settles)):
        at(3 * i, plane_sum.start)
        at(3 * i + 2, plane_sum.middle)
        at(3 * i + 4, plane_sum.end, settle.start)
        at(3 * i + 7, settle.middle)
        at(3 * i + 8, settle.forward)
    for item in first:
        at(6, item.middle)
        at(7, item.forward)

    @pl.when(passage == 0)
    def _():
        for i in range(count):
            span = slice(i * BLK, (i + 1) * BLK)
            q_t = q_ref[span, :].T
            grads_t = do_ref[span, :].T
            prod = (do_ref[span, :].astype(F32) * o_ref[span, :].astype(F32)).T
            for head in range(2):
                delta = jnp.sum(prod[head * HD : (head + 1) * HD, :], axis=0, keepdims=True)
                q_h[head, :, span] = head_rows(q_t, head, lse_ref[0, head : head + 1, span])
                do_h[head, :, span] = head_rows(grads_t, head, delta)
        dq_t[...] = jnp.zeros_like(dq_t)

    keys = dk_ref.shape[0] // BLK
    slots = [index_ref[passage * keys + j] for j in range(keys)]
    k_t = jnp.concatenate([k_ref[slot].T for slot in slots], axis=1)
    units = [(head, j, i) for head in range(2) for j in range(keys) for i in range(count)]

    def products(unit):
        head, j, i = unit
        span = slice(i * BLK, (i + 1) * BLK)
        return (
            mm(ones_in(k_ref[slots[j]], head), q_h[head, :, span]),
            mm(ones_in(v_ref[slots[j]], head), do_h[head, :, span]),
        )

    coming = products(units[0])
    halves = []
    for n, (head, j, i) in enumerate(units):
        scores, dprobs = coming
        if n + 1 < len(units):
            coming = products(units[n + 1])
        tile, span = slice(j * BLK, (j + 1) * BLK), slice(i * BLK, (i + 1) * BLK)
        probs = jnp.exp(scores)
        p_vm[head, tile, span] = probs.astype(BF16)
        ds_vm[head, tile, span] = (probs * dprobs).astype(BF16)
        if (j, i) == (keys - 1, count - 1):
            half = slice(head * HD, (head + 1) * HD)
            halves.append((mm(p_vm[head], do_ref[...]), mm(ds_vm[head], q_ref[...])))
            dq_t[half, :] += mm(k_t[half, :], ds_vm[head])
    dv_ref[...] = pick_heads(halves[0][0], halves[1][0]).astype(BF16)
    dk_ref[...] = pick_heads(halves[0][1], halves[1][1]).astype(BF16)

    @pl.when(passage == pl.num_programs(1) - 1)
    def _():
        dq_ref[...] = dq_t[...].T.astype(BF16)

    @pl.when(step == steps - 1)
    def _():
        for settle in first + settles:
            settle.end()
        for item in sums:
            item.wait_send()


def cross_backward(n_mem, plane, planes, index, q, k, v, o, do, lse, grads, ready):
    rows, width = q.shape
    pairs = width // (2 * HD)
    block = 2 * PLEN
    keys = index.shape[0] * PLEN
    passages = keys // block
    question = pl.BlockSpec((rows, 2 * HD), lambda h, u: (0, h))
    memory = pl.BlockSpec(k.shape[:2] + (2 * HD,), lambda h, u: (0, 0, h))
    grads_of = pl.BlockSpec((block, 2 * HD), lambda h, u: (u, h))
    shapes, chunks, scratch = [], [], []
    for which, (grad, columns, pieces) in enumerate(grads):
        lead, _, _, depth, cols = grad.shape
        count = depth // pieces
        shapes.append(reduce_out(grad.shape, columns, plane))
        for i in range(pieces):
            chunks.append((which, columns, (i * count, count)))
            scratch.append(pltpu.VMEM((lead, n_mem, count, cols), BF16))
            scratch += plane_sum_scratch(grad.shape, n_mem, count)
            scratch += settle_scratch(grad.shape, n_mem, plane, planes, count)
    settled = tuple(columns for _, columns in ready)
    for item, columns in ready:
        shape = item.shape[:2] + (plane,) + item.shape[2:]
        shapes.append(reduce_out(shape, columns, plane))
        scratch += settle_scratch(shape, n_mem, plane, planes, shape[3])
    outs = pl.pallas_call(
        functools.partial(cross_backward_kernel, n_mem, plane, planes, tuple(chunks), settled),
        grid=(pairs, passages),
        in_specs=[
            pl.BlockSpec(memory_space=pltpu.SMEM),
            question,
            memory,
            memory,
            question,
            question,
            pl.BlockSpec((1, 2, rows), lambda h, u: (h, 0, 0)),
        ]
        + [ANY] * len(grads)
        + [whole(item.shape) for item, _ in ready],
        out_specs=[question, grads_of, grads_of]
        + [whole(item.shape) for item in shapes],
        out_shape=[
            jax.ShapeDtypeStruct((rows, width), BF16),
            jax.ShapeDtypeStruct((keys, width), BF16),
            jax.ShapeDtypeStruct((keys, width), BF16),
        ]
        + shapes,
        scratch_shapes=[
            pltpu.VMEM((2, 2 * HD, rows), BF16),
            pltpu.VMEM((2, 2 * HD, rows), BF16),
            pltpu.VMEM((2 * HD, rows), F32),
            pltpu.VMEM((2, block, rows), BF16),
            pltpu.VMEM((2, block, rows), BF16),
        ]
        + scratch
        + [
            pltpu.SemaphoreType.DMA(
                (
                    len(chunks) * PLANE_SUM_SEMS
                    + (len(chunks) + len(ready)) * settle_sems(n_mem, plane, planes),
                )
            )
        ],
        compiler_params=pltpu.CompilerParams(
            vmem_limit_bytes=56 * 2**20, collective_id=5, has_side_effects=True
        ),
        cost_estimate=pl.CostEstimate(
            flops=rows * keys * width * 40,
            bytes_accessed=rows * width * 10 + k.size * 8,
            transcendentals=rows * keys * pairs * 2,
        ),
        name="cross_backward",
    )(index, q, k, v, o, do, lse, *[item[0] for item in grads], *[item for item, _ in ready])
    return outs[:3], outs[3:]


def widen_kernel(*refs):
    count = len(refs) // 2
    for src, dst in zip(refs[:count], refs[count:]):
        dst[...] = src[...].astype(F32)


def widen(pairs):
    steps = 8
    flats = [value.reshape(-1, like.shape[-1]) for value, like in pairs]
    blocks = [
        pl.BlockSpec((item.shape[0] // steps, item.shape[1]), lambda i: (i, 0)) for item in flats
    ]
    outs = pl.pallas_call(
        widen_kernel,
        grid=(steps,),
        in_specs=blocks,
        out_specs=blocks,
        out_shape=[jax.ShapeDtypeStruct(item.shape, F32) for item in flats],
        compiler_params=pltpu.CompilerParams(vmem_limit_bytes=60 * 2**20),
        cost_estimate=pl.CostEstimate(
            flops=0, bytes_accessed=6 * sum(item.size for item in flats), transcendentals=0
        ),
        name="widen",
    )(*flats)
    return [out.reshape(like.shape) for out, (_, like) in zip(outs, pairs)]


def body(
    hidden_in,
    encoder_rows,
    passage_map,
    self_qkv,
    self_out,
    cross_qkv,
    cross_out,
    ffn_in,
    ffn_out,
    ffn_in_bias,
    biases,
    gains,
    cotangent,
):
    n_pb = lax.axis_size("pb")
    n_mem = lax.axis_size("mem")
    columns = n_pb // 2
    plane = min(columns, 4)
    pb = lax.axis_index("pb")
    core = pb % 2
    width = hidden_in.shape[2]
    planes = columns // plane

    enc_local = encoder_rows.reshape(-1, PLEN, width)
    n_bias, n_gain = biases.shape[0], gains.shape[0]
    small = jnp.concatenate([biases, gains, ffn_in_bias.reshape(-1, biases.shape[1])], axis=0)
    n_small = small.shape[0]
    small_rows = -(-n_small // 16) * 16
    small = jnp.pad(small, ((0, small_rows - n_small), (0, 0)))
    rows_out, halves, kept = front(
        n_mem,
        plane,
        (n_bias, n_gain),
        hidden_in,
        enc_local,
        passage_map,
        small,
        [(self_qkv, True), (self_out, False), (cross_qkv, True)],
    )
    x_full, enc_full, index, small = rows_out
    sq, sk, sv, sa, self_lse, h1_full, unit1, scale1, cq, ck, cv = kept
    index = index.reshape(-1)

    def flat(half):
        lead, _, _, _, cols = half.shape
        return half.reshape(lead, -1, cols)

    w_self, w_cross = flat(halves[0]), flat(halves[2])
    w_self_out = flat(halves[1])[0]
    small = small.astype(F32)
    vectors = small[:, : n_bias + n_gain].transpose(1, 0, 2).reshape(n_bias + n_gain, width)
    bias, gain = vectors[:n_bias], vectors[n_bias:]
    ffn_bias = small[:, n_bias + n_gain : n_small].reshape(-1)

    def half_of(vector):
        parts = vector.reshape(n_mem, 2, -1)
        return jnp.where(core == 0, parts[:, 0], parts[:, 1]).reshape(-1)

    order = jnp.arange(encoder_rows.shape[1] * n_mem, dtype=jnp.int32)
    hits = index[None, :] == order[:, None]
    member = jnp.any(hits, axis=1).astype(F32)
    slot = jnp.sum(jnp.where(hits, jnp.arange(index.shape[0], dtype=jnp.int32)[None], 0), axis=1)
    (ca, cross_lse), halves = cross_forward(
        n_mem,
        plane,
        index,
        cq,
        ck,
        cv,
        [(ffn_in[None], True), (ffn_out, False), (cross_out, False)],
    )
    w_ffn_in, w_ffn_out, w_cross_out = flat(halves[0])[0], halves[1], flat(halves[2])[0]

    rows_of = jnp.stack(
        [gain[0], bias[6], bias[5], gain[1], bias[7], bias[9], gain[2], bias[8]]
    )
    layer_out, dca, dz2, feed_sums, hidden_sums, own_ffn_out, dw_ffn_in, dw_cross_out = feed(
        n_mem,
        plane,
        cotangent,
        rows_of,
        half_of(ffn_bias)[None],
        ca,
        unit1,
        w_cross_out,
        w_ffn_in,
        w_ffn_out,
    )
    (dcq, dck, dcv), ffn_sums = cross_backward(
        n_mem,
        plane,
        planes,
        index,
        cq,
        ck,
        cv,
        ca,
        dca,
        cross_lse,
        [(dw_ffn_in, True, 2), (dw_cross_out, False, 1)],
        [(own_ffn_out, False)],
    )
    (dsa, dz1, middle_sums, enc_sum), (own_cross, own_so), _ = middle(
        n_mem,
        plane,
        planes,
        slot,
        member,
        index,
        dcq,
        dck,
        dcv,
        w_cross,
        w_self_out,
        sa,
        h1_full,
        enc_full.reshape(-1, PLEN, width),
        dz2,
        unit1,
        scale1,
        gain[0][None],
        [],
    )

    vec, dx, sums = last(
        n_mem,
        plane,
        planes,
        sq,
        sk,
        sv,
        sa,
        dsa,
        self_lse,
        x_full,
        w_self,
        dz1,
        [feed_sums, hidden_sums, middle_sums],
        small.shape,
        [(own_so, False), (own_cross, True)],
    )
    (
        grad_in,
        grad_encoder,
        out_self_qkv,
        out_self_out,
        out_cross_qkv,
        out_cross_out,
        out_ffn_in,
        out_ffn_out,
    ) = widen(
        [
            (dx, hidden_in),
            (enc_sum, encoder_rows),
            (sums[0], self_qkv),
            (sums[1], self_out),
            (sums[2], cross_qkv),
            (ffn_sums[1], cross_out),
            (ffn_sums[0], ffn_in),
            (ffn_sums[2], ffn_out),
        ]
    )
    out_ffn_bias = vec[n_bias + n_gain : n_small].reshape(-1)
    return (
        layer_out,
        grad_in,
        grad_encoder,
        out_self_qkv,
        out_self_out,
        out_cross_qkv,
        out_cross_out,
        out_ffn_in,
        out_ffn_out,
        out_ffn_bias,
        vec[:n_bias],
        vec[n_bias : n_bias + n_gain],
    )


def solution(mesh):
    placed = (
        P("pb", "mem", None),
        P("pb", "mem", None, None),
        P("pb", None),
        P(None, "mem", None),
        P("mem", None),
        P(None, "mem", None),
        P("mem", None),
        P("mem", None),
        P("mem", None),
        P("mem"),
        P(None, "mem"),
        P(None, "mem"),
        P("pb", "mem", None),
    )
    return jax.shard_map(
        body,
        mesh=mesh,
        in_specs=placed,
        out_specs=(
            P("pb", "mem", None),
            P("pb", "mem", None),
            P("pb", "mem", None, None),
            P(None, "mem", None),
            P("mem", None),
            P(None, "mem", None),
            P("mem", None),
            P("mem", None),
            P("mem", None),
            P("mem"),
            P(None, "mem"),
            P(None, "mem"),
        ),
        check_vma=False,
    )
```

```python
import functools

import jax
import jax.numpy as jnp
from jax import lax
from jax.experimental import pallas as pl
from jax.experimental.pallas import tpu as pltpu
from jax.sharding import PartitionSpec as P

HD = 64
PLEN = 256
BLK = 256
F32 = jnp.float32
BF16 = jnp.bfloat16

NN = (((1,), (0,)), ((), ()))
NT = (((1,), (1,)), ((), ()))


def mm(a, b, dims=NN):
    return lax.dot_general(a, b, dims, preferred_element_type=F32)


def head_mask_rows(block, head):
    rows = lax.broadcasted_iota(jnp.int32, block.shape, 0)
    return jnp.where((rows // HD) == head, block, jnp.zeros_like(block))


def head_rows(block, head, extra=None):
    block = block.astype(F32)
    rows = lax.broadcasted_iota(jnp.int32, block.shape, 0)
    out = jnp.where((rows // HD) == head, block, 0.0)
    if extra is not None:
        rest = -extra
        for i in range(3):
            term = rest.astype(BF16).astype(F32)
            rest = rest - term
            out = jnp.where(rows == (1 - head) * HD + i, term, out)
    return out.astype(BF16)


def ones_in(block, head):
    lanes = lax.broadcasted_iota(jnp.int32, block.shape, 1)
    first = (1 - head) * HD
    return jnp.where((lanes >= first) & (lanes < first + 3), jnp.ones_like(block), block)


def pick_heads(first, second):
    lanes = lax.broadcasted_iota(jnp.int32, first.shape, 1)
    return jnp.where(lanes < HD, first, second)


MESH = pl.DeviceIdType.MESH
ANY = pl.BlockSpec(memory_space=pl.ANY)
VMEM = pl.BlockSpec(memory_space=pltpu.VMEM)
PLANE = 4


def flip(index, bits):
    bit = 1
    while bit <= bits:
        if bits & bit:
            unit = jnp.int32(bit)
            index = index + unit - 2 * unit * lax.rem(lax.div(index, unit), jnp.int32(2))
        bit *= 2
    return index


class Place:
    def __init__(self, plane, planes=1):
        self.pb = lax.axis_index("pb")
        self.mem = lax.axis_index("mem")
        two = jnp.int32(2)
        self.core = lax.rem(self.pb, two)
        self.quarter = lax.rem(lax.div(self.pb, two), jnp.int32(plane))
        self.parity = lax.rem(self.mem, two)
        self.half = lax.div(self.mem, two)
        self.plane = plane
        self.planes = planes

    def near(self, t):
        return (flip(self.pb, 2 * t), self.mem)

    def far(self, r):
        return (flip(self.pb, 2 * self.plane * r), self.mem)

    def line(self, s):
        return (self.pb, flip(self.mem, s))

    def twin(self):
        return (flip(self.pb, 1), self.mem)

    def pair(self):
        return (self.pb, flip(self.mem, 1))

    def worker(self, k):
        return (self.pb - self.core + self.half, 2 * self.core + flip(self.parity, k))

    def at_home(self):
        return self.half == self.core

    def meet(self, peers):
        barrier = pltpu.get_barrier_semaphore()
        for pb_bits, mem_bits in peers:
            pl.semaphore_signal(
                barrier,
                inc=1,
                device_id=(flip(self.pb, pb_bits), flip(self.mem, mem_bits)),
                device_id_type=MESH,
            )
        pl.semaphore_wait(barrier, len(peers))


def column_peers(n_mem):
    return [(a, b) for a in range(2) for b in range(n_mem) if (a, b) != (0, 0)]


def plane_peers(plane):
    return [(2 * t, 0) for t in range(1, plane)]


class Sems:
    def __init__(self, ref):
        self.ref = ref
        self.used = 0

    def take(self, count):
        first = self.used
        self.used += count
        return [self.ref.at[first + i] for i in range(count)]


def remote(src, dst, send_sem, recv_sem, device):
    return pltpu.make_async_remote_copy(
        src_ref=src,
        dst_ref=dst,
        send_sem=send_sem,
        recv_sem=recv_sem,
        device_id=device,
        device_id_type=MESH,
    )


class Spread:
    def __init__(self, place, sems, src, dst, kinds=(0, 1)):
        self.place, self.src, self.dst, self.kinds = place, src, dst, kinds
        self.send = sems.take(2)
        self.recv = sems.take(2)

    def copy(self, k):
        return remote(self.src(k), self.dst(k), self.send[k], self.recv[k], self.place.worker(k))

    def start(self):
        for k in self.kinds:
            if k == 0:
                home = self.place.at_home()

                @pl.when(home)
                def _():
                    pltpu.make_async_copy(self.src(0), self.dst(0), self.recv[0]).start()

                @pl.when(jnp.logical_not(home))
                def _():
                    self.copy(0).start()
            else:
                self.copy(k).start()

    def wait_recv(self, k):
        if k == 0:
            home = self.place.at_home()

            @pl.when(home)
            def _():
                pltpu.make_async_copy(self.src(0), self.dst(0), self.recv[0]).wait()

            @pl.when(jnp.logical_not(home))
            def _():
                self.copy(0).wait_recv()
        else:
            self.copy(k).wait_recv()

    def wait_send(self):
        for k in self.kinds:
            if k == 0:

                @pl.when(jnp.logical_not(self.place.at_home()))
                def _():
                    self.copy(0).wait_send()
            else:
                self.copy(k).wait_send()


class Own:
    def __init__(self, place, sems, shard, full, columns, n_mem):
        self.copies = []
        mem, core = place.mem, place.core
        if columns:
            unit = full.shape[-1] // n_mem
            for b, sem in zip(range(n_mem), sems.take(n_mem)):
                start = pl.multiple_of(2 * unit * b + unit * core, unit)
                src = shard.at[:, :, :, pl.ds(start, unit)]
                dst = full.at[:, mem, :, :, pl.ds(unit * b, unit)]
                self.copies.append(pltpu.make_async_copy(src, dst, sem))
        else:
            (sem,) = sems.take(1)
            self.copies.append(pltpu.make_async_copy(shard.at[core], full.at[0, mem], sem))

    def start(self):
        for copy in self.copies:
            copy.start()

    def wait(self):
        for copy in self.copies:
            copy.wait()


class Line:
    def __init__(self, place, sems, src, dst, n_mem):
        send, recv = sems.take(n_mem - 1), sems.take(n_mem - 1)
        self.copies = [
            remote(src(s), dst(s), send[s - 1], recv[s - 1], place.line(s)) for s in range(1, n_mem)
        ]

    def start(self):
        for copy in self.copies:
            copy.start()

    def wait_recv(self, s):
        self.copies[s - 1].wait_recv()

    def wait_send(self):
        for copy in self.copies:
            copy.wait_send()


class Share:
    def __init__(self, place, sems, src, block):
        send, recv = sems.take(4), sems.take(4)
        rows = src.shape[-2]
        half = rows // 2

        def part(ref, i):
            return ref.at[:, pl.ds(i * half, half)]

        self.first = [
            remote(src, block(0), send[t - 1], recv[t - 1], place.near(t)) for t in (1, 2)
        ]
        self.second = [
            remote(part(block(t), t - 1), part(block(t), t - 1), send[t + 1], recv[t + 1], place.near(3 - t))
            for t in (1, 2)
        ]

    def start(self):
        for copy in self.first:
            copy.start()

    def forward(self):
        for direct, onward in zip(self.first, self.second):
            direct.wait_recv()
            onward.start()

    def wait(self):
        for copy in self.first:
            copy.wait_send()
        for copy in self.second:
            copy.wait()


class Chain:
    def __init__(self, place, sems, block, n_mem):
        self.place, self.block, self.n = place, block, n_mem
        self.sems = {way: (sems.take(n_mem - 1), sems.take(n_mem - 1)) for way in (1, -1)}

    def copy(self, way, hops):
        mem = self.place.mem
        source = lax.rem(mem + jnp.int32(self.n - way * hops), jnp.int32(self.n))
        target = lax.rem(mem + jnp.int32(self.n + way), jnp.int32(self.n))
        send, recv = self.sems[way]
        piece = self.block(source)
        return remote(piece, piece, send[hops], recv[hops], (self.place.pb, target))

    def comes(self, way, hops):
        mem = self.place.mem
        return mem >= hops if way == 1 else mem + hops < self.n

    def goes(self, way, hops):
        mem = self.place.mem
        ahead = mem + 1 < self.n if way == 1 else mem >= 1
        return jnp.logical_and(ahead, self.comes(way, hops))

    def start(self):
        for way in (1, -1):

            @pl.when(self.goes(way, 0))
            def _():
                self.copy(way, 0).start()

    def relay(self, hops, arrived):
        for way in (1, -1):

            @pl.when(self.comes(way, hops))
            def _():
                self.copy(way, hops - 1).wait_recv()
                if hops < self.n - 1:

                    @pl.when(self.goes(way, hops))
                    def _():
                        self.copy(way, hops).start()

                arrived(hops if way == 1 else self.n - hops)

    def wait_send(self):
        for hops in range(self.n - 1):
            for way in (1, -1):

                @pl.when(self.goes(way, hops))
                def _():
                    self.copy(way, hops).wait_send()


class Gather:
    def __init__(self, place, sems, shard, full, columns, n_mem, in_plane=True):
        mem, quarter = place.mem, place.quarter
        self.n_mem = n_mem
        self.in_plane = in_plane
        self.own = Own(place, sems, shard, full, columns, n_mem)
        self.chain = Chain(place, sems, lambda i: full.at[:, i, quarter], n_mem)
        self.shares = {}
        for d in range(1, n_mem if in_plane else 1):
            source = lax.rem(mem + jnp.int32(n_mem - d), jnp.int32(n_mem))

            def block(t, source=source):
                return full.at[:, source, flip(quarter, t)]

            self.shares[d] = Share(place, sems, block(0), block)

    def begin(self):
        self.own.wait()
        self.chain.start()

    def share(self, hops):
        self.chain.relay(hops, lambda d: self.shares[d].start() if self.in_plane else None)

    def forward(self, hops):
        for way, d in ((1, hops), (-1, self.n_mem - hops)):

            @pl.when(self.chain.comes(way, hops))
            def _():
                self.shares[d].forward()

    def finish(self):
        self.chain.wait_send()
        for share in self.shares.values():
            share.wait()


GATHER_SEMS = 44


def half_views(shard, columns, n_mem, plane):
    if columns:
        lead, depth, hidden = shard.shape
        part = depth // plane
        return shard.reshape(lead, plane, part, hidden), (lead, n_mem, plane, part, hidden // 2)
    depth, width = shard.shape
    part = depth // 2 // plane
    return shard.reshape(2, plane, part, width), (1, n_mem, plane, part, width)


class Walk:
    def __init__(self, refs):
        self.refs = list(refs)

    def take(self, count):
        out, self.refs = self.refs[:count], self.refs[count:]
        return out

    def one(self):
        return self.take(1)[0]


def softmax_units(units, finish, serve=None):
    def scores_of(unit, j):
        return unit[0][j]()

    ready = [scores_of(units[0], j) for j in range(len(units[0][0]))]
    for n, (_, values, tag) in enumerate(units):
        if serve is not None:
            serve(n)
        coming = list(range(len(units[n + 1][0]))) if n + 1 < len(units) else []
        following = []
        top = functools.reduce(
            jnp.maximum, [jnp.max(tile, axis=0, keepdims=True) for tile in ready]
        )
        total = jnp.zeros_like(top)
        acc = None
        share = -(-len(coming) // len(ready))
        for j, tile in enumerate(ready):
            for i in coming[j * share : (j + 1) * share]:
                following.append(scores_of(units[n + 1], i))
            probs = jnp.exp(tile - top)
            total += jnp.sum(probs, axis=0, keepdims=True)
            part = mm(values[j](), probs.astype(BF16))
            acc = part if acc is None else acc + part
        finish(tag, acc / total, top + jnp.log(total))
        ready = following


def self_attend(place, pair, q_vm, k_vm, v_vm, o_vm, lse_vm, v_t, o_t):
    base = 2 * place.core + place.parity
    count = q_vm.shape[0] // BLK
    lanes = pl.ds(pl.multiple_of(pair * 2 * HD, 2 * HD), 2 * HD)

    def rows(i):
        return pl.ds(pl.multiple_of(flip(base, i) * BLK, BLK), BLK)

    for j in range(count):
        v_t[:, j * BLK : (j + 1) * BLK] = v_vm[rows(j), lanes].T
    key_pos = lax.broadcasted_iota(jnp.int32, (BLK, BLK), 0)
    query_pos = lax.broadcasted_iota(jnp.int32, (BLK, BLK), 1)
    units = []
    for i in range(count):
        q_t = q_vm[rows(i), lanes].T
        for head in range(2):
            q_head = head_rows(q_t, head)

            def score(j, i=i, q_head=q_head):
                tile = mm(k_vm[rows(j), lanes], q_head)
                return jnp.where(key_pos <= query_pos, tile, -1000000000.0) if j == i else tile

            def value(j, head=head):
                return v_t[head * HD : (head + 1) * HD, j * BLK : (j + 1) * BLK]

            units.append(
                (
                    [functools.partial(score, j) for j in range(i + 1)],
                    [functools.partial(value, j) for j in range(i + 1)],
                    (i, head),
                )
            )

    def finish(tag, mixed, lse):
        i, head = tag
        span = slice(i * BLK, (i + 1) * BLK)
        o_t[head * HD : (head + 1) * HD, span] = mixed
        lse_vm[pair, head : head + 1, span] = lse

    softmax_units(units, finish)
    for i in range(count):
        o_vm[rows(i), lanes] = o_t[:, i * BLK : (i + 1) * BLK].T.astype(BF16)


def tiles(rows, step):
    def run(i, carry):
        step(pl.ds(pl.multiple_of(i * BLK, BLK), BLK))
        return carry

    lax.fori_loop(0, rows // BLK, run, 0)


def front_kernel(n_mem, plane, kinds, places, x_ref, enc_ref, map_ref, small_ref, *refs):
    refs = Walk(refs)
    count = len(kinds)
    shards = refs.take(count)
    x_out, enc_out, index_out, small_out = refs.take(4)
    halves = refs.take(count)
    kept = refs.take(11)
    x_vm, w_vm, so_vm, cq_w, small_vm = refs.take(5)
    q_vm, k_vm, v_vm, sa_vm, lse_vm, h1_vm, unit_vm, scale_vm, cq_vm = refs.take(9)
    k_all, v_all, v_t, o_t, part_vm, twin_vm, kv_w, enc_vm, map_in = refs.take(9)
    sems = Sems(refs.one())
    place = Place(plane)
    n_bias, n_gain = places
    rows = x_ref.shape[1]
    gathers = [
        Gather(place, sems, shard, half, columns, n_mem)
        for shard, half, columns in zip(shards, halves, kinds)
    ]
    spread = Spread(
        place,
        sems,
        lambda k: x_ref.at[flip(place.parity, k)],
        lambda k: x_out.at[pl.ds(rows * k, rows)],
    )
    twin_send, twin_recv = sems.take(2), sems.take(2)
    twin = [
        remote(
            x_out.at[pl.ds(rows * k, rows)],
            x_out.at[pl.ds(rows * (k + 2), rows)],
            twin_send[k],
            twin_recv[k],
            place.twin(),
        )
        for k in range(2)
    ]
    map_sems = sems.take(2)
    map_copy = remote(map_ref, map_in, map_sems[0], map_sems[1], place.twin())
    (small_sem,) = sems.take(1)
    small_own = pltpu.make_async_copy(small_ref, small_out.at[place.mem], small_sem)
    small_line = Line(
        place, sems, lambda s: small_ref, lambda s: small_out.at[place.mem], n_mem
    )
    units = enc_vm.shape[1]
    encs, enc_twins, enc_pairs, enc_onwards, enc_ends = [], [], [], [], []
    for u in range(units):
        encs.append(
            Spread(
                place, sems, lambda k, u=u: enc_ref.at[u], lambda k, u=u: enc_vm.at[0, u], kinds=(0,)
            )
        )
        pair_sems, twin_sems, end_sems = sems.take(2), sems.take(2), sems.take(2)
        enc_pairs.append(remote(enc_ref.at[u], enc_vm.at[1, u], *pair_sems, place.pair()))
        enc_onwards.append(remote(enc_vm.at[0, u], enc_vm.at[1, u], *pair_sems, place.pair()))
        enc_twins.append(remote(enc_vm.at[0, u], enc_vm.at[2, u], *twin_sems, place.twin()))
        enc_ends.append(remote(enc_vm.at[1, u], enc_vm.at[3, u], *end_sems, place.twin()))
    enc_keeps = [
        pltpu.make_async_copy(enc_vm.at[i], enc_out.at[i], sem) for i, sem in enumerate(sems.take(4))
    ]
    home = place.at_home()
    away = jnp.logical_not(home)
    loads = [
        pltpu.make_async_copy(src, dst, sem)
        for src, dst, sem in zip(
            (x_out, halves[0], halves[1], halves[2].at[0], small_out, halves[2].at[pl.ds(1, 2)]),
            (x_vm, w_vm, so_vm, cq_w, small_vm, kv_w),
            sems.take(6),
        )
    ]
    keeps = [
        pltpu.make_async_copy(src, dst, sem)
        for src, dst, sem in zip(
            (q_vm, k_vm, v_vm, sa_vm, lse_vm, h1_vm, unit_vm, scale_vm, cq_vm, k_all, v_all),
            kept,
            sems.take(11),
        )
    ]
    swap_sems = sems.take(4)
    own = 2 * rows
    swap_part = remote(part_vm, twin_vm, swap_sems[0], swap_sems[1], place.twin())
    swap_h1 = remote(
        h1_vm.at[pl.ds(0, own)], h1_vm.at[pl.ds(own, own)], swap_sems[2], swap_sems[3], place.twin()
    )

    for gather in gathers:
        gather.own.start()
    small_own.start()
    place.meet(column_peers(n_mem) + plane_peers(plane))
    for gather in gathers:
        gather.begin()
    small_line.start()
    map_copy.start()
    spread.start()
    for gather in gathers:
        gather.share(1)
    for gather in gathers:
        gather.share(2)
    gathers[0].forward(1)
    for k in range(2):
        spread.wait_recv(k)
        twin[k].start()
    for gather in gathers:
        gather.share(3)
    def send_passage(u):
        encs[u].start()

        @pl.when(home)
        def _():
            enc_pairs[u].start()

    send_passage(0)

    def first_arrival(u):
        encs[u].wait_recv(0)

        @pl.when(away)
        def _():
            enc_onwards[u].start()

        enc_twins[u].start()

    def second_arrival(u):
        @pl.when(home)
        def _():
            enc_pairs[u].wait()

        @pl.when(away)
        def _():
            enc_onwards[u].wait()

        enc_ends[u].start()

    gathers[0].forward(2)
    gathers[0].forward(3)
    send_passage(1)
    for hops in (1, 2, 3):
        for gather in gathers[1:]:
            gather.forward(hops)
    for u in range(2, units):
        send_passage(u)
    for copy in twin:
        copy.wait_recv()
    small_own.wait()
    for s in range(1, n_mem):
        small_line.wait_recv(s)
    gathers[0].finish()
    for copy in (loads[0], loads[1], loads[4]):
        copy.start()
    for copy in (loads[0], loads[1], loads[4]):
        copy.wait()

    def half_row(row):
        lanes = pl.ds(pl.multiple_of(place.core * 2 * HD, 2 * HD), 2 * HD)
        return jnp.concatenate(
            [small_vm[b, :, lanes].astype(F32)[row : row + 1] for b in range(n_mem)], axis=1
        )

    def full_row(row):
        return jnp.concatenate(
            [small_vm[b].astype(F32)[row : row + 1] for b in range(n_mem)], axis=1
        )

    bias_q, bias_v = half_row(0), half_row(1)
    depth = x_vm.shape[1]

    def weight(ref):
        return ref[...].reshape(-1, ref.shape[-1])

    def project(span):
        x_tile = x_vm[span, :]
        q_vm[span, :] = ((mm(x_tile, weight(w_vm.at[0])) + bias_q) * 0.125).astype(BF16)
        k_vm[span, :] = mm(x_tile, weight(w_vm.at[1])).astype(BF16)
        v_vm[span, :] = (mm(x_tile, weight(w_vm.at[2])) + bias_v).astype(BF16)

    tiles(x_vm.shape[0], project)
    for copy in keeps[:3]:
        copy.start()
    pairs = q_vm.shape[1] // (2 * HD)
    for pair in range(pairs):
        self_attend(place, pair, q_vm, k_vm, v_vm, sa_vm, lse_vm, v_t, o_t)
        if pair in (0, pairs // 2):
            first_arrival(min(pair, 1))
    for copy in keeps[3:5]:
        copy.start()
    for gather in gathers[1:]:
        gather.finish()
    for copy in (loads[2], loads[3], loads[5]):
        copy.start()
    for copy in (loads[2], loads[3], loads[5]):
        copy.wait()

    def other_part(span):
        part_vm[span, :] = mm(
            sa_vm[pl.ds(pl.multiple_of(span.start + own, BLK), BLK), :], weight(so_vm)
        ).astype(BF16)

    tiles(own, other_part)
    swap_part.start()

    def own_part(span):
        unit_vm[span, :] = mm(sa_vm[span, :], weight(so_vm)) + x_vm[span, :].astype(F32)

    tiles(own, own_part)
    for u in range(2, units):
        first_arrival(u)
    bias_out = full_row(2)
    gain, shift = full_row(n_bias), full_row(6)
    swap_part.wait()

    def normalise(span):
        values = unit_vm[span, :] + twin_vm[span, :].astype(F32) + bias_out
        centre = values - jnp.mean(values, axis=-1, keepdims=True)
        scale = lax.rsqrt(jnp.mean(centre * centre, axis=-1, keepdims=True) + 1e-05)
        unit = centre * scale
        unit_vm[span, :] = unit
        scale_vm[span, :] = jnp.broadcast_to(scale, (BLK, scale_vm.shape[1]))
        h1_vm[span, :] = (unit * gain + shift).astype(BF16)

    tiles(own, normalise)
    swap_h1.start()
    for copy in keeps[6:8]:
        copy.start()
    bias_cq = half_row(3)

    def queries(span):
        cq_vm[span, :] = ((mm(h1_vm[span, :], weight(cq_w)) + bias_cq) * 0.125).astype(BF16)

    tiles(own, queries)
    swap_h1.wait()
    keeps[5].start()

    def other_queries(span):
        queries(pl.ds(pl.multiple_of(span.start + own, BLK), BLK))

    tiles(own, other_queries)
    keeps[8].start()

    map_copy.wait()
    near_map, far_map = map_ref[...], map_in[...]
    both_maps = jnp.where(home, near_map, far_map)
    mine = jnp.where(place.parity == 0, both_maps[:1], both_maps[1:])
    group = lax.div(mine, jnp.full_like(mine, units))
    index_out[...] = (group ^ (2 * place.core + place.parity)) * units + lax.rem(
        mine, jnp.full_like(mine, units)
    )

    bias_cv = half_row(4)

    def memory(block, u):
        rows_here = enc_vm[block, u]
        k_all[block * units + u] = mm(rows_here, weight(kv_w.at[0])).astype(BF16)
        v_all[block * units + u] = (mm(rows_here, weight(kv_w.at[1])) + bias_cv).astype(BF16)

    for u in range(units):
        second_arrival(u)
        memory(0, u)
    enc_keeps[0].start()
    enc_keeps[1].start()
    for block, copies in ((2, enc_twins), (1, None), (3, enc_ends)):
        for u in range(units):
            if copies is not None:
                copies[u].wait_recv()
            memory(block, u)
    enc_keeps[2].start()
    enc_keeps[3].start()
    for copy in keeps[9:]:
        copy.start()
    spread.wait_send()
    for copy in twin:
        copy.wait_send()
    small_line.wait_send()
    for item in encs:
        item.wait_send()
    for copy in enc_twins + enc_ends:
        copy.wait_send()
    for copy in keeps + enc_keeps:
        copy.wait()


def front(n_mem, plane, places, hidden_in, enc, passage_map, small, params):
    kinds = tuple(columns for _, columns in params)
    views = [half_views(shard, columns, n_mem, plane) for shard, columns in params]
    seg, width = hidden_in.shape[1:]
    rows, own = 4 * seg, 2 * seg
    part = width // 2
    pairs = part // (2 * HD)
    passages = 4 * enc.shape[0]
    shapes = (
        [((rows, width), BF16), ((4,) + enc.shape, BF16), ((1, passage_map.shape[1]), jnp.int32)]
        + [((n_mem,) + small.shape, BF16)]
        + [(full, BF16) for _, full in views]
    )
    kept = [
        ((rows, part), BF16),
        ((rows, part), BF16),
        ((rows, part), BF16),
        ((rows, part), BF16),
        ((pairs, 2, rows), F32),
        ((rows, width), BF16),
        ((own, width), F32),
        ((own, 2 * HD), F32),
        ((rows, part), BF16),
        ((passages, PLEN, part), BF16),
        ((passages, PLEN, part), BF16),
    ]
    scratch = [
        ((rows, width), BF16),
        (views[0][1], BF16),
        (views[1][1][1:], BF16),
        (views[2][1][1:], BF16),
        ((n_mem,) + small.shape, BF16),
    ] + kept + [
        ((2 * HD, rows), BF16),
        ((2 * HD, rows), F32),
        ((own, width), BF16),
        ((own, width), BF16),
        ((2,) + views[2][1][1:], BF16),
        ((4,) + enc.shape, BF16),
        (passage_map.shape, jnp.int32),
    ]
    scratch[2] = (views[1][1], BF16)
    outs = pl.pallas_call(
        functools.partial(front_kernel, n_mem, plane, kinds, places),
        in_specs=[VMEM] * (4 + len(params)),
        out_specs=[ANY, ANY, VMEM] + [ANY] * (len(shapes) + len(kept) - 3),
        out_shape=[jax.ShapeDtypeStruct(*item) for item in shapes + kept],
        scratch_shapes=[pltpu.VMEM(*item) for item in scratch]
        + [pltpu.SemaphoreType.DMA((90 + GATHER_SEMS * len(params),))],
        compiler_params=pltpu.CompilerParams(
            collective_id=0, has_side_effects=True, vmem_limit_bytes=60 * 2**20
        ),
        cost_estimate=pl.CostEstimate(
            flops=rows * width * part * 10, bytes_accessed=40 * 2**20, transcendentals=rows * rows * 8
        ),
        name="front",
    )(hidden_in, enc, passage_map, small, *[view for view, _ in views])
    count = 4 + len(params)
    return outs[:4], outs[4:count], outs[count:]


class PlaneSum:
    def __init__(self, place, sems, grad, own, bufs, rows, lanes=None):
        self.own = own
        self.from_near, self.via, self.add = bufs
        quarter = place.quarter
        first, count = rows
        half = count // 2
        self.lead, self.n_mem = own.shape[:2]
        lanes = pl.ds(*(lanes or (0, grad.shape[-1])))

        def piece(t, lo, size):
            return grad.at[:, :, flip(quarter, t), pl.ds(first + lo, size), lanes]

        loads = sems.take(3)
        self.loads = [pltpu.make_async_copy(piece(0, 0, count), own, loads[0])]
        send, recv = sems.take(6), sems.take(6)
        self.onward, self.direct, self.summed = [], [], []
        for t in (1, 2):
            lo = (t - 1) * half
            self.onward.append(
                remote(piece(3, lo, half), self.via.at[t - 1], send[t - 1], recv[t - 1], place.near(t))
            )
            self.direct.append(
                remote(
                    piece(t, lo, half),
                    self.from_near.at[t - 1, :, :, pl.ds(lo, half)],
                    send[t + 1],
                    recv[t + 1],
                    place.near(t),
                )
            )
            other = half - lo
            self.loads.append(
                pltpu.make_async_copy(piece(t, other, half), self.add.at[t - 1], loads[t])
            )
            self.summed.append(
                remote(
                    self.add.at[t - 1],
                    self.from_near.at[t - 1, :, :, pl.ds(other, half)],
                    send[t + 3],
                    recv[t + 3],
                    place.near(t),
                )
            )

    def start(self):
        for copy in self.onward + self.loads + self.direct:
            copy.start()

    def each(self, step):
        def run(i, carry):
            step(lax.div(i, jnp.int32(self.n_mem)), lax.rem(i, jnp.int32(self.n_mem)))
            return carry

        lax.fori_loop(0, self.lead * self.n_mem, run, 0)

    def middle(self):
        for copy in self.loads:
            copy.wait()
        for t in (1, 2):
            self.onward[2 - t].wait_recv()

            def add(l, m, t=t):
                total = self.add[t - 1, l, m].astype(F32) + self.via[2 - t, l, m].astype(F32)
                self.add[t - 1, l, m] = total.astype(BF16)

            self.each(add)
            self.summed[t - 1].start()

    def end(self):
        for copy in self.direct + self.summed:
            copy.wait_recv()

        def add(l, m):
            total = self.own[l, m].astype(F32)
            for t in range(2):
                total += self.from_near[t, l, m].astype(F32)
            self.own[l, m] = total.astype(BF16)

        self.each(add)

    def wait_send(self):
        for copy in self.onward + self.direct + self.summed:
            copy.wait_send()


class Settle:
    def __init__(self, place, sems, own, out, bufs, columns, n_mem, rows, lane=0):
        self.place, self.n_mem, self.columns, self.rows = place, n_mem, columns, rows
        self.lane = lane
        self.own, self.out = own, out
        self.line_in, self.far_in, self.slots = bufs
        quarter, mem, core = place.quarter, place.mem, place.core
        slots = self.slots

        def slot(t):
            return slots.at[flip(quarter, t), core]

        self.line = Line(
            place, sems, lambda s: own.at[:, flip(mem, s)], lambda s: self.line_in.at[s - 1], n_mem
        )
        others = place.planes - 1
        far_send, far_recv = sems.take(others), sems.take(others)
        self.far = [
            remote(slot(0), self.far_in.at[r - 1], far_send[r - 1], far_recv[r - 1], place.far(r))
            for r in range(1, place.planes)
        ]
        self.share = Share(place, sems, slot(0), slot)
        twin_send, twin_recv = sems.take(place.plane), sems.take(place.plane)
        self.twin = [
            remote(slot(t), slot(t), twin_send[t], twin_recv[t], place.twin())
            for t in range(place.plane)
        ]

    def start(self):
        self.line.start()

    def middle(self):
        for s in range(1, self.n_mem):
            self.line.wait_recv(s)
        quarter, core, mem = self.place.quarter, self.place.core, self.place.mem
        lead = self.own.shape[0]
        for l in range(lead):
            total = self.own[l, mem].astype(F32)
            for s in range(self.n_mem - 1):
                total += self.line_in[s, l].astype(F32)
            self.slots[quarter, core, l] = total.astype(BF16)
        if self.far:
            for copy in self.far:
                copy.start()
            for copy in self.far:
                copy.wait()
            for l in range(lead):
                total = self.slots[quarter, core, l].astype(F32)
                for r in range(len(self.far)):
                    total += self.far_in[r, l].astype(F32)
                self.slots[quarter, core, l] = total.astype(BF16)
        self.share.start()
        self.twin[0].start()

    def forward(self):
        self.share.forward()
        self.twin[1].start()
        self.twin[2].start()

    def end(self):
        self.share.wait()
        self.twin[3].start()
        for copy in self.twin:
            copy.wait()
        self.line.wait_send()
        lead = self.own.shape[0]
        wide = self.slots.shape[-1]
        first, count = self.rows
        for q in range(self.place.plane):
            for c in range(2):
                for l in range(lead):
                    if self.columns:
                        unit = self.out.shape[-1] // (2 * self.n_mem)
                        for b in range(wide // unit):
                            start = unit * (2 * (self.lane // unit + b) + c)
                            self.out[l, q, first : first + count, start : start + unit] = self.slots[
                                q, c, l, :, b * unit : (b + 1) * unit
                            ]
                    else:
                        self.out[c, q, first : first + count] = self.slots[q, c, l]


PLANE_SUM_SEMS = 15


def settle_sems(n_mem, plane, planes):
    return 2 * (n_mem - 1) + 2 * (planes - 1) + 8 + 2 * plane


def plane_sum_scratch(grad_shape, n_mem, count, cols=None):
    lead, cols = grad_shape[0], cols or grad_shape[-1]
    return [
        pltpu.VMEM((2, lead, n_mem, count, cols), BF16),
        pltpu.VMEM((2, lead, n_mem, count // 2, cols), BF16),
        pltpu.VMEM((2, lead, n_mem, count // 2, cols), BF16),
    ]


def settle_scratch(grad_shape, n_mem, plane, planes, count, cols=None):
    lead, cols = grad_shape[0], cols or grad_shape[-1]
    return [
        pltpu.VMEM((n_mem - 1, lead, count, cols), BF16),
        pltpu.VMEM((max(planes - 1, 1), lead, count, cols), BF16),
        pltpu.VMEM((plane, 2, lead, count, cols), BF16),
    ]


def sum_shape(grad_shape):
    lead, n_mem, _, rows, cols = grad_shape
    return jax.ShapeDtypeStruct((lead, n_mem, rows, cols), BF16)


def reduce_out(grad_shape, columns, plane):
    lead, _, _, rows, cols = grad_shape
    shape = (lead, plane, rows, 2 * cols) if columns else (2, plane, rows, cols)
    return jax.ShapeDtypeStruct(shape, BF16)


def reduce_peers(n_mem, plane, planes):
    return (
        [(1, 0)]
        + [(0, s) for s in range(1, n_mem)]
        + plane_peers(plane)
        + [(2 * plane * r, 0) for r in range(1, planes)]
    )


def whole(shape):
    return pl.BlockSpec(shape, lambda *grid: (0,) * len(shape))


class Fetch:
    def __init__(self, sems, src, dst):
        self.copy = pltpu.make_async_copy(src, dst, sems.take(1)[0])
        self.dst = dst
        self.here = False

    def start(self):
        self.copy.start()

    def get(self):
        if not self.here:
            self.copy.wait()
            self.here = True
        return self.dst


def unit_norm(values):
    centre = values - jnp.mean(values, axis=-1, keepdims=True)
    scale = lax.rsqrt(jnp.mean(centre * centre, axis=-1, keepdims=True) + 1e-05)
    return centre * scale, scale


def unit_norm_back(grad, unit, scale, gain):
    inner = grad * gain
    return (
        inner
        - jnp.mean(inner, axis=-1, keepdims=True)
        - unit * jnp.mean(inner * unit, axis=-1, keepdims=True)
    ) * scale


def feed_kernel(n_mem, plane, cot_vm, rows_ref, bias_ref, *refs):
    refs = Walk(refs)
    fetched = refs.take(4)
    out_part = refs.one()
    final_out, dca_ref, dz2_ref, sums_ref, bias_sum, own_out, dw_in, dw_co = refs.take(8)
    kept = refs.take(4)
    out_w = refs.one()
    h2_vm, unit_vm, scale_vm, act_vm, slope_vm, p_vm, part_vm, twin_vm = refs.take(8)
    final_vm, df_vm, dco_vm, dw_out = refs.take(4)
    bufs = refs.take(3)
    sems = Sems(refs.one())
    place = Place(plane)
    ca, unit1, w_co, w_in = [Fetch(sems, src, dst) for src, dst in zip(fetched, kept)]
    mem, quarter = place.mem, place.quarter
    pieces = [Fetch(sems, out_part.at[0, mem], out_w.at[0, mem])]
    shares = []
    for d in range(1, n_mem):
        source = lax.rem(mem + jnp.int32(n_mem - d), jnp.int32(n_mem))

        def place_of(t, source=source):
            return out_w.at[:, source, flip(quarter, t)]

        pieces.append(Fetch(sems, out_part.at[:, source, quarter], place_of(0)))
        shares.append(Share(place, sems, place_of(0), place_of))
    rows = h2_vm.shape[0]
    own = rows // 2
    seg = own // 2
    hidden = act_vm.shape[1]
    block = hidden // n_mem
    out_sum = PlaneSum(place, sems, dw_out, own_out, bufs, (0, dw_out.shape[3]))
    spread_final = Spread(
        place,
        sems,
        lambda k: final_vm.at[pl.ds(seg * k, seg)],
        lambda k: final_out.at[place.parity],
    )

    def swap(src, dst):
        send, recv = sems.take(2)
        return remote(src, dst, send, recv, place.twin())

    def half_lanes(ref, i):
        wide = ref.shape[1] // 2
        return ref.at[:, pl.ds(i * wide, wide)]

    swap_co = swap(part_vm, twin_vm)
    swap_h2 = swap(h2_vm.at[pl.ds(0, own)], h2_vm.at[pl.ds(own, own)])
    swap_ffn = [swap(half_lanes(part_vm, i), half_lanes(twin_vm, i)) for i in range(2)]
    swap_df = swap(df_vm.at[pl.ds(0, own)], df_vm.at[pl.ds(own, own)])
    swap_dh2 = [swap(half_lanes(part_vm, i), half_lanes(twin_vm, i)) for i in range(2)]
    swap_dco = swap(dco_vm.at[pl.ds(0, own)], dco_vm.at[pl.ds(own, own)])

    for item in [ca, w_co] + pieces + [unit1, w_in]:
        item.start()
    place.meet(column_peers(n_mem) + plane_peers(plane))
    for item in pieces:
        item.get()
    for share in shares:
        share.start()
    row = {name: rows_ref[i : i + 1, :] for i, name in enumerate(("g0", "b6", "b5", "g1", "b7", "b9", "g2", "b8"))}
    sums_ref[...] = jnp.zeros_like(sums_ref)
    bias_sum[...] = jnp.zeros_like(bias_sum)

    def after(span):
        return pl.ds(pl.multiple_of(span.start + own, BLK), BLK)

    ca, w_co = ca.get(), w_co.get()

    def co_other(span):
        part_vm[span, :] = mm(ca[after(span), :], w_co[...]).astype(BF16)

    tiles(own, co_other)
    swap_co.start()
    unit1 = unit1.get()

    def co_own(span):
        p_vm[span, :] = unit1[span, :] * row["g0"] + row["b6"] + mm(ca[span, :], w_co[...])

    tiles(own, co_own)
    swap_co.wait()

    def second_norm(span):
        values = p_vm[span, :] + twin_vm[span, :].astype(F32) + row["b5"]
        unit, scale = unit_norm(values)
        unit_vm[span, :] = unit
        scale_vm[span, :] = jnp.broadcast_to(scale, (BLK, scale_vm.shape[1]))
        h2_vm[span, :] = (unit * row["g1"] + row["b7"]).astype(BF16)

    tiles(own, second_norm)
    swap_h2.start()
    w_in = w_in.get()

    def forward(span):
        def part(i, carry):
            lanes = pl.ds(pl.multiple_of(i * block, block), block)
            pre = mm(h2_vm[span, :], w_in[:, lanes]) + bias_ref[:, lanes]
            cdf = 0.5 * (1.0 + lax.erf(pre * 0.7071067811865476))
            act_vm[span, lanes] = (pre * cdf).astype(BF16)
            density = jnp.exp(-0.5 * pre * pre) * 0.3989422804014327
            slope_vm[span, lanes] = (cdf + pre * density).astype(BF16)
            return carry

        lax.fori_loop(0, n_mem, part, 0)

    ours, others = pl.ds(0, own), pl.ds(own, own)
    width = h2_vm.shape[1]
    column = width // 2
    forward(ours)
    for share in shares:
        share.forward()
    swap_h2.wait()
    forward(others)
    for share in shares:
        share.wait()
    for i in range(2):
        lanes = slice(i * column, (i + 1) * column)
        weights = out_w[0, :, :, :, lanes].reshape(hidden, column)
        part_vm[:, lanes] = mm(act_vm[others, :], weights).astype(BF16)
        swap_ffn[i].start()
    p_vm[...] = mm(act_vm[ours, :], out_w[0].reshape(hidden, width))
    for copy in swap_ffn:
        copy.wait()

    def third_norm(span):
        values = (
            unit_vm[span, :] * row["g1"]
            + row["b7"]
            + p_vm[span, :]
            + twin_vm[span, :].astype(F32)
            + row["b9"]
        )
        unit, scale = unit_norm(values)
        final_vm[span, :] = (unit * row["g2"] + row["b8"]).astype(BF16)
        grad = cot_vm[span, :].astype(F32)
        out = unit_norm_back(grad, unit, scale, row["g2"])
        dz2_ref[span, :] = out
        low = out.astype(BF16)
        df_vm[span, :] = low
        sums_ref[0:1, :] += jnp.sum(grad * unit, axis=0, keepdims=True)
        sums_ref[1:2, :] += jnp.sum(grad, axis=0, keepdims=True)
        sums_ref[2:3, :] += jnp.sum(low.astype(F32), axis=0, keepdims=True)

    tiles(own, third_norm)
    swap_df.start()
    spread_final.start()
    swap_df.wait()

    def out_weights(m, carry):
        lanes = pl.ds(pl.multiple_of(m * block, block), block)
        dw_out[0, m] = mm(act_vm[:, lanes].T, df_vm[...]).astype(BF16).reshape(dw_out.shape[2:])
        return carry

    lax.fori_loop(0, n_mem, out_weights, 0)
    out_sum.start()

    def hidden_grad(i, carry):
        lanes = pl.ds(pl.multiple_of(i * block, block), block)
        weights = out_w[0, i].reshape(block, width)
        grad = mm(df_vm[...], weights, NT) * slope_vm[:, lanes].astype(F32)
        low = grad.astype(BF16)
        slope_vm[:, lanes] = low
        bias_sum[:, lanes] = jnp.sum(low.astype(F32), axis=0, keepdims=True)
        return carry

    lax.fori_loop(0, n_mem, hidden_grad, 0)
    narrow = width // 4
    for i in range(2):
        for j in (2 * i, 2 * i + 1):
            lanes = slice(j * narrow, (j + 1) * narrow)
            grad = mm(slope_vm[...], w_in[lanes, :], NT)
            part_vm[:, lanes] = grad[own:].astype(BF16)
            dz2_ref[:, lanes] += grad[:own]
        swap_dh2[i].start()
    out_sum.middle()
    for copy in swap_dh2:
        copy.wait()

    def second_back(span):
        grad = dz2_ref[span, :] + twin_vm[span, :].astype(F32)
        unit = unit_vm[span, :]
        out = unit_norm_back(grad, unit, scale_vm[span, :1], row["g1"])
        dz2_ref[span, :] = out
        low = out.astype(BF16)
        dco_vm[span, :] = low
        sums_ref[3:4, :] += jnp.sum(grad * unit, axis=0, keepdims=True)
        sums_ref[4:5, :] += jnp.sum(grad, axis=0, keepdims=True)
        sums_ref[5:6, :] += jnp.sum(low.astype(F32), axis=0, keepdims=True)

    tiles(own, second_back)
    swap_dco.start()
    depth = h2_vm.shape[1] // n_mem

    def in_weights(m, carry):
        lanes = pl.ds(pl.multiple_of(m * depth, depth), depth)
        dw_in[0, m] = mm(h2_vm[:, lanes].T, slope_vm[...]).astype(BF16).reshape(dw_in.shape[2:])
        return carry

    lax.fori_loop(0, n_mem, in_weights, 0)
    swap_dco.wait()

    dca_ref[...] = mm(dco_vm[...], w_co[...], NT).astype(BF16)
    heads = ca.shape[1] // n_mem

    def co_weights(m, carry):
        lanes = pl.ds(pl.multiple_of(m * heads, heads), heads)
        dw_co[0, m] = mm(ca[:, lanes].T, dco_vm[...]).astype(BF16).reshape(dw_co.shape[2:])
        return carry

    lax.fori_loop(0, n_mem, co_weights, 0)
    out_sum.end()
    out_sum.wait_send()
    for k in range(2):
        spread_final.wait_recv(k)
    spread_final.wait_send()


def feed(n_mem, plane, cotangent, vectors, bias, ca, unit1, w_co, w_in, w_out):
    rows, part = ca.shape
    width, hidden = w_in.shape
    own = rows // 2

    def grad_shape(depth, cols):
        return (1, n_mem, plane, depth // (n_mem * plane), cols)

    out_shape, in_shape = grad_shape(hidden, width), grad_shape(width, hidden)
    shapes = [
        jax.ShapeDtypeStruct((2, own // 2, width), BF16),
        jax.ShapeDtypeStruct((rows, part), BF16),
        jax.ShapeDtypeStruct((own, width), F32),
        jax.ShapeDtypeStruct((8, width), F32),
        jax.ShapeDtypeStruct((1, hidden), F32),
        sum_shape(out_shape),
        jax.ShapeDtypeStruct(in_shape, BF16),
        jax.ShapeDtypeStruct(grad_shape(part, width), BF16),
    ]
    fetched = [ca, unit1, w_co, w_in, w_out]
    scratch = [pltpu.VMEM(item.shape, item.dtype) for item in fetched] + [
        pltpu.VMEM((rows, width), BF16),
        pltpu.VMEM((own, width), F32),
        pltpu.VMEM((own, 2 * HD), F32),
        pltpu.VMEM((rows, hidden), BF16),
        pltpu.VMEM((rows, hidden), BF16),
        pltpu.VMEM((own, width), F32),
        pltpu.VMEM((own, width), BF16),
        pltpu.VMEM((own, width), BF16),
        pltpu.VMEM((own, width), BF16),
        pltpu.VMEM((rows, width), BF16),
        pltpu.VMEM((rows, width), BF16),
        pltpu.VMEM(out_shape, BF16),
    ]
    scratch += plane_sum_scratch(out_shape, n_mem, out_shape[3])
    scratch += [pltpu.SemaphoreType.DMA((PLANE_SUM_SEMS + 60,))]
    return pl.pallas_call(
        functools.partial(feed_kernel, n_mem, plane),
        in_specs=[VMEM] * 3 + [ANY] * len(fetched),
        out_specs=[ANY] + [VMEM] * (len(shapes) - 1),
        out_shape=shapes,
        scratch_shapes=scratch,
        compiler_params=pltpu.CompilerParams(
            vmem_limit_bytes=60 * 2**20, collective_id=1, has_side_effects=True
        ),
        cost_estimate=pl.CostEstimate(
            flops=rows * width * hidden * 12, bytes_accessed=40 * 2**20, transcendentals=rows * hidden * 2
        ),
        name="feed",
    )(cotangent, vectors, bias, *fetched)


def middle_kernel(n_mem, plane, planes, settled, slot_ref, member_ref, index_ref, *refs):
    refs = Walk(refs)
    dq_ref, dk_ref, dv_ref, wc_ref, scale_ref, gain_ref = refs.take(6)
    fetched = refs.take(6)
    ready = refs.take(len(settled))
    dsa_ref, dz1_ref, sums_ref, enc_out, own_cross, own_so = refs.take(6)
    outs = refs.take(len(settled))
    kept = refs.take(6)
    wk_t, wv_t, named_ref = refs.take(3)
    theirs, mine, twin_in, pair_in, dw_cross, dw_so, part_vm, twin_vm, dso_vm = refs.take(9)
    cross_bufs, so_bufs = refs.take(3), refs.take(3)
    settle_bufs = [refs.take(3) for _ in settled]
    sems = Sems(refs.one())
    place = Place(plane, planes)
    fetches = [Fetch(sems, src, dst) for src, dst in zip(fetched, kept)]
    h1_ref, enc_ref, dz2_ref, unit_ref, so_ref, sa_ref = kept
    settles = [
        Settle(
            place, sems, ready[i], outs[i], settle_bufs[i], columns, n_mem, (0, ready[i].shape[2])
        )
        for i, columns in enumerate(settled)
    ]
    cross_sum = PlaneSum(place, sems, dw_cross, own_cross, cross_bufs, (0, dw_cross.shape[3]))
    so_sum = PlaneSum(place, sems, dw_so, own_so, so_bufs, (0, dw_so.shape[3]))
    passages = mine.shape[0]
    units = passages // 2
    twin_sems = sems.take(2 * passages)
    twins = [
        remote(theirs.at[u], twin_in.at[u], twin_sems[2 * u], twin_sems[2 * u + 1], place.twin())
        for u in range(passages)
    ]
    pair_sems = sems.take(2 * units)
    pairs = [
        remote(
            mine.at[units + u], pair_in.at[u], pair_sems[2 * u], pair_sems[2 * u + 1], place.pair()
        )
        for u in range(units)
    ]
    homes = [
        Spread(place, sems, lambda k, u=u: mine.at[u], lambda k, u=u: enc_out.at[u], kinds=(0,))
        for u in range(units)
    ]
    swap_sems = sems.take(4)
    own = dz2_ref.shape[0]
    swap_part = remote(part_vm, twin_vm, swap_sems[0], swap_sems[1], place.twin())
    swap_dso = remote(
        dso_vm.at[pl.ds(0, own)], dso_vm.at[pl.ds(own, own)], swap_sems[2], swap_sems[3], place.twin()
    )

    for item in fetches:
        item.start()
    wk_t[...] = wc_ref[1].T
    wv_t[...] = wc_ref[2].T
    place.meet(
        column_peers(n_mem) + plane_peers(plane) + [(2 * plane * r, 0) for r in range(1, planes)]
    )
    for item in settles:
        item.start()

    def passage_grad(u):
        slot = slot_ref[u]
        value = mm(dk_ref[slot], wk_t[...]) + mm(dv_ref[slot], wv_t[...])
        return (value * member_ref[u]).astype(BF16)

    def add_twin(u):
        twins[u].wait_recv()

        def add(i, carry):
            span = pl.ds(pl.multiple_of(i * 64, 64), 64)
            total = mine[u, span, :].astype(F32) + twin_in[u, span, :].astype(F32)
            mine[u, span, :] = total.astype(BF16)
            return carry

        lax.fori_loop(0, PLEN // 64, add, 0)

    def send_home(u):
        add_twin(u)
        pairs[u].wait_recv()

        def add(i, carry):
            span = pl.ds(pl.multiple_of(i * 64, 64), 64)
            total = mine[u, span, :].astype(F32) + pair_in[u, span, :].astype(F32)
            mine[u, span, :] = total.astype(BF16)
            return carry

        lax.fori_loop(0, PLEN // 64, add, 0)
        homes[u].start()

    for group in (range(units, passages), range(units)):
        for u in group:
            theirs[u] = passage_grad(passages + u)
            twins[u].start()
        for u in group:
            mine[u] = passage_grad(u)
        if group.start:
            for u in group:
                add_twin(u)
                pairs[u - units].start()

    for item in fetches:
        item.get()
    for j in range(index_ref.shape[0]):
        named_ref[j * PLEN : (j + 1) * PLEN, :] = enc_ref[index_ref[j]]

    part = dw_cross.shape[-1]
    depth = h1_ref.shape[1] // n_mem

    def stacked(ref):
        return ref[...].reshape(-1, ref.shape[-1])

    def cross_weights(m, carry):
        lanes = pl.ds(pl.multiple_of(m * depth, depth), depth)
        split = dw_cross.shape[2:]
        dw_cross[0, m] = (
            (mm(h1_ref[:, lanes].T, dq_ref[...]) * 0.125).astype(BF16).reshape(split)
        )
        named_t = named_ref[:, lanes].T
        dw_cross[1, m] = mm(named_t, stacked(dk_ref)).astype(BF16).reshape(split)
        dw_cross[2, m] = mm(named_t, stacked(dv_ref)).astype(BF16).reshape(split)
        return carry

    lax.fori_loop(0, n_mem // 2, cross_weights, 0)
    send_home(0)
    lax.fori_loop(n_mem // 2, n_mem, cross_weights, 0)
    cross_sum.start()

    part_vm[...] = (mm(dq_ref[own:, :], wc_ref[0], NT) * 0.125).astype(BF16)
    swap_part.start()
    dz1_ref[...] = dz2_ref[...] + mm(dq_ref[:own, :], wc_ref[0], NT) * 0.125
    sums_ref[...] = jnp.zeros_like(sums_ref)
    sums_ref[3:4, :part] = 0.125 * jnp.sum(dq_ref[...].astype(F32), axis=0, keepdims=True)
    sums_ref[4:5, :part] = jnp.sum(stacked(dv_ref).astype(F32), axis=0, keepdims=True)
    send_home(1)
    swap_part.wait()
    gain = gain_ref[...]

    def norm(span):
        grad = dz1_ref[span, :] + twin_vm[span, :].astype(F32)
        unit = unit_ref[span, :]
        inner = grad * gain
        out = (
            inner
            - jnp.mean(inner, axis=-1, keepdims=True)
            - unit * jnp.mean(inner * unit, axis=-1, keepdims=True)
        ) * scale_ref[span, :1]
        dz1_ref[span, :] = out
        low = out.astype(BF16)
        dso_vm[span, :] = low
        sums_ref[0:1, :] += jnp.sum(grad * unit, axis=0, keepdims=True)
        sums_ref[1:2, :] += jnp.sum(grad, axis=0, keepdims=True)
        sums_ref[2:3, :] += jnp.sum(low.astype(F32), axis=0, keepdims=True)

    tiles(own, norm)
    swap_dso.start()
    cross_sum.middle()

    dsa_ref[:own, :] = mm(dso_vm[:own, :], so_ref[...], NT).astype(BF16)
    for u in range(2, units):
        send_home(u)
    swap_dso.wait()
    dsa_ref[own:, :] = mm(dso_vm[own:, :], so_ref[...], NT).astype(BF16)
    block = sa_ref.shape[1] // n_mem

    def so_weights(m, carry):
        lanes = pl.ds(pl.multiple_of(m * block, block), block)
        dw_so[0, m] = (
            mm(sa_ref[:, lanes].T, dso_vm[...]).astype(BF16).reshape(dw_so.shape[2:])
        )
        return carry

    lax.fori_loop(0, n_mem, so_weights, 0)
    so_sum.start()
    for item in settles:
        item.middle()
    cross_sum.end()
    for item in settles:
        item.forward()
    so_sum.middle()
    for item in settles:
        item.end()
    so_sum.end()
    cross_sum.wait_send()
    so_sum.wait_send()
    for copy in twins + pairs:
        copy.wait_send()
    for item in homes:
        item.wait_recv(0)
        item.wait_send()


def middle(
    n_mem, plane, planes, slot, member, index, dq, dk, dv, wc, so, sa, h1, enc, dz2, unit, scale, gain, ready
):
    rows, part = dq.shape
    width = h1.shape[1]
    own = rows // 2
    passages = slot.shape[0] // 2
    settled = tuple(columns for _, columns in ready)
    settled_shapes = [item.shape[:2] + (plane,) + item.shape[2:] for item, _ in ready]
    cross_shape = (3, n_mem, plane, width // (n_mem * plane), part)
    so_shape = (1, n_mem, plane, part // (n_mem * plane), width)
    shapes = [
        jax.ShapeDtypeStruct((rows, part), BF16),
        jax.ShapeDtypeStruct((own, width), F32),
        jax.ShapeDtypeStruct((8, width), F32),
        jax.ShapeDtypeStruct((passages // 2, PLEN, width), BF16),
        sum_shape(cross_shape),
        sum_shape(so_shape),
    ] + [reduce_out(shape, columns, plane) for shape, columns in zip(settled_shapes, settled)]
    fetched = [h1, enc, dz2, unit, so, sa]
    scratch = [pltpu.VMEM(item.shape, item.dtype) for item in fetched] + [
        pltpu.VMEM((part, width), BF16),
        pltpu.VMEM((part, width), BF16),
        pltpu.VMEM(dk.shape[:1] + (width,), BF16),
        pltpu.VMEM((passages, PLEN, width), BF16),
        pltpu.VMEM((passages, PLEN, width), BF16),
        pltpu.VMEM((passages, PLEN, width), BF16),
        pltpu.VMEM((passages // 2, PLEN, width), BF16),
        pltpu.VMEM(cross_shape, BF16),
        pltpu.VMEM(so_shape, BF16),
        pltpu.VMEM((own, width), BF16),
        pltpu.VMEM((own, width), BF16),
        pltpu.VMEM((rows, width), BF16),
    ]
    scratch += plane_sum_scratch(cross_shape, n_mem, cross_shape[3])
    scratch += plane_sum_scratch(so_shape, n_mem, so_shape[3])
    for shape in settled_shapes:
        scratch += settle_scratch(shape, n_mem, plane, planes, shape[3])
    count = (
        len(ready) * settle_sems(n_mem, plane, planes) + 2 * PLANE_SUM_SEMS + 2 * passages
        + passages + 4 * passages // 2 + 4 + 6
    )
    smem = pl.BlockSpec(memory_space=pltpu.SMEM)
    outs = pl.pallas_call(
        functools.partial(middle_kernel, n_mem, plane, planes, settled),
        in_specs=[smem, smem, smem] + [VMEM] * 6 + [ANY] * 6 + [VMEM] * len(ready),
        out_specs=[VMEM] * 3 + [ANY] + [VMEM] * (2 + len(ready)),
        out_shape=shapes,
        scratch_shapes=scratch + [pltpu.SemaphoreType.DMA((count,))],
        compiler_params=pltpu.CompilerParams(
            vmem_limit_bytes=60 * 2**20, collective_id=3, has_side_effects=True
        ),
        cost_estimate=pl.CostEstimate(
            flops=rows * part * width * 30, bytes_accessed=40 * 2**20, transcendentals=0
        ),
        name="middle",
    )(
        slot,
        member,
        index,
        dq,
        dk.reshape(-1, PLEN, part),
        dv.reshape(-1, PLEN, part),
        wc,
        scale,
        gain,
        *fetched,
        *[item for item, _ in ready],
    )
    return outs[:4], outs[4:6], outs[6:]


def self_attend_back(place, pair, q_vm, k_vm, v_vm, o_vm, do_vm, lse_vm, outs, scratch):
    dq_vm, dk_vm, dv_vm = outs
    q_a, do_a, k_t, q_h, do_h, p_vm, ds_vm = scratch
    base = 2 * place.core + place.parity
    count = q_vm.shape[0] // BLK
    lanes = pl.ds(pl.multiple_of(pair * 2 * HD, 2 * HD), 2 * HD)

    def rows(i):
        return pl.ds(pl.multiple_of(flip(base, i) * BLK, BLK), BLK)

    for i in range(count):
        span = slice(i * BLK, (i + 1) * BLK)
        q_a[span, :] = q_vm[rows(i), lanes]
        do_a[span, :] = do_vm[rows(i), lanes]
        k_t[:, span] = k_vm[rows(i), lanes].T
        q_t = q_a[span, :].T
        do_t = do_a[span, :].T
        prod = (do_a[span, :].astype(F32) * o_vm[rows(i), lanes].astype(F32)).T
        for head in range(2):
            delta = jnp.sum(prod[head * HD : (head + 1) * HD, :], axis=0, keepdims=True)
            q_h[head, :, span] = head_rows(q_t, head, lse_vm[pair, head : head + 1, span])
            do_h[head, :, span] = head_rows(do_t, head, delta)
    key_pos = lax.broadcasted_iota(jnp.int32, (BLK, BLK), 0)
    query_pos = lax.broadcasted_iota(jnp.int32, (BLK, BLK), 1)
    units = [(j, i, head) for j in range(count) for head in range(2) for i in range(j, count)]

    def products(unit):
        j, i, head = unit
        span = slice(i * BLK, (i + 1) * BLK)
        return (
            mm(ones_in(k_vm[rows(j), lanes], head), q_h[head, :, span]),
            mm(ones_in(v_vm[rows(j), lanes], head), do_h[head, :, span]),
        )

    ready = products(units[0])
    halves = {}
    for n, (j, i, head) in enumerate(units):
        coming = products(units[n + 1]) if n + 1 < len(units) else None
        scores, dprobs = ready
        probs = jnp.exp(scores)
        if i == j:
            probs = jnp.where(key_pos <= query_pos, probs, 0.0)
        keys, span = slice(j * BLK, (j + 1) * BLK), slice(i * BLK, (i + 1) * BLK)
        p_vm[head, keys, span] = probs.astype(BF16)
        ds_vm[head, keys, span] = (probs * dprobs).astype(BF16)
        if i == count - 1:
            late = slice(j * BLK, count * BLK)
            halves[head] = (
                mm(p_vm[head, keys, late], do_a[late, :]),
                mm(ds_vm[head, keys, late], q_a[late, :]),
            )
            if head == 1:
                dv_vm[rows(j), lanes] = pick_heads(halves[0][0], halves[1][0]).astype(BF16)
                dk_vm[rows(j), lanes] = pick_heads(halves[0][1], halves[1][1]).astype(BF16)
        ready = coming
    for i in range(count):
        span, keys = slice(i * BLK, (i + 1) * BLK), slice(0, (i + 1) * BLK)
        dq_t = jnp.concatenate(
            [
                mm(k_t[head * HD : (head + 1) * HD, keys], ds_vm[head, keys, span])
                for head in range(2)
            ],
            axis=0,
        )
        dq_vm[rows(i), lanes] = dq_t.T.astype(BF16) * BF16(0.125)


def last_kernel(n_mem, plane, planes, settled, chunks, *refs):
    refs = Walk(refs)
    q_ref, k_ref, v_ref, o_ref, do_ref, lse_ref, feed_ref, hidden_ref, middle_ref = refs.take(9)
    fetched = refs.take(3)
    ready = refs.take(len(settled))
    small_out, dx_out, self_out = refs.take(3)
    outs = refs.take(len(settled))
    x_ref, w_ref, dz1_ref = kept = refs.take(3)
    dq_vm, dk_vm, dv_vm = refs.take(3)
    attend_scratch = refs.take(7)
    x_t, dw_vm = refs.take(2)
    part_vm, twin_vm, dx_vm = refs.take(3)
    chunk_own = [refs.one() for _ in range(chunks)]
    chunk_bufs = [refs.take(3) for _ in range(chunks)]
    chunk_settle = [refs.take(3) for _ in range(chunks)]
    settle_bufs = [refs.take(3) for _ in settled]
    small_near, small_line, small_twin, small_far, small_sum, sem_ref = refs.take(6)
    sems = Sems(sem_ref)
    place = Place(plane, planes)
    fetches = [Fetch(sems, src, dst) for src, dst in zip(fetched, kept)]
    settles = [
        Settle(
            place, sems, ready[i], outs[i], settle_bufs[i], columns, n_mem, (0, ready[i].shape[2])
        )
        for i, columns in enumerate(settled)
    ]
    rows, part = q_ref.shape
    lanes = part // chunks
    depth = dw_vm.shape[3]
    sums = [
        PlaneSum(
            place, sems, dw_vm, chunk_own[c], chunk_bufs[c], (0, depth), (c * lanes, lanes)
        )
        for c in range(chunks)
    ]
    ends = [
        Settle(
            place, sems, chunk_own[c], self_out, chunk_settle[c], True, n_mem, (0, depth), c * lanes
        )
        for c in range(chunks)
    ]
    near_sems = sems.take(6)
    near = [
        remote(
            small_sum, small_near.at[t - 1], near_sems[2 * t - 2], near_sems[2 * t - 1], place.near(t)
        )
        for t in range(1, plane)
    ]
    line = Line(
        place, sems, lambda s: small_sum.at[flip(place.mem, s)], lambda s: small_line.at[s - 1], n_mem
    )
    twin_sems = sems.take(2)
    twin = remote(small_sum.at[place.mem], small_twin, twin_sems[0], twin_sems[1], place.twin())
    far_sems = sems.take(2 * (planes - 1))
    far = [
        remote(
            small_sum.at[place.mem],
            small_far.at[r - 1],
            far_sems[2 * r - 2],
            far_sems[2 * r - 1],
            place.far(r),
        )
        for r in range(1, planes)
    ]
    seg = dx_out.shape[1]
    own = 2 * seg
    spread = Spread(
        place,
        sems,
        lambda k: dx_vm.at[pl.ds(seg * k, seg)],
        lambda k: dx_out.at[place.parity],
    )
    swap_sems = sems.take(2)
    swap_part = remote(part_vm, twin_vm, swap_sems[0], swap_sems[1], place.twin())

    for item in fetches:
        item.start()
    place.meet(
        column_peers(n_mem) + plane_peers(plane) + [(2 * plane * r, 0) for r in range(1, planes)]
    )
    for item in settles:
        item.start()
    block = x_ref.shape[1] // n_mem

    def input_part(span):
        return (
            mm(dq_vm[span, :], w_ref[0], NT)
            + mm(dk_vm[span, :], w_ref[1], NT)
            + mm(dv_vm[span, :], w_ref[2], NT)
        )

    pairs = part // (2 * HD)
    late = []
    for c in range(chunks):
        for pair in range(c * pairs // chunks, (c + 1) * pairs // chunks):
            self_attend_back(
                place,
                pair,
                q_ref,
                k_ref,
                v_ref,
                o_ref,
                do_ref,
                lse_ref,
                (dq_vm, dk_vm, dv_vm),
                attend_scratch,
            )
        if c == 0:
            for item in fetches:
                item.get()
            for m in range(n_mem):
                x_t[m] = x_ref[:, m * block : (m + 1) * block].T
        span = slice(c * lanes, (c + 1) * lanes)

        def weights(m, carry, span=span):
            for i, grad in enumerate((dq_vm, dk_vm, dv_vm)):
                dw_vm[i, m, :, :, span] = (
                    mm(x_t[m], grad[:, span]).astype(BF16).reshape(plane, depth, lanes)
                )
            return carry

        if c < chunks - 2:
            lax.fori_loop(0, n_mem, weights, 0)
            sums[c].start()
        if c == 1:
            sums[0].middle()
        if c == 2:
            for item in settles:
                item.middle()
            sums[0].end()
            ends[0].start()
            sums[1].middle()
        late.append(weights)
    part_vm[...] = input_part(slice(own, 2 * own)).astype(BF16)
    swap_part.start()
    lax.fori_loop(0, n_mem, late[-2], 0)
    sums[-2].start()
    swap_part.wait()
    total = dz1_ref[...] + input_part(slice(0, own)) + twin_vm[...].astype(F32)
    dx_vm[...] = total.astype(BF16)
    spread.start()
    lax.fori_loop(0, n_mem, late[-1], 0)
    sums[-1].start()
    sums[1].end()
    ends[1].start()
    for item in settles:
        item.forward()
    sums[-2].middle()

    small_sum[...] = jnp.zeros_like(small_sum)
    wide = small_sum.shape[2]
    unit = wide // 2
    first = place.core == 0
    for row, ref, at in (
        (2, middle_ref, 2),
        (5, feed_ref, 5),
        (6, middle_ref, 1),
        (7, feed_ref, 4),
        (8, feed_ref, 1),
        (9, feed_ref, 2),
        (10, middle_ref, 0),
        (11, feed_ref, 3),
        (12, feed_ref, 0),
    ):
        for b in range(n_mem):
            small_sum[b, row : row + 1, :] = ref[at : at + 1, b * wide : (b + 1) * wide]
    for row, value in (
        (0, jnp.sum(dq_vm[...].astype(F32), axis=0, keepdims=True)),
        (1, jnp.sum(dv_vm[...].astype(F32), axis=0, keepdims=True)),
        (3, middle_ref[3:4, :part]),
        (4, middle_ref[4:5, :part]),
    ):
        for b in range(n_mem):
            side = value[:, b * unit : (b + 1) * unit]
            none = jnp.zeros_like(side)
            small_sum[b, row : row + 1, :unit] = jnp.where(first, side, none)
            small_sum[b, row : row + 1, unit:] = jnp.where(first, none, side)
    count = hidden_ref.shape[1] // (n_mem * wide)
    for b in range(n_mem):
        for i in range(count):
            at = (b * count + i) * wide
            side = hidden_ref[:, at : at + wide]
            none = jnp.zeros_like(side)
            row = 13 + i
            small_sum[b, row : row + 1, :] = jnp.where(first, side, none)
            small_sum[b, row + count : row + count + 1, :] = jnp.where(first, none, side)
    for copy in near:
        copy.start()
    sums[-1].middle()
    sums[-2].end()
    ends[-2].start()
    ends[0].middle()
    for copy in near:
        copy.wait()
    total = small_sum[...]
    for t in range(plane - 1):
        total += small_near[t]
    small_sum[...] = total
    line.start()
    sums[-1].end()
    ends[-1].start()
    ends[1].middle()
    ends[0].forward()
    for item in settles:
        item.end()
    ends[-2].middle()
    ends[1].forward()
    for s in range(1, n_mem):
        line.wait_recv(s)
    line.wait_send()
    value = small_sum[place.mem]
    for s in range(n_mem - 1):
        value += small_line[s]
    small_sum[place.mem] = value
    twin.start()
    ends[-1].middle()
    ends[-2].forward()
    for item in ends[:-2]:
        item.end()
    twin.wait()
    value = small_sum[place.mem] + small_twin[...]
    if far:
        small_sum[place.mem] = value
        for copy in far:
            copy.start()
        for copy in far:
            copy.wait()
        for r in range(planes - 1):
            value += small_far[r]
    small_out[...] = value
    ends[-1].forward()
    ends[-2].end()
    ends[-1].end()
    for item in sums:
        item.wait_send()
    for k in range(2):
        spread.wait_recv(k)
    spread.wait_send()


def last(n_mem, plane, planes, q, k, v, o, do, lse, x, w, dz1, sums, small_shape, ready):
    rows, part = q.shape
    chunks = part // (2 * HD)
    width = x.shape[1]
    own = rows // 2
    settled = tuple(columns for _, columns in ready)
    settled_shapes = [item.shape[:2] + (plane,) + item.shape[2:] for item, _ in ready]
    grad_shape = (3, n_mem, plane, width // (n_mem * plane), part)
    depth, lanes = grad_shape[3], part // chunks
    small_part = small_shape[1:]
    shapes = [
        jax.ShapeDtypeStruct(small_part, F32),
        jax.ShapeDtypeStruct((2, own // 2, width), BF16),
        reduce_out(grad_shape, True, plane),
    ] + [reduce_out(shape, columns, plane) for shape, columns in zip(settled_shapes, settled)]
    fetched = [x, w, dz1]
    scratch = (
        [pltpu.VMEM(item.shape, item.dtype) for item in fetched]
        + [pltpu.VMEM((rows, part), BF16)] * 3
        + [
            pltpu.VMEM((rows, 2 * HD), BF16),
            pltpu.VMEM((rows, 2 * HD), BF16),
            pltpu.VMEM((2 * HD, rows), BF16),
            pltpu.VMEM((2, 2 * HD, rows), BF16),
            pltpu.VMEM((2, 2 * HD, rows), BF16),
            pltpu.VMEM((2, rows, rows), BF16),
            pltpu.VMEM((2, rows, rows), BF16),
            pltpu.VMEM((n_mem, width // n_mem, rows), BF16),
            pltpu.VMEM(grad_shape, BF16),
        ]
        + [pltpu.VMEM((own, width), BF16)] * 3
        + [pltpu.VMEM((3, n_mem, depth, lanes), BF16)] * chunks
    )
    for _ in range(chunks):
        scratch += plane_sum_scratch(grad_shape, n_mem, depth, lanes)
    for _ in range(chunks):
        scratch += settle_scratch(grad_shape, n_mem, plane, planes, depth, lanes)
    for shape in settled_shapes:
        scratch += settle_scratch(shape, n_mem, plane, planes, shape[3])
    scratch += [
        pltpu.VMEM((plane - 1,) + small_shape, F32),
        pltpu.VMEM((n_mem - 1,) + small_part, F32),
        pltpu.VMEM(small_part, F32),
        pltpu.VMEM((max(planes - 1, 1),) + small_part, F32),
        pltpu.VMEM(small_shape, F32),
        pltpu.SemaphoreType.DMA(
            (
                (len(ready) + chunks) * settle_sems(n_mem, plane, planes)
                + chunks * PLANE_SUM_SEMS
                + 24
                + 2 * planes,
            )
        ),
    ]
    outs = pl.pallas_call(
        functools.partial(last_kernel, n_mem, plane, planes, settled, chunks),
        in_specs=[VMEM] * 9 + [ANY] * 3 + [VMEM] * len(ready),
        out_specs=[VMEM, ANY, VMEM] + [VMEM] * len(ready),
        out_shape=shapes,
        scratch_shapes=scratch,
        compiler_params=pltpu.CompilerParams(
            vmem_limit_bytes=60 * 2**20, collective_id=4, has_side_effects=True
        ),
        cost_estimate=pl.CostEstimate(
            flops=rows * rows * width * 40, bytes_accessed=40 * 2**20, transcendentals=rows * rows * 8
        ),
        name="last",
    )(q, k, v, o, do, lse, *sums, *fetched, *[item for item, _ in ready])
    return outs[0], outs[1], outs[2:]


def cross_forward_kernel(n_mem, plane, kinds, index_ref, q_ref, k_ref, v_ref, cot_ref, *refs):
    refs = Walk(refs)
    count_w = len(kinds)
    shards = refs.take(count_w)
    o_ref, lse_ref, cot_out = refs.take(3)
    halves = refs.take(count_w)
    v_t, o_t, sem_ref = refs.take(3)
    sems = Sems(sem_ref)
    place = Place(plane)
    step = pl.program_id(0) * pl.num_programs(1) + pl.program_id(1)
    last = pl.num_programs(0) * pl.num_programs(1) - 1
    seg = cot_ref.shape[1]
    spread = Spread(
        place,
        sems,
        lambda k: cot_ref.at[flip(place.parity, k)],
        lambda k: cot_out.at[pl.ds(seg * k, seg)],
    )
    gathers = [
        Gather(place, sems, shard, half, columns, n_mem, i != 1)
        for i, (shard, half, columns) in enumerate(zip(shards, halves, kinds))
    ]
    @pl.when(step == 0)
    def _():
        for gather in gathers:
            gather.own.start()
        place.meet(column_peers(n_mem) + plane_peers(plane))
        for gather in gathers:
            gather.begin()

    rows = q_ref.shape[0]
    count = index_ref.shape[0]

    @pl.when(pl.program_id(1) == 0)
    def _():
        for j in range(count):
            v_t[:, j * BLK : (j + 1) * BLK] = v_ref[index_ref[j]].T

    units = []
    for i in range(rows // BLK):
        q_t = q_ref[i * BLK : (i + 1) * BLK, :].T
        for head in range(2):
            q_head = head_rows(q_t, head)

            def score(j, q_head=q_head):
                return mm(k_ref[index_ref[j]], q_head)

            def value(j, head=head):
                return v_t[head * HD : (head + 1) * HD, j * BLK : (j + 1) * BLK]

            units.append(
                (
                    [functools.partial(score, j) for j in range(count)],
                    [functools.partial(value, j) for j in range(count)],
                    (i, head),
                )
            )

    def finish(tag, mixed, lse):
        i, head = tag
        span = slice(i * BLK, (i + 1) * BLK)
        o_t[head * HD : (head + 1) * HD, span] = mixed
        lse_ref[0, head : head + 1, span] = lse

    whole_one, line_one = gathers
    plan = {
        4: [lambda: whole_one.share(1)],
        6: [lambda: line_one.share(1)],
        10: [lambda: whole_one.share(2), lambda: whole_one.forward(1)],
        12: [lambda: line_one.share(2)],
        14: [spread.start],
        17: [lambda: whole_one.share(3), lambda: whole_one.forward(2)],
        19: [lambda: line_one.share(3)],
        23: [lambda: whole_one.forward(3)],
    }

    def serve(n):
        for when, calls in plan.items():
            if when % len(units) == n:

                @pl.when(step == when // len(units))
                def _():
                    for call in calls:
                        call()

    softmax_units(units, finish, serve)
    o_ref[...] = o_t[...].T.astype(BF16)

    @pl.when(step == last)
    def _():
        for gather in gathers:
            gather.finish()
        for k in range(2):
            spread.wait_recv(k)
        spread.wait_send()


def cross_forward(n_mem, plane, index, q, k, v, cotangent, params):
    rows, width = q.shape
    pairs = width // (2 * HD)
    keys = index.shape[0] * PLEN
    block = 2 * BLK
    question = pl.BlockSpec((block, 2 * HD), lambda h, i: (i, h))
    memory = pl.BlockSpec(k.shape[:2] + (2 * HD,), lambda h, i: (0, 0, h))
    kinds = tuple(columns for _, columns in params)
    views = [half_views(shard, columns, n_mem, plane) for shard, columns in params]
    outs = pl.pallas_call(
        functools.partial(cross_forward_kernel, n_mem, plane, kinds),
        grid=(pairs, rows // block),
        in_specs=[
            pl.BlockSpec(memory_space=pltpu.SMEM),
            question,
            memory,
            memory,
            whole(cotangent.shape),
        ]
        + [whole(view.shape) for view, _ in views],
        out_specs=[question, pl.BlockSpec((1, 2, block), lambda h, i: (h, 0, i)), ANY]
        + [ANY] * len(params),
        out_shape=[
            jax.ShapeDtypeStruct((rows, width), BF16),
            jax.ShapeDtypeStruct((pairs, 2, rows), F32),
            jax.ShapeDtypeStruct((2 * cotangent.shape[1], cotangent.shape[2]), BF16),
        ]
        + [jax.ShapeDtypeStruct(full, BF16) for _, full in views],
        scratch_shapes=[
            pltpu.VMEM((2 * HD, keys), BF16),
            pltpu.VMEM((2 * HD, block), F32),
            pltpu.SemaphoreType.DMA((4 + GATHER_SEMS * len(params),)),
        ],
        compiler_params=pltpu.CompilerParams(
            vmem_limit_bytes=60 * 2**20, collective_id=2, has_side_effects=True
        ),
        cost_estimate=pl.CostEstimate(
            flops=rows * keys * width * 16,
            bytes_accessed=rows * width * 4 + k.size * 4,
            transcendentals=rows * keys * pairs * 2,
        ),
        name="cross_forward",
    )(index, q, k, v, cotangent, *[view for view, _ in views])
    return outs[:3], outs[3:]


def cross_backward_kernel(
    n_mem, plane, planes, chunks, settled, index_ref, q_ref, k_ref, v_ref, o_ref, do_ref, lse_ref, *refs
):
    refs = Walk(refs)
    kinds = {which: columns for which, columns, _ in chunks}
    grads = refs.take(len(kinds))
    ready = refs.take(len(settled))
    dq_ref, dk_ref, dv_ref = refs.take(3)
    outs = refs.take(len(kinds))
    ready_outs = refs.take(len(settled))
    q_h, do_h, dq_t, p_vm, ds_vm = refs.take(5)
    sems = Sems(refs.refs[-1])
    place = Place(plane, planes)
    sums, settles = [], []
    for which, columns, rows_of in chunks:
        own = refs.one()
        sums.append(PlaneSum(place, sems, grads[which], own, refs.take(3), rows_of))
        settles.append(
            Settle(place, sems, own, outs[which], refs.take(3), columns, n_mem, rows_of)
        )
    first = [
        Settle(
            place, sems, ready[i], ready_outs[i], refs.take(3), columns, n_mem, (0, ready[i].shape[2])
        )
        for i, columns in enumerate(settled)
    ]
    passage = pl.program_id(1)
    step = pl.program_id(0) * pl.num_programs(1) + passage
    steps = pl.num_programs(0) * pl.num_programs(1)
    rows = q_ref.shape[0]
    count = rows // BLK

    @pl.when(step == 0)
    def _():
        place.meet(
            column_peers(n_mem) + plane_peers(plane) + [(2 * plane * r, 0) for r in range(1, planes)]
        )
        for item in first:
            item.start()

    def at(when, *calls):
        @pl.when(step == when)
        def _():
            for call in calls:
                call()

    for i, (plane_sum, settle) in enumerate(zip(sums, settles)):
        at(3 * i, plane_sum.start)
        at(3 * i + 2, plane_sum.middle)
        at(3 * i + 4, plane_sum.end, settle.start)
        at(3 * i + 7, settle.middle)
        at(3 * i + 8, settle.forward)
    for item in first:
        at(6, item.middle)
        at(7, item.forward)

    @pl.when(passage == 0)
    def _():
        for i in range(count):
            span = slice(i * BLK, (i + 1) * BLK)
            q_t = q_ref[span, :].T
            grads_t = do_ref[span, :].T
            prod = (do_ref[span, :].astype(F32) * o_ref[span, :].astype(F32)).T
            for head in range(2):
                delta = jnp.sum(prod[head * HD : (head + 1) * HD, :], axis=0, keepdims=True)
                q_h[head, :, span] = head_rows(q_t, head, lse_ref[0, head : head + 1, span])
                do_h[head, :, span] = head_rows(grads_t, head, delta)
        dq_t[...] = jnp.zeros_like(dq_t)

    keys = dk_ref.shape[0] // BLK
    slots = [index_ref[passage * keys + j] for j in range(keys)]
    k_t = jnp.concatenate([k_ref[slot].T for slot in slots], axis=1)
    units = [(head, j, i) for head in range(2) for j in range(keys) for i in range(count)]

    def products(unit):
        head, j, i = unit
        span = slice(i * BLK, (i + 1) * BLK)
        return (
            mm(ones_in(k_ref[slots[j]], head), q_h[head, :, span]),
            mm(ones_in(v_ref[slots[j]], head), do_h[head, :, span]),
        )

    coming = products(units[0])
    halves = []
    for n, (head, j, i) in enumerate(units):
        scores, dprobs = coming
        if n + 1 < len(units):
            coming = products(units[n + 1])
        tile, span = slice(j * BLK, (j + 1) * BLK), slice(i * BLK, (i + 1) * BLK)
        probs = jnp.exp(scores)
        p_vm[head, tile, span] = probs.astype(BF16)
        ds_vm[head, tile, span] = (probs * dprobs).astype(BF16)
        if (j, i) == (keys - 1, count - 1):
            half = slice(head * HD, (head + 1) * HD)
            halves.append((mm(p_vm[head], do_ref[...]), mm(ds_vm[head], q_ref[...])))
            dq_t[half, :] += mm(k_t[half, :], ds_vm[head])
    dv_ref[...] = pick_heads(halves[0][0], halves[1][0]).astype(BF16)
    dk_ref[...] = pick_heads(halves[0][1], halves[1][1]).astype(BF16)

    @pl.when(passage == pl.num_programs(1) - 1)
    def _():
        dq_ref[...] = dq_t[...].T.astype(BF16)

    @pl.when(step == steps - 1)
    def _():
        for settle in first + settles:
            settle.end()
        for item in sums:
            item.wait_send()


def cross_backward(n_mem, plane, planes, index, q, k, v, o, do, lse, grads, ready):
    rows, width = q.shape
    pairs = width // (2 * HD)
    block = 2 * PLEN
    keys = index.shape[0] * PLEN
    passages = keys // block
    question = pl.BlockSpec((rows, 2 * HD), lambda h, u: (0, h))
    memory = pl.BlockSpec(k.shape[:2] + (2 * HD,), lambda h, u: (0, 0, h))
    grads_of = pl.BlockSpec((block, 2 * HD), lambda h, u: (u, h))
    shapes, chunks, scratch = [], [], []
    for which, (grad, columns, pieces) in enumerate(grads):
        lead, _, _, depth, cols = grad.shape
        count = depth // pieces
        shapes.append(reduce_out(grad.shape, columns, plane))
        for i in range(pieces):
            chunks.append((which, columns, (i * count, count)))
            scratch.append(pltpu.VMEM((lead, n_mem, count, cols), BF16))
            scratch += plane_sum_scratch(grad.shape, n_mem, count)
            scratch += settle_scratch(grad.shape, n_mem, plane, planes, count)
    settled = tuple(columns for _, columns in ready)
    for item, columns in ready:
        shape = item.shape[:2] + (plane,) + item.shape[2:]
        shapes.append(reduce_out(shape, columns, plane))
        scratch += settle_scratch(shape, n_mem, plane, planes, shape[3])
    outs = pl.pallas_call(
        functools.partial(cross_backward_kernel, n_mem, plane, planes, tuple(chunks), settled),
        grid=(pairs, passages),
        in_specs=[
            pl.BlockSpec(memory_space=pltpu.SMEM),
            question,
            memory,
            memory,
            question,
            question,
            pl.BlockSpec((1, 2, rows), lambda h, u: (h, 0, 0)),
        ]
        + [ANY] * len(grads)
        + [whole(item.shape) for item, _ in ready],
        out_specs=[question, grads_of, grads_of]
        + [whole(item.shape) for item in shapes],
        out_shape=[
            jax.ShapeDtypeStruct((rows, width), BF16),
            jax.ShapeDtypeStruct((keys, width), BF16),
            jax.ShapeDtypeStruct((keys, width), BF16),
        ]
        + shapes,
        scratch_shapes=[
            pltpu.VMEM((2, 2 * HD, rows), BF16),
            pltpu.VMEM((2, 2 * HD, rows), BF16),
            pltpu.VMEM((2 * HD, rows), F32),
            pltpu.VMEM((2, block, rows), BF16),
            pltpu.VMEM((2, block, rows), BF16),
        ]
        + scratch
        + [
            pltpu.SemaphoreType.DMA(
                (
                    len(chunks) * PLANE_SUM_SEMS
                    + (len(chunks) + len(ready)) * settle_sems(n_mem, plane, planes),
                )
            )
        ],
        compiler_params=pltpu.CompilerParams(
            vmem_limit_bytes=56 * 2**20, collective_id=5, has_side_effects=True
        ),
        cost_estimate=pl.CostEstimate(
            flops=rows * keys * width * 40,
            bytes_accessed=rows * width * 10 + k.size * 8,
            transcendentals=rows * keys * pairs * 2,
        ),
        name="cross_backward",
    )(index, q, k, v, o, do, lse, *[item[0] for item in grads], *[item for item, _ in ready])
    return outs[:3], outs[3:]


def widen_kernel(*refs):
    count = len(refs) // 2
    for src, dst in zip(refs[:count], refs[count:]):
        dst[...] = src[...].astype(F32)


def widen(pairs):
    steps = 8
    flats = [value.reshape(-1, like.shape[-1]) for value, like in pairs]
    blocks = [
        pl.BlockSpec((item.shape[0] // steps, item.shape[1]), lambda i: (i, 0)) for item in flats
    ]
    outs = pl.pallas_call(
        widen_kernel,
        grid=(steps,),
        in_specs=blocks,
        out_specs=blocks,
        out_shape=[jax.ShapeDtypeStruct(item.shape, F32) for item in flats],
        compiler_params=pltpu.CompilerParams(vmem_limit_bytes=60 * 2**20),
        cost_estimate=pl.CostEstimate(
            flops=0, bytes_accessed=6 * sum(item.size for item in flats), transcendentals=0
        ),
        name="widen",
    )(*flats)
    return [out.reshape(like.shape) for out, (_, like) in zip(outs, pairs)]


def body(
    hidden_in,
    encoder_rows,
    passage_map,
    self_qkv,
    self_out,
    cross_qkv,
    cross_out,
    ffn_in,
    ffn_out,
    ffn_in_bias,
    biases,
    gains,
    cotangent,
):
    n_pb = lax.axis_size("pb")
    n_mem = lax.axis_size("mem")
    columns = n_pb // 2
    plane = min(columns, 4)
    pb = lax.axis_index("pb")
    core = pb % 2
    width = hidden_in.shape[2]
    planes = columns // plane

    enc_local = encoder_rows.reshape(-1, PLEN, width)
    n_bias, n_gain = biases.shape[0], gains.shape[0]
    small = jnp.concatenate([biases, gains, ffn_in_bias.reshape(-1, biases.shape[1])], axis=0)
    n_small = small.shape[0]
    small_rows = -(-n_small // 16) * 16
    small = jnp.pad(small, ((0, small_rows - n_small), (0, 0)))
    rows_out, halves, kept = front(
        n_mem,
        plane,
        (n_bias, n_gain),
        hidden_in,
        enc_local,
        passage_map,
        small,
        [(self_qkv, True), (self_out, False), (cross_qkv, True), (cross_out, False)],
    )
    x_full, enc_full, index, small = rows_out
    sq, sk, sv, sa, self_lse, h1_full, unit1, scale1, cq, ck, cv = kept
    index = index.reshape(-1)

    def flat(half):
        lead, _, _, _, cols = half.shape
        return half.reshape(lead, -1, cols)

    w_self, w_cross = flat(halves[0]), flat(halves[2])
    w_self_out, w_cross_out = flat(halves[1])[0], flat(halves[3])[0]
    small = small.astype(F32)
    vectors = small[:, : n_bias + n_gain].transpose(1, 0, 2).reshape(n_bias + n_gain, width)
    bias, gain = vectors[:n_bias], vectors[n_bias:]
    ffn_bias = small[:, n_bias + n_gain : n_small].reshape(-1)

    def half_of(vector):
        parts = vector.reshape(n_mem, 2, -1)
        return jnp.where(core == 0, parts[:, 0], parts[:, 1]).reshape(-1)

    order = jnp.arange(encoder_rows.shape[1] * n_mem, dtype=jnp.int32)
    hits = index[None, :] == order[:, None]
    member = jnp.any(hits, axis=1).astype(F32)
    slot = jnp.sum(jnp.where(hits, jnp.arange(index.shape[0], dtype=jnp.int32)[None], 0), axis=1)
    (ca, cross_lse, grad_own), halves = cross_forward(
        n_mem,
        plane,
        index,
        cq,
        ck,
        cv,
        cotangent,
        [(ffn_in[None], True), (ffn_out, False)],
    )
    w_ffn_in, w_ffn_out = flat(halves[0])[0], halves[1]

    rows_of = jnp.stack(
        [gain[0], bias[6], bias[5], gain[1], bias[7], bias[9], gain[2], bias[8]]
    )
    layer_out, dca, dz2, feed_sums, hidden_sums, own_ffn_out, dw_ffn_in, dw_cross_out = feed(
        n_mem,
        plane,
        grad_own,
        rows_of,
        half_of(ffn_bias)[None],
        ca,
        unit1,
        w_cross_out,
        w_ffn_in,
        w_ffn_out,
    )
    (dcq, dck, dcv), ffn_sums = cross_backward(
        n_mem,
        plane,
        planes,
        index,
        cq,
        ck,
        cv,
        ca,
        dca,
        cross_lse,
        [(dw_ffn_in, True, 2), (dw_cross_out, False, 1)],
        [(own_ffn_out, False)],
    )
    (dsa, dz1, middle_sums, enc_sum), (own_cross, own_so), _ = middle(
        n_mem,
        plane,
        planes,
        slot,
        member,
        index,
        dcq,
        dck,
        dcv,
        w_cross,
        w_self_out,
        sa,
        h1_full,
        enc_full.reshape(-1, PLEN, width),
        dz2,
        unit1,
        scale1,
        gain[0][None],
        [],
    )

    vec, dx, sums = last(
        n_mem,
        plane,
        planes,
        sq,
        sk,
        sv,
        sa,
        dsa,
        self_lse,
        x_full,
        w_self,
        dz1,
        [feed_sums, hidden_sums, middle_sums],
        small.shape,
        [(own_so, False), (own_cross, True)],
    )
    (
        grad_in,
        grad_encoder,
        out_self_qkv,
        out_self_out,
        out_cross_qkv,
        out_cross_out,
        out_ffn_in,
        out_ffn_out,
    ) = widen(
        [
            (dx, hidden_in),
            (enc_sum, encoder_rows),
            (sums[0], self_qkv),
            (sums[1], self_out),
            (sums[2], cross_qkv),
            (ffn_sums[1], cross_out),
            (ffn_sums[0], ffn_in),
            (ffn_sums[2], ffn_out),
        ]
    )
    out_ffn_bias = vec[n_bias + n_gain : n_small].reshape(-1)
    return (
        layer_out,
        grad_in,
        grad_encoder,
        out_self_qkv,
        out_self_out,
        out_cross_qkv,
        out_cross_out,
        out_ffn_in,
        out_ffn_out,
        out_ffn_bias,
        vec[:n_bias],
        vec[n_bias : n_bias + n_gain],
    )


def solution(mesh):
    placed = (
        P("pb", "mem", None),
        P("pb", "mem", None, None),
        P("pb", None),
        P(None, "mem", None),
        P("mem", None),
        P(None, "mem", None),
        P("mem", None),
        P("mem", None),
        P("mem", None),
        P("mem"),
        P(None, "mem"),
        P(None, "mem"),
        P("pb", "mem", None),
    )
    return jax.shard_map(
        body,
        mesh=mesh,
        in_specs=placed,
        out_specs=(
            P("pb", "mem", None),
            P("pb", "mem", None),
            P("pb", "mem", None, None),
            P(None, "mem", None),
            P("mem", None),
            P(None, "mem", None),
            P("mem", None),
            P("mem", None),
            P("mem", None),
            P("mem"),
            P(None, "mem"),
            P(None, "mem"),
        ),
        check_vma=False,
    )
```

```python
import functools

import jax
import jax.numpy as jnp
from jax import lax
from jax.experimental import pallas as pl
from jax.experimental.pallas import tpu as pltpu
from jax.sharding import PartitionSpec as P

HD = 64
PLEN = 256
BLK = 256
F32 = jnp.float32
BF16 = jnp.bfloat16

NN = (((1,), (0,)), ((), ()))
NT = (((1,), (1,)), ((), ()))


def mm(a, b, dims=NN):
    return lax.dot_general(a, b, dims, preferred_element_type=F32)


def head_mask_rows(block, head):
    rows = lax.broadcasted_iota(jnp.int32, block.shape, 0)
    return jnp.where((rows // HD) == head, block, jnp.zeros_like(block))


def head_rows(block, head, extra=None):
    block = block.astype(F32)
    rows = lax.broadcasted_iota(jnp.int32, block.shape, 0)
    out = jnp.where((rows // HD) == head, block, 0.0)
    if extra is not None:
        rest = -extra
        for i in range(3):
            term = rest.astype(BF16).astype(F32)
            rest = rest - term
            out = jnp.where(rows == (1 - head) * HD + i, term, out)
    return out.astype(BF16)


def ones_in(block, head):
    lanes = lax.broadcasted_iota(jnp.int32, block.shape, 1)
    first = (1 - head) * HD
    return jnp.where((lanes >= first) & (lanes < first + 3), jnp.ones_like(block), block)


def pick_heads(first, second):
    lanes = lax.broadcasted_iota(jnp.int32, first.shape, 1)
    return jnp.where(lanes < HD, first, second)


MESH = pl.DeviceIdType.MESH
ANY = pl.BlockSpec(memory_space=pl.ANY)
VMEM = pl.BlockSpec(memory_space=pltpu.VMEM)
PLANE = 4


def flip(index, bits):
    bit = 1
    while bit <= bits:
        if bits & bit:
            unit = jnp.int32(bit)
            index = index + unit - 2 * unit * lax.rem(lax.div(index, unit), jnp.int32(2))
        bit *= 2
    return index


class Place:
    def __init__(self, plane, planes=1):
        self.pb = lax.axis_index("pb")
        self.mem = lax.axis_index("mem")
        two = jnp.int32(2)
        self.core = lax.rem(self.pb, two)
        self.quarter = lax.rem(lax.div(self.pb, two), jnp.int32(plane))
        self.parity = lax.rem(self.mem, two)
        self.half = lax.div(self.mem, two)
        self.plane = plane
        self.planes = planes

    def near(self, t):
        return (flip(self.pb, 2 * t), self.mem)

    def far(self, r):
        return (flip(self.pb, 2 * self.plane * r), self.mem)

    def line(self, s):
        return (self.pb, flip(self.mem, s))

    def twin(self):
        return (flip(self.pb, 1), self.mem)

    def pair(self):
        return (self.pb, flip(self.mem, 1))

    def worker(self, k):
        return (self.pb - self.core + self.half, 2 * self.core + flip(self.parity, k))

    def at_home(self):
        return self.half == self.core

    def meet(self, peers):
        barrier = pltpu.get_barrier_semaphore()
        for pb_bits, mem_bits in peers:
            pl.semaphore_signal(
                barrier,
                inc=1,
                device_id=(flip(self.pb, pb_bits), flip(self.mem, mem_bits)),
                device_id_type=MESH,
            )
        pl.semaphore_wait(barrier, len(peers))


def column_peers(n_mem):
    return [(a, b) for a in range(2) for b in range(n_mem) if (a, b) != (0, 0)]


def plane_peers(plane):
    return [(2 * t, 0) for t in range(1, plane)]


class Sems:
    def __init__(self, ref):
        self.ref = ref
        self.used = 0

    def take(self, count):
        first = self.used
        self.used += count
        return [self.ref.at[first + i] for i in range(count)]


def remote(src, dst, send_sem, recv_sem, device):
    return pltpu.make_async_remote_copy(
        src_ref=src,
        dst_ref=dst,
        send_sem=send_sem,
        recv_sem=recv_sem,
        device_id=device,
        device_id_type=MESH,
    )


class Spread:
    def __init__(self, place, sems, src, dst, kinds=(0, 1)):
        self.place, self.src, self.dst, self.kinds = place, src, dst, kinds
        self.send = sems.take(2)
        self.recv = sems.take(2)

    def copy(self, k):
        return remote(self.src(k), self.dst(k), self.send[k], self.recv[k], self.place.worker(k))

    def start(self):
        for k in self.kinds:
            if k == 0:
                home = self.place.at_home()

                @pl.when(home)
                def _():
                    pltpu.make_async_copy(self.src(0), self.dst(0), self.recv[0]).start()

                @pl.when(jnp.logical_not(home))
                def _():
                    self.copy(0).start()
            else:
                self.copy(k).start()

    def wait_recv(self, k):
        if k == 0:
            home = self.place.at_home()

            @pl.when(home)
            def _():
                pltpu.make_async_copy(self.src(0), self.dst(0), self.recv[0]).wait()

            @pl.when(jnp.logical_not(home))
            def _():
                self.copy(0).wait_recv()
        else:
            self.copy(k).wait_recv()

    def wait_send(self):
        for k in self.kinds:
            if k == 0:

                @pl.when(jnp.logical_not(self.place.at_home()))
                def _():
                    self.copy(0).wait_send()
            else:
                self.copy(k).wait_send()


class Own:
    def __init__(self, place, sems, shard, full, columns, n_mem):
        self.copies = []
        mem, core = place.mem, place.core
        if columns:
            unit = full.shape[-1] // n_mem
            for b, sem in zip(range(n_mem), sems.take(n_mem)):
                start = pl.multiple_of(2 * unit * b + unit * core, unit)
                src = shard.at[:, :, :, pl.ds(start, unit)]
                dst = full.at[:, mem, :, :, pl.ds(unit * b, unit)]
                self.copies.append(pltpu.make_async_copy(src, dst, sem))
        else:
            (sem,) = sems.take(1)
            self.copies.append(pltpu.make_async_copy(shard.at[core], full.at[0, mem], sem))

    def start(self):
        for copy in self.copies:
            copy.start()

    def wait(self):
        for copy in self.copies:
            copy.wait()


class Line:
    def __init__(self, place, sems, src, dst, n_mem):
        send, recv = sems.take(n_mem - 1), sems.take(n_mem - 1)
        self.copies = [
            remote(src(s), dst(s), send[s - 1], recv[s - 1], place.line(s)) for s in range(1, n_mem)
        ]

    def start(self):
        for copy in self.copies:
            copy.start()

    def wait_recv(self, s):
        self.copies[s - 1].wait_recv()

    def wait_send(self):
        for copy in self.copies:
            copy.wait_send()


class Share:
    def __init__(self, place, sems, src, block):
        send, recv = sems.take(4), sems.take(4)
        rows = src.shape[-2]
        half = rows // 2

        def part(ref, i):
            return ref.at[:, pl.ds(i * half, half)]

        self.first = [
            remote(src, block(0), send[t - 1], recv[t - 1], place.near(t)) for t in (1, 2)
        ]
        self.second = [
            remote(part(block(t), t - 1), part(block(t), t - 1), send[t + 1], recv[t + 1], place.near(3 - t))
            for t in (1, 2)
        ]

    def start(self):
        for copy in self.first:
            copy.start()

    def forward(self):
        for direct, onward in zip(self.first, self.second):
            direct.wait_recv()
            onward.start()

    def wait(self):
        for copy in self.first:
            copy.wait_send()
        for copy in self.second:
            copy.wait()


class Chain:
    def __init__(self, place, sems, block, n_mem):
        self.place, self.block, self.n = place, block, n_mem
        self.sems = {way: (sems.take(n_mem - 1), sems.take(n_mem - 1)) for way in (1, -1)}

    def copy(self, way, hops):
        mem = self.place.mem
        source = lax.rem(mem + jnp.int32(self.n - way * hops), jnp.int32(self.n))
        target = lax.rem(mem + jnp.int32(self.n + way), jnp.int32(self.n))
        send, recv = self.sems[way]
        piece = self.block(source)
        return remote(piece, piece, send[hops], recv[hops], (self.place.pb, target))

    def comes(self, way, hops):
        mem = self.place.mem
        return mem >= hops if way == 1 else mem + hops < self.n

    def goes(self, way, hops):
        mem = self.place.mem
        ahead = mem + 1 < self.n if way == 1 else mem >= 1
        return jnp.logical_and(ahead, self.comes(way, hops))

    def start(self):
        for way in (1, -1):

            @pl.when(self.goes(way, 0))
            def _():
                self.copy(way, 0).start()

    def relay(self, hops, arrived):
        for way in (1, -1):

            @pl.when(self.comes(way, hops))
            def _():
                self.copy(way, hops - 1).wait_recv()
                if hops < self.n - 1:

                    @pl.when(self.goes(way, hops))
                    def _():
                        self.copy(way, hops).start()

                arrived(hops if way == 1 else self.n - hops)

    def wait_send(self):
        for hops in range(self.n - 1):
            for way in (1, -1):

                @pl.when(self.goes(way, hops))
                def _():
                    self.copy(way, hops).wait_send()


class Gather:
    def __init__(self, place, sems, shard, full, columns, n_mem, in_plane=None):
        mem, quarter = place.mem, place.quarter
        self.n_mem = n_mem
        self.in_plane = tuple(range(1, n_mem)) if in_plane is None else in_plane
        self.own = Own(place, sems, shard, full, columns, n_mem)
        self.chain = Chain(place, sems, lambda i: full.at[:, i, quarter], n_mem)
        self.shares = {}
        for d in range(1, n_mem):
            if d not in self.in_plane and n_mem - d not in self.in_plane:
                continue
            source = lax.rem(mem + jnp.int32(n_mem - d), jnp.int32(n_mem))

            def block(t, source=source):
                return full.at[:, source, flip(quarter, t)]

            self.shares[d] = Share(place, sems, block(0), block)

    def begin(self):
        self.own.wait()
        self.chain.start()

    def share(self, hops):
        self.chain.relay(
            hops, lambda d: self.shares[d].start() if hops in self.in_plane else None
        )

    def forward(self, hops):
        for way, d in ((1, hops), (-1, self.n_mem - hops)):

            @pl.when(self.chain.comes(way, hops))
            def _():
                self.shares[d].forward()

    def finish(self):
        self.chain.wait_send()
        for hops in self.in_plane:
            for way, d in ((1, hops), (-1, self.n_mem - hops)):

                @pl.when(self.chain.comes(way, hops))
                def _():
                    self.shares[d].wait()


GATHER_SEMS = 44


def half_views(shard, columns, n_mem, plane):
    if columns:
        lead, depth, hidden = shard.shape
        part = depth // plane
        return shard.reshape(lead, plane, part, hidden), (lead, n_mem, plane, part, hidden // 2)
    depth, width = shard.shape
    part = depth // 2 // plane
    return shard.reshape(2, plane, part, width), (1, n_mem, plane, part, width)


class Walk:
    def __init__(self, refs):
        self.refs = list(refs)

    def take(self, count):
        out, self.refs = self.refs[:count], self.refs[count:]
        return out

    def one(self):
        return self.take(1)[0]


def softmax_units(units, finish, serve=None):
    def scores_of(unit, j):
        return unit[0][j]()

    ready = [scores_of(units[0], j) for j in range(len(units[0][0]))]
    for n, (_, values, tag) in enumerate(units):
        if serve is not None:
            serve(n)
        coming = list(range(len(units[n + 1][0]))) if n + 1 < len(units) else []
        following = []
        top = functools.reduce(
            jnp.maximum, [jnp.max(tile, axis=0, keepdims=True) for tile in ready]
        )
        total = jnp.zeros_like(top)
        acc = None
        share = -(-len(coming) // len(ready))
        for j, tile in enumerate(ready):
            for i in coming[j * share : (j + 1) * share]:
                following.append(scores_of(units[n + 1], i))
            probs = jnp.exp(tile - top)
            total += jnp.sum(probs, axis=0, keepdims=True)
            part = mm(values[j](), probs.astype(BF16))
            acc = part if acc is None else acc + part
        finish(tag, acc / total, top + jnp.log(total))
        ready = following


def self_attend(place, pair, q_vm, k_vm, v_vm, o_vm, lse_vm, v_t, o_t):
    base = 2 * place.core + place.parity
    count = q_vm.shape[0] // BLK
    lanes = pl.ds(pl.multiple_of(pair * 2 * HD, 2 * HD), 2 * HD)

    def rows(i):
        return pl.ds(pl.multiple_of(flip(base, i) * BLK, BLK), BLK)

    for j in range(count):
        v_t[:, j * BLK : (j + 1) * BLK] = v_vm[rows(j), lanes].T
    key_pos = lax.broadcasted_iota(jnp.int32, (BLK, BLK), 0)
    query_pos = lax.broadcasted_iota(jnp.int32, (BLK, BLK), 1)
    units = []
    for i in range(count):
        q_t = q_vm[rows(i), lanes].T
        for head in range(2):
            q_head = head_rows(q_t, head)

            def score(j, i=i, q_head=q_head):
                tile = mm(k_vm[rows(j), lanes], q_head)
                return jnp.where(key_pos <= query_pos, tile, -1000000000.0) if j == i else tile

            def value(j, head=head):
                return v_t[head * HD : (head + 1) * HD, j * BLK : (j + 1) * BLK]

            units.append(
                (
                    [functools.partial(score, j) for j in range(i + 1)],
                    [functools.partial(value, j) for j in range(i + 1)],
                    (i, head),
                )
            )

    def finish(tag, mixed, lse):
        i, head = tag
        span = slice(i * BLK, (i + 1) * BLK)
        o_t[head * HD : (head + 1) * HD, span] = mixed
        lse_vm[pair, head : head + 1, span] = lse

    softmax_units(units, finish)
    for i in range(count):
        o_vm[rows(i), lanes] = o_t[:, i * BLK : (i + 1) * BLK].T.astype(BF16)


def tiles(rows, step):
    def run(i, carry):
        step(pl.ds(pl.multiple_of(i * BLK, BLK), BLK))
        return carry

    lax.fori_loop(0, rows // BLK, run, 0)


def front_kernel(n_mem, plane, kinds, places, x_ref, enc_ref, map_ref, small_ref, *refs):
    refs = Walk(refs)
    count = len(kinds)
    shards = refs.take(count)
    x_out, enc_out, index_out, small_out = refs.take(4)
    halves = refs.take(count)
    kept = refs.take(11)
    x_vm, w_vm, so_vm, cq_w, small_vm = refs.take(5)
    q_vm, k_vm, v_vm, sa_vm, lse_vm, h1_vm, unit_vm, scale_vm, cq_vm = refs.take(9)
    k_all, v_all, v_t, o_t, part_vm, twin_vm, kv_w, enc_vm, map_in = refs.take(9)
    sems = Sems(refs.one())
    place = Place(plane)
    n_bias, n_gain = places
    rows = x_ref.shape[1]
    gathers = [
        Gather(place, sems, shard, half, columns, n_mem)
        for shard, half, columns in zip(shards, halves, kinds)
    ]
    spread = Spread(
        place,
        sems,
        lambda k: x_ref.at[flip(place.parity, k)],
        lambda k: x_out.at[pl.ds(rows * k, rows)],
    )
    twin_send, twin_recv = sems.take(2), sems.take(2)
    twin = [
        remote(
            x_out.at[pl.ds(rows * k, rows)],
            x_out.at[pl.ds(rows * (k + 2), rows)],
            twin_send[k],
            twin_recv[k],
            place.twin(),
        )
        for k in range(2)
    ]
    map_sems = sems.take(2)
    map_copy = remote(map_ref, map_in, map_sems[0], map_sems[1], place.twin())
    (small_sem,) = sems.take(1)
    small_own = pltpu.make_async_copy(small_ref, small_out.at[place.mem], small_sem)
    small_line = Line(
        place, sems, lambda s: small_ref, lambda s: small_out.at[place.mem], n_mem
    )
    units = enc_vm.shape[1]
    encs, enc_twins, enc_pairs, enc_onwards, enc_ends = [], [], [], [], []
    for u in range(units):
        encs.append(
            Spread(
                place, sems, lambda k, u=u: enc_ref.at[u], lambda k, u=u: enc_vm.at[0, u], kinds=(0,)
            )
        )
        pair_sems, twin_sems, end_sems = sems.take(2), sems.take(2), sems.take(2)
        enc_pairs.append(remote(enc_ref.at[u], enc_vm.at[1, u], *pair_sems, place.pair()))
        enc_onwards.append(remote(enc_vm.at[0, u], enc_vm.at[1, u], *pair_sems, place.pair()))
        enc_twins.append(remote(enc_vm.at[0, u], enc_vm.at[2, u], *twin_sems, place.twin()))
        enc_ends.append(remote(enc_vm.at[1, u], enc_vm.at[3, u], *end_sems, place.twin()))
    enc_keeps = [
        pltpu.make_async_copy(enc_vm.at[i], enc_out.at[i], sem) for i, sem in enumerate(sems.take(4))
    ]
    home = place.at_home()
    away = jnp.logical_not(home)
    loads = [
        pltpu.make_async_copy(src, dst, sem)
        for src, dst, sem in zip(
            (x_out, halves[0], halves[1], halves[2].at[0], small_out, halves[2].at[pl.ds(1, 2)]),
            (x_vm, w_vm, so_vm, cq_w, small_vm, kv_w),
            sems.take(6),
        )
    ]
    keeps = [
        pltpu.make_async_copy(src, dst, sem)
        for src, dst, sem in zip(
            (q_vm, k_vm, v_vm, sa_vm, lse_vm, h1_vm, unit_vm, scale_vm, cq_vm, k_all, v_all),
            kept,
            sems.take(11),
        )
    ]
    swap_sems = sems.take(4)
    own = 2 * rows
    swap_part = remote(part_vm, twin_vm, swap_sems[0], swap_sems[1], place.twin())
    swap_h1 = remote(
        h1_vm.at[pl.ds(0, own)], h1_vm.at[pl.ds(own, own)], swap_sems[2], swap_sems[3], place.twin()
    )

    for gather in gathers:
        gather.own.start()
    small_own.start()
    place.meet(column_peers(n_mem) + plane_peers(plane))
    for gather in gathers:
        gather.begin()
    small_line.start()
    map_copy.start()
    spread.start()
    for gather in gathers:
        gather.share(1)
    for gather in gathers:
        gather.share(2)
    gathers[0].forward(1)
    for k in range(2):
        spread.wait_recv(k)
        twin[k].start()
    for gather in gathers:
        gather.share(3)
    for u in range(units):
        encs[u].start()

        @pl.when(home)
        def _():
            enc_pairs[u].start()

    def first_arrival(u):
        encs[u].wait_recv(0)

        @pl.when(away)
        def _():
            enc_onwards[u].start()

        enc_twins[u].start()

    def second_arrival(u):
        @pl.when(home)
        def _():
            enc_pairs[u].wait()

        @pl.when(away)
        def _():
            enc_onwards[u].wait()

        enc_ends[u].start()

    for hops in (2, 3):
        gathers[0].forward(hops)
    for hops in (1, 2, 3):
        for gather in gathers[1:]:
            gather.forward(hops)
    for copy in twin:
        copy.wait_recv()
    small_own.wait()
    for s in range(1, n_mem):
        small_line.wait_recv(s)
    gathers[0].finish()
    for copy in (loads[0], loads[1], loads[4]):
        copy.start()
    for copy in (loads[0], loads[1], loads[4]):
        copy.wait()

    def half_row(row):
        lanes = pl.ds(pl.multiple_of(place.core * 2 * HD, 2 * HD), 2 * HD)
        return jnp.concatenate(
            [small_vm[b, :, lanes].astype(F32)[row : row + 1] for b in range(n_mem)], axis=1
        )

    def full_row(row):
        return jnp.concatenate(
            [small_vm[b].astype(F32)[row : row + 1] for b in range(n_mem)], axis=1
        )

    bias_q, bias_v = half_row(0), half_row(1)
    depth = x_vm.shape[1]

    def weight(ref):
        return ref[...].reshape(-1, ref.shape[-1])

    def project(span):
        x_tile = x_vm[span, :]
        q_vm[span, :] = ((mm(x_tile, weight(w_vm.at[0])) + bias_q) * 0.125).astype(BF16)
        k_vm[span, :] = mm(x_tile, weight(w_vm.at[1])).astype(BF16)
        v_vm[span, :] = (mm(x_tile, weight(w_vm.at[2])) + bias_v).astype(BF16)

    tiles(x_vm.shape[0], project)
    for copy in keeps[:3]:
        copy.start()
    pairs = q_vm.shape[1] // (2 * HD)
    for pair in range(pairs):
        self_attend(place, pair, q_vm, k_vm, v_vm, sa_vm, lse_vm, v_t, o_t)
        if pair in (0, pairs // 2):
            first_arrival(min(pair, 1))
    for copy in keeps[3:5]:
        copy.start()
    for gather in gathers[1:]:
        gather.finish()
    for copy in (loads[2], loads[3], loads[5]):
        copy.start()
    for copy in (loads[2], loads[3], loads[5]):
        copy.wait()

    def other_part(span):
        part_vm[span, :] = mm(
            sa_vm[pl.ds(pl.multiple_of(span.start + own, BLK), BLK), :], weight(so_vm)
        ).astype(BF16)

    tiles(own, other_part)
    swap_part.start()

    def own_part(span):
        unit_vm[span, :] = mm(sa_vm[span, :], weight(so_vm)) + x_vm[span, :].astype(F32)

    tiles(own, own_part)
    for u in range(2, units):
        first_arrival(u)
    bias_out = full_row(2)
    gain, shift = full_row(n_bias), full_row(6)
    swap_part.wait()

    def normalise(span):
        values = unit_vm[span, :] + twin_vm[span, :].astype(F32) + bias_out
        centre = values - jnp.mean(values, axis=-1, keepdims=True)
        scale = lax.rsqrt(jnp.mean(centre * centre, axis=-1, keepdims=True) + 1e-05)
        unit = centre * scale
        unit_vm[span, :] = unit
        scale_vm[span, :] = jnp.broadcast_to(scale, (BLK, scale_vm.shape[1]))
        h1_vm[span, :] = (unit * gain + shift).astype(BF16)

    tiles(own, normalise)
    swap_h1.start()
    for copy in keeps[6:8]:
        copy.start()
    bias_cq = half_row(3)

    def queries(span):
        cq_vm[span, :] = ((mm(h1_vm[span, :], weight(cq_w)) + bias_cq) * 0.125).astype(BF16)

    tiles(own, queries)
    swap_h1.wait()
    keeps[5].start()

    def other_queries(span):
        queries(pl.ds(pl.multiple_of(span.start + own, BLK), BLK))

    tiles(own, other_queries)
    keeps[8].start()

    map_copy.wait()
    near_map, far_map = map_ref[...], map_in[...]
    both_maps = jnp.where(home, near_map, far_map)
    mine = jnp.where(place.parity == 0, both_maps[:1], both_maps[1:])
    group = lax.div(mine, jnp.full_like(mine, units))
    index_out[...] = (group ^ (2 * place.core + place.parity)) * units + lax.rem(
        mine, jnp.full_like(mine, units)
    )

    bias_cv = half_row(4)

    def memory(block, u):
        rows_here = enc_vm[block, u]
        k_all[block * units + u] = mm(rows_here, weight(kv_w.at[0])).astype(BF16)
        v_all[block * units + u] = (mm(rows_here, weight(kv_w.at[1])) + bias_cv).astype(BF16)

    for u in range(units):
        second_arrival(u)
        memory(0, u)
    enc_keeps[0].start()
    enc_keeps[1].start()
    for block, copies in ((2, enc_twins), (1, None), (3, enc_ends)):
        for u in range(units):
            if copies is not None:
                copies[u].wait_recv()
            memory(block, u)
    enc_keeps[2].start()
    enc_keeps[3].start()
    for copy in keeps[9:]:
        copy.start()
    spread.wait_send()
    for copy in twin:
        copy.wait_send()
    small_line.wait_send()
    for item in encs:
        item.wait_send()
    for copy in enc_twins + enc_ends:
        copy.wait_send()
    for copy in keeps + enc_keeps:
        copy.wait()


def front(n_mem, plane, places, hidden_in, enc, passage_map, small, params):
    kinds = tuple(columns for _, columns in params)
    views = [half_views(shard, columns, n_mem, plane) for shard, columns in params]
    seg, width = hidden_in.shape[1:]
    rows, own = 4 * seg, 2 * seg
    part = width // 2
    pairs = part // (2 * HD)
    passages = 4 * enc.shape[0]
    shapes = (
        [((rows, width), BF16), ((4,) + enc.shape, BF16), ((1, passage_map.shape[1]), jnp.int32)]
        + [((n_mem,) + small.shape, BF16)]
        + [(full, BF16) for _, full in views]
    )
    kept = [
        ((rows, part), BF16),
        ((rows, part), BF16),
        ((rows, part), BF16),
        ((rows, part), BF16),
        ((pairs, 2, rows), F32),
        ((rows, width), BF16),
        ((own, width), F32),
        ((own, 2 * HD), F32),
        ((rows, part), BF16),
        ((passages, PLEN, part), BF16),
        ((passages, PLEN, part), BF16),
    ]
    scratch = [
        ((rows, width), BF16),
        (views[0][1], BF16),
        (views[1][1][1:], BF16),
        (views[2][1][1:], BF16),
        ((n_mem,) + small.shape, BF16),
    ] + kept + [
        ((2 * HD, rows), BF16),
        ((2 * HD, rows), F32),
        ((own, width), BF16),
        ((own, width), BF16),
        ((2,) + views[2][1][1:], BF16),
        ((4,) + enc.shape, BF16),
        (passage_map.shape, jnp.int32),
    ]
    scratch[2] = (views[1][1], BF16)
    outs = pl.pallas_call(
        functools.partial(front_kernel, n_mem, plane, kinds, places),
        in_specs=[VMEM] * (4 + len(params)),
        out_specs=[ANY, ANY, VMEM] + [ANY] * (len(shapes) + len(kept) - 3),
        out_shape=[jax.ShapeDtypeStruct(*item) for item in shapes + kept],
        scratch_shapes=[pltpu.VMEM(*item) for item in scratch]
        + [pltpu.SemaphoreType.DMA((90 + GATHER_SEMS * len(params),))],
        compiler_params=pltpu.CompilerParams(
            collective_id=0, has_side_effects=True, vmem_limit_bytes=60 * 2**20
        ),
        cost_estimate=pl.CostEstimate(
            flops=rows * width * part * 10, bytes_accessed=40 * 2**20, transcendentals=rows * rows * 8
        ),
        name="front",
    )(hidden_in, enc, passage_map, small, *[view for view, _ in views])
    count = 4 + len(params)
    return outs[:4], outs[4:count], outs[count:]


class PlaneSum:
    def __init__(self, place, sems, grad, own, bufs, rows, lanes=None):
        self.own = own
        self.from_near, self.via, self.add = bufs
        quarter = place.quarter
        first, count = rows
        half = count // 2
        self.lead, self.n_mem = own.shape[:2]
        lanes = pl.ds(*(lanes or (0, grad.shape[-1])))

        def piece(t, lo, size):
            return grad.at[:, :, flip(quarter, t), pl.ds(first + lo, size), lanes]

        loads = sems.take(3)
        self.loads = [pltpu.make_async_copy(piece(0, 0, count), own, loads[0])]
        send, recv = sems.take(6), sems.take(6)
        self.onward, self.direct, self.summed = [], [], []
        for t in (1, 2):
            lo = (t - 1) * half
            self.onward.append(
                remote(piece(3, lo, half), self.via.at[t - 1], send[t - 1], recv[t - 1], place.near(t))
            )
            self.direct.append(
                remote(
                    piece(t, lo, half),
                    self.from_near.at[t - 1, :, :, pl.ds(lo, half)],
                    send[t + 1],
                    recv[t + 1],
                    place.near(t),
                )
            )
            other = half - lo
            self.loads.append(
                pltpu.make_async_copy(piece(t, other, half), self.add.at[t - 1], loads[t])
            )
            self.summed.append(
                remote(
                    self.add.at[t - 1],
                    self.from_near.at[t - 1, :, :, pl.ds(other, half)],
                    send[t + 3],
                    recv[t + 3],
                    place.near(t),
                )
            )

    def start(self):
        for copy in self.onward + self.loads + self.direct:
            copy.start()

    def each(self, step):
        def run(i, carry):
            step(lax.div(i, jnp.int32(self.n_mem)), lax.rem(i, jnp.int32(self.n_mem)))
            return carry

        lax.fori_loop(0, self.lead * self.n_mem, run, 0)

    def middle(self):
        for copy in self.loads:
            copy.wait()
        for t in (1, 2):
            self.onward[2 - t].wait_recv()

            def add(l, m, t=t):
                total = self.add[t - 1, l, m].astype(F32) + self.via[2 - t, l, m].astype(F32)
                self.add[t - 1, l, m] = total.astype(BF16)

            self.each(add)
            self.summed[t - 1].start()

    def end(self):
        for copy in self.direct + self.summed:
            copy.wait_recv()

        def add(l, m):
            total = self.own[l, m].astype(F32)
            for t in range(2):
                total += self.from_near[t, l, m].astype(F32)
            self.own[l, m] = total.astype(BF16)

        self.each(add)

    def wait_send(self):
        for copy in self.onward + self.direct + self.summed:
            copy.wait_send()


class Settle:
    def __init__(self, place, sems, own, out, bufs, columns, n_mem, rows, lane=0):
        self.place, self.n_mem, self.columns, self.rows = place, n_mem, columns, rows
        self.lane = lane
        self.own, self.out = own, out
        self.line_in, self.far_in, self.slots = bufs
        quarter, mem, core = place.quarter, place.mem, place.core
        slots = self.slots

        def slot(t):
            return slots.at[flip(quarter, t), core]

        self.line = Line(
            place, sems, lambda s: own.at[:, flip(mem, s)], lambda s: self.line_in.at[s - 1], n_mem
        )
        others = place.planes - 1
        far_send, far_recv = sems.take(others), sems.take(others)
        self.far = [
            remote(slot(0), self.far_in.at[r - 1], far_send[r - 1], far_recv[r - 1], place.far(r))
            for r in range(1, place.planes)
        ]
        self.share = Share(place, sems, slot(0), slot)
        twin_send, twin_recv = sems.take(place.plane), sems.take(place.plane)
        self.twin = [
            remote(slot(t), slot(t), twin_send[t], twin_recv[t], place.twin())
            for t in range(place.plane)
        ]

    def start(self):
        self.line.start()

    def middle(self):
        for s in range(1, self.n_mem):
            self.line.wait_recv(s)
        quarter, core, mem = self.place.quarter, self.place.core, self.place.mem
        lead = self.own.shape[0]
        for l in range(lead):
            total = self.own[l, mem].astype(F32)
            for s in range(self.n_mem - 1):
                total += self.line_in[s, l].astype(F32)
            self.slots[quarter, core, l] = total.astype(BF16)
        if self.far:
            for copy in self.far:
                copy.start()
            for copy in self.far:
                copy.wait()
            for l in range(lead):
                total = self.slots[quarter, core, l].astype(F32)
                for r in range(len(self.far)):
                    total += self.far_in[r, l].astype(F32)
                self.slots[quarter, core, l] = total.astype(BF16)
        self.share.start()
        self.twin[0].start()

    def forward(self):
        self.share.forward()
        self.twin[1].start()
        self.twin[2].start()

    def end(self):
        self.share.wait()
        self.twin[3].start()
        for copy in self.twin:
            copy.wait()
        self.line.wait_send()
        lead = self.own.shape[0]
        wide = self.slots.shape[-1]
        first, count = self.rows
        for q in range(self.place.plane):
            for c in range(2):
                for l in range(lead):
                    if self.columns:
                        unit = self.out.shape[-1] // (2 * self.n_mem)
                        for b in range(wide // unit):
                            start = unit * (2 * (self.lane // unit + b) + c)
                            self.out[l, q, first : first + count, start : start + unit] = self.slots[
                                q, c, l, :, b * unit : (b + 1) * unit
                            ]
                    else:
                        self.out[c, q, first : first + count] = self.slots[q, c, l]


PLANE_SUM_SEMS = 15


def settle_sems(n_mem, plane, planes):
    return 2 * (n_mem - 1) + 2 * (planes - 1) + 8 + 2 * plane


def plane_sum_scratch(grad_shape, n_mem, count, cols=None):
    lead, cols = grad_shape[0], cols or grad_shape[-1]
    return [
        pltpu.VMEM((2, lead, n_mem, count, cols), BF16),
        pltpu.VMEM((2, lead, n_mem, count // 2, cols), BF16),
        pltpu.VMEM((2, lead, n_mem, count // 2, cols), BF16),
    ]


def settle_scratch(grad_shape, n_mem, plane, planes, count, cols=None):
    lead, cols = grad_shape[0], cols or grad_shape[-1]
    return [
        pltpu.VMEM((n_mem - 1, lead, count, cols), BF16),
        pltpu.VMEM((max(planes - 1, 1), lead, count, cols), BF16),
        pltpu.VMEM((plane, 2, lead, count, cols), BF16),
    ]


def sum_shape(grad_shape):
    lead, n_mem, _, rows, cols = grad_shape
    return jax.ShapeDtypeStruct((lead, n_mem, rows, cols), BF16)


def reduce_out(grad_shape, columns, plane):
    lead, _, _, rows, cols = grad_shape
    shape = (lead, plane, rows, 2 * cols) if columns else (2, plane, rows, cols)
    return jax.ShapeDtypeStruct(shape, BF16)


def reduce_peers(n_mem, plane, planes):
    return (
        [(1, 0)]
        + [(0, s) for s in range(1, n_mem)]
        + plane_peers(plane)
        + [(2 * plane * r, 0) for r in range(1, planes)]
    )


def whole(shape):
    return pl.BlockSpec(shape, lambda *grid: (0,) * len(shape))


class Fetch:
    def __init__(self, sems, src, dst):
        self.copy = pltpu.make_async_copy(src, dst, sems.take(1)[0])
        self.dst = dst
        self.here = False

    def start(self):
        self.copy.start()

    def get(self):
        if not self.here:
            self.copy.wait()
            self.here = True
        return self.dst


def unit_norm(values):
    centre = values - jnp.mean(values, axis=-1, keepdims=True)
    scale = lax.rsqrt(jnp.mean(centre * centre, axis=-1, keepdims=True) + 1e-05)
    return centre * scale, scale


def unit_norm_back(grad, unit, scale, gain):
    inner = grad * gain
    return (
        inner
        - jnp.mean(inner, axis=-1, keepdims=True)
        - unit * jnp.mean(inner * unit, axis=-1, keepdims=True)
    ) * scale


def feed_kernel(n_mem, plane, cot_ref, rows_ref, bias_ref, *refs):
    refs = Walk(refs)
    fetched = refs.take(4)
    out_part = refs.one()
    final_out, dca_ref, dz2_ref, sums_ref, bias_sum, own_out, dw_in, dw_co, dw_out = refs.take(9)
    kept = refs.take(4)
    out_w = refs.one()
    cot_vm, h2_vm, unit_vm, scale_vm, act_vm, slope_vm, p_vm, part_vm, twin_vm = refs.take(9)
    final_vm, df_vm, dco_vm = refs.take(3)
    bufs = refs.take(3)
    sems = Sems(refs.one())
    place = Place(plane)
    ca, unit1, w_co, w_in = [Fetch(sems, src, dst) for src, dst in zip(fetched, kept)]
    mem, quarter = place.mem, place.quarter
    own_piece = Fetch(sems, out_part.at[0, mem], out_w.at[0, mem])
    pieces = []
    for d in range(1, n_mem):
        source = lax.rem(mem + jnp.int32(n_mem - d), jnp.int32(n_mem))

        def place_of(t, source=source):
            return out_w.at[:, source, flip(quarter, t)]

        (sem,) = sems.take(1)
        pieces.append(
            (
                mem < d if d == 1 else mem >= (d if d == n_mem - 1 else 0),
                pltpu.make_async_copy(out_part.at[0, source], out_w.at[0, source], sem),
                pltpu.make_async_copy(out_part.at[:, source, quarter], place_of(0), sem),
                Share(place, sems, place_of(0), place_of),
            )
        )

    def each_piece(whole_step, part_step):
        for part, whole_copy, part_copy, share in pieces:
            if whole_step is not None:

                @pl.when(jnp.logical_not(part))
                def _():
                    whole_step(whole_copy)

            @pl.when(part)
            def _():
                part_step(part_copy, share)

    rows = h2_vm.shape[0]
    own = rows // 2
    seg = own // 2
    hidden = act_vm.shape[1]
    block = hidden // n_mem
    out_sum = PlaneSum(place, sems, dw_out, own_out, bufs, (0, own_out.shape[2]))
    spread_cot = Spread(
        place,
        sems,
        lambda k: cot_ref.at[flip(place.parity, k)],
        lambda k: cot_vm.at[pl.ds(seg * k, seg)],
    )
    spread_final = Spread(
        place,
        sems,
        lambda k: final_vm.at[pl.ds(seg * k, seg)],
        lambda k: final_out.at[place.parity],
    )

    def swap(src, dst):
        send, recv = sems.take(2)
        return remote(src, dst, send, recv, place.twin())

    def half_lanes(ref, i):
        wide = ref.shape[1] // 2
        return ref.at[:, pl.ds(i * wide, wide)]

    swap_co = swap(part_vm, twin_vm)
    swap_h2 = swap(h2_vm.at[pl.ds(0, own)], h2_vm.at[pl.ds(own, own)])
    swap_ffn = [swap(half_lanes(part_vm, i), half_lanes(twin_vm, i)) for i in range(2)]
    swap_df = swap(df_vm.at[pl.ds(0, own)], df_vm.at[pl.ds(own, own)])
    swap_dh2 = [swap(half_lanes(part_vm, i), half_lanes(twin_vm, i)) for i in range(2)]
    swap_dco = swap(dco_vm.at[pl.ds(0, own)], dco_vm.at[pl.ds(own, own)])

    for item in (ca, w_co, own_piece):
        item.start()
    each_piece(lambda copy: copy.start(), lambda copy, share: copy.start())
    for item in (unit1, w_in):
        item.start()
    place.meet(column_peers(n_mem) + plane_peers(plane))
    spread_cot.start()

    def share_start(copy, share):
        copy.wait()
        share.start()

    each_piece(None, share_start)
    row = {name: rows_ref[i : i + 1, :] for i, name in enumerate(("g0", "b6", "b5", "g1", "b7", "b9", "g2", "b8"))}
    sums_ref[...] = jnp.zeros_like(sums_ref)
    bias_sum[...] = jnp.zeros_like(bias_sum)

    def after(span):
        return pl.ds(pl.multiple_of(span.start + own, BLK), BLK)

    ca, w_co = ca.get(), w_co.get()

    def co_other(span):
        part_vm[span, :] = mm(ca[after(span), :], w_co[...]).astype(BF16)

    tiles(own, co_other)
    swap_co.start()
    unit1 = unit1.get()

    def co_own(span):
        p_vm[span, :] = unit1[span, :] * row["g0"] + row["b6"] + mm(ca[span, :], w_co[...])

    tiles(own, co_own)
    swap_co.wait()

    def second_norm(span):
        values = p_vm[span, :] + twin_vm[span, :].astype(F32) + row["b5"]
        unit, scale = unit_norm(values)
        unit_vm[span, :] = unit
        scale_vm[span, :] = jnp.broadcast_to(scale, (BLK, scale_vm.shape[1]))
        h2_vm[span, :] = (unit * row["g1"] + row["b7"]).astype(BF16)

    tiles(own, second_norm)
    swap_h2.start()
    w_in = w_in.get()

    def forward(span):
        def part(i, carry):
            lanes = pl.ds(pl.multiple_of(i * block, block), block)
            pre = mm(h2_vm[span, :], w_in[:, lanes]) + bias_ref[:, lanes]
            cdf = 0.5 * (1.0 + lax.erf(pre * 0.7071067811865476))
            act_vm[span, lanes] = (pre * cdf).astype(BF16)
            density = jnp.exp(-0.5 * pre * pre) * 0.3989422804014327
            slope_vm[span, lanes] = (cdf + pre * density).astype(BF16)
            return carry

        lax.fori_loop(0, n_mem, part, 0)

    ours, others = pl.ds(0, own), pl.ds(own, own)
    width = h2_vm.shape[1]
    column = width // 2
    each_piece(None, lambda copy, share: share.forward())
    forward(ours)
    swap_h2.wait()
    forward(others)
    own_piece.get()
    each_piece(lambda copy: copy.wait(), lambda copy, share: share.wait())
    for i in range(2):
        lanes = slice(i * column, (i + 1) * column)
        weights = out_w[0, :, :, :, lanes].reshape(hidden, column)
        part_vm[:, lanes] = mm(act_vm[others, :], weights).astype(BF16)
        swap_ffn[i].start()
    p_vm[...] = mm(act_vm[ours, :], out_w[0].reshape(hidden, width))
    for k in range(2):
        spread_cot.wait_recv(k)
    for copy in swap_ffn:
        copy.wait()

    def third_norm(span):
        values = (
            unit_vm[span, :] * row["g1"]
            + row["b7"]
            + p_vm[span, :]
            + twin_vm[span, :].astype(F32)
            + row["b9"]
        )
        unit, scale = unit_norm(values)
        final_vm[span, :] = (unit * row["g2"] + row["b8"]).astype(BF16)
        grad = cot_vm[span, :].astype(F32)
        out = unit_norm_back(grad, unit, scale, row["g2"])
        dz2_ref[span, :] = out
        low = out.astype(BF16)
        df_vm[span, :] = low
        sums_ref[0:1, :] += jnp.sum(grad * unit, axis=0, keepdims=True)
        sums_ref[1:2, :] += jnp.sum(grad, axis=0, keepdims=True)
        sums_ref[2:3, :] += jnp.sum(low.astype(F32), axis=0, keepdims=True)

    tiles(own, third_norm)
    swap_df.start()
    spread_final.start()
    swap_df.wait()

    def out_weights(m, carry):
        lanes = pl.ds(pl.multiple_of(m * block, block), block)
        dw_out[0, m] = mm(act_vm[:, lanes].T, df_vm[...]).astype(BF16).reshape(dw_out.shape[2:])
        return carry

    lax.fori_loop(0, n_mem, out_weights, 0)
    out_sum.start()

    def hidden_grad(i, carry):
        lanes = pl.ds(pl.multiple_of(i * block, block), block)
        weights = out_w[0, i].reshape(block, width)
        grad = mm(df_vm[...], weights, NT) * slope_vm[:, lanes].astype(F32)
        low = grad.astype(BF16)
        slope_vm[:, lanes] = low
        bias_sum[:, lanes] = jnp.sum(low.astype(F32), axis=0, keepdims=True)
        return carry

    lax.fori_loop(0, n_mem, hidden_grad, 0)
    narrow = width // 4
    for i in range(2):
        for j in (2 * i, 2 * i + 1):
            lanes = slice(j * narrow, (j + 1) * narrow)
            grad = mm(slope_vm[...], w_in[lanes, :], NT)
            part_vm[:, lanes] = grad[own:].astype(BF16)
            dz2_ref[:, lanes] += grad[:own]
        swap_dh2[i].start()
    out_sum.middle()
    for copy in swap_dh2:
        copy.wait()

    def second_back(span):
        grad = dz2_ref[span, :] + twin_vm[span, :].astype(F32)
        unit = unit_vm[span, :]
        out = unit_norm_back(grad, unit, scale_vm[span, :1], row["g1"])
        dz2_ref[span, :] = out
        low = out.astype(BF16)
        dco_vm[span, :] = low
        sums_ref[3:4, :] += jnp.sum(grad * unit, axis=0, keepdims=True)
        sums_ref[4:5, :] += jnp.sum(grad, axis=0, keepdims=True)
        sums_ref[5:6, :] += jnp.sum(low.astype(F32), axis=0, keepdims=True)

    tiles(own, second_back)
    swap_dco.start()
    depth = h2_vm.shape[1] // n_mem

    def in_weights(m, carry):
        lanes = pl.ds(pl.multiple_of(m * depth, depth), depth)
        dw_in[0, m] = mm(h2_vm[:, lanes].T, slope_vm[...]).astype(BF16).reshape(dw_in.shape[2:])
        return carry

    lax.fori_loop(0, n_mem, in_weights, 0)
    swap_dco.wait()

    dca_ref[...] = mm(dco_vm[...], w_co[...], NT).astype(BF16)
    heads = ca.shape[1] // n_mem

    def co_weights(m, carry):
        lanes = pl.ds(pl.multiple_of(m * heads, heads), heads)
        dw_co[0, m] = mm(ca[:, lanes].T, dco_vm[...]).astype(BF16).reshape(dw_co.shape[2:])
        return carry

    lax.fori_loop(0, n_mem, co_weights, 0)
    out_sum.end()
    out_sum.wait_send()
    spread_cot.wait_send()
    for k in range(2):
        spread_final.wait_recv(k)
    spread_final.wait_send()


def feed(n_mem, plane, cotangent, vectors, bias, ca, unit1, w_co, w_in, w_out):
    rows, part = ca.shape
    width, hidden = w_in.shape
    own = rows // 2

    def grad_shape(depth, cols):
        return (1, n_mem, plane, depth // (n_mem * plane), cols)

    out_shape, in_shape = grad_shape(hidden, width), grad_shape(width, hidden)
    shapes = [
        jax.ShapeDtypeStruct((2, own // 2, width), BF16),
        jax.ShapeDtypeStruct((rows, part), BF16),
        jax.ShapeDtypeStruct((own, width), F32),
        jax.ShapeDtypeStruct((8, width), F32),
        jax.ShapeDtypeStruct((1, hidden), F32),
        jax.ShapeDtypeStruct((1, n_mem, out_shape[3] // 2, width), BF16),
        jax.ShapeDtypeStruct(in_shape, BF16),
        jax.ShapeDtypeStruct(grad_shape(part, width), BF16),
        jax.ShapeDtypeStruct(out_shape, BF16),
    ]
    fetched = [ca, unit1, w_co, w_in, w_out]
    scratch = [pltpu.VMEM(item.shape, item.dtype) for item in fetched] + [
        pltpu.VMEM((own, width), BF16),
        pltpu.VMEM((rows, width), BF16),
        pltpu.VMEM((own, width), F32),
        pltpu.VMEM((own, 2 * HD), F32),
        pltpu.VMEM((rows, hidden), BF16),
        pltpu.VMEM((rows, hidden), BF16),
        pltpu.VMEM((own, width), F32),
        pltpu.VMEM((own, width), BF16),
        pltpu.VMEM((own, width), BF16),
        pltpu.VMEM((own, width), BF16),
        pltpu.VMEM((rows, width), BF16),
        pltpu.VMEM((rows, width), BF16),
    ]
    scratch += plane_sum_scratch(out_shape, n_mem, out_shape[3] // 2)
    scratch += [pltpu.SemaphoreType.DMA((PLANE_SUM_SEMS + 60,))]
    return pl.pallas_call(
        functools.partial(feed_kernel, n_mem, plane),
        in_specs=[VMEM] * 3 + [ANY] * len(fetched),
        out_specs=[ANY] + [VMEM] * (len(shapes) - 1),
        out_shape=shapes,
        scratch_shapes=scratch,
        compiler_params=pltpu.CompilerParams(
            vmem_limit_bytes=60 * 2**20, collective_id=1, has_side_effects=True
        ),
        cost_estimate=pl.CostEstimate(
            flops=rows * width * hidden * 12, bytes_accessed=40 * 2**20, transcendentals=rows * hidden * 2
        ),
        name="feed",
    )(cotangent, vectors, bias, *fetched)


def middle_kernel(n_mem, plane, planes, settled, slot_ref, member_ref, index_ref, *refs):
    refs = Walk(refs)
    dq_ref, dk_ref, dv_ref, wc_ref, scale_ref, gain_ref = refs.take(6)
    fetched = refs.take(6)
    ready = refs.take(len(settled))
    dsa_ref, dz1_ref, sums_ref, enc_out, own_cross, own_so = refs.take(6)
    outs = refs.take(len(settled))
    kept = refs.take(6)
    wk_t, wv_t, named_ref = refs.take(3)
    theirs, mine, twin_in, pair_in, dw_cross, dw_so, part_vm, twin_vm, dso_vm = refs.take(9)
    cross_bufs, so_bufs = refs.take(3), refs.take(3)
    settle_bufs = [refs.take(3) for _ in settled]
    sems = Sems(refs.one())
    place = Place(plane, planes)
    fetches = [Fetch(sems, src, dst) for src, dst in zip(fetched, kept)]
    h1_ref, enc_ref, dz2_ref, unit_ref, so_ref, sa_ref = kept
    settles = [
        Settle(
            place, sems, ready[i], outs[i], settle_bufs[i], columns, n_mem, (0, ready[i].shape[2])
        )
        for i, columns in enumerate(settled)
    ]
    cross_sum = PlaneSum(place, sems, dw_cross, own_cross, cross_bufs, (0, dw_cross.shape[3]))
    so_sum = PlaneSum(place, sems, dw_so, own_so, so_bufs, (0, dw_so.shape[3]))
    passages = mine.shape[0]
    units = passages // 2
    twin_sems = sems.take(2 * passages)
    twins = [
        remote(theirs.at[u], twin_in.at[u], twin_sems[2 * u], twin_sems[2 * u + 1], place.twin())
        for u in range(passages)
    ]
    pair_sems = sems.take(2 * units)
    pairs = [
        remote(
            mine.at[units + u], pair_in.at[u], pair_sems[2 * u], pair_sems[2 * u + 1], place.pair()
        )
        for u in range(units)
    ]
    homes = [
        Spread(place, sems, lambda k, u=u: mine.at[u], lambda k, u=u: enc_out.at[u], kinds=(0,))
        for u in range(units)
    ]
    swap_sems = sems.take(4)
    own = dz2_ref.shape[0]
    swap_part = remote(part_vm, twin_vm, swap_sems[0], swap_sems[1], place.twin())
    swap_dso = remote(
        dso_vm.at[pl.ds(0, own)], dso_vm.at[pl.ds(own, own)], swap_sems[2], swap_sems[3], place.twin()
    )

    for item in fetches:
        item.start()
    wk_t[...] = wc_ref[1].T
    wv_t[...] = wc_ref[2].T
    place.meet(
        column_peers(n_mem) + plane_peers(plane) + [(2 * plane * r, 0) for r in range(1, planes)]
    )
    for item in settles:
        item.start()

    def passage_grad(u):
        slot = slot_ref[u]
        value = mm(dk_ref[slot], wk_t[...]) + mm(dv_ref[slot], wv_t[...])
        return (value * member_ref[u]).astype(BF16)

    def add_twin(u):
        twins[u].wait_recv()

        def add(i, carry):
            span = pl.ds(pl.multiple_of(i * 64, 64), 64)
            total = mine[u, span, :].astype(F32) + twin_in[u, span, :].astype(F32)
            mine[u, span, :] = total.astype(BF16)
            return carry

        lax.fori_loop(0, PLEN // 64, add, 0)

    def send_home(u):
        add_twin(u)
        pairs[u].wait_recv()

        def add(i, carry):
            span = pl.ds(pl.multiple_of(i * 64, 64), 64)
            total = mine[u, span, :].astype(F32) + pair_in[u, span, :].astype(F32)
            mine[u, span, :] = total.astype(BF16)
            return carry

        lax.fori_loop(0, PLEN // 64, add, 0)
        homes[u].start()

    for group in (range(units, passages), range(units)):
        for u in group:
            theirs[u] = passage_grad(passages + u)
            twins[u].start()
        for u in group:
            mine[u] = passage_grad(u)
        if group.start:
            for u in group:
                add_twin(u)
                pairs[u - units].start()

    for item in fetches:
        item.get()
    for j in range(index_ref.shape[0]):
        named_ref[j * PLEN : (j + 1) * PLEN, :] = enc_ref[index_ref[j]]

    part = dw_cross.shape[-1]
    depth = h1_ref.shape[1] // n_mem

    def stacked(ref):
        return ref[...].reshape(-1, ref.shape[-1])

    def cross_weights(m, carry):
        lanes = pl.ds(pl.multiple_of(m * depth, depth), depth)
        split = dw_cross.shape[2:]
        dw_cross[0, m] = (
            (mm(h1_ref[:, lanes].T, dq_ref[...]) * 0.125).astype(BF16).reshape(split)
        )
        named_t = named_ref[:, lanes].T
        dw_cross[1, m] = mm(named_t, stacked(dk_ref)).astype(BF16).reshape(split)
        dw_cross[2, m] = mm(named_t, stacked(dv_ref)).astype(BF16).reshape(split)
        return carry

    lax.fori_loop(0, n_mem // 2, cross_weights, 0)
    send_home(0)
    lax.fori_loop(n_mem // 2, n_mem, cross_weights, 0)
    cross_sum.start()

    part_vm[...] = (mm(dq_ref[own:, :], wc_ref[0], NT) * 0.125).astype(BF16)
    swap_part.start()
    dz1_ref[...] = dz2_ref[...] + mm(dq_ref[:own, :], wc_ref[0], NT) * 0.125
    sums_ref[...] = jnp.zeros_like(sums_ref)
    sums_ref[3:4, :part] = 0.125 * jnp.sum(dq_ref[...].astype(F32), axis=0, keepdims=True)
    sums_ref[4:5, :part] = jnp.sum(stacked(dv_ref).astype(F32), axis=0, keepdims=True)
    send_home(1)
    swap_part.wait()
    gain = gain_ref[...]

    def norm(span):
        grad = dz1_ref[span, :] + twin_vm[span, :].astype(F32)
        unit = unit_ref[span, :]
        inner = grad * gain
        out = (
            inner
            - jnp.mean(inner, axis=-1, keepdims=True)
            - unit * jnp.mean(inner * unit, axis=-1, keepdims=True)
        ) * scale_ref[span, :1]
        dz1_ref[span, :] = out
        low = out.astype(BF16)
        dso_vm[span, :] = low
        sums_ref[0:1, :] += jnp.sum(grad * unit, axis=0, keepdims=True)
        sums_ref[1:2, :] += jnp.sum(grad, axis=0, keepdims=True)
        sums_ref[2:3, :] += jnp.sum(low.astype(F32), axis=0, keepdims=True)

    tiles(own, norm)
    swap_dso.start()
    cross_sum.middle()

    dsa_ref[:own, :] = mm(dso_vm[:own, :], so_ref[...], NT).astype(BF16)
    for u in range(2, units):
        send_home(u)
    swap_dso.wait()
    dsa_ref[own:, :] = mm(dso_vm[own:, :], so_ref[...], NT).astype(BF16)
    block = sa_ref.shape[1] // n_mem

    def so_weights(m, carry):
        lanes = pl.ds(pl.multiple_of(m * block, block), block)
        dw_so[0, m] = (
            mm(sa_ref[:, lanes].T, dso_vm[...]).astype(BF16).reshape(dw_so.shape[2:])
        )
        return carry

    lax.fori_loop(0, n_mem, so_weights, 0)
    so_sum.start()
    for item in settles:
        item.middle()
    cross_sum.end()
    for item in settles:
        item.forward()
    so_sum.middle()
    for item in settles:
        item.end()
    so_sum.end()
    cross_sum.wait_send()
    so_sum.wait_send()
    for copy in twins + pairs:
        copy.wait_send()
    for item in homes:
        item.wait_recv(0)
        item.wait_send()


def middle(
    n_mem, plane, planes, slot, member, index, dq, dk, dv, wc, so, sa, h1, enc, dz2, unit, scale, gain, ready
):
    rows, part = dq.shape
    width = h1.shape[1]
    own = rows // 2
    passages = slot.shape[0] // 2
    settled = tuple(columns for _, columns in ready)
    settled_shapes = [item.shape[:2] + (plane,) + item.shape[2:] for item, _ in ready]
    cross_shape = (3, n_mem, plane, width // (n_mem * plane), part)
    so_shape = (1, n_mem, plane, part // (n_mem * plane), width)
    shapes = [
        jax.ShapeDtypeStruct((rows, part), BF16),
        jax.ShapeDtypeStruct((own, width), F32),
        jax.ShapeDtypeStruct((8, width), F32),
        jax.ShapeDtypeStruct((passages // 2, PLEN, width), BF16),
        sum_shape(cross_shape),
        sum_shape(so_shape),
    ] + [reduce_out(shape, columns, plane) for shape, columns in zip(settled_shapes, settled)]
    fetched = [h1, enc, dz2, unit, so, sa]
    scratch = [pltpu.VMEM(item.shape, item.dtype) for item in fetched] + [
        pltpu.VMEM((part, width), BF16),
        pltpu.VMEM((part, width), BF16),
        pltpu.VMEM(dk.shape[:1] + (width,), BF16),
        pltpu.VMEM((passages, PLEN, width), BF16),
        pltpu.VMEM((passages, PLEN, width), BF16),
        pltpu.VMEM((passages, PLEN, width), BF16),
        pltpu.VMEM((passages // 2, PLEN, width), BF16),
        pltpu.VMEM(cross_shape, BF16),
        pltpu.VMEM(so_shape, BF16),
        pltpu.VMEM((own, width), BF16),
        pltpu.VMEM((own, width), BF16),
        pltpu.VMEM((rows, width), BF16),
    ]
    scratch += plane_sum_scratch(cross_shape, n_mem, cross_shape[3])
    scratch += plane_sum_scratch(so_shape, n_mem, so_shape[3])
    for shape in settled_shapes:
        scratch += settle_scratch(shape, n_mem, plane, planes, shape[3])
    count = (
        len(ready) * settle_sems(n_mem, plane, planes) + 2 * PLANE_SUM_SEMS + 2 * passages
        + passages + 4 * passages // 2 + 4 + 6
    )
    smem = pl.BlockSpec(memory_space=pltpu.SMEM)
    outs = pl.pallas_call(
        functools.partial(middle_kernel, n_mem, plane, planes, settled),
        in_specs=[smem, smem, smem] + [VMEM] * 6 + [ANY] * 6 + [VMEM] * len(ready),
        out_specs=[VMEM] * 3 + [ANY] + [VMEM] * (2 + len(ready)),
        out_shape=shapes,
        scratch_shapes=scratch + [pltpu.SemaphoreType.DMA((count,))],
        compiler_params=pltpu.CompilerParams(
            vmem_limit_bytes=60 * 2**20, collective_id=3, has_side_effects=True
        ),
        cost_estimate=pl.CostEstimate(
            flops=rows * part * width * 30, bytes_accessed=40 * 2**20, transcendentals=0
        ),
        name="middle",
    )(
        slot,
        member,
        index,
        dq,
        dk.reshape(-1, PLEN, part),
        dv.reshape(-1, PLEN, part),
        wc,
        scale,
        gain,
        *fetched,
        *[item for item, _ in ready],
    )
    return outs[:4], outs[4:6], outs[6:]


def self_attend_back(place, pair, q_vm, k_vm, v_vm, o_vm, do_vm, lse_vm, outs, scratch):
    dq_vm, dk_vm, dv_vm = outs
    q_a, do_a, k_t, q_h, do_h, p_vm, ds_vm = scratch
    base = 2 * place.core + place.parity
    count = q_vm.shape[0] // BLK
    lanes = pl.ds(pl.multiple_of(pair * 2 * HD, 2 * HD), 2 * HD)

    def rows(i):
        return pl.ds(pl.multiple_of(flip(base, i) * BLK, BLK), BLK)

    for i in range(count):
        span = slice(i * BLK, (i + 1) * BLK)
        q_a[span, :] = q_vm[rows(i), lanes]
        do_a[span, :] = do_vm[rows(i), lanes]
        k_t[:, span] = k_vm[rows(i), lanes].T
        q_t = q_a[span, :].T
        do_t = do_a[span, :].T
        prod = (do_a[span, :].astype(F32) * o_vm[rows(i), lanes].astype(F32)).T
        for head in range(2):
            delta = jnp.sum(prod[head * HD : (head + 1) * HD, :], axis=0, keepdims=True)
            q_h[head, :, span] = head_rows(q_t, head, lse_vm[pair, head : head + 1, span])
            do_h[head, :, span] = head_rows(do_t, head, delta)
    key_pos = lax.broadcasted_iota(jnp.int32, (BLK, BLK), 0)
    query_pos = lax.broadcasted_iota(jnp.int32, (BLK, BLK), 1)
    units = [(j, i, head) for j in range(count) for head in range(2) for i in range(j, count)]

    def products(unit):
        j, i, head = unit
        span = slice(i * BLK, (i + 1) * BLK)
        return (
            mm(ones_in(k_vm[rows(j), lanes], head), q_h[head, :, span]),
            mm(ones_in(v_vm[rows(j), lanes], head), do_h[head, :, span]),
        )

    ready = products(units[0])
    halves = {}
    for n, (j, i, head) in enumerate(units):
        coming = products(units[n + 1]) if n + 1 < len(units) else None
        scores, dprobs = ready
        probs = jnp.exp(scores)
        if i == j:
            probs = jnp.where(key_pos <= query_pos, probs, 0.0)
        keys, span = slice(j * BLK, (j + 1) * BLK), slice(i * BLK, (i + 1) * BLK)
        p_vm[head, keys, span] = probs.astype(BF16)
        ds_vm[head, keys, span] = (probs * dprobs).astype(BF16)
        if i == count - 1:
            late = slice(j * BLK, count * BLK)
            halves[head] = (
                mm(p_vm[head, keys, late], do_a[late, :]),
                mm(ds_vm[head, keys, late], q_a[late, :]),
            )
            if head == 1:
                dv_vm[rows(j), lanes] = pick_heads(halves[0][0], halves[1][0]).astype(BF16)
                dk_vm[rows(j), lanes] = pick_heads(halves[0][1], halves[1][1]).astype(BF16)
        ready = coming
    for i in range(count):
        span, keys = slice(i * BLK, (i + 1) * BLK), slice(0, (i + 1) * BLK)
        dq_t = jnp.concatenate(
            [
                mm(k_t[head * HD : (head + 1) * HD, keys], ds_vm[head, keys, span])
                for head in range(2)
            ],
            axis=0,
        )
        dq_vm[rows(i), lanes] = dq_t.T.astype(BF16) * BF16(0.125)


def last_kernel(n_mem, plane, planes, settled, chunks, *refs):
    refs = Walk(refs)
    q_ref, k_ref, v_ref, o_ref, do_ref, lse_ref, feed_ref, hidden_ref, middle_ref = refs.take(9)
    fetched = refs.take(3)
    ready = refs.take(len(settled))
    small_out, dx_out, self_out = refs.take(3)
    outs = refs.take(len(settled))
    x_ref, w_ref, dz1_ref = kept = refs.take(3)
    dq_vm, dk_vm, dv_vm = refs.take(3)
    attend_scratch = refs.take(7)
    x_t, dw_vm = refs.take(2)
    part_vm, twin_vm, dx_vm = refs.take(3)
    chunk_own = [refs.one() for _ in range(chunks)]
    chunk_bufs = [refs.take(3) for _ in range(chunks)]
    chunk_settle = [refs.take(3) for _ in range(chunks)]
    settle_bufs = [refs.take(3) for _ in settled]
    small_near, small_line, small_twin, small_far, small_sum, sem_ref = refs.take(6)
    sems = Sems(sem_ref)
    place = Place(plane, planes)
    fetches = [Fetch(sems, src, dst) for src, dst in zip(fetched, kept)]
    settles = [
        Settle(
            place, sems, ready[i], outs[i], settle_bufs[i], columns, n_mem, (0, ready[i].shape[2])
        )
        for i, columns in enumerate(settled)
    ]
    rows, part = q_ref.shape
    lanes = part // chunks
    depth = dw_vm.shape[3]
    sums = [
        PlaneSum(
            place, sems, dw_vm, chunk_own[c], chunk_bufs[c], (0, depth), (c * lanes, lanes)
        )
        for c in range(chunks)
    ]
    ends = [
        Settle(
            place, sems, chunk_own[c], self_out, chunk_settle[c], True, n_mem, (0, depth), c * lanes
        )
        for c in range(chunks)
    ]
    near_sems = sems.take(6)
    near = [
        remote(
            small_sum, small_near.at[t - 1], near_sems[2 * t - 2], near_sems[2 * t - 1], place.near(t)
        )
        for t in range(1, plane)
    ]
    line = Line(
        place, sems, lambda s: small_sum.at[flip(place.mem, s)], lambda s: small_line.at[s - 1], n_mem
    )
    twin_sems = sems.take(2)
    twin = remote(small_sum.at[place.mem], small_twin, twin_sems[0], twin_sems[1], place.twin())
    far_sems = sems.take(2 * (planes - 1))
    far = [
        remote(
            small_sum.at[place.mem],
            small_far.at[r - 1],
            far_sems[2 * r - 2],
            far_sems[2 * r - 1],
            place.far(r),
        )
        for r in range(1, planes)
    ]
    seg = dx_out.shape[1]
    own = 2 * seg
    spread = Spread(
        place,
        sems,
        lambda k: dx_vm.at[pl.ds(seg * k, seg)],
        lambda k: dx_out.at[place.parity],
    )
    swap_sems = sems.take(2)
    swap_part = remote(part_vm, twin_vm, swap_sems[0], swap_sems[1], place.twin())

    for item in fetches:
        item.start()
    place.meet(
        column_peers(n_mem) + plane_peers(plane) + [(2 * plane * r, 0) for r in range(1, planes)]
    )
    for item in settles:
        item.start()
    block = x_ref.shape[1] // n_mem

    def input_part(span):
        return (
            mm(dq_vm[span, :], w_ref[0], NT)
            + mm(dk_vm[span, :], w_ref[1], NT)
            + mm(dv_vm[span, :], w_ref[2], NT)
        )

    pairs = part // (2 * HD)
    late = []
    for c in range(chunks):
        for pair in range(c * pairs // chunks, (c + 1) * pairs // chunks):
            self_attend_back(
                place,
                pair,
                q_ref,
                k_ref,
                v_ref,
                o_ref,
                do_ref,
                lse_ref,
                (dq_vm, dk_vm, dv_vm),
                attend_scratch,
            )
        if c == 0:
            for item in fetches:
                item.get()
            for m in range(n_mem):
                x_t[m] = x_ref[:, m * block : (m + 1) * block].T
        span = slice(c * lanes, (c + 1) * lanes)

        def weights(m, carry, span=span):
            for i, grad in enumerate((dq_vm, dk_vm, dv_vm)):
                dw_vm[i, m, :, :, span] = (
                    mm(x_t[m], grad[:, span]).astype(BF16).reshape(plane, depth, lanes)
                )
            return carry

        if c < chunks - 2:
            lax.fori_loop(0, n_mem, weights, 0)
            sums[c].start()
        if c == 1:
            sums[0].middle()
        if c == 2:
            for item in settles:
                item.middle()
            sums[0].end()
            ends[0].start()
            sums[1].middle()
        late.append(weights)
    part_vm[...] = input_part(slice(own, 2 * own)).astype(BF16)
    swap_part.start()
    lax.fori_loop(0, n_mem, late[-2], 0)
    sums[-2].start()
    swap_part.wait()
    total = dz1_ref[...] + input_part(slice(0, own)) + twin_vm[...].astype(F32)
    dx_vm[...] = total.astype(BF16)
    spread.start()
    lax.fori_loop(0, n_mem, late[-1], 0)
    sums[-1].start()
    sums[1].end()
    ends[1].start()
    for item in settles:
        item.forward()
    sums[-2].middle()

    small_sum[...] = jnp.zeros_like(small_sum)
    wide = small_sum.shape[2]
    unit = wide // 2
    first = place.core == 0
    for row, ref, at in (
        (2, middle_ref, 2),
        (5, feed_ref, 5),
        (6, middle_ref, 1),
        (7, feed_ref, 4),
        (8, feed_ref, 1),
        (9, feed_ref, 2),
        (10, middle_ref, 0),
        (11, feed_ref, 3),
        (12, feed_ref, 0),
    ):
        for b in range(n_mem):
            small_sum[b, row : row + 1, :] = ref[at : at + 1, b * wide : (b + 1) * wide]
    for row, value in (
        (0, jnp.sum(dq_vm[...].astype(F32), axis=0, keepdims=True)),
        (1, jnp.sum(dv_vm[...].astype(F32), axis=0, keepdims=True)),
        (3, middle_ref[3:4, :part]),
        (4, middle_ref[4:5, :part]),
    ):
        for b in range(n_mem):
            side = value[:, b * unit : (b + 1) * unit]
            none = jnp.zeros_like(side)
            small_sum[b, row : row + 1, :unit] = jnp.where(first, side, none)
            small_sum[b, row : row + 1, unit:] = jnp.where(first, none, side)
    count = hidden_ref.shape[1] // (n_mem * wide)
    for b in range(n_mem):
        for i in range(count):
            at = (b * count + i) * wide
            side = hidden_ref[:, at : at + wide]
            none = jnp.zeros_like(side)
            row = 13 + i
            small_sum[b, row : row + 1, :] = jnp.where(first, side, none)
            small_sum[b, row + count : row + count + 1, :] = jnp.where(first, none, side)
    for copy in near:
        copy.start()
    sums[-1].middle()
    sums[-2].end()
    ends[-2].start()
    ends[0].middle()
    for copy in near:
        copy.wait()
    total = small_sum[...]
    for t in range(plane - 1):
        total += small_near[t]
    small_sum[...] = total
    line.start()
    sums[-1].end()
    ends[-1].start()
    ends[1].middle()
    ends[0].forward()
    for item in settles:
        item.end()
    ends[-2].middle()
    ends[1].forward()
    for s in range(1, n_mem):
        line.wait_recv(s)
    line.wait_send()
    value = small_sum[place.mem]
    for s in range(n_mem - 1):
        value += small_line[s]
    small_sum[place.mem] = value
    twin.start()
    ends[-1].middle()
    ends[-2].forward()
    for item in ends[:-2]:
        item.end()
    twin.wait()
    value = small_sum[place.mem] + small_twin[...]
    if far:
        small_sum[place.mem] = value
        for copy in far:
            copy.start()
        for copy in far:
            copy.wait()
        for r in range(planes - 1):
            value += small_far[r]
    small_out[...] = value
    ends[-1].forward()
    ends[-2].end()
    ends[-1].end()
    for item in sums:
        item.wait_send()
    for k in range(2):
        spread.wait_recv(k)
    spread.wait_send()


def last(n_mem, plane, planes, q, k, v, o, do, lse, x, w, dz1, sums, small_shape, ready):
    rows, part = q.shape
    chunks = part // (2 * HD)
    width = x.shape[1]
    own = rows // 2
    settled = tuple(columns for _, columns in ready)
    settled_shapes = [item.shape[:2] + (plane,) + item.shape[2:] for item, _ in ready]
    grad_shape = (3, n_mem, plane, width // (n_mem * plane), part)
    depth, lanes = grad_shape[3], part // chunks
    small_part = small_shape[1:]
    shapes = [
        jax.ShapeDtypeStruct(small_part, F32),
        jax.ShapeDtypeStruct((2, own // 2, width), BF16),
        reduce_out(grad_shape, True, plane),
    ] + [reduce_out(shape, columns, plane) for shape, columns in zip(settled_shapes, settled)]
    fetched = [x, w, dz1]
    scratch = (
        [pltpu.VMEM(item.shape, item.dtype) for item in fetched]
        + [pltpu.VMEM((rows, part), BF16)] * 3
        + [
            pltpu.VMEM((rows, 2 * HD), BF16),
            pltpu.VMEM((rows, 2 * HD), BF16),
            pltpu.VMEM((2 * HD, rows), BF16),
            pltpu.VMEM((2, 2 * HD, rows), BF16),
            pltpu.VMEM((2, 2 * HD, rows), BF16),
            pltpu.VMEM((2, rows, rows), BF16),
            pltpu.VMEM((2, rows, rows), BF16),
            pltpu.VMEM((n_mem, width // n_mem, rows), BF16),
            pltpu.VMEM(grad_shape, BF16),
        ]
        + [pltpu.VMEM((own, width), BF16)] * 3
        + [pltpu.VMEM((3, n_mem, depth, lanes), BF16)] * chunks
    )
    for _ in range(chunks):
        scratch += plane_sum_scratch(grad_shape, n_mem, depth, lanes)
    for _ in range(chunks):
        scratch += settle_scratch(grad_shape, n_mem, plane, planes, depth, lanes)
    for shape in settled_shapes:
        scratch += settle_scratch(shape, n_mem, plane, planes, shape[3])
    scratch += [
        pltpu.VMEM((plane - 1,) + small_shape, F32),
        pltpu.VMEM((n_mem - 1,) + small_part, F32),
        pltpu.VMEM(small_part, F32),
        pltpu.VMEM((max(planes - 1, 1),) + small_part, F32),
        pltpu.VMEM(small_shape, F32),
        pltpu.SemaphoreType.DMA(
            (
                (len(ready) + chunks) * settle_sems(n_mem, plane, planes)
                + chunks * PLANE_SUM_SEMS
                + 24
                + 2 * planes,
            )
        ),
    ]
    outs = pl.pallas_call(
        functools.partial(last_kernel, n_mem, plane, planes, settled, chunks),
        in_specs=[VMEM] * 9 + [ANY] * 3 + [VMEM] * len(ready),
        out_specs=[VMEM, ANY, VMEM] + [VMEM] * len(ready),
        out_shape=shapes,
        scratch_shapes=scratch,
        compiler_params=pltpu.CompilerParams(
            vmem_limit_bytes=60 * 2**20, collective_id=4, has_side_effects=True
        ),
        cost_estimate=pl.CostEstimate(
            flops=rows * rows * width * 40, bytes_accessed=40 * 2**20, transcendentals=rows * rows * 8
        ),
        name="last",
    )(q, k, v, o, do, lse, *sums, *fetched, *[item for item, _ in ready])
    return outs[0], outs[1], outs[2:]


def cross_forward_kernel(n_mem, plane, kinds, index_ref, q_ref, k_ref, v_ref, *refs):
    refs = Walk(refs)
    count_w = len(kinds)
    shards = refs.take(count_w)
    o_ref, lse_ref = refs.take(2)
    halves = refs.take(count_w)
    v_t, o_t, sem_ref = refs.take(3)
    sems = Sems(sem_ref)
    place = Place(plane)
    step = pl.program_id(0) * pl.num_programs(1) + pl.program_id(1)
    last = pl.num_programs(0) * pl.num_programs(1) - 1
    gathers = [
        Gather(place, sems, shard, half, columns, n_mem, (1,) if i == 1 else None)
        for i, (shard, half, columns) in enumerate(zip(shards, halves, kinds))
    ]
    @pl.when(step == 0)
    def _():
        for gather in gathers:
            gather.own.start()
        place.meet(column_peers(n_mem) + plane_peers(plane))
        for gather in gathers:
            gather.begin()

    rows = q_ref.shape[0]
    count = index_ref.shape[0]

    @pl.when(pl.program_id(1) == 0)
    def _():
        for j in range(count):
            v_t[:, j * BLK : (j + 1) * BLK] = v_ref[index_ref[j]].T

    units = []
    for i in range(rows // BLK):
        q_t = q_ref[i * BLK : (i + 1) * BLK, :].T
        for head in range(2):
            q_head = head_rows(q_t, head)

            def score(j, q_head=q_head):
                return mm(k_ref[index_ref[j]], q_head)

            def value(j, head=head):
                return v_t[head * HD : (head + 1) * HD, j * BLK : (j + 1) * BLK]

            units.append(
                (
                    [functools.partial(score, j) for j in range(count)],
                    [functools.partial(value, j) for j in range(count)],
                    (i, head),
                )
            )

    def finish(tag, mixed, lse):
        i, head = tag
        span = slice(i * BLK, (i + 1) * BLK)
        o_t[head * HD : (head + 1) * HD, span] = mixed
        lse_ref[0, head : head + 1, span] = lse

    whole_one, line_one = gathers
    plan = {
        4: [(whole_one.share, 1)],
        6: [(line_one.share, 1)],
        10: [(whole_one.share, 2)],
        12: [(line_one.share, 2), (whole_one.forward, 1)],
        14: [(line_one.forward, 1)],
        17: [(whole_one.share, 3)],
        19: [(line_one.share, 3), (whole_one.forward, 2)],
        24: [(whole_one.forward, 3)],
    }

    def serve(n):
        for when, calls in plan.items():
            if when % len(units) == n:

                @pl.when(step == when // len(units))
                def _():
                    for call, hops in calls:
                        call(hops)

    softmax_units(units, finish, serve)
    o_ref[...] = o_t[...].T.astype(BF16)

    @pl.when(step == last)
    def _():
        for gather in gathers:
            gather.finish()


def cross_forward(n_mem, plane, index, q, k, v, params):
    rows, width = q.shape
    pairs = width // (2 * HD)
    keys = index.shape[0] * PLEN
    block = 2 * BLK
    question = pl.BlockSpec((block, 2 * HD), lambda h, i: (i, h))
    memory = pl.BlockSpec(k.shape[:2] + (2 * HD,), lambda h, i: (0, 0, h))
    kinds = tuple(columns for _, columns in params)
    views = [half_views(shard, columns, n_mem, plane) for shard, columns in params]
    outs = pl.pallas_call(
        functools.partial(cross_forward_kernel, n_mem, plane, kinds),
        grid=(pairs, rows // block),
        in_specs=[pl.BlockSpec(memory_space=pltpu.SMEM), question, memory, memory]
        + [whole(view.shape) for view, _ in views],
        out_specs=[question, pl.BlockSpec((1, 2, block), lambda h, i: (h, 0, i))]
        + [ANY] * len(params),
        out_shape=[
            jax.ShapeDtypeStruct((rows, width), BF16),
            jax.ShapeDtypeStruct((pairs, 2, rows), F32),
        ]
        + [jax.ShapeDtypeStruct(full, BF16) for _, full in views],
        scratch_shapes=[
            pltpu.VMEM((2 * HD, keys), BF16),
            pltpu.VMEM((2 * HD, block), F32),
            pltpu.SemaphoreType.DMA((4 + GATHER_SEMS * len(params),)),
        ],
        compiler_params=pltpu.CompilerParams(
            vmem_limit_bytes=60 * 2**20, collective_id=2, has_side_effects=True
        ),
        cost_estimate=pl.CostEstimate(
            flops=rows * keys * width * 16,
            bytes_accessed=rows * width * 4 + k.size * 4,
            transcendentals=rows * keys * pairs * 2,
        ),
        name="cross_forward",
    )(index, q, k, v, *[view for view, _ in views])
    return outs[:2], outs[2:]


def cross_backward_kernel(
    n_mem, plane, planes, chunks, settled, index_ref, q_ref, k_ref, v_ref, o_ref, do_ref, lse_ref, *refs
):
    refs = Walk(refs)
    kinds = {which: columns for which, columns, _ in chunks}
    grads = refs.take(len(kinds))
    ready = refs.take(len(settled))
    dq_ref, dk_ref, dv_ref = refs.take(3)
    outs = refs.take(len(kinds))
    q_h, do_h, dq_t, p_vm, ds_vm = refs.take(5)
    sems = Sems(refs.refs[-1])
    place = Place(plane, planes)
    sums, settles = [], []
    for which, columns, rows_of in chunks:
        own = refs.one()
        sums.append(PlaneSum(place, sems, grads[which], own, refs.take(3), rows_of))
        settles.append(
            Settle(place, sems, own, outs[which], refs.take(3), columns, n_mem, rows_of)
        )
    first = [
        Settle(
            place, sems, ready[i], outs[which], refs.take(3), columns, n_mem, (0, ready[i].shape[2])
        )
        for i, (which, columns) in enumerate(settled)
    ]
    passage = pl.program_id(1)
    step = pl.program_id(0) * pl.num_programs(1) + passage
    steps = pl.num_programs(0) * pl.num_programs(1)
    rows = q_ref.shape[0]
    count = rows // BLK

    @pl.when(step == 0)
    def _():
        place.meet(
            column_peers(n_mem) + plane_peers(plane) + [(2 * plane * r, 0) for r in range(1, planes)]
        )
        for item in first:
            item.start()

    def at(when, *calls):
        @pl.when(step == when)
        def _():
            for call in calls:
                call()

    plan = ((0, 2, 4, 7, 8), (2, 4, 6, 9, 10), (5, 7, 9, 12, 13), (8, 10, 11, 13, 14))
    for i, (plane_sum, settle) in enumerate(zip(sums, settles)):
        start, middle, end, line, near = plan[i]
        at(start, plane_sum.start)
        at(middle, plane_sum.middle)
        at(end, plane_sum.end, settle.start)
        at(line, settle.middle)
        at(near, settle.forward)
    for item in first:
        at(6, item.middle)
        at(7, item.forward)

    @pl.when(passage == 0)
    def _():
        for i in range(count):
            span = slice(i * BLK, (i + 1) * BLK)
            q_t = q_ref[span, :].T
            grads_t = do_ref[span, :].T
            prod = (do_ref[span, :].astype(F32) * o_ref[span, :].astype(F32)).T
            for head in range(2):
                delta = jnp.sum(prod[head * HD : (head + 1) * HD, :], axis=0, keepdims=True)
                q_h[head, :, span] = head_rows(q_t, head, lse_ref[0, head : head + 1, span])
                do_h[head, :, span] = head_rows(grads_t, head, delta)
        dq_t[...] = jnp.zeros_like(dq_t)

    keys = dk_ref.shape[0] // BLK
    slots = [index_ref[passage * keys + j] for j in range(keys)]
    k_t = jnp.concatenate([k_ref[slot].T for slot in slots], axis=1)
    units = [(head, j, i) for head in range(2) for j in range(keys) for i in range(count)]

    def products(unit):
        head, j, i = unit
        span = slice(i * BLK, (i + 1) * BLK)
        return (
            mm(ones_in(k_ref[slots[j]], head), q_h[head, :, span]),
            mm(ones_in(v_ref[slots[j]], head), do_h[head, :, span]),
        )

    coming = products(units[0])
    halves = []
    for n, (head, j, i) in enumerate(units):
        scores, dprobs = coming
        if n + 1 < len(units):
            coming = products(units[n + 1])
        tile, span = slice(j * BLK, (j + 1) * BLK), slice(i * BLK, (i + 1) * BLK)
        probs = jnp.exp(scores)
        p_vm[head, tile, span] = probs.astype(BF16)
        ds_vm[head, tile, span] = (probs * dprobs).astype(BF16)
        if (j, i) == (keys - 1, count - 1):
            half = slice(head * HD, (head + 1) * HD)
            halves.append((mm(p_vm[head], do_ref[...]), mm(ds_vm[head], q_ref[...])))
            dq_t[half, :] += mm(k_t[half, :], ds_vm[head])
    dv_ref[...] = pick_heads(halves[0][0], halves[1][0]).astype(BF16)
    dk_ref[...] = pick_heads(halves[0][1], halves[1][1]).astype(BF16)

    @pl.when(passage == pl.num_programs(1) - 1)
    def _():
        dq_ref[...] = dq_t[...].T.astype(BF16)

    @pl.when(step == steps - 1)
    def _():
        for settle in first + settles:
            settle.end()
        for item in sums:
            item.wait_send()


def cross_backward(n_mem, plane, planes, index, q, k, v, o, do, lse, grads, ready):
    rows, width = q.shape
    pairs = width // (2 * HD)
    block = 2 * PLEN
    keys = index.shape[0] * PLEN
    passages = keys // block
    question = pl.BlockSpec((rows, 2 * HD), lambda h, u: (0, h))
    memory = pl.BlockSpec(k.shape[:2] + (2 * HD,), lambda h, u: (0, 0, h))
    grads_of = pl.BlockSpec((block, 2 * HD), lambda h, u: (u, h))
    shapes, chunks, scratch = [], [], []
    for which, (grad, columns, pieces, begin) in enumerate(grads):
        lead, _, _, depth, cols = grad.shape
        count = depth // pieces
        shapes.append(reduce_out(grad.shape, columns, plane))
        for i in range(begin, pieces):
            chunks.append((which, columns, (i * count, count)))
            scratch.append(pltpu.VMEM((lead, n_mem, count, cols), BF16))
            scratch += plane_sum_scratch(grad.shape, n_mem, count)
            scratch += settle_scratch(grad.shape, n_mem, plane, planes, count)
    settled = tuple((which, grads[which][1]) for _, which in ready)
    for item, _ in ready:
        shape = item.shape[:2] + (plane,) + item.shape[2:]
        scratch += settle_scratch(shape, n_mem, plane, planes, shape[3])
    outs = pl.pallas_call(
        functools.partial(cross_backward_kernel, n_mem, plane, planes, tuple(chunks), settled),
        grid=(pairs, passages),
        in_specs=[
            pl.BlockSpec(memory_space=pltpu.SMEM),
            question,
            memory,
            memory,
            question,
            question,
            pl.BlockSpec((1, 2, rows), lambda h, u: (h, 0, 0)),
        ]
        + [ANY] * len(grads)
        + [whole(item.shape) for item, _ in ready],
        out_specs=[question, grads_of, grads_of]
        + [whole(item.shape) for item in shapes],
        out_shape=[
            jax.ShapeDtypeStruct((rows, width), BF16),
            jax.ShapeDtypeStruct((keys, width), BF16),
            jax.ShapeDtypeStruct((keys, width), BF16),
        ]
        + shapes,
        scratch_shapes=[
            pltpu.VMEM((2, 2 * HD, rows), BF16),
            pltpu.VMEM((2, 2 * HD, rows), BF16),
            pltpu.VMEM((2 * HD, rows), F32),
            pltpu.VMEM((2, block, rows), BF16),
            pltpu.VMEM((2, block, rows), BF16),
        ]
        + scratch
        + [
            pltpu.SemaphoreType.DMA(
                (
                    len(chunks) * PLANE_SUM_SEMS
                    + (len(chunks) + len(ready)) * settle_sems(n_mem, plane, planes),
                )
            )
        ],
        compiler_params=pltpu.CompilerParams(
            vmem_limit_bytes=56 * 2**20, collective_id=5, has_side_effects=True
        ),
        cost_estimate=pl.CostEstimate(
            flops=rows * keys * width * 40,
            bytes_accessed=rows * width * 10 + k.size * 8,
            transcendentals=rows * keys * pairs * 2,
        ),
        name="cross_backward",
    )(index, q, k, v, o, do, lse, *[item[0] for item in grads], *[item for item, _ in ready])
    return outs[:3], outs[3:]


def widen_kernel(*refs):
    count = len(refs) // 2
    for src, dst in zip(refs[:count], refs[count:]):
        dst[...] = src[...].astype(F32)


def widen(pairs):
    steps = 8
    flats = [value.reshape(-1, like.shape[-1]) for value, like in pairs]
    blocks = [
        pl.BlockSpec((item.shape[0] // steps, item.shape[1]), lambda i: (i, 0)) for item in flats
    ]
    outs = pl.pallas_call(
        widen_kernel,
        grid=(steps,),
        in_specs=blocks,
        out_specs=blocks,
        out_shape=[jax.ShapeDtypeStruct(item.shape, F32) for item in flats],
        compiler_params=pltpu.CompilerParams(vmem_limit_bytes=60 * 2**20),
        cost_estimate=pl.CostEstimate(
            flops=0, bytes_accessed=6 * sum(item.size for item in flats), transcendentals=0
        ),
        name="widen",
    )(*flats)
    return [out.reshape(like.shape) for out, (_, like) in zip(outs, pairs)]


def body(
    hidden_in,
    encoder_rows,
    passage_map,
    self_qkv,
    self_out,
    cross_qkv,
    cross_out,
    ffn_in,
    ffn_out,
    ffn_in_bias,
    biases,
    gains,
    cotangent,
):
    n_pb = lax.axis_size("pb")
    n_mem = lax.axis_size("mem")
    columns = n_pb // 2
    plane = min(columns, 4)
    pb = lax.axis_index("pb")
    core = pb % 2
    width = hidden_in.shape[2]
    planes = columns // plane

    enc_local = encoder_rows.reshape(-1, PLEN, width)
    n_bias, n_gain = biases.shape[0], gains.shape[0]
    small = jnp.concatenate([biases, gains, ffn_in_bias.reshape(-1, biases.shape[1])], axis=0)
    n_small = small.shape[0]
    small_rows = -(-n_small // 16) * 16
    small = jnp.pad(small, ((0, small_rows - n_small), (0, 0)))
    rows_out, halves, kept = front(
        n_mem,
        plane,
        (n_bias, n_gain),
        hidden_in,
        enc_local,
        passage_map,
        small,
        [(self_qkv, True), (self_out, False), (cross_qkv, True), (cross_out, False)],
    )
    x_full, enc_full, index, small = rows_out
    sq, sk, sv, sa, self_lse, h1_full, unit1, scale1, cq, ck, cv = kept
    index = index.reshape(-1)

    def flat(half):
        lead, _, _, _, cols = half.shape
        return half.reshape(lead, -1, cols)

    w_self, w_cross = flat(halves[0]), flat(halves[2])
    w_self_out, w_cross_out = flat(halves[1])[0], flat(halves[3])[0]
    small = small.astype(F32)
    vectors = small[:, : n_bias + n_gain].transpose(1, 0, 2).reshape(n_bias + n_gain, width)
    bias, gain = vectors[:n_bias], vectors[n_bias:]
    ffn_bias = small[:, n_bias + n_gain : n_small].reshape(-1)

    def half_of(vector):
        parts = vector.reshape(n_mem, 2, -1)
        return jnp.where(core == 0, parts[:, 0], parts[:, 1]).reshape(-1)

    order = jnp.arange(encoder_rows.shape[1] * n_mem, dtype=jnp.int32)
    hits = index[None, :] == order[:, None]
    member = jnp.any(hits, axis=1).astype(F32)
    slot = jnp.sum(jnp.where(hits, jnp.arange(index.shape[0], dtype=jnp.int32)[None], 0), axis=1)
    (ca, cross_lse), halves = cross_forward(
        n_mem,
        plane,
        index,
        cq,
        ck,
        cv,
        [(ffn_in[None], True), (ffn_out, False)],
    )
    w_ffn_in, w_ffn_out = flat(halves[0])[0], halves[1]

    rows_of = jnp.stack(
        [gain[0], bias[6], bias[5], gain[1], bias[7], bias[9], gain[2], bias[8]]
    )
    layer_out, dca, dz2, feed_sums, hidden_sums, own_ffn_out, dw_ffn_in, dw_cross_out, dw_ffn_out = feed(
        n_mem,
        plane,
        cotangent,
        rows_of,
        half_of(ffn_bias)[None],
        ca,
        unit1,
        w_cross_out,
        w_ffn_in,
        w_ffn_out,
    )
    (dcq, dck, dcv), ffn_sums = cross_backward(
        n_mem,
        plane,
        planes,
        index,
        cq,
        ck,
        cv,
        ca,
        dca,
        cross_lse,
        [(dw_ffn_out, False, 2, 1), (dw_ffn_in, True, 2, 0), (dw_cross_out, False, 1, 0)],
        [(own_ffn_out, 0)],
    )
    (dsa, dz1, middle_sums, enc_sum), (own_cross, own_so), _ = middle(
        n_mem,
        plane,
        planes,
        slot,
        member,
        index,
        dcq,
        dck,
        dcv,
        w_cross,
        w_self_out,
        sa,
        h1_full,
        enc_full.reshape(-1, PLEN, width),
        dz2,
        unit1,
        scale1,
        gain[0][None],
        [],
    )

    vec, dx, sums = last(
        n_mem,
        plane,
        planes,
        sq,
        sk,
        sv,
        sa,
        dsa,
        self_lse,
        x_full,
        w_self,
        dz1,
        [feed_sums, hidden_sums, middle_sums],
        small.shape,
        [(own_so, False), (own_cross, True)],
    )
    (
        grad_in,
        grad_encoder,
        out_self_qkv,
        out_self_out,
        out_cross_qkv,
        out_cross_out,
        out_ffn_in,
        out_ffn_out,
    ) = widen(
        [
            (dx, hidden_in),
            (enc_sum, encoder_rows),
            (sums[0], self_qkv),
            (sums[1], self_out),
            (sums[2], cross_qkv),
            (ffn_sums[2], cross_out),
            (ffn_sums[1], ffn_in),
            (ffn_sums[0], ffn_out),
        ]
    )
    out_ffn_bias = vec[n_bias + n_gain : n_small].reshape(-1)
    return (
        layer_out,
        grad_in,
        grad_encoder,
        out_self_qkv,
        out_self_out,
        out_cross_qkv,
        out_cross_out,
        out_ffn_in,
        out_ffn_out,
        out_ffn_bias,
        vec[:n_bias],
        vec[n_bias : n_bias + n_gain],
    )


def solution(mesh):
    placed = (
        P("pb", "mem", None),
        P("pb", "mem", None, None),
        P("pb", None),
        P(None, "mem", None),
        P("mem", None),
        P(None, "mem", None),
        P("mem", None),
        P("mem", None),
        P("mem", None),
        P("mem"),
        P(None, "mem"),
        P(None, "mem"),
        P("pb", "mem", None),
    )
    return jax.shard_map(
        body,
        mesh=mesh,
        in_specs=placed,
        out_specs=(
            P("pb", "mem", None),
            P("pb", "mem", None),
            P("pb", "mem", None, None),
            P(None, "mem", None),
            P("mem", None),
            P(None, "mem", None),
            P("mem", None),
            P("mem", None),
            P("mem", None),
            P("mem"),
            P(None, "mem"),
            P(None, "mem"),
        ),
        check_vma=False,
    )
```

```python
import functools

import jax
import jax.numpy as jnp
from jax import lax
from jax.experimental import pallas as pl
from jax.experimental.pallas import tpu as pltpu
from jax.sharding import PartitionSpec as P

HD = 64
PLEN = 256
BLK = 256
F32 = jnp.float32
BF16 = jnp.bfloat16

NN = (((1,), (0,)), ((), ()))
NT = (((1,), (1,)), ((), ()))


def mm(a, b, dims=NN):
    return lax.dot_general(a, b, dims, preferred_element_type=F32)


def head_mask_rows(block, head):
    rows = lax.broadcasted_iota(jnp.int32, block.shape, 0)
    return jnp.where((rows // HD) == head, block, jnp.zeros_like(block))


def head_rows(block, head, extra=None):
    block = block.astype(F32)
    rows = lax.broadcasted_iota(jnp.int32, block.shape, 0)
    out = jnp.where((rows // HD) == head, block, 0.0)
    if extra is not None:
        rest = -extra
        for i in range(3):
            term = rest.astype(BF16).astype(F32)
            rest = rest - term
            out = jnp.where(rows == (1 - head) * HD + i, term, out)
    return out.astype(BF16)


def ones_in(block, head):
    lanes = lax.broadcasted_iota(jnp.int32, block.shape, 1)
    first = (1 - head) * HD
    return jnp.where((lanes >= first) & (lanes < first + 3), jnp.ones_like(block), block)


def pick_heads(first, second):
    lanes = lax.broadcasted_iota(jnp.int32, first.shape, 1)
    return jnp.where(lanes < HD, first, second)


MESH = pl.DeviceIdType.MESH
ANY = pl.BlockSpec(memory_space=pl.ANY)
VMEM = pl.BlockSpec(memory_space=pltpu.VMEM)
PLANE = 4


def flip(index, bits):
    bit = 1
    while bit <= bits:
        if bits & bit:
            unit = jnp.int32(bit)
            index = index + unit - 2 * unit * lax.rem(lax.div(index, unit), jnp.int32(2))
        bit *= 2
    return index


class Place:
    def __init__(self, plane, planes=1):
        self.pb = lax.axis_index("pb")
        self.mem = lax.axis_index("mem")
        two = jnp.int32(2)
        self.core = lax.rem(self.pb, two)
        self.quarter = lax.rem(lax.div(self.pb, two), jnp.int32(plane))
        self.parity = lax.rem(self.mem, two)
        self.half = lax.div(self.mem, two)
        self.plane = plane
        self.planes = planes

    def near(self, t):
        return (flip(self.pb, 2 * t), self.mem)

    def far(self, r):
        return (flip(self.pb, 2 * self.plane * r), self.mem)

    def line(self, s):
        return (self.pb, flip(self.mem, s))

    def twin(self):
        return (flip(self.pb, 1), self.mem)

    def pair(self):
        return (self.pb, flip(self.mem, 1))

    def worker(self, k):
        return (self.pb - self.core + self.half, 2 * self.core + flip(self.parity, k))

    def at_home(self):
        return self.half == self.core

    def meet(self, peers):
        barrier = pltpu.get_barrier_semaphore()
        for pb_bits, mem_bits in peers:
            pl.semaphore_signal(
                barrier,
                inc=1,
                device_id=(flip(self.pb, pb_bits), flip(self.mem, mem_bits)),
                device_id_type=MESH,
            )
        pl.semaphore_wait(barrier, len(peers))


def column_peers(n_mem):
    return [(a, b) for a in range(2) for b in range(n_mem) if (a, b) != (0, 0)]


def plane_peers(plane):
    return [(2 * t, 0) for t in range(1, plane)]


class Sems:
    def __init__(self, ref):
        self.ref = ref
        self.used = 0

    def take(self, count):
        first = self.used
        self.used += count
        return [self.ref.at[first + i] for i in range(count)]


def remote(src, dst, send_sem, recv_sem, device):
    return pltpu.make_async_remote_copy(
        src_ref=src,
        dst_ref=dst,
        send_sem=send_sem,
        recv_sem=recv_sem,
        device_id=device,
        device_id_type=MESH,
    )


class Spread:
    def __init__(self, place, sems, src, dst, kinds=(0, 1)):
        self.place, self.src, self.dst, self.kinds = place, src, dst, kinds
        self.send = sems.take(2)
        self.recv = sems.take(2)

    def copy(self, k):
        return remote(self.src(k), self.dst(k), self.send[k], self.recv[k], self.place.worker(k))

    def start(self):
        for k in self.kinds:
            if k == 0:
                home = self.place.at_home()

                @pl.when(home)
                def _():
                    pltpu.make_async_copy(self.src(0), self.dst(0), self.recv[0]).start()

                @pl.when(jnp.logical_not(home))
                def _():
                    self.copy(0).start()
            else:
                self.copy(k).start()

    def wait_recv(self, k):
        if k == 0:
            home = self.place.at_home()

            @pl.when(home)
            def _():
                pltpu.make_async_copy(self.src(0), self.dst(0), self.recv[0]).wait()

            @pl.when(jnp.logical_not(home))
            def _():
                self.copy(0).wait_recv()
        else:
            self.copy(k).wait_recv()

    def wait_send(self):
        for k in self.kinds:
            if k == 0:

                @pl.when(jnp.logical_not(self.place.at_home()))
                def _():
                    self.copy(0).wait_send()
            else:
                self.copy(k).wait_send()


class Own:
    def __init__(self, place, sems, shard, full, columns, n_mem):
        self.copies = []
        mem, core = place.mem, place.core
        if columns:
            unit = full.shape[-1] // n_mem
            for b, sem in zip(range(n_mem), sems.take(n_mem)):
                start = pl.multiple_of(2 * unit * b + unit * core, unit)
                src = shard.at[:, :, :, pl.ds(start, unit)]
                dst = full.at[:, mem, :, :, pl.ds(unit * b, unit)]
                self.copies.append(pltpu.make_async_copy(src, dst, sem))
        else:
            (sem,) = sems.take(1)
            self.copies.append(pltpu.make_async_copy(shard.at[core], full.at[0, mem], sem))

    def start(self):
        for copy in self.copies:
            copy.start()

    def wait(self):
        for copy in self.copies:
            copy.wait()


class Line:
    def __init__(self, place, sems, src, dst, n_mem):
        send, recv = sems.take(n_mem - 1), sems.take(n_mem - 1)
        self.copies = [
            remote(src(s), dst(s), send[s - 1], recv[s - 1], place.line(s)) for s in range(1, n_mem)
        ]

    def start(self):
        for copy in self.copies:
            copy.start()

    def wait_recv(self, s):
        self.copies[s - 1].wait_recv()

    def wait_send(self):
        for copy in self.copies:
            copy.wait_send()


class Share:
    def __init__(self, place, sems, src, block):
        send, recv = sems.take(4), sems.take(4)
        rows = src.shape[-2]
        half = rows // 2

        def part(ref, i):
            return ref.at[:, pl.ds(i * half, half)]

        self.first = [
            remote(src, block(0), send[t - 1], recv[t - 1], place.near(t)) for t in (1, 2)
        ]
        self.second = [
            remote(part(block(t), t - 1), part(block(t), t - 1), send[t + 1], recv[t + 1], place.near(3 - t))
            for t in (1, 2)
        ]

    def start(self):
        for copy in self.first:
            copy.start()

    def forward(self):
        for direct, onward in zip(self.first, self.second):
            direct.wait_recv()
            onward.start()

    def wait(self):
        for copy in self.first:
            copy.wait_send()
        for copy in self.second:
            copy.wait()


class Chain:
    def __init__(self, place, sems, block, n_mem):
        self.place, self.block, self.n = place, block, n_mem
        self.sems = {way: (sems.take(n_mem - 1), sems.take(n_mem - 1)) for way in (1, -1)}

    def copy(self, way, hops):
        mem = self.place.mem
        source = lax.rem(mem + jnp.int32(self.n - way * hops), jnp.int32(self.n))
        target = lax.rem(mem + jnp.int32(self.n + way), jnp.int32(self.n))
        send, recv = self.sems[way]
        piece = self.block(source)
        return remote(piece, piece, send[hops], recv[hops], (self.place.pb, target))

    def comes(self, way, hops):
        mem = self.place.mem
        return mem >= hops if way == 1 else mem + hops < self.n

    def goes(self, way, hops):
        mem = self.place.mem
        ahead = mem + 1 < self.n if way == 1 else mem >= 1
        return jnp.logical_and(ahead, self.comes(way, hops))

    def start(self):
        for way in (1, -1):

            @pl.when(self.goes(way, 0))
            def _():
                self.copy(way, 0).start()

    def relay(self, hops, arrived):
        for way in (1, -1):

            @pl.when(self.comes(way, hops))
            def _():
                self.copy(way, hops - 1).wait_recv()
                if hops < self.n - 1:

                    @pl.when(self.goes(way, hops))
                    def _():
                        self.copy(way, hops).start()

                arrived(hops if way == 1 else self.n - hops)

    def wait_send(self):
        for hops in range(self.n - 1):
            for way in (1, -1):

                @pl.when(self.goes(way, hops))
                def _():
                    self.copy(way, hops).wait_send()


class Gather:
    def __init__(self, place, sems, shard, full, columns, n_mem, in_plane=None):
        mem, quarter = place.mem, place.quarter
        self.n_mem = n_mem
        self.in_plane = tuple(range(1, n_mem)) if in_plane is None else in_plane
        self.own = Own(place, sems, shard, full, columns, n_mem)
        self.chain = Chain(place, sems, lambda i: full.at[:, i, quarter], n_mem)
        self.shares = {}
        for d in range(1, n_mem):
            if d not in self.in_plane and n_mem - d not in self.in_plane:
                continue
            source = lax.rem(mem + jnp.int32(n_mem - d), jnp.int32(n_mem))

            def block(t, source=source):
                return full.at[:, source, flip(quarter, t)]

            self.shares[d] = Share(place, sems, block(0), block)

    def begin(self):
        self.own.wait()
        self.chain.start()

    def share(self, hops):
        self.chain.relay(
            hops, lambda d: self.shares[d].start() if hops in self.in_plane else None
        )

    def forward(self, hops):
        for way, d in ((1, hops), (-1, self.n_mem - hops)):

            @pl.when(self.chain.comes(way, hops))
            def _():
                self.shares[d].forward()

    def finish(self):
        self.chain.wait_send()
        for hops in self.in_plane:
            for way, d in ((1, hops), (-1, self.n_mem - hops)):

                @pl.when(self.chain.comes(way, hops))
                def _():
                    self.shares[d].wait()


GATHER_SEMS = 44


def half_views(shard, columns, n_mem, plane):
    if columns:
        lead, depth, hidden = shard.shape
        part = depth // plane
        return shard.reshape(lead, plane, part, hidden), (lead, n_mem, plane, part, hidden // 2)
    depth, width = shard.shape
    part = depth // 2 // plane
    return shard.reshape(2, plane, part, width), (1, n_mem, plane, part, width)


class Walk:
    def __init__(self, refs):
        self.refs = list(refs)

    def take(self, count):
        out, self.refs = self.refs[:count], self.refs[count:]
        return out

    def one(self):
        return self.take(1)[0]


def softmax_units(units, finish, serve=None):
    def scores_of(unit, j):
        return unit[0][j]()

    ready = [scores_of(units[0], j) for j in range(len(units[0][0]))]
    for n, (_, values, tag) in enumerate(units):
        if serve is not None:
            serve(n)
        coming = list(range(len(units[n + 1][0]))) if n + 1 < len(units) else []
        following = []
        top = functools.reduce(
            jnp.maximum, [jnp.max(tile, axis=0, keepdims=True) for tile in ready]
        )
        total = jnp.zeros_like(top)
        acc = None
        share = -(-len(coming) // len(ready))
        for j, tile in enumerate(ready):
            for i in coming[j * share : (j + 1) * share]:
                following.append(scores_of(units[n + 1], i))
            probs = jnp.exp(tile - top)
            total += jnp.sum(probs, axis=0, keepdims=True)
            part = mm(values[j](), probs.astype(BF16))
            acc = part if acc is None else acc + part
        finish(tag, acc / total, top + jnp.log(total))
        ready = following


def self_attend(place, pair, q_vm, k_vm, v_vm, o_vm, lse_vm, v_t, o_t):
    base = 2 * place.core + place.parity
    count = q_vm.shape[0] // BLK
    lanes = pl.ds(pl.multiple_of(pair * 2 * HD, 2 * HD), 2 * HD)

    def rows(i):
        return pl.ds(pl.multiple_of(flip(base, i) * BLK, BLK), BLK)

    for j in range(count):
        v_t[:, j * BLK : (j + 1) * BLK] = v_vm[rows(j), lanes].T
    key_pos = lax.broadcasted_iota(jnp.int32, (BLK, BLK), 0)
    query_pos = lax.broadcasted_iota(jnp.int32, (BLK, BLK), 1)
    units = []
    for i in range(count):
        q_t = q_vm[rows(i), lanes].T
        for head in range(2):
            q_head = head_rows(q_t, head)

            def score(j, i=i, q_head=q_head):
                tile = mm(k_vm[rows(j), lanes], q_head)
                return jnp.where(key_pos <= query_pos, tile, -1000000000.0) if j == i else tile

            def value(j, head=head):
                return v_t[head * HD : (head + 1) * HD, j * BLK : (j + 1) * BLK]

            units.append(
                (
                    [functools.partial(score, j) for j in range(i + 1)],
                    [functools.partial(value, j) for j in range(i + 1)],
                    (i, head),
                )
            )

    def finish(tag, mixed, lse):
        i, head = tag
        span = slice(i * BLK, (i + 1) * BLK)
        o_t[head * HD : (head + 1) * HD, span] = mixed
        lse_vm[pair, head : head + 1, span] = lse

    softmax_units(units, finish)
    for i in range(count):
        o_vm[rows(i), lanes] = o_t[:, i * BLK : (i + 1) * BLK].T.astype(BF16)


def tiles(rows, step):
    def run(i, carry):
        step(pl.ds(pl.multiple_of(i * BLK, BLK), BLK))
        return carry

    lax.fori_loop(0, rows // BLK, run, 0)


def front_kernel(n_mem, plane, kinds, places, x_ref, enc_ref, map_ref, small_ref, *refs):
    refs = Walk(refs)
    count = len(kinds)
    shards = refs.take(count)
    x_out, enc_out, index_out, small_out = refs.take(4)
    halves = refs.take(count)
    kept = refs.take(11)
    x_vm, w_vm, so_vm, cq_w, small_vm = refs.take(5)
    q_vm, k_vm, v_vm, sa_vm, lse_vm, h1_vm, unit_vm, scale_vm, cq_vm = refs.take(9)
    k_all, v_all, v_t, o_t, part_vm, twin_vm, kv_w, enc_vm, map_in = refs.take(9)
    sems = Sems(refs.one())
    place = Place(plane)
    n_bias, n_gain = places
    rows = x_ref.shape[1]
    gathers = [
        Gather(place, sems, shard, half, columns, n_mem)
        for shard, half, columns in zip(shards, halves, kinds)
    ]
    spread = Spread(
        place,
        sems,
        lambda k: x_ref.at[flip(place.parity, k)],
        lambda k: x_out.at[pl.ds(rows * k, rows)],
    )
    twin_send, twin_recv = sems.take(2), sems.take(2)
    twin = [
        remote(
            x_out.at[pl.ds(rows * k, rows)],
            x_out.at[pl.ds(rows * (k + 2), rows)],
            twin_send[k],
            twin_recv[k],
            place.twin(),
        )
        for k in range(2)
    ]
    map_sems = sems.take(2)
    map_copy = remote(map_ref, map_in, map_sems[0], map_sems[1], place.twin())
    (small_sem,) = sems.take(1)
    small_own = pltpu.make_async_copy(small_ref, small_out.at[place.mem], small_sem)
    small_line = Line(
        place, sems, lambda s: small_ref, lambda s: small_out.at[place.mem], n_mem
    )
    units = enc_vm.shape[1]
    encs, enc_twins, enc_pairs, enc_onwards, enc_ends = [], [], [], [], []
    for u in range(units):
        encs.append(
            Spread(
                place, sems, lambda k, u=u: enc_ref.at[u], lambda k, u=u: enc_vm.at[0, u], kinds=(0,)
            )
        )
        pair_sems, twin_sems, end_sems = sems.take(2), sems.take(2), sems.take(2)
        enc_pairs.append(remote(enc_ref.at[u], enc_vm.at[1, u], *pair_sems, place.pair()))
        enc_onwards.append(remote(enc_vm.at[0, u], enc_vm.at[1, u], *pair_sems, place.pair()))
        enc_twins.append(remote(enc_vm.at[0, u], enc_vm.at[2, u], *twin_sems, place.twin()))
        enc_ends.append(remote(enc_vm.at[1, u], enc_vm.at[3, u], *end_sems, place.twin()))
    enc_keeps = [
        pltpu.make_async_copy(enc_vm.at[i], enc_out.at[i], sem) for i, sem in enumerate(sems.take(4))
    ]
    home = place.at_home()
    away = jnp.logical_not(home)
    loads = [
        pltpu.make_async_copy(src, dst, sem)
        for src, dst, sem in zip(
            (x_out, halves[0], halves[1], halves[2].at[0], small_out, halves[2].at[pl.ds(1, 2)]),
            (x_vm, w_vm, so_vm, cq_w, small_vm, kv_w),
            sems.take(6),
        )
    ]
    keeps = [
        pltpu.make_async_copy(src, dst, sem)
        for src, dst, sem in zip(
            (q_vm, k_vm, v_vm, sa_vm, lse_vm, h1_vm, unit_vm, scale_vm, cq_vm, k_all, v_all),
            kept,
            sems.take(11),
        )
    ]
    swap_sems = sems.take(4)
    own = 2 * rows
    swap_part = remote(part_vm, twin_vm, swap_sems[0], swap_sems[1], place.twin())
    swap_h1 = remote(
        h1_vm.at[pl.ds(0, own)], h1_vm.at[pl.ds(own, own)], swap_sems[2], swap_sems[3], place.twin()
    )

    for gather in gathers:
        gather.own.start()
    small_own.start()
    place.meet(column_peers(n_mem) + plane_peers(plane))
    for gather in gathers:
        gather.begin()
    small_line.start()
    map_copy.start()
    spread.start()
    for gather in gathers:
        gather.share(1)
    for gather in gathers:
        gather.share(2)
    gathers[0].forward(1)
    for k in range(2):
        spread.wait_recv(k)
        twin[k].start()
    for gather in gathers:
        gather.share(3)
    for u in range(units):
        encs[u].start()

        @pl.when(home)
        def _():
            enc_pairs[u].start()

    def first_arrival(u):
        encs[u].wait_recv(0)

        @pl.when(away)
        def _():
            enc_onwards[u].start()

        enc_twins[u].start()

    def second_arrival(u):
        @pl.when(home)
        def _():
            enc_pairs[u].wait()

        @pl.when(away)
        def _():
            enc_onwards[u].wait()

        enc_ends[u].start()

    for hops in (2, 3):
        gathers[0].forward(hops)
    for hops in (1, 2, 3):
        for gather in gathers[1:]:
            gather.forward(hops)
    for copy in twin:
        copy.wait_recv()
    small_own.wait()
    for s in range(1, n_mem):
        small_line.wait_recv(s)
    gathers[0].finish()
    for copy in (loads[0], loads[1], loads[4]):
        copy.start()
    for copy in (loads[0], loads[1], loads[4]):
        copy.wait()

    def half_row(row):
        lanes = pl.ds(pl.multiple_of(place.core * 2 * HD, 2 * HD), 2 * HD)
        return jnp.concatenate(
            [small_vm[b, :, lanes].astype(F32)[row : row + 1] for b in range(n_mem)], axis=1
        )

    def full_row(row):
        return jnp.concatenate(
            [small_vm[b].astype(F32)[row : row + 1] for b in range(n_mem)], axis=1
        )

    bias_q, bias_v = half_row(0), half_row(1)
    depth = x_vm.shape[1]

    def weight(ref):
        return ref[...].reshape(-1, ref.shape[-1])

    def project(span):
        x_tile = x_vm[span, :]
        q_vm[span, :] = ((mm(x_tile, weight(w_vm.at[0])) + bias_q) * 0.125).astype(BF16)
        k_vm[span, :] = mm(x_tile, weight(w_vm.at[1])).astype(BF16)
        v_vm[span, :] = (mm(x_tile, weight(w_vm.at[2])) + bias_v).astype(BF16)

    tiles(x_vm.shape[0], project)
    for copy in keeps[:3]:
        copy.start()
    pairs = q_vm.shape[1] // (2 * HD)
    for pair in range(pairs):
        self_attend(place, pair, q_vm, k_vm, v_vm, sa_vm, lse_vm, v_t, o_t)
        if pair in (0, pairs // 2):
            first_arrival(min(pair, 1))
    for copy in keeps[3:5]:
        copy.start()
    for gather in gathers[1:]:
        gather.finish()
    for copy in (loads[2], loads[3], loads[5]):
        copy.start()
    for copy in (loads[2], loads[3], loads[5]):
        copy.wait()

    def other_part(span):
        part_vm[span, :] = mm(
            sa_vm[pl.ds(pl.multiple_of(span.start + own, BLK), BLK), :], weight(so_vm)
        ).astype(BF16)

    tiles(own, other_part)
    swap_part.start()

    def own_part(span):
        unit_vm[span, :] = mm(sa_vm[span, :], weight(so_vm)) + x_vm[span, :].astype(F32)

    tiles(own, own_part)
    for u in range(2, units):
        first_arrival(u)
    bias_out = full_row(2)
    gain, shift = full_row(n_bias), full_row(6)
    swap_part.wait()

    def normalise(span):
        values = unit_vm[span, :] + twin_vm[span, :].astype(F32) + bias_out
        centre = values - jnp.mean(values, axis=-1, keepdims=True)
        scale = lax.rsqrt(jnp.mean(centre * centre, axis=-1, keepdims=True) + 1e-05)
        unit = centre * scale
        unit_vm[span, :] = unit
        scale_vm[span, :] = jnp.broadcast_to(scale, (BLK, scale_vm.shape[1]))
        h1_vm[span, :] = (unit * gain + shift).astype(BF16)

    tiles(own, normalise)
    swap_h1.start()
    for copy in keeps[6:8]:
        copy.start()
    bias_cq = half_row(3)

    def queries(span):
        cq_vm[span, :] = ((mm(h1_vm[span, :], weight(cq_w)) + bias_cq) * 0.125).astype(BF16)

    tiles(own, queries)
    swap_h1.wait()
    keeps[5].start()

    def other_queries(span):
        queries(pl.ds(pl.multiple_of(span.start + own, BLK), BLK))

    tiles(own, other_queries)
    keeps[8].start()

    map_copy.wait()
    near_map, far_map = map_ref[...], map_in[...]
    both_maps = jnp.where(home, near_map, far_map)
    mine = jnp.where(place.parity == 0, both_maps[:1], both_maps[1:])
    group = lax.div(mine, jnp.full_like(mine, units))
    index_out[...] = (group ^ (2 * place.core + place.parity)) * units + lax.rem(
        mine, jnp.full_like(mine, units)
    )

    bias_cv = half_row(4)

    def memory(block, u):
        rows_here = enc_vm[block, u]
        k_all[block * units + u] = mm(rows_here, weight(kv_w.at[0])).astype(BF16)
        v_all[block * units + u] = (mm(rows_here, weight(kv_w.at[1])) + bias_cv).astype(BF16)

    for u in range(units):
        second_arrival(u)
        memory(0, u)
    enc_keeps[0].start()
    enc_keeps[1].start()
    for block, copies in ((2, enc_twins), (1, None), (3, enc_ends)):
        for u in range(units):
            if copies is not None:
                copies[u].wait_recv()
            memory(block, u)
    enc_keeps[2].start()
    enc_keeps[3].start()
    for copy in keeps[9:]:
        copy.start()
    spread.wait_send()
    for copy in twin:
        copy.wait_send()
    small_line.wait_send()
    for item in encs:
        item.wait_send()
    for copy in enc_twins + enc_ends:
        copy.wait_send()
    for copy in keeps + enc_keeps:
        copy.wait()


def front(n_mem, plane, places, hidden_in, enc, passage_map, small, params):
    kinds = tuple(columns for _, columns in params)
    views = [half_views(shard, columns, n_mem, plane) for shard, columns in params]
    seg, width = hidden_in.shape[1:]
    rows, own = 4 * seg, 2 * seg
    part = width // 2
    pairs = part // (2 * HD)
    passages = 4 * enc.shape[0]
    shapes = (
        [((rows, width), BF16), ((4,) + enc.shape, BF16), ((1, passage_map.shape[1]), jnp.int32)]
        + [((n_mem,) + small.shape, BF16)]
        + [(full, BF16) for _, full in views]
    )
    kept = [
        ((rows, part), BF16),
        ((rows, part), BF16),
        ((rows, part), BF16),
        ((rows, part), BF16),
        ((pairs, 2, rows), F32),
        ((rows, width), BF16),
        ((own, width), F32),
        ((own, 2 * HD), F32),
        ((rows, part), BF16),
        ((passages, PLEN, part), BF16),
        ((passages, PLEN, part), BF16),
    ]
    scratch = [
        ((rows, width), BF16),
        (views[0][1], BF16),
        (views[1][1][1:], BF16),
        (views[2][1][1:], BF16),
        ((n_mem,) + small.shape, BF16),
    ] + kept + [
        ((2 * HD, rows), BF16),
        ((2 * HD, rows), F32),
        ((own, width), BF16),
        ((own, width), BF16),
        ((2,) + views[2][1][1:], BF16),
        ((4,) + enc.shape, BF16),
        (passage_map.shape, jnp.int32),
    ]
    scratch[2] = (views[1][1], BF16)
    outs = pl.pallas_call(
        functools.partial(front_kernel, n_mem, plane, kinds, places),
        in_specs=[VMEM] * (4 + len(params)),
        out_specs=[ANY, ANY, VMEM] + [ANY] * (len(shapes) + len(kept) - 3),
        out_shape=[jax.ShapeDtypeStruct(*item) for item in shapes + kept],
        scratch_shapes=[pltpu.VMEM(*item) for item in scratch]
        + [pltpu.SemaphoreType.DMA((90 + GATHER_SEMS * len(params),))],
        compiler_params=pltpu.CompilerParams(
            collective_id=0, has_side_effects=True, vmem_limit_bytes=60 * 2**20
        ),
        cost_estimate=pl.CostEstimate(
            flops=rows * width * part * 10, bytes_accessed=40 * 2**20, transcendentals=rows * rows * 8
        ),
        name="front",
    )(hidden_in, enc, passage_map, small, *[view for view, _ in views])
    count = 4 + len(params)
    return outs[:4], outs[4:count], outs[count:]


class PlaneSum:
    def __init__(self, place, sems, grad, own, bufs, rows, lanes=None):
        self.own = own
        self.from_near, self.via, self.add = bufs
        quarter = place.quarter
        first, count = rows
        half = count // 2
        self.lead, self.n_mem = own.shape[:2]
        lanes = pl.ds(*(lanes or (0, grad.shape[-1])))

        def piece(t, lo, size):
            return grad.at[:, :, flip(quarter, t), pl.ds(first + lo, size), lanes]

        loads = sems.take(3)
        self.loads = [pltpu.make_async_copy(piece(0, 0, count), own, loads[0])]
        send, recv = sems.take(6), sems.take(6)
        self.onward, self.direct, self.summed = [], [], []
        for t in (1, 2):
            lo = (t - 1) * half
            self.onward.append(
                remote(piece(3, lo, half), self.via.at[t - 1], send[t - 1], recv[t - 1], place.near(t))
            )
            self.direct.append(
                remote(
                    piece(t, lo, half),
                    self.from_near.at[t - 1, :, :, pl.ds(lo, half)],
                    send[t + 1],
                    recv[t + 1],
                    place.near(t),
                )
            )
            other = half - lo
            self.loads.append(
                pltpu.make_async_copy(piece(t, other, half), self.add.at[t - 1], loads[t])
            )
            self.summed.append(
                remote(
                    self.add.at[t - 1],
                    self.from_near.at[t - 1, :, :, pl.ds(other, half)],
                    send[t + 3],
                    recv[t + 3],
                    place.near(t),
                )
            )

    def start(self):
        for copy in self.onward + self.loads + self.direct:
            copy.start()

    def each(self, step):
        def run(i, carry):
            step(lax.div(i, jnp.int32(self.n_mem)), lax.rem(i, jnp.int32(self.n_mem)))
            return carry

        lax.fori_loop(0, self.lead * self.n_mem, run, 0)

    def middle(self):
        for copy in self.loads:
            copy.wait()
        for t in (1, 2):
            self.onward[2 - t].wait_recv()

            def add(l, m, t=t):
                total = self.add[t - 1, l, m].astype(F32) + self.via[2 - t, l, m].astype(F32)
                self.add[t - 1, l, m] = total.astype(BF16)

            self.each(add)
            self.summed[t - 1].start()

    def end(self):
        for copy in self.direct + self.summed:
            copy.wait_recv()

        def add(l, m):
            total = self.own[l, m].astype(F32)
            for t in range(2):
                total += self.from_near[t, l, m].astype(F32)
            self.own[l, m] = total.astype(BF16)

        self.each(add)

    def wait_send(self):
        for copy in self.onward + self.direct + self.summed:
            copy.wait_send()


class Settle:
    def __init__(self, place, sems, own, out, bufs, columns, n_mem, rows, lane=0):
        self.place, self.n_mem, self.columns, self.rows = place, n_mem, columns, rows
        self.lane = lane
        self.own, self.out = own, out
        self.line_in, self.far_in, self.slots = bufs
        quarter, mem, core = place.quarter, place.mem, place.core
        slots = self.slots

        def slot(t):
            return slots.at[flip(quarter, t), core]

        self.line = Line(
            place, sems, lambda s: own.at[:, flip(mem, s)], lambda s: self.line_in.at[s - 1], n_mem
        )
        others = place.planes - 1
        far_send, far_recv = sems.take(others), sems.take(others)
        self.far = [
            remote(slot(0), self.far_in.at[r - 1], far_send[r - 1], far_recv[r - 1], place.far(r))
            for r in range(1, place.planes)
        ]
        self.share = Share(place, sems, slot(0), slot)
        twin_send, twin_recv = sems.take(place.plane), sems.take(place.plane)
        self.twin = [
            remote(slot(t), slot(t), twin_send[t], twin_recv[t], place.twin())
            for t in range(place.plane)
        ]

    def start(self):
        self.line.start()

    def middle(self):
        for s in range(1, self.n_mem):
            self.line.wait_recv(s)
        quarter, core, mem = self.place.quarter, self.place.core, self.place.mem
        lead = self.own.shape[0]
        for l in range(lead):
            total = self.own[l, mem].astype(F32)
            for s in range(self.n_mem - 1):
                total += self.line_in[s, l].astype(F32)
            self.slots[quarter, core, l] = total.astype(BF16)
        if self.far:
            for copy in self.far:
                copy.start()
            for copy in self.far:
                copy.wait()
            for l in range(lead):
                total = self.slots[quarter, core, l].astype(F32)
                for r in range(len(self.far)):
                    total += self.far_in[r, l].astype(F32)
                self.slots[quarter, core, l] = total.astype(BF16)
        self.share.start()
        self.twin[0].start()

    def forward(self):
        self.share.forward()
        self.twin[1].start()
        self.twin[2].start()

    def end(self):
        self.share.wait()
        self.twin[3].start()
        for copy in self.twin:
            copy.wait()
        self.line.wait_send()
        lead = self.own.shape[0]
        wide = self.slots.shape[-1]
        first, count = self.rows
        for q in range(self.place.plane):
            for c in range(2):
                for l in range(lead):
                    if self.columns:
                        unit = self.out.shape[-1] // (2 * self.n_mem)
                        for b in range(wide // unit):
                            start = unit * (2 * (self.lane // unit + b) + c)
                            self.out[l, q, first : first + count, start : start + unit] = self.slots[
                                q, c, l, :, b * unit : (b + 1) * unit
                            ]
                    else:
                        self.out[c, q, first : first + count] = self.slots[q, c, l]


PLANE_SUM_SEMS = 15


def settle_sems(n_mem, plane, planes):
    return 2 * (n_mem - 1) + 2 * (planes - 1) + 8 + 2 * plane


def plane_sum_scratch(grad_shape, n_mem, count, cols=None):
    lead, cols = grad_shape[0], cols or grad_shape[-1]
    return [
        pltpu.VMEM((2, lead, n_mem, count, cols), BF16),
        pltpu.VMEM((2, lead, n_mem, count // 2, cols), BF16),
        pltpu.VMEM((2, lead, n_mem, count // 2, cols), BF16),
    ]


def settle_scratch(grad_shape, n_mem, plane, planes, count, cols=None):
    lead, cols = grad_shape[0], cols or grad_shape[-1]
    return [
        pltpu.VMEM((n_mem - 1, lead, count, cols), BF16),
        pltpu.VMEM((max(planes - 1, 1), lead, count, cols), BF16),
        pltpu.VMEM((plane, 2, lead, count, cols), BF16),
    ]


def sum_shape(grad_shape):
    lead, n_mem, _, rows, cols = grad_shape
    return jax.ShapeDtypeStruct((lead, n_mem, rows, cols), BF16)


def reduce_out(grad_shape, columns, plane):
    lead, _, _, rows, cols = grad_shape
    shape = (lead, plane, rows, 2 * cols) if columns else (2, plane, rows, cols)
    return jax.ShapeDtypeStruct(shape, BF16)


def reduce_peers(n_mem, plane, planes):
    return (
        [(1, 0)]
        + [(0, s) for s in range(1, n_mem)]
        + plane_peers(plane)
        + [(2 * plane * r, 0) for r in range(1, planes)]
    )


def whole(shape):
    return pl.BlockSpec(shape, lambda *grid: (0,) * len(shape))


class Fetch:
    def __init__(self, sems, src, dst):
        self.copy = pltpu.make_async_copy(src, dst, sems.take(1)[0])
        self.dst = dst
        self.here = False

    def start(self):
        self.copy.start()

    def get(self):
        if not self.here:
            self.copy.wait()
            self.here = True
        return self.dst


def unit_norm(values):
    centre = values - jnp.mean(values, axis=-1, keepdims=True)
    scale = lax.rsqrt(jnp.mean(centre * centre, axis=-1, keepdims=True) + 1e-05)
    return centre * scale, scale


def unit_norm_back(grad, unit, scale, gain):
    inner = grad * gain
    return (
        inner
        - jnp.mean(inner, axis=-1, keepdims=True)
        - unit * jnp.mean(inner * unit, axis=-1, keepdims=True)
    ) * scale


def feed_kernel(n_mem, plane, cot_ref, rows_ref, bias_ref, *refs):
    refs = Walk(refs)
    fetched = refs.take(4)
    out_part = refs.one()
    final_out, dca_ref, dz2_ref, sums_ref, bias_sum, own_out, dw_in, dw_co = refs.take(8)
    kept = refs.take(4)
    out_w = refs.one()
    cot_vm, h2_vm, unit_vm, scale_vm, act_vm, slope_vm, p_vm, part_vm, twin_vm = refs.take(9)
    final_vm, df_vm, dco_vm, dw_out = refs.take(4)
    bufs = refs.take(3)
    sems = Sems(refs.one())
    place = Place(plane)
    ca, unit1, w_co, w_in = [Fetch(sems, src, dst) for src, dst in zip(fetched, kept)]
    mem, quarter = place.mem, place.quarter
    own_piece = Fetch(sems, out_part.at[0, mem], out_w.at[0, mem])
    pieces = []
    for d in range(1, n_mem):
        source = lax.rem(mem + jnp.int32(n_mem - d), jnp.int32(n_mem))

        def place_of(t, source=source):
            return out_w.at[:, source, flip(quarter, t)]

        (sem,) = sems.take(1)
        pieces.append(
            (
                mem < d if d == 1 else mem >= (d if d == n_mem - 1 else 0),
                pltpu.make_async_copy(out_part.at[0, source], out_w.at[0, source], sem),
                pltpu.make_async_copy(out_part.at[:, source, quarter], place_of(0), sem),
                Share(place, sems, place_of(0), place_of),
            )
        )

    def each_piece(whole_step, part_step):
        for part, whole_copy, part_copy, share in pieces:
            if whole_step is not None:

                @pl.when(jnp.logical_not(part))
                def _():
                    whole_step(whole_copy)

            @pl.when(part)
            def _():
                part_step(part_copy, share)

    rows = h2_vm.shape[0]
    own = rows // 2
    seg = own // 2
    hidden = act_vm.shape[1]
    block = hidden // n_mem
    out_sum = PlaneSum(place, sems, dw_out, own_out, bufs, (0, own_out.shape[2]))
    spread_cot = Spread(
        place,
        sems,
        lambda k: cot_ref.at[flip(place.parity, k)],
        lambda k: cot_vm.at[pl.ds(seg * k, seg)],
    )
    spread_final = Spread(
        place,
        sems,
        lambda k: final_vm.at[pl.ds(seg * k, seg)],
        lambda k: final_out.at[place.parity],
    )

    def swap(src, dst):
        send, recv = sems.take(2)
        return remote(src, dst, send, recv, place.twin())

    def half_lanes(ref, i):
        wide = ref.shape[1] // 2
        return ref.at[:, pl.ds(i * wide, wide)]

    swap_co = swap(part_vm, twin_vm)
    swap_h2 = swap(h2_vm.at[pl.ds(0, own)], h2_vm.at[pl.ds(own, own)])
    swap_ffn = [swap(half_lanes(part_vm, i), half_lanes(twin_vm, i)) for i in range(2)]
    swap_df = swap(df_vm.at[pl.ds(0, own)], df_vm.at[pl.ds(own, own)])
    swap_dh2 = [swap(half_lanes(part_vm, i), half_lanes(twin_vm, i)) for i in range(2)]
    swap_dco = swap(dco_vm.at[pl.ds(0, own)], dco_vm.at[pl.ds(own, own)])

    for item in (ca, w_co, own_piece):
        item.start()
    each_piece(lambda copy: copy.start(), lambda copy, share: copy.start())
    for item in (unit1, w_in):
        item.start()
    place.meet(column_peers(n_mem) + plane_peers(plane))
    spread_cot.start()

    def share_start(copy, share):
        copy.wait()
        share.start()

    each_piece(None, share_start)
    row = {name: rows_ref[i : i + 1, :] for i, name in enumerate(("g0", "b6", "b5", "g1", "b7", "b9", "g2", "b8"))}
    sums_ref[...] = jnp.zeros_like(sums_ref)
    bias_sum[...] = jnp.zeros_like(bias_sum)

    def after(span):
        return pl.ds(pl.multiple_of(span.start + own, BLK), BLK)

    ca, w_co = ca.get(), w_co.get()

    def co_other(span):
        part_vm[span, :] = mm(ca[after(span), :], w_co[...]).astype(BF16)

    tiles(own, co_other)
    swap_co.start()
    unit1 = unit1.get()

    def co_own(span):
        p_vm[span, :] = unit1[span, :] * row["g0"] + row["b6"] + mm(ca[span, :], w_co[...])

    tiles(own, co_own)
    swap_co.wait()

    def second_norm(span):
        values = p_vm[span, :] + twin_vm[span, :].astype(F32) + row["b5"]
        unit, scale = unit_norm(values)
        unit_vm[span, :] = unit
        scale_vm[span, :] = jnp.broadcast_to(scale, (BLK, scale_vm.shape[1]))
        h2_vm[span, :] = (unit * row["g1"] + row["b7"]).astype(BF16)

    tiles(own, second_norm)
    swap_h2.start()
    w_in = w_in.get()

    def forward(span):
        def part(i, carry):
            lanes = pl.ds(pl.multiple_of(i * block, block), block)
            pre = mm(h2_vm[span, :], w_in[:, lanes]) + bias_ref[:, lanes]
            cdf = 0.5 * (1.0 + lax.erf(pre * 0.7071067811865476))
            act_vm[span, lanes] = (pre * cdf).astype(BF16)
            density = jnp.exp(-0.5 * pre * pre) * 0.3989422804014327
            slope_vm[span, lanes] = (cdf + pre * density).astype(BF16)
            return carry

        lax.fori_loop(0, n_mem, part, 0)

    ours, others = pl.ds(0, own), pl.ds(own, own)
    width = h2_vm.shape[1]
    column = width // 2
    each_piece(None, lambda copy, share: share.forward())
    forward(ours)
    swap_h2.wait()
    forward(others)
    own_piece.get()
    each_piece(lambda copy: copy.wait(), lambda copy, share: share.wait())
    for i in range(2):
        lanes = slice(i * column, (i + 1) * column)
        weights = out_w[0, :, :, :, lanes].reshape(hidden, column)
        part_vm[:, lanes] = mm(act_vm[others, :], weights).astype(BF16)
        swap_ffn[i].start()
    p_vm[...] = mm(act_vm[ours, :], out_w[0].reshape(hidden, width))
    for k in range(2):
        spread_cot.wait_recv(k)
    for copy in swap_ffn:
        copy.wait()

    def third_norm(span):
        values = (
            unit_vm[span, :] * row["g1"]
            + row["b7"]
            + p_vm[span, :]
            + twin_vm[span, :].astype(F32)
            + row["b9"]
        )
        unit, scale = unit_norm(values)
        final_vm[span, :] = (unit * row["g2"] + row["b8"]).astype(BF16)
        grad = cot_vm[span, :].astype(F32)
        out = unit_norm_back(grad, unit, scale, row["g2"])
        dz2_ref[span, :] = out
        low = out.astype(BF16)
        df_vm[span, :] = low
        sums_ref[0:1, :] += jnp.sum(grad * unit, axis=0, keepdims=True)
        sums_ref[1:2, :] += jnp.sum(grad, axis=0, keepdims=True)
        sums_ref[2:3, :] += jnp.sum(low.astype(F32), axis=0, keepdims=True)

    tiles(own, third_norm)
    swap_df.start()
    spread_final.start()
    swap_df.wait()

    def out_weights(m, carry):
        lanes = pl.ds(pl.multiple_of(m * block, block), block)
        dw_out[0, m] = mm(act_vm[:, lanes].T, df_vm[...]).astype(BF16).reshape(dw_out.shape[2:])
        return carry

    lax.fori_loop(0, n_mem, out_weights, 0)
    out_sum.start()

    def hidden_grad(i, carry):
        lanes = pl.ds(pl.multiple_of(i * block, block), block)
        weights = out_w[0, i].reshape(block, width)
        grad = mm(df_vm[...], weights, NT) * slope_vm[:, lanes].astype(F32)
        low = grad.astype(BF16)
        slope_vm[:, lanes] = low
        bias_sum[:, lanes] = jnp.sum(low.astype(F32), axis=0, keepdims=True)
        return carry

    lax.fori_loop(0, n_mem, hidden_grad, 0)
    narrow = width // 4
    for i in range(2):
        for j in (2 * i, 2 * i + 1):
            lanes = slice(j * narrow, (j + 1) * narrow)
            grad = mm(slope_vm[...], w_in[lanes, :], NT)
            part_vm[:, lanes] = grad[own:].astype(BF16)
            dz2_ref[:, lanes] += grad[:own]
        swap_dh2[i].start()
    out_sum.middle()
    for copy in swap_dh2:
        copy.wait()

    def second_back(span):
        grad = dz2_ref[span, :] + twin_vm[span, :].astype(F32)
        unit = unit_vm[span, :]
        out = unit_norm_back(grad, unit, scale_vm[span, :1], row["g1"])
        dz2_ref[span, :] = out
        low = out.astype(BF16)
        dco_vm[span, :] = low
        sums_ref[3:4, :] += jnp.sum(grad * unit, axis=0, keepdims=True)
        sums_ref[4:5, :] += jnp.sum(grad, axis=0, keepdims=True)
        sums_ref[5:6, :] += jnp.sum(low.astype(F32), axis=0, keepdims=True)

    tiles(own, second_back)
    swap_dco.start()
    depth = h2_vm.shape[1] // n_mem

    def in_weights(m, carry):
        lanes = pl.ds(pl.multiple_of(m * depth, depth), depth)
        dw_in[0, m] = mm(h2_vm[:, lanes].T, slope_vm[...]).astype(BF16).reshape(dw_in.shape[2:])
        return carry

    lax.fori_loop(0, n_mem, in_weights, 0)
    swap_dco.wait()

    dca_ref[...] = mm(dco_vm[...], w_co[...], NT).astype(BF16)
    heads = ca.shape[1] // n_mem

    def co_weights(m, carry):
        lanes = pl.ds(pl.multiple_of(m * heads, heads), heads)
        dw_co[0, m] = mm(ca[:, lanes].T, dco_vm[...]).astype(BF16).reshape(dw_co.shape[2:])
        return carry

    lax.fori_loop(0, n_mem, co_weights, 0)
    out_sum.end()
    out_sum.wait_send()
    spread_cot.wait_send()
    for k in range(2):
        spread_final.wait_recv(k)
    spread_final.wait_send()


def feed(n_mem, plane, cotangent, vectors, bias, ca, unit1, w_co, w_in, w_out):
    rows, part = ca.shape
    width, hidden = w_in.shape
    own = rows // 2

    def grad_shape(depth, cols):
        return (1, n_mem, plane, depth // (n_mem * plane), cols)

    out_shape, in_shape = grad_shape(hidden, width), grad_shape(width, hidden)
    shapes = [
        jax.ShapeDtypeStruct((2, own // 2, width), BF16),
        jax.ShapeDtypeStruct((rows, part), BF16),
        jax.ShapeDtypeStruct((own, width), F32),
        jax.ShapeDtypeStruct((8, width), F32),
        jax.ShapeDtypeStruct((1, hidden), F32),
        sum_shape(out_shape),
        jax.ShapeDtypeStruct(in_shape, BF16),
        jax.ShapeDtypeStruct(grad_shape(part, width), BF16),
    ]
    fetched = [ca, unit1, w_co, w_in, w_out]
    scratch = [pltpu.VMEM(item.shape, item.dtype) for item in fetched] + [
        pltpu.VMEM((own, width), BF16),
        pltpu.VMEM((rows, width), BF16),
        pltpu.VMEM((own, width), F32),
        pltpu.VMEM((own, 2 * HD), F32),
        pltpu.VMEM((rows, hidden), BF16),
        pltpu.VMEM((rows, hidden), BF16),
        pltpu.VMEM((own, width), F32),
        pltpu.VMEM((own, width), BF16),
        pltpu.VMEM((own, width), BF16),
        pltpu.VMEM((own, width), BF16),
        pltpu.VMEM((rows, width), BF16),
        pltpu.VMEM((rows, width), BF16),
        pltpu.VMEM(out_shape, BF16),
    ]
    scratch += plane_sum_scratch(out_shape, n_mem, out_shape[3])
    scratch += [pltpu.SemaphoreType.DMA((PLANE_SUM_SEMS + 60,))]
    return pl.pallas_call(
        functools.partial(feed_kernel, n_mem, plane),
        in_specs=[VMEM] * 3 + [ANY] * len(fetched),
        out_specs=[ANY] + [VMEM] * (len(shapes) - 1),
        out_shape=shapes,
        scratch_shapes=scratch,
        compiler_params=pltpu.CompilerParams(
            vmem_limit_bytes=60 * 2**20, collective_id=1, has_side_effects=True
        ),
        cost_estimate=pl.CostEstimate(
            flops=rows * width * hidden * 12, bytes_accessed=40 * 2**20, transcendentals=rows * hidden * 2
        ),
        name="feed",
    )(cotangent, vectors, bias, *fetched)


def middle_kernel(n_mem, plane, planes, settled, slot_ref, member_ref, index_ref, *refs):
    refs = Walk(refs)
    dq_ref, dk_ref, dv_ref, wc_ref, scale_ref, gain_ref = refs.take(6)
    fetched = refs.take(6)
    ready = refs.take(len(settled))
    dsa_ref, dz1_ref, sums_ref, enc_out, own_cross, own_so = refs.take(6)
    outs = refs.take(len(settled))
    kept = refs.take(6)
    wk_t, wv_t, named_ref = refs.take(3)
    theirs, mine, twin_in, pair_in, dw_cross, dw_so, part_vm, twin_vm, dso_vm = refs.take(9)
    cross_bufs, so_bufs = refs.take(3), refs.take(3)
    settle_bufs = [refs.take(3) for _ in settled]
    sems = Sems(refs.one())
    place = Place(plane, planes)
    fetches = [Fetch(sems, src, dst) for src, dst in zip(fetched, kept)]
    h1_ref, enc_ref, dz2_ref, unit_ref, so_ref, sa_ref = kept
    settles = [
        Settle(
            place, sems, ready[i], outs[i], settle_bufs[i], columns, n_mem, (0, ready[i].shape[2])
        )
        for i, columns in enumerate(settled)
    ]
    cross_sum = PlaneSum(place, sems, dw_cross, own_cross, cross_bufs, (0, dw_cross.shape[3]))
    so_sum = PlaneSum(place, sems, dw_so, own_so, so_bufs, (0, dw_so.shape[3]))
    passages = mine.shape[0]
    units = passages // 2
    twin_sems = sems.take(2 * passages)
    twins = [
        remote(theirs.at[u], twin_in.at[u], twin_sems[2 * u], twin_sems[2 * u + 1], place.twin())
        for u in range(passages)
    ]
    pair_sems = sems.take(2 * units)
    pairs = [
        remote(
            mine.at[units + u], pair_in.at[u], pair_sems[2 * u], pair_sems[2 * u + 1], place.pair()
        )
        for u in range(units)
    ]
    homes = [
        Spread(place, sems, lambda k, u=u: mine.at[u], lambda k, u=u: enc_out.at[u], kinds=(0,))
        for u in range(units)
    ]
    swap_sems = sems.take(4)
    own = dz2_ref.shape[0]
    swap_part = remote(part_vm, twin_vm, swap_sems[0], swap_sems[1], place.twin())
    swap_dso = remote(
        dso_vm.at[pl.ds(0, own)], dso_vm.at[pl.ds(own, own)], swap_sems[2], swap_sems[3], place.twin()
    )

    for item in fetches:
        item.start()
    wk_t[...] = wc_ref[1].T
    wv_t[...] = wc_ref[2].T
    place.meet(
        column_peers(n_mem) + plane_peers(plane) + [(2 * plane * r, 0) for r in range(1, planes)]
    )
    for item in settles:
        item.start()

    def passage_grad(u):
        slot = slot_ref[u]
        value = mm(dk_ref[slot], wk_t[...]) + mm(dv_ref[slot], wv_t[...])
        return (value * member_ref[u]).astype(BF16)

    def add_twin(u):
        twins[u].wait_recv()

        def add(i, carry):
            span = pl.ds(pl.multiple_of(i * 64, 64), 64)
            total = mine[u, span, :].astype(F32) + twin_in[u, span, :].astype(F32)
            mine[u, span, :] = total.astype(BF16)
            return carry

        lax.fori_loop(0, PLEN // 64, add, 0)

    def send_home(u):
        add_twin(u)
        pairs[u].wait_recv()

        def add(i, carry):
            span = pl.ds(pl.multiple_of(i * 64, 64), 64)
            total = mine[u, span, :].astype(F32) + pair_in[u, span, :].astype(F32)
            mine[u, span, :] = total.astype(BF16)
            return carry

        lax.fori_loop(0, PLEN // 64, add, 0)
        homes[u].start()

    for group in (range(units, passages), range(units)):
        for u in group:
            theirs[u] = passage_grad(passages + u)
            twins[u].start()
        for u in group:
            mine[u] = passage_grad(u)
        if group.start:
            for u in group:
                add_twin(u)
                pairs[u - units].start()

    for item in fetches:
        item.get()
    for j in range(index_ref.shape[0]):
        named_ref[j * PLEN : (j + 1) * PLEN, :] = enc_ref[index_ref[j]]

    part = dw_cross.shape[-1]
    depth = h1_ref.shape[1] // n_mem

    def stacked(ref):
        return ref[...].reshape(-1, ref.shape[-1])

    def cross_weights(m, carry):
        lanes = pl.ds(pl.multiple_of(m * depth, depth), depth)
        split = dw_cross.shape[2:]
        dw_cross[0, m] = (
            (mm(h1_ref[:, lanes].T, dq_ref[...]) * 0.125).astype(BF16).reshape(split)
        )
        named_t = named_ref[:, lanes].T
        dw_cross[1, m] = mm(named_t, stacked(dk_ref)).astype(BF16).reshape(split)
        dw_cross[2, m] = mm(named_t, stacked(dv_ref)).astype(BF16).reshape(split)
        return carry

    lax.fori_loop(0, n_mem // 2, cross_weights, 0)
    send_home(0)
    lax.fori_loop(n_mem // 2, n_mem, cross_weights, 0)
    cross_sum.start()

    part_vm[...] = (mm(dq_ref[own:, :], wc_ref[0], NT) * 0.125).astype(BF16)
    swap_part.start()
    dz1_ref[...] = dz2_ref[...] + mm(dq_ref[:own, :], wc_ref[0], NT) * 0.125
    sums_ref[...] = jnp.zeros_like(sums_ref)
    sums_ref[3:4, :part] = 0.125 * jnp.sum(dq_ref[...].astype(F32), axis=0, keepdims=True)
    sums_ref[4:5, :part] = jnp.sum(stacked(dv_ref).astype(F32), axis=0, keepdims=True)
    send_home(1)
    swap_part.wait()
    gain = gain_ref[...]

    def norm(span):
        grad = dz1_ref[span, :] + twin_vm[span, :].astype(F32)
        unit = unit_ref[span, :]
        inner = grad * gain
        out = (
            inner
            - jnp.mean(inner, axis=-1, keepdims=True)
            - unit * jnp.mean(inner * unit, axis=-1, keepdims=True)
        ) * scale_ref[span, :1]
        dz1_ref[span, :] = out
        low = out.astype(BF16)
        dso_vm[span, :] = low
        sums_ref[0:1, :] += jnp.sum(grad * unit, axis=0, keepdims=True)
        sums_ref[1:2, :] += jnp.sum(grad, axis=0, keepdims=True)
        sums_ref[2:3, :] += jnp.sum(low.astype(F32), axis=0, keepdims=True)

    tiles(own, norm)
    swap_dso.start()
    cross_sum.middle()

    dsa_ref[:own, :] = mm(dso_vm[:own, :], so_ref[...], NT).astype(BF16)
    for u in range(2, units):
        send_home(u)
    swap_dso.wait()
    dsa_ref[own:, :] = mm(dso_vm[own:, :], so_ref[...], NT).astype(BF16)
    block = sa_ref.shape[1] // n_mem

    def so_weights(m, carry):
        lanes = pl.ds(pl.multiple_of(m * block, block), block)
        dw_so[0, m] = (
            mm(sa_ref[:, lanes].T, dso_vm[...]).astype(BF16).reshape(dw_so.shape[2:])
        )
        return carry

    lax.fori_loop(0, n_mem, so_weights, 0)
    so_sum.start()
    for item in settles:
        item.middle()
    cross_sum.end()
    for item in settles:
        item.forward()
    so_sum.middle()
    for item in settles:
        item.end()
    so_sum.end()
    cross_sum.wait_send()
    so_sum.wait_send()
    for copy in twins + pairs:
        copy.wait_send()
    for item in homes:
        item.wait_recv(0)
        item.wait_send()


def middle(
    n_mem, plane, planes, slot, member, index, dq, dk, dv, wc, so, sa, h1, enc, dz2, unit, scale, gain, ready
):
    rows, part = dq.shape
    width = h1.shape[1]
    own = rows // 2
    passages = slot.shape[0] // 2
    settled = tuple(columns for _, columns in ready)
    settled_shapes = [item.shape[:2] + (plane,) + item.shape[2:] for item, _ in ready]
    cross_shape = (3, n_mem, plane, width // (n_mem * plane), part)
    so_shape = (1, n_mem, plane, part // (n_mem * plane), width)
    shapes = [
        jax.ShapeDtypeStruct((rows, part), BF16),
        jax.ShapeDtypeStruct((own, width), F32),
        jax.ShapeDtypeStruct((8, width), F32),
        jax.ShapeDtypeStruct((passages // 2, PLEN, width), BF16),
        sum_shape(cross_shape),
        sum_shape(so_shape),
    ] + [reduce_out(shape, columns, plane) for shape, columns in zip(settled_shapes, settled)]
    fetched = [h1, enc, dz2, unit, so, sa]
    scratch = [pltpu.VMEM(item.shape, item.dtype) for item in fetched] + [
        pltpu.VMEM((part, width), BF16),
        pltpu.VMEM((part, width), BF16),
        pltpu.VMEM(dk.shape[:1] + (width,), BF16),
        pltpu.VMEM((passages, PLEN, width), BF16),
        pltpu.VMEM((passages, PLEN, width), BF16),
        pltpu.VMEM((passages, PLEN, width), BF16),
        pltpu.VMEM((passages // 2, PLEN, width), BF16),
        pltpu.VMEM(cross_shape, BF16),
        pltpu.VMEM(so_shape, BF16),
        pltpu.VMEM((own, width), BF16),
        pltpu.VMEM((own, width), BF16),
        pltpu.VMEM((rows, width), BF16),
    ]
    scratch += plane_sum_scratch(cross_shape, n_mem, cross_shape[3])
    scratch += plane_sum_scratch(so_shape, n_mem, so_shape[3])
    for shape in settled_shapes:
        scratch += settle_scratch(shape, n_mem, plane, planes, shape[3])
    count = (
        len(ready) * settle_sems(n_mem, plane, planes) + 2 * PLANE_SUM_SEMS + 2 * passages
        + passages + 4 * passages // 2 + 4 + 6
    )
    smem = pl.BlockSpec(memory_space=pltpu.SMEM)
    outs = pl.pallas_call(
        functools.partial(middle_kernel, n_mem, plane, planes, settled),
        in_specs=[smem, smem, smem] + [VMEM] * 6 + [ANY] * 6 + [VMEM] * len(ready),
        out_specs=[VMEM] * 3 + [ANY] + [VMEM] * (2 + len(ready)),
        out_shape=shapes,
        scratch_shapes=scratch + [pltpu.SemaphoreType.DMA((count,))],
        compiler_params=pltpu.CompilerParams(
            vmem_limit_bytes=60 * 2**20, collective_id=3, has_side_effects=True
        ),
        cost_estimate=pl.CostEstimate(
            flops=rows * part * width * 30, bytes_accessed=40 * 2**20, transcendentals=0
        ),
        name="middle",
    )(
        slot,
        member,
        index,
        dq,
        dk.reshape(-1, PLEN, part),
        dv.reshape(-1, PLEN, part),
        wc,
        scale,
        gain,
        *fetched,
        *[item for item, _ in ready],
    )
    return outs[:4], outs[4:6], outs[6:]


def self_attend_back(place, pair, q_vm, k_vm, v_vm, o_vm, do_vm, lse_vm, outs, scratch):
    dq_vm, dk_vm, dv_vm = outs
    q_a, do_a, k_t, q_h, do_h, p_vm, ds_vm = scratch
    base = 2 * place.core + place.parity
    count = q_vm.shape[0] // BLK
    lanes = pl.ds(pl.multiple_of(pair * 2 * HD, 2 * HD), 2 * HD)

    def rows(i):
        return pl.ds(pl.multiple_of(flip(base, i) * BLK, BLK), BLK)

    for i in range(count):
        span = slice(i * BLK, (i + 1) * BLK)
        q_a[span, :] = q_vm[rows(i), lanes]
        do_a[span, :] = do_vm[rows(i), lanes]
        k_t[:, span] = k_vm[rows(i), lanes].T
        q_t = q_a[span, :].T
        do_t = do_a[span, :].T
        prod = (do_a[span, :].astype(F32) * o_vm[rows(i), lanes].astype(F32)).T
        for head in range(2):
            delta = jnp.sum(prod[head * HD : (head + 1) * HD, :], axis=0, keepdims=True)
            q_h[head, :, span] = head_rows(q_t, head, lse_vm[pair, head : head + 1, span])
            do_h[head, :, span] = head_rows(do_t, head, delta)
    key_pos = lax.broadcasted_iota(jnp.int32, (BLK, BLK), 0)
    query_pos = lax.broadcasted_iota(jnp.int32, (BLK, BLK), 1)
    units = [(j, i, head) for j in range(count) for head in range(2) for i in range(j, count)]

    def products(unit):
        j, i, head = unit
        span = slice(i * BLK, (i + 1) * BLK)
        return (
            mm(ones_in(k_vm[rows(j), lanes], head), q_h[head, :, span]),
            mm(ones_in(v_vm[rows(j), lanes], head), do_h[head, :, span]),
        )

    ready = products(units[0])
    halves = {}
    for n, (j, i, head) in enumerate(units):
        coming = products(units[n + 1]) if n + 1 < len(units) else None
        scores, dprobs = ready
        probs = jnp.exp(scores)
        if i == j:
            probs = jnp.where(key_pos <= query_pos, probs, 0.0)
        keys, span = slice(j * BLK, (j + 1) * BLK), slice(i * BLK, (i + 1) * BLK)
        p_vm[head, keys, span] = probs.astype(BF16)
        ds_vm[head, keys, span] = (probs * dprobs).astype(BF16)
        if i == count - 1:
            late = slice(j * BLK, count * BLK)
            halves[head] = (
                mm(p_vm[head, keys, late], do_a[late, :]),
                mm(ds_vm[head, keys, late], q_a[late, :]),
            )
            if head == 1:
                dv_vm[rows(j), lanes] = pick_heads(halves[0][0], halves[1][0]).astype(BF16)
                dk_vm[rows(j), lanes] = pick_heads(halves[0][1], halves[1][1]).astype(BF16)
        ready = coming
    for i in range(count):
        span, keys = slice(i * BLK, (i + 1) * BLK), slice(0, (i + 1) * BLK)
        dq_t = jnp.concatenate(
            [
                mm(k_t[head * HD : (head + 1) * HD, keys], ds_vm[head, keys, span])
                for head in range(2)
            ],
            axis=0,
        )
        dq_vm[rows(i), lanes] = dq_t.T.astype(BF16) * BF16(0.125)


def last_kernel(n_mem, plane, planes, settled, chunks, *refs):
    refs = Walk(refs)
    q_ref, k_ref, v_ref, o_ref, do_ref, lse_ref, feed_ref, hidden_ref, middle_ref = refs.take(9)
    fetched = refs.take(3)
    ready = refs.take(len(settled))
    small_out, dx_out, self_out = refs.take(3)
    outs = refs.take(len(settled))
    x_ref, w_ref, dz1_ref = kept = refs.take(3)
    dq_vm, dk_vm, dv_vm = refs.take(3)
    attend_scratch = refs.take(7)
    x_t, dw_vm = refs.take(2)
    part_vm, twin_vm, dx_vm = refs.take(3)
    chunk_own = [refs.one() for _ in range(chunks)]
    chunk_bufs = [refs.take(3) for _ in range(chunks)]
    chunk_settle = [refs.take(3) for _ in range(chunks)]
    settle_bufs = [refs.take(3) for _ in settled]
    small_near, small_line, small_twin, small_far, small_sum, sem_ref = refs.take(6)
    sems = Sems(sem_ref)
    place = Place(plane, planes)
    fetches = [Fetch(sems, src, dst) for src, dst in zip(fetched, kept)]
    settles = [
        Settle(
            place, sems, ready[i], outs[i], settle_bufs[i], columns, n_mem, (0, ready[i].shape[2])
        )
        for i, columns in enumerate(settled)
    ]
    rows, part = q_ref.shape
    lanes = part // chunks
    depth = dw_vm.shape[3]
    sums = [
        PlaneSum(
            place, sems, dw_vm, chunk_own[c], chunk_bufs[c], (0, depth), (c * lanes, lanes)
        )
        for c in range(chunks)
    ]
    ends = [
        Settle(
            place, sems, chunk_own[c], self_out, chunk_settle[c], True, n_mem, (0, depth), c * lanes
        )
        for c in range(chunks)
    ]
    near_sems = sems.take(6)
    near = [
        remote(
            small_sum, small_near.at[t - 1], near_sems[2 * t - 2], near_sems[2 * t - 1], place.near(t)
        )
        for t in range(1, plane)
    ]
    line = Line(
        place, sems, lambda s: small_sum.at[flip(place.mem, s)], lambda s: small_line.at[s - 1], n_mem
    )
    twin_sems = sems.take(2)
    twin = remote(small_sum.at[place.mem], small_twin, twin_sems[0], twin_sems[1], place.twin())
    far_sems = sems.take(2 * (planes - 1))
    far = [
        remote(
            small_sum.at[place.mem],
            small_far.at[r - 1],
            far_sems[2 * r - 2],
            far_sems[2 * r - 1],
            place.far(r),
        )
        for r in range(1, planes)
    ]
    seg = dx_out.shape[1]
    own = 2 * seg
    spread = Spread(
        place,
        sems,
        lambda k: dx_vm.at[pl.ds(seg * k, seg)],
        lambda k: dx_out.at[place.parity],
    )
    swap_sems = sems.take(2)
    swap_part = remote(part_vm, twin_vm, swap_sems[0], swap_sems[1], place.twin())

    for item in fetches:
        item.start()
    place.meet(
        column_peers(n_mem) + plane_peers(plane) + [(2 * plane * r, 0) for r in range(1, planes)]
    )
    for item in settles:
        item.start()
    block = x_ref.shape[1] // n_mem

    def input_part(span):
        return (
            mm(dq_vm[span, :], w_ref[0], NT)
            + mm(dk_vm[span, :], w_ref[1], NT)
            + mm(dv_vm[span, :], w_ref[2], NT)
        )

    pairs = part // (2 * HD)
    late = []
    for c in range(chunks):
        for pair in range(c * pairs // chunks, (c + 1) * pairs // chunks):
            self_attend_back(
                place,
                pair,
                q_ref,
                k_ref,
                v_ref,
                o_ref,
                do_ref,
                lse_ref,
                (dq_vm, dk_vm, dv_vm),
                attend_scratch,
            )
        if c == 0:
            for item in fetches:
                item.get()
            for m in range(n_mem):
                x_t[m] = x_ref[:, m * block : (m + 1) * block].T
        span = slice(c * lanes, (c + 1) * lanes)

        def weights(m, carry, span=span):
            for i, grad in enumerate((dq_vm, dk_vm, dv_vm)):
                dw_vm[i, m, :, :, span] = (
                    mm(x_t[m], grad[:, span]).astype(BF16).reshape(plane, depth, lanes)
                )
            return carry

        if c < chunks - 2:
            lax.fori_loop(0, n_mem, weights, 0)
            sums[c].start()
        if c == 1:
            sums[0].middle()
        if c == 2:
            for item in settles:
                item.middle()
            sums[0].end()
            ends[0].start()
            sums[1].middle()
        late.append(weights)
    part_vm[...] = input_part(slice(own, 2 * own)).astype(BF16)
    swap_part.start()
    lax.fori_loop(0, n_mem, late[-2], 0)
    sums[-2].start()
    swap_part.wait()
    total = dz1_ref[...] + input_part(slice(0, own)) + twin_vm[...].astype(F32)
    dx_vm[...] = total.astype(BF16)
    spread.start()
    lax.fori_loop(0, n_mem, late[-1], 0)
    sums[-1].start()
    sums[1].end()
    ends[1].start()
    for item in settles:
        item.forward()
    sums[-2].middle()

    small_sum[...] = jnp.zeros_like(small_sum)
    wide = small_sum.shape[2]
    unit = wide // 2
    first = place.core == 0
    for row, ref, at in (
        (2, middle_ref, 2),
        (5, feed_ref, 5),
        (6, middle_ref, 1),
        (7, feed_ref, 4),
        (8, feed_ref, 1),
        (9, feed_ref, 2),
        (10, middle_ref, 0),
        (11, feed_ref, 3),
        (12, feed_ref, 0),
    ):
        for b in range(n_mem):
            small_sum[b, row : row + 1, :] = ref[at : at + 1, b * wide : (b + 1) * wide]
    for row, value in (
        (0, jnp.sum(dq_vm[...].astype(F32), axis=0, keepdims=True)),
        (1, jnp.sum(dv_vm[...].astype(F32), axis=0, keepdims=True)),
        (3, middle_ref[3:4, :part]),
        (4, middle_ref[4:5, :part]),
    ):
        for b in range(n_mem):
            side = value[:, b * unit : (b + 1) * unit]
            none = jnp.zeros_like(side)
            small_sum[b, row : row + 1, :unit] = jnp.where(first, side, none)
            small_sum[b, row : row + 1, unit:] = jnp.where(first, none, side)
    count = hidden_ref.shape[1] // (n_mem * wide)
    for b in range(n_mem):
        for i in range(count):
            at = (b * count + i) * wide
            side = hidden_ref[:, at : at + wide]
            none = jnp.zeros_like(side)
            row = 13 + i
            small_sum[b, row : row + 1, :] = jnp.where(first, side, none)
            small_sum[b, row + count : row + count + 1, :] = jnp.where(first, none, side)
    for copy in near:
        copy.start()
    sums[-1].middle()
    sums[-2].end()
    ends[-2].start()
    ends[0].middle()
    for copy in near:
        copy.wait()
    total = small_sum[...]
    for t in range(plane - 1):
        total += small_near[t]
    small_sum[...] = total
    line.start()
    sums[-1].end()
    ends[-1].start()
    ends[1].middle()
    ends[0].forward()
    for item in settles:
        item.end()
    ends[-2].middle()
    ends[1].forward()
    for s in range(1, n_mem):
        line.wait_recv(s)
    line.wait_send()
    value = small_sum[place.mem]
    for s in range(n_mem - 1):
        value += small_line[s]
    small_sum[place.mem] = value
    twin.start()
    ends[-1].middle()
    ends[-2].forward()
    for item in ends[:-2]:
        item.end()
    twin.wait()
    value = small_sum[place.mem] + small_twin[...]
    if far:
        small_sum[place.mem] = value
        for copy in far:
            copy.start()
        for copy in far:
            copy.wait()
        for r in range(planes - 1):
            value += small_far[r]
    small_out[...] = value
    ends[-1].forward()
    ends[-2].end()
    ends[-1].end()
    for item in sums:
        item.wait_send()
    for k in range(2):
        spread.wait_recv(k)
    spread.wait_send()


def last(n_mem, plane, planes, q, k, v, o, do, lse, x, w, dz1, sums, small_shape, ready):
    rows, part = q.shape
    chunks = part // (2 * HD)
    width = x.shape[1]
    own = rows // 2
    settled = tuple(columns for _, columns in ready)
    settled_shapes = [item.shape[:2] + (plane,) + item.shape[2:] for item, _ in ready]
    grad_shape = (3, n_mem, plane, width // (n_mem * plane), part)
    depth, lanes = grad_shape[3], part // chunks
    small_part = small_shape[1:]
    shapes = [
        jax.ShapeDtypeStruct(small_part, F32),
        jax.ShapeDtypeStruct((2, own // 2, width), BF16),
        reduce_out(grad_shape, True, plane),
    ] + [reduce_out(shape, columns, plane) for shape, columns in zip(settled_shapes, settled)]
    fetched = [x, w, dz1]
    scratch = (
        [pltpu.VMEM(item.shape, item.dtype) for item in fetched]
        + [pltpu.VMEM((rows, part), BF16)] * 3
        + [
            pltpu.VMEM((rows, 2 * HD), BF16),
            pltpu.VMEM((rows, 2 * HD), BF16),
            pltpu.VMEM((2 * HD, rows), BF16),
            pltpu.VMEM((2, 2 * HD, rows), BF16),
            pltpu.VMEM((2, 2 * HD, rows), BF16),
            pltpu.VMEM((2, rows, rows), BF16),
            pltpu.VMEM((2, rows, rows), BF16),
            pltpu.VMEM((n_mem, width // n_mem, rows), BF16),
            pltpu.VMEM(grad_shape, BF16),
        ]
        + [pltpu.VMEM((own, width), BF16)] * 3
        + [pltpu.VMEM((3, n_mem, depth, lanes), BF16)] * chunks
    )
    for _ in range(chunks):
        scratch += plane_sum_scratch(grad_shape, n_mem, depth, lanes)
    for _ in range(chunks):
        scratch += settle_scratch(grad_shape, n_mem, plane, planes, depth, lanes)
    for shape in settled_shapes:
        scratch += settle_scratch(shape, n_mem, plane, planes, shape[3])
    scratch += [
        pltpu.VMEM((plane - 1,) + small_shape, F32),
        pltpu.VMEM((n_mem - 1,) + small_part, F32),
        pltpu.VMEM(small_part, F32),
        pltpu.VMEM((max(planes - 1, 1),) + small_part, F32),
        pltpu.VMEM(small_shape, F32),
        pltpu.SemaphoreType.DMA(
            (
                (len(ready) + chunks) * settle_sems(n_mem, plane, planes)
                + chunks * PLANE_SUM_SEMS
                + 24
                + 2 * planes,
            )
        ),
    ]
    outs = pl.pallas_call(
        functools.partial(last_kernel, n_mem, plane, planes, settled, chunks),
        in_specs=[VMEM] * 9 + [ANY] * 3 + [VMEM] * len(ready),
        out_specs=[VMEM, ANY, VMEM] + [VMEM] * len(ready),
        out_shape=shapes,
        scratch_shapes=scratch,
        compiler_params=pltpu.CompilerParams(
            vmem_limit_bytes=60 * 2**20, collective_id=4, has_side_effects=True
        ),
        cost_estimate=pl.CostEstimate(
            flops=rows * rows * width * 40, bytes_accessed=40 * 2**20, transcendentals=rows * rows * 8
        ),
        name="last",
    )(q, k, v, o, do, lse, *sums, *fetched, *[item for item, _ in ready])
    return outs[0], outs[1], outs[2:]


def cross_forward_kernel(n_mem, plane, kinds, index_ref, q_ref, k_ref, v_ref, *refs):
    refs = Walk(refs)
    count_w = len(kinds)
    shards = refs.take(count_w)
    o_ref, lse_ref = refs.take(2)
    halves = refs.take(count_w)
    v_t, o_t, sem_ref = refs.take(3)
    sems = Sems(sem_ref)
    place = Place(plane)
    step = pl.program_id(0) * pl.num_programs(1) + pl.program_id(1)
    last = pl.num_programs(0) * pl.num_programs(1) - 1
    gathers = [
        Gather(place, sems, shard, half, columns, n_mem, (1,) if i == 1 else None)
        for i, (shard, half, columns) in enumerate(zip(shards, halves, kinds))
    ]
    @pl.when(step == 0)
    def _():
        for gather in gathers:
            gather.own.start()
        place.meet(column_peers(n_mem) + plane_peers(plane))
        for gather in gathers:
            gather.begin()

    rows = q_ref.shape[0]
    count = index_ref.shape[0]

    @pl.when(pl.program_id(1) == 0)
    def _():
        for j in range(count):
            v_t[:, j * BLK : (j + 1) * BLK] = v_ref[index_ref[j]].T

    units = []
    for i in range(rows // BLK):
        q_t = q_ref[i * BLK : (i + 1) * BLK, :].T
        for head in range(2):
            q_head = head_rows(q_t, head)

            def score(j, q_head=q_head):
                return mm(k_ref[index_ref[j]], q_head)

            def value(j, head=head):
                return v_t[head * HD : (head + 1) * HD, j * BLK : (j + 1) * BLK]

            units.append(
                (
                    [functools.partial(score, j) for j in range(count)],
                    [functools.partial(value, j) for j in range(count)],
                    (i, head),
                )
            )

    def finish(tag, mixed, lse):
        i, head = tag
        span = slice(i * BLK, (i + 1) * BLK)
        o_t[head * HD : (head + 1) * HD, span] = mixed
        lse_ref[0, head : head + 1, span] = lse

    whole_one, line_one = gathers
    plan = {
        4: [(whole_one.share, 1)],
        6: [(line_one.share, 1)],
        10: [(whole_one.share, 2)],
        12: [(line_one.share, 2), (whole_one.forward, 1)],
        14: [(line_one.forward, 1)],
        17: [(whole_one.share, 3)],
        19: [(line_one.share, 3), (whole_one.forward, 2)],
        24: [(whole_one.forward, 3)],
    }

    def serve(n):
        for when, calls in plan.items():
            if when % len(units) == n:

                @pl.when(step == when // len(units))
                def _():
                    for call, hops in calls:
                        call(hops)

    softmax_units(units, finish, serve)
    o_ref[...] = o_t[...].T.astype(BF16)

    @pl.when(step == last)
    def _():
        for gather in gathers:
            gather.finish()


def cross_forward(n_mem, plane, index, q, k, v, params):
    rows, width = q.shape
    pairs = width // (2 * HD)
    keys = index.shape[0] * PLEN
    block = 2 * BLK
    question = pl.BlockSpec((block, 2 * HD), lambda h, i: (i, h))
    memory = pl.BlockSpec(k.shape[:2] + (2 * HD,), lambda h, i: (0, 0, h))
    kinds = tuple(columns for _, columns in params)
    views = [half_views(shard, columns, n_mem, plane) for shard, columns in params]
    outs = pl.pallas_call(
        functools.partial(cross_forward_kernel, n_mem, plane, kinds),
        grid=(pairs, rows // block),
        in_specs=[pl.BlockSpec(memory_space=pltpu.SMEM), question, memory, memory]
        + [whole(view.shape) for view, _ in views],
        out_specs=[question, pl.BlockSpec((1, 2, block), lambda h, i: (h, 0, i))]
        + [ANY] * len(params),
        out_shape=[
            jax.ShapeDtypeStruct((rows, width), BF16),
            jax.ShapeDtypeStruct((pairs, 2, rows), F32),
        ]
        + [jax.ShapeDtypeStruct(full, BF16) for _, full in views],
        scratch_shapes=[
            pltpu.VMEM((2 * HD, keys), BF16),
            pltpu.VMEM((2 * HD, block), F32),
            pltpu.SemaphoreType.DMA((4 + GATHER_SEMS * len(params),)),
        ],
        compiler_params=pltpu.CompilerParams(
            vmem_limit_bytes=60 * 2**20, collective_id=2, has_side_effects=True
        ),
        cost_estimate=pl.CostEstimate(
            flops=rows * keys * width * 16,
            bytes_accessed=rows * width * 4 + k.size * 4,
            transcendentals=rows * keys * pairs * 2,
        ),
        name="cross_forward",
    )(index, q, k, v, *[view for view, _ in views])
    return outs[:2], outs[2:]


def cross_backward_kernel(
    n_mem, plane, planes, chunks, settled, index_ref, q_ref, k_ref, v_ref, o_ref, do_ref, lse_ref, *refs
):
    refs = Walk(refs)
    kinds = {which: columns for which, columns, _ in chunks}
    grads = refs.take(len(kinds))
    ready = refs.take(len(settled))
    dq_ref, dk_ref, dv_ref = refs.take(3)
    outs = refs.take(len(kinds))
    ready_outs = refs.take(len(settled))
    q_h, do_h, dq_t, p_vm, ds_vm = refs.take(5)
    sems = Sems(refs.refs[-1])
    place = Place(plane, planes)
    sums, settles = [], []
    for which, columns, rows_of in chunks:
        own = refs.one()
        sums.append(PlaneSum(place, sems, grads[which], own, refs.take(3), rows_of))
        settles.append(
            Settle(place, sems, own, outs[which], refs.take(3), columns, n_mem, rows_of)
        )
    first = [
        Settle(
            place, sems, ready[i], ready_outs[i], refs.take(3), columns, n_mem, (0, ready[i].shape[2])
        )
        for i, columns in enumerate(settled)
    ]
    passage = pl.program_id(1)
    step = pl.program_id(0) * pl.num_programs(1) + passage
    steps = pl.num_programs(0) * pl.num_programs(1)
    rows = q_ref.shape[0]
    count = rows // BLK

    @pl.when(step == 0)
    def _():
        place.meet(
            column_peers(n_mem) + plane_peers(plane) + [(2 * plane * r, 0) for r in range(1, planes)]
        )
        for item in first:
            item.start()

    def at(when, *calls):
        @pl.when(step == when)
        def _():
            for call in calls:
                call()

    plan = ((0, 2, 5, 9, 10), (4, 6, 9, 13, 14), (8, 9, 11, 14, 15))
    for i, (plane_sum, settle) in enumerate(zip(sums, settles)):
        start, middle, end, line, near = plan[i]
        at(start, plane_sum.start)
        at(middle, plane_sum.middle)
        at(end, plane_sum.end, settle.start)
        at(line, settle.middle)
        at(near, settle.forward)
    for item in first:
        at(7, item.middle)
        at(9, item.forward)

    @pl.when(passage == 0)
    def _():
        for i in range(count):
            span = slice(i * BLK, (i + 1) * BLK)
            q_t = q_ref[span, :].T
            grads_t = do_ref[span, :].T
            prod = (do_ref[span, :].astype(F32) * o_ref[span, :].astype(F32)).T
            for head in range(2):
                delta = jnp.sum(prod[head * HD : (head + 1) * HD, :], axis=0, keepdims=True)
                q_h[head, :, span] = head_rows(q_t, head, lse_ref[0, head : head + 1, span])
                do_h[head, :, span] = head_rows(grads_t, head, delta)
        dq_t[...] = jnp.zeros_like(dq_t)

    keys = dk_ref.shape[0] // BLK
    slots = [index_ref[passage * keys + j] for j in range(keys)]
    k_t = jnp.concatenate([k_ref[slot].T for slot in slots], axis=1)
    units = [(head, j, i) for head in range(2) for j in range(keys) for i in range(count)]

    def products(unit):
        head, j, i = unit
        span = slice(i * BLK, (i + 1) * BLK)
        return (
            mm(ones_in(k_ref[slots[j]], head), q_h[head, :, span]),
            mm(ones_in(v_ref[slots[j]], head), do_h[head, :, span]),
        )

    coming = products(units[0])
    halves = []
    for n, (head, j, i) in enumerate(units):
        scores, dprobs = coming
        if n + 1 < len(units):
            coming = products(units[n + 1])
        tile, span = slice(j * BLK, (j + 1) * BLK), slice(i * BLK, (i + 1) * BLK)
        probs = jnp.exp(scores)
        p_vm[head, tile, span] = probs.astype(BF16)
        ds_vm[head, tile, span] = (probs * dprobs).astype(BF16)
        if (j, i) == (keys - 1, count - 1):
            half = slice(head * HD, (head + 1) * HD)
            halves.append((mm(p_vm[head], do_ref[...]), mm(ds_vm[head], q_ref[...])))
            dq_t[half, :] += mm(k_t[half, :], ds_vm[head])
    dv_ref[...] = pick_heads(halves[0][0], halves[1][0]).astype(BF16)
    dk_ref[...] = pick_heads(halves[0][1], halves[1][1]).astype(BF16)

    @pl.when(passage == pl.num_programs(1) - 1)
    def _():
        dq_ref[...] = dq_t[...].T.astype(BF16)

    @pl.when(step == steps - 1)
    def _():
        for settle in first + settles:
            settle.end()
        for item in sums:
            item.wait_send()


def cross_backward(n_mem, plane, planes, index, q, k, v, o, do, lse, grads, ready):
    rows, width = q.shape
    pairs = width // (2 * HD)
    block = 2 * PLEN
    keys = index.shape[0] * PLEN
    passages = keys // block
    question = pl.BlockSpec((rows, 2 * HD), lambda h, u: (0, h))
    memory = pl.BlockSpec(k.shape[:2] + (2 * HD,), lambda h, u: (0, 0, h))
    grads_of = pl.BlockSpec((block, 2 * HD), lambda h, u: (u, h))
    shapes, chunks, scratch = [], [], []
    for which, (grad, columns, pieces) in enumerate(grads):
        lead, _, _, depth, cols = grad.shape
        count = depth // pieces
        shapes.append(reduce_out(grad.shape, columns, plane))
        for i in range(pieces):
            chunks.append((which, columns, (i * count, count)))
            scratch.append(pltpu.VMEM((lead, n_mem, count, cols), BF16))
            scratch += plane_sum_scratch(grad.shape, n_mem, count)
            scratch += settle_scratch(grad.shape, n_mem, plane, planes, count)
    settled = tuple(columns for _, columns in ready)
    for item, columns in ready:
        shape = item.shape[:2] + (plane,) + item.shape[2:]
        shapes.append(reduce_out(shape, columns, plane))
        scratch += settle_scratch(shape, n_mem, plane, planes, shape[3])
    outs = pl.pallas_call(
        functools.partial(cross_backward_kernel, n_mem, plane, planes, tuple(chunks), settled),
        grid=(pairs, passages),
        in_specs=[
            pl.BlockSpec(memory_space=pltpu.SMEM),
            question,
            memory,
            memory,
            question,
            question,
            pl.BlockSpec((1, 2, rows), lambda h, u: (h, 0, 0)),
        ]
        + [ANY] * len(grads)
        + [whole(item.shape) for item, _ in ready],
        out_specs=[question, grads_of, grads_of]
        + [whole(item.shape) for item in shapes],
        out_shape=[
            jax.ShapeDtypeStruct((rows, width), BF16),
            jax.ShapeDtypeStruct((keys, width), BF16),
            jax.ShapeDtypeStruct((keys, width), BF16),
        ]
        + shapes,
        scratch_shapes=[
            pltpu.VMEM((2, 2 * HD, rows), BF16),
            pltpu.VMEM((2, 2 * HD, rows), BF16),
            pltpu.VMEM((2 * HD, rows), F32),
            pltpu.VMEM((2, block, rows), BF16),
            pltpu.VMEM((2, block, rows), BF16),
        ]
        + scratch
        + [
            pltpu.SemaphoreType.DMA(
                (
                    len(chunks) * PLANE_SUM_SEMS
                    + (len(chunks) + len(ready)) * settle_sems(n_mem, plane, planes),
                )
            )
        ],
        compiler_params=pltpu.CompilerParams(
            vmem_limit_bytes=56 * 2**20, collective_id=5, has_side_effects=True
        ),
        cost_estimate=pl.CostEstimate(
            flops=rows * keys * width * 40,
            bytes_accessed=rows * width * 10 + k.size * 8,
            transcendentals=rows * keys * pairs * 2,
        ),
        name="cross_backward",
    )(index, q, k, v, o, do, lse, *[item[0] for item in grads], *[item for item, _ in ready])
    return outs[:3], outs[3:]


def widen_kernel(*refs):
    count = len(refs) // 2
    for src, dst in zip(refs[:count], refs[count:]):
        dst[...] = src[...].astype(F32)


def widen(pairs):
    steps = 8
    flats = [value.reshape(-1, like.shape[-1]) for value, like in pairs]
    blocks = [
        pl.BlockSpec((item.shape[0] // steps, item.shape[1]), lambda i: (i, 0)) for item in flats
    ]
    outs = pl.pallas_call(
        widen_kernel,
        grid=(steps,),
        in_specs=blocks,
        out_specs=blocks,
        out_shape=[jax.ShapeDtypeStruct(item.shape, F32) for item in flats],
        compiler_params=pltpu.CompilerParams(vmem_limit_bytes=60 * 2**20),
        cost_estimate=pl.CostEstimate(
            flops=0, bytes_accessed=6 * sum(item.size for item in flats), transcendentals=0
        ),
        name="widen",
    )(*flats)
    return [out.reshape(like.shape) for out, (_, like) in zip(outs, pairs)]


def body(
    hidden_in,
    encoder_rows,
    passage_map,
    self_qkv,
    self_out,
    cross_qkv,
    cross_out,
    ffn_in,
    ffn_out,
    ffn_in_bias,
    biases,
    gains,
    cotangent,
):
    n_pb = lax.axis_size("pb")
    n_mem = lax.axis_size("mem")
    columns = n_pb // 2
    plane = min(columns, 4)
    pb = lax.axis_index("pb")
    core = pb % 2
    width = hidden_in.shape[2]
    planes = columns // plane

    enc_local = encoder_rows.reshape(-1, PLEN, width)
    n_bias, n_gain = biases.shape[0], gains.shape[0]
    small = jnp.concatenate([biases, gains, ffn_in_bias.reshape(-1, biases.shape[1])], axis=0)
    n_small = small.shape[0]
    small_rows = -(-n_small // 16) * 16
    small = jnp.pad(small, ((0, small_rows - n_small), (0, 0)))
    rows_out, halves, kept = front(
        n_mem,
        plane,
        (n_bias, n_gain),
        hidden_in,
        enc_local,
        passage_map,
        small,
        [(self_qkv, True), (self_out, False), (cross_qkv, True), (cross_out, False)],
    )
    x_full, enc_full, index, small = rows_out
    sq, sk, sv, sa, self_lse, h1_full, unit1, scale1, cq, ck, cv = kept
    index = index.reshape(-1)

    def flat(half):
        lead, _, _, _, cols = half.shape
        return half.reshape(lead, -1, cols)

    w_self, w_cross = flat(halves[0]), flat(halves[2])
    w_self_out, w_cross_out = flat(halves[1])[0], flat(halves[3])[0]
    small = small.astype(F32)
    vectors = small[:, : n_bias + n_gain].transpose(1, 0, 2).reshape(n_bias + n_gain, width)
    bias, gain = vectors[:n_bias], vectors[n_bias:]
    ffn_bias = small[:, n_bias + n_gain : n_small].reshape(-1)

    def half_of(vector):
        parts = vector.reshape(n_mem, 2, -1)
        return jnp.where(core == 0, parts[:, 0], parts[:, 1]).reshape(-1)

    order = jnp.arange(encoder_rows.shape[1] * n_mem, dtype=jnp.int32)
    hits = index[None, :] == order[:, None]
    member = jnp.any(hits, axis=1).astype(F32)
    slot = jnp.sum(jnp.where(hits, jnp.arange(index.shape[0], dtype=jnp.int32)[None], 0), axis=1)
    (ca, cross_lse), halves = cross_forward(
        n_mem,
        plane,
        index,
        cq,
        ck,
        cv,
        [(ffn_in[None], True), (ffn_out, False)],
    )
    w_ffn_in, w_ffn_out = flat(halves[0])[0], halves[1]

    rows_of = jnp.stack(
        [gain[0], bias[6], bias[5], gain[1], bias[7], bias[9], gain[2], bias[8]]
    )
    layer_out, dca, dz2, feed_sums, hidden_sums, own_ffn_out, dw_ffn_in, dw_cross_out = feed(
        n_mem,
        plane,
        cotangent,
        rows_of,
        half_of(ffn_bias)[None],
        ca,
        unit1,
        w_cross_out,
        w_ffn_in,
        w_ffn_out,
    )
    (dcq, dck, dcv), ffn_sums = cross_backward(
        n_mem,
        plane,
        planes,
        index,
        cq,
        ck,
        cv,
        ca,
        dca,
        cross_lse,
        [(dw_ffn_in, True, 2), (dw_cross_out, False, 1)],
        [(own_ffn_out, False)],
    )
    (dsa, dz1, middle_sums, enc_sum), (own_cross, own_so), _ = middle(
        n_mem,
        plane,
        planes,
        slot,
        member,
        index,
        dcq,
        dck,
        dcv,
        w_cross,
        w_self_out,
        sa,
        h1_full,
        enc_full.reshape(-1, PLEN, width),
        dz2,
        unit1,
        scale1,
        gain[0][None],
        [],
    )

    vec, dx, sums = last(
        n_mem,
        plane,
        planes,
        sq,
        sk,
        sv,
        sa,
        dsa,
        self_lse,
        x_full,
        w_self,
        dz1,
        [feed_sums, hidden_sums, middle_sums],
        small.shape,
        [(own_so, False), (own_cross, True)],
    )
    (
        grad_in,
        grad_encoder,
        out_self_qkv,
        out_self_out,
        out_cross_qkv,
        out_cross_out,
        out_ffn_in,
        out_ffn_out,
    ) = widen(
        [
            (dx, hidden_in),
            (enc_sum, encoder_rows),
            (sums[0], self_qkv),
            (sums[1], self_out),
            (sums[2], cross_qkv),
            (ffn_sums[1], cross_out),
            (ffn_sums[0], ffn_in),
            (ffn_sums[2], ffn_out),
        ]
    )
    out_ffn_bias = vec[n_bias + n_gain : n_small].reshape(-1)
    return (
        layer_out,
        grad_in,
        grad_encoder,
        out_self_qkv,
        out_self_out,
        out_cross_qkv,
        out_cross_out,
        out_ffn_in,
        out_ffn_out,
        out_ffn_bias,
        vec[:n_bias],
        vec[n_bias : n_bias + n_gain],
    )


def solution(mesh):
    placed = (
        P("pb", "mem", None),
        P("pb", "mem", None, None),
        P("pb", None),
        P(None, "mem", None),
        P("mem", None),
        P(None, "mem", None),
        P("mem", None),
        P("mem", None),
        P("mem", None),
        P("mem"),
        P(None, "mem"),
        P(None, "mem"),
        P("pb", "mem", None),
    )
    return jax.shard_map(
        body,
        mesh=mesh,
        in_specs=placed,
        out_specs=(
            P("pb", "mem", None),
            P("pb", "mem", None),
            P("pb", "mem", None, None),
            P(None, "mem", None),
            P("mem", None),
            P(None, "mem", None),
            P("mem", None),
            P("mem", None),
            P("mem", None),
            P("mem"),
            P(None, "mem"),
            P(None, "mem"),
        ),
        check_vma=False,
    )
```

```python
import functools

import jax
import jax.numpy as jnp
from jax import lax
from jax.experimental import pallas as pl
from jax.experimental.pallas import tpu as pltpu
from jax.sharding import PartitionSpec as P

HD = 64
PLEN = 256
BLK = 256
F32 = jnp.float32
BF16 = jnp.bfloat16

NN = (((1,), (0,)), ((), ()))
NT = (((1,), (1,)), ((), ()))


def mm(a, b, dims=NN):
    return lax.dot_general(a, b, dims, preferred_element_type=F32)


def head_mask_rows(block, head):
    rows = lax.broadcasted_iota(jnp.int32, block.shape, 0)
    return jnp.where((rows // HD) == head, block, jnp.zeros_like(block))


def head_rows(block, head, extra=None):
    block = block.astype(F32)
    rows = lax.broadcasted_iota(jnp.int32, block.shape, 0)
    out = jnp.where((rows // HD) == head, block, 0.0)
    if extra is not None:
        rest = -extra
        for i in range(3):
            term = rest.astype(BF16).astype(F32)
            rest = rest - term
            out = jnp.where(rows == (1 - head) * HD + i, term, out)
    return out.astype(BF16)


def ones_in(block, head):
    lanes = lax.broadcasted_iota(jnp.int32, block.shape, 1)
    first = (1 - head) * HD
    return jnp.where((lanes >= first) & (lanes < first + 3), jnp.ones_like(block), block)


def pick_heads(first, second):
    lanes = lax.broadcasted_iota(jnp.int32, first.shape, 1)
    return jnp.where(lanes < HD, first, second)


MESH = pl.DeviceIdType.MESH
ANY = pl.BlockSpec(memory_space=pl.ANY)
VMEM = pl.BlockSpec(memory_space=pltpu.VMEM)
PLANE = 4


def flip(index, bits):
    bit = 1
    while bit <= bits:
        if bits & bit:
            unit = jnp.int32(bit)
            index = index + unit - 2 * unit * lax.rem(lax.div(index, unit), jnp.int32(2))
        bit *= 2
    return index


class Place:
    def __init__(self, plane, planes=1):
        self.pb = lax.axis_index("pb")
        self.mem = lax.axis_index("mem")
        two = jnp.int32(2)
        self.core = lax.rem(self.pb, two)
        self.quarter = lax.rem(lax.div(self.pb, two), jnp.int32(plane))
        self.parity = lax.rem(self.mem, two)
        self.half = lax.div(self.mem, two)
        self.plane = plane
        self.planes = planes

    def near(self, t):
        return (flip(self.pb, 2 * t), self.mem)

    def far(self, r):
        return (flip(self.pb, 2 * self.plane * r), self.mem)

    def line(self, s):
        return (self.pb, flip(self.mem, s))

    def twin(self):
        return (flip(self.pb, 1), self.mem)

    def pair(self):
        return (self.pb, flip(self.mem, 1))

    def worker(self, k):
        return (self.pb - self.core + self.half, 2 * self.core + flip(self.parity, k))

    def at_home(self):
        return self.half == self.core

    def meet(self, peers):
        barrier = pltpu.get_barrier_semaphore()
        for pb_bits, mem_bits in peers:
            pl.semaphore_signal(
                barrier,
                inc=1,
                device_id=(flip(self.pb, pb_bits), flip(self.mem, mem_bits)),
                device_id_type=MESH,
            )
        pl.semaphore_wait(barrier, len(peers))


def column_peers(n_mem):
    return [(a, b) for a in range(2) for b in range(n_mem) if (a, b) != (0, 0)]


def plane_peers(plane):
    return [(2 * t, 0) for t in range(1, plane)]


class Sems:
    def __init__(self, ref):
        self.ref = ref
        self.used = 0

    def take(self, count):
        first = self.used
        self.used += count
        return [self.ref.at[first + i] for i in range(count)]


def remote(src, dst, send_sem, recv_sem, device):
    return pltpu.make_async_remote_copy(
        src_ref=src,
        dst_ref=dst,
        send_sem=send_sem,
        recv_sem=recv_sem,
        device_id=device,
        device_id_type=MESH,
    )


class Spread:
    def __init__(self, place, sems, src, dst, kinds=(0, 1)):
        self.place, self.src, self.dst, self.kinds = place, src, dst, kinds
        self.send = sems.take(2)
        self.recv = sems.take(2)

    def copy(self, k):
        return remote(self.src(k), self.dst(k), self.send[k], self.recv[k], self.place.worker(k))

    def start(self):
        for k in self.kinds:
            if k == 0:
                home = self.place.at_home()

                @pl.when(home)
                def _():
                    pltpu.make_async_copy(self.src(0), self.dst(0), self.recv[0]).start()

                @pl.when(jnp.logical_not(home))
                def _():
                    self.copy(0).start()
            else:
                self.copy(k).start()

    def wait_recv(self, k):
        if k == 0:
            home = self.place.at_home()

            @pl.when(home)
            def _():
                pltpu.make_async_copy(self.src(0), self.dst(0), self.recv[0]).wait()

            @pl.when(jnp.logical_not(home))
            def _():
                self.copy(0).wait_recv()
        else:
            self.copy(k).wait_recv()

    def wait_send(self):
        for k in self.kinds:
            if k == 0:

                @pl.when(jnp.logical_not(self.place.at_home()))
                def _():
                    self.copy(0).wait_send()
            else:
                self.copy(k).wait_send()


class Own:
    def __init__(self, place, sems, shard, full, columns, n_mem):
        self.copies = []
        mem, core = place.mem, place.core
        if columns:
            unit = full.shape[-1] // n_mem
            for b, sem in zip(range(n_mem), sems.take(n_mem)):
                start = pl.multiple_of(2 * unit * b + unit * core, unit)
                src = shard.at[:, :, :, pl.ds(start, unit)]
                dst = full.at[:, mem, :, :, pl.ds(unit * b, unit)]
                self.copies.append(pltpu.make_async_copy(src, dst, sem))
        else:
            (sem,) = sems.take(1)
            self.copies.append(pltpu.make_async_copy(shard.at[core], full.at[0, mem], sem))

    def start(self):
        for copy in self.copies:
            copy.start()

    def wait(self):
        for copy in self.copies:
            copy.wait()


class Line:
    def __init__(self, place, sems, src, dst, n_mem):
        send, recv = sems.take(n_mem - 1), sems.take(n_mem - 1)
        self.copies = [
            remote(src(s), dst(s), send[s - 1], recv[s - 1], place.line(s)) for s in range(1, n_mem)
        ]

    def start(self):
        for copy in self.copies:
            copy.start()

    def wait_recv(self, s):
        self.copies[s - 1].wait_recv()

    def wait_send(self):
        for copy in self.copies:
            copy.wait_send()


class Share:
    def __init__(self, place, sems, src, block):
        send, recv = sems.take(4), sems.take(4)
        rows = src.shape[-2]
        half = rows // 2

        def part(ref, i):
            return ref.at[:, pl.ds(i * half, half)]

        self.first = [
            remote(src, block(0), send[t - 1], recv[t - 1], place.near(t)) for t in (1, 2)
        ]
        self.second = [
            remote(part(block(t), t - 1), part(block(t), t - 1), send[t + 1], recv[t + 1], place.near(3 - t))
            for t in (1, 2)
        ]

    def start(self):
        for copy in self.first:
            copy.start()

    def forward(self):
        for direct, onward in zip(self.first, self.second):
            direct.wait_recv()
            onward.start()

    def wait(self):
        for copy in self.first:
            copy.wait_send()
        for copy in self.second:
            copy.wait()


class Chain:
    def __init__(self, place, sems, block, n_mem):
        self.place, self.block, self.n = place, block, n_mem
        self.sems = {way: (sems.take(n_mem - 1), sems.take(n_mem - 1)) for way in (1, -1)}

    def copy(self, way, hops):
        mem = self.place.mem
        source = lax.rem(mem + jnp.int32(self.n - way * hops), jnp.int32(self.n))
        target = lax.rem(mem + jnp.int32(self.n + way), jnp.int32(self.n))
        send, recv = self.sems[way]
        piece = self.block(source)
        return remote(piece, piece, send[hops], recv[hops], (self.place.pb, target))

    def comes(self, way, hops):
        mem = self.place.mem
        return mem >= hops if way == 1 else mem + hops < self.n

    def goes(self, way, hops):
        mem = self.place.mem
        ahead = mem + 1 < self.n if way == 1 else mem >= 1
        return jnp.logical_and(ahead, self.comes(way, hops))

    def start(self):
        for way in (1, -1):

            @pl.when(self.goes(way, 0))
            def _():
                self.copy(way, 0).start()

    def relay(self, hops, arrived):
        for way in (1, -1):

            @pl.when(self.comes(way, hops))
            def _():
                self.copy(way, hops - 1).wait_recv()
                if hops < self.n - 1:

                    @pl.when(self.goes(way, hops))
                    def _():
                        self.copy(way, hops).start()

                arrived(hops if way == 1 else self.n - hops)

    def wait_send(self):
        for hops in range(self.n - 1):
            for way in (1, -1):

                @pl.when(self.goes(way, hops))
                def _():
                    self.copy(way, hops).wait_send()


class Gather:
    def __init__(self, place, sems, shard, full, columns, n_mem, in_plane=None):
        mem, quarter = place.mem, place.quarter
        self.n_mem = n_mem
        self.in_plane = tuple(range(1, n_mem)) if in_plane is None else in_plane
        self.own = Own(place, sems, shard, full, columns, n_mem)
        self.chain = Chain(place, sems, lambda i: full.at[:, i, quarter], n_mem)
        self.shares = {}
        for d in range(1, n_mem):
            if d not in self.in_plane and n_mem - d not in self.in_plane:
                continue
            source = lax.rem(mem + jnp.int32(n_mem - d), jnp.int32(n_mem))

            def block(t, source=source):
                return full.at[:, source, flip(quarter, t)]

            self.shares[d] = Share(place, sems, block(0), block)

    def begin(self):
        self.own.wait()
        self.chain.start()

    def share(self, hops):
        self.chain.relay(
            hops, lambda d: self.shares[d].start() if hops in self.in_plane else None
        )

    def forward(self, hops):
        for way, d in ((1, hops), (-1, self.n_mem - hops)):

            @pl.when(self.chain.comes(way, hops))
            def _():
                self.shares[d].forward()

    def finish(self):
        self.chain.wait_send()
        for hops in self.in_plane:
            for way, d in ((1, hops), (-1, self.n_mem - hops)):

                @pl.when(self.chain.comes(way, hops))
                def _():
                    self.shares[d].wait()


GATHER_SEMS = 44


def half_views(shard, columns, n_mem, plane):
    if columns:
        lead, depth, hidden = shard.shape
        part = depth // plane
        return shard.reshape(lead, plane, part, hidden), (lead, n_mem, plane, part, hidden // 2)
    depth, width = shard.shape
    part = depth // 2 // plane
    return shard.reshape(2, plane, part, width), (1, n_mem, plane, part, width)


class Walk:
    def __init__(self, refs):
        self.refs = list(refs)

    def take(self, count):
        out, self.refs = self.refs[:count], self.refs[count:]
        return out

    def one(self):
        return self.take(1)[0]


def softmax_units(units, finish, serve=None):
    def scores_of(unit, j):
        return unit[0][j]()

    ready = [scores_of(units[0], j) for j in range(len(units[0][0]))]
    for n, (_, values, tag) in enumerate(units):
        if serve is not None:
            serve(n)
        coming = list(range(len(units[n + 1][0]))) if n + 1 < len(units) else []
        following = []
        top = functools.reduce(
            jnp.maximum, [jnp.max(tile, axis=0, keepdims=True) for tile in ready]
        )
        total = jnp.zeros_like(top)
        acc = None
        share = -(-len(coming) // len(ready))
        for j, tile in enumerate(ready):
            for i in coming[j * share : (j + 1) * share]:
                following.append(scores_of(units[n + 1], i))
            probs = jnp.exp(tile - top)
            total += jnp.sum(probs, axis=0, keepdims=True)
            part = mm(values[j](), probs.astype(BF16))
            acc = part if acc is None else acc + part
        finish(tag, acc / total, top + jnp.log(total))
        ready = following


def self_attend(place, pair, q_vm, k_vm, v_vm, o_vm, lse_vm, v_t, o_t):
    base = 2 * place.core + place.parity
    count = q_vm.shape[0] // BLK
    lanes = pl.ds(pl.multiple_of(pair * 2 * HD, 2 * HD), 2 * HD)

    def rows(i):
        return pl.ds(pl.multiple_of(flip(base, i) * BLK, BLK), BLK)

    for j in range(count):
        v_t[:, j * BLK : (j + 1) * BLK] = v_vm[rows(j), lanes].T
    key_pos = lax.broadcasted_iota(jnp.int32, (BLK, BLK), 0)
    query_pos = lax.broadcasted_iota(jnp.int32, (BLK, BLK), 1)
    units = []
    for i in range(count):
        q_t = q_vm[rows(i), lanes].T
        for head in range(2):
            q_head = head_rows(q_t, head)

            def score(j, i=i, q_head=q_head):
                tile = mm(k_vm[rows(j), lanes], q_head)
                return jnp.where(key_pos <= query_pos, tile, -1000000000.0) if j == i else tile

            def value(j, head=head):
                return v_t[head * HD : (head + 1) * HD, j * BLK : (j + 1) * BLK]

            units.append(
                (
                    [functools.partial(score, j) for j in range(i + 1)],
                    [functools.partial(value, j) for j in range(i + 1)],
                    (i, head),
                )
            )

    def finish(tag, mixed, lse):
        i, head = tag
        span = slice(i * BLK, (i + 1) * BLK)
        o_t[head * HD : (head + 1) * HD, span] = mixed
        lse_vm[pair, head : head + 1, span] = lse

    softmax_units(units, finish)
    for i in range(count):
        o_vm[rows(i), lanes] = o_t[:, i * BLK : (i + 1) * BLK].T.astype(BF16)


def tiles(rows, step):
    def run(i, carry):
        step(pl.ds(pl.multiple_of(i * BLK, BLK), BLK))
        return carry

    lax.fori_loop(0, rows // BLK, run, 0)


def front_kernel(n_mem, plane, kinds, places, x_ref, enc_ref, map_ref, small_ref, *refs):
    refs = Walk(refs)
    count = len(kinds)
    shards = refs.take(count)
    x_out, enc_out, index_out, small_out = refs.take(4)
    halves = refs.take(count)
    kept = refs.take(11)
    x_vm, w_vm, so_vm, cq_w, small_vm = refs.take(5)
    q_vm, k_vm, v_vm, sa_vm, lse_vm, h1_vm, unit_vm, scale_vm, cq_vm = refs.take(9)
    k_all, v_all, v_t, o_t, part_vm, twin_vm, kv_w, enc_vm, map_in = refs.take(9)
    sems = Sems(refs.one())
    place = Place(plane)
    n_bias, n_gain = places
    rows = x_ref.shape[1]
    gathers = [
        Gather(place, sems, shard, half, columns, n_mem)
        for shard, half, columns in zip(shards, halves, kinds)
    ]
    spread = Spread(
        place,
        sems,
        lambda k: x_ref.at[flip(place.parity, k)],
        lambda k: x_out.at[pl.ds(rows * k, rows)],
    )
    twin_send, twin_recv = sems.take(2), sems.take(2)
    twin = [
        remote(
            x_out.at[pl.ds(rows * k, rows)],
            x_out.at[pl.ds(rows * (k + 2), rows)],
            twin_send[k],
            twin_recv[k],
            place.twin(),
        )
        for k in range(2)
    ]
    map_sems = sems.take(2)
    map_copy = remote(map_ref, map_in, map_sems[0], map_sems[1], place.twin())
    (small_sem,) = sems.take(1)
    small_own = pltpu.make_async_copy(small_ref, small_out.at[place.mem], small_sem)
    small_line = Line(
        place, sems, lambda s: small_ref, lambda s: small_out.at[place.mem], n_mem
    )
    units = enc_vm.shape[1]
    encs, enc_twins, enc_pairs, enc_onwards, enc_ends = [], [], [], [], []
    for u in range(units):
        encs.append(
            Spread(
                place, sems, lambda k, u=u: enc_ref.at[u], lambda k, u=u: enc_vm.at[0, u], kinds=(0,)
            )
        )
        pair_sems, twin_sems, end_sems = sems.take(2), sems.take(2), sems.take(2)
        enc_pairs.append(remote(enc_ref.at[u], enc_vm.at[1, u], *pair_sems, place.pair()))
        enc_onwards.append(remote(enc_vm.at[0, u], enc_vm.at[1, u], *pair_sems, place.pair()))
        enc_twins.append(remote(enc_vm.at[0, u], enc_vm.at[2, u], *twin_sems, place.twin()))
        enc_ends.append(remote(enc_vm.at[1, u], enc_vm.at[3, u], *end_sems, place.twin()))
    enc_keeps = [
        pltpu.make_async_copy(enc_vm.at[i], enc_out.at[i], sem) for i, sem in enumerate(sems.take(4))
    ]
    home = place.at_home()
    away = jnp.logical_not(home)
    loads = [
        pltpu.make_async_copy(src, dst, sem)
        for src, dst, sem in zip(
            (x_out, halves[0], halves[1], halves[2].at[0], small_out, halves[2].at[pl.ds(1, 2)]),
            (x_vm, w_vm, so_vm, cq_w, small_vm, kv_w),
            sems.take(6),
        )
    ]
    keeps = [
        pltpu.make_async_copy(src, dst, sem)
        for src, dst, sem in zip(
            (q_vm, k_vm, v_vm, sa_vm, lse_vm, h1_vm, unit_vm, scale_vm, cq_vm, k_all, v_all),
            kept,
            sems.take(11),
        )
    ]
    swap_sems = sems.take(4)
    own = 2 * rows
    swap_part = remote(part_vm, twin_vm, swap_sems[0], swap_sems[1], place.twin())
    swap_h1 = remote(
        h1_vm.at[pl.ds(0, own)], h1_vm.at[pl.ds(own, own)], swap_sems[2], swap_sems[3], place.twin()
    )

    for gather in gathers:
        gather.own.start()
    small_own.start()
    place.meet(column_peers(n_mem) + plane_peers(plane))
    for gather in gathers:
        gather.begin()
    small_line.start()
    map_copy.start()
    spread.start()
    for gather in gathers:
        gather.share(1)
    for gather in gathers:
        gather.share(2)
    gathers[0].forward(1)
    for k in range(2):
        spread.wait_recv(k)
        twin[k].start()
    for gather in gathers:
        gather.share(3)
    for u in range(units):
        encs[u].start()

        @pl.when(home)
        def _():
            enc_pairs[u].start()

    def first_arrival(u):
        encs[u].wait_recv(0)

        @pl.when(away)
        def _():
            enc_onwards[u].start()

        enc_twins[u].start()

    def second_arrival(u):
        @pl.when(home)
        def _():
            enc_pairs[u].wait()

        @pl.when(away)
        def _():
            enc_onwards[u].wait()

        enc_ends[u].start()

    for hops in (2, 3):
        gathers[0].forward(hops)
    for hops in (1, 2, 3):
        for gather in gathers[1:]:
            gather.forward(hops)
    for copy in twin:
        copy.wait_recv()
    small_own.wait()
    for s in range(1, n_mem):
        small_line.wait_recv(s)
    gathers[0].finish()
    for copy in (loads[0], loads[1], loads[4]):
        copy.start()
    for copy in (loads[0], loads[1], loads[4]):
        copy.wait()

    def half_row(row):
        lanes = pl.ds(pl.multiple_of(place.core * 2 * HD, 2 * HD), 2 * HD)
        return jnp.concatenate(
            [small_vm[b, :, lanes].astype(F32)[row : row + 1] for b in range(n_mem)], axis=1
        )

    def full_row(row):
        return jnp.concatenate(
            [small_vm[b].astype(F32)[row : row + 1] for b in range(n_mem)], axis=1
        )

    bias_q, bias_v = half_row(0), half_row(1)
    depth = x_vm.shape[1]

    def weight(ref):
        return ref[...].reshape(-1, ref.shape[-1])

    def project(span):
        x_tile = x_vm[span, :]
        q_vm[span, :] = ((mm(x_tile, weight(w_vm.at[0])) + bias_q) * 0.125).astype(BF16)
        k_vm[span, :] = mm(x_tile, weight(w_vm.at[1])).astype(BF16)
        v_vm[span, :] = (mm(x_tile, weight(w_vm.at[2])) + bias_v).astype(BF16)

    tiles(x_vm.shape[0], project)
    for copy in keeps[:3]:
        copy.start()
    pairs = q_vm.shape[1] // (2 * HD)
    for pair in range(pairs):
        self_attend(place, pair, q_vm, k_vm, v_vm, sa_vm, lse_vm, v_t, o_t)
        if pair in (0, pairs // 2):
            first_arrival(min(pair, 1))
    for copy in keeps[3:5]:
        copy.start()
    for gather in gathers[1:]:
        gather.finish()
    for copy in (loads[2], loads[3], loads[5]):
        copy.start()
    for copy in (loads[2], loads[3], loads[5]):
        copy.wait()

    def other_part(span):
        part_vm[span, :] = mm(
            sa_vm[pl.ds(pl.multiple_of(span.start + own, BLK), BLK), :], weight(so_vm)
        ).astype(BF16)

    tiles(own, other_part)
    swap_part.start()

    def own_part(span):
        unit_vm[span, :] = mm(sa_vm[span, :], weight(so_vm)) + x_vm[span, :].astype(F32)

    tiles(own, own_part)
    for u in range(2, units):
        first_arrival(u)
    bias_out = full_row(2)
    gain, shift = full_row(n_bias), full_row(6)
    swap_part.wait()

    def normalise(span):
        values = unit_vm[span, :] + twin_vm[span, :].astype(F32) + bias_out
        centre = values - jnp.mean(values, axis=-1, keepdims=True)
        scale = lax.rsqrt(jnp.mean(centre * centre, axis=-1, keepdims=True) + 1e-05)
        unit = centre * scale
        unit_vm[span, :] = unit
        scale_vm[span, :] = jnp.broadcast_to(scale, (BLK, scale_vm.shape[1]))
        h1_vm[span, :] = (unit * gain + shift).astype(BF16)

    tiles(own, normalise)
    swap_h1.start()
    for copy in keeps[6:8]:
        copy.start()
    bias_cq = half_row(3)

    def queries(span):
        cq_vm[span, :] = ((mm(h1_vm[span, :], weight(cq_w)) + bias_cq) * 0.125).astype(BF16)

    tiles(own, queries)
    swap_h1.wait()
    keeps[5].start()

    def other_queries(span):
        queries(pl.ds(pl.multiple_of(span.start + own, BLK), BLK))

    tiles(own, other_queries)
    keeps[8].start()

    map_copy.wait()
    near_map, far_map = map_ref[...], map_in[...]
    both_maps = jnp.where(home, near_map, far_map)
    mine = jnp.where(place.parity == 0, both_maps[:1], both_maps[1:])
    group = lax.div(mine, jnp.full_like(mine, units))
    index_out[...] = (group ^ (2 * place.core + place.parity)) * units + lax.rem(
        mine, jnp.full_like(mine, units)
    )

    bias_cv = half_row(4)

    def memory(block, u):
        rows_here = enc_vm[block, u]
        k_all[block * units + u] = mm(rows_here, weight(kv_w.at[0])).astype(BF16)
        v_all[block * units + u] = (mm(rows_here, weight(kv_w.at[1])) + bias_cv).astype(BF16)

    for u in range(units):
        second_arrival(u)
        memory(0, u)
    enc_keeps[0].start()
    enc_keeps[1].start()
    for block, copies in ((2, enc_twins), (1, None), (3, enc_ends)):
        for u in range(units):
            if copies is not None:
                copies[u].wait_recv()
            memory(block, u)
    enc_keeps[2].start()
    enc_keeps[3].start()
    for copy in keeps[9:]:
        copy.start()
    spread.wait_send()
    for copy in twin:
        copy.wait_send()
    small_line.wait_send()
    for item in encs:
        item.wait_send()
    for copy in enc_twins + enc_ends:
        copy.wait_send()
    for copy in keeps + enc_keeps:
        copy.wait()


def front(n_mem, plane, places, hidden_in, enc, passage_map, small, params):
    kinds = tuple(columns for _, columns in params)
    views = [half_views(shard, columns, n_mem, plane) for shard, columns in params]
    seg, width = hidden_in.shape[1:]
    rows, own = 4 * seg, 2 * seg
    part = width // 2
    pairs = part // (2 * HD)
    passages = 4 * enc.shape[0]
    shapes = (
        [((rows, width), BF16), ((4,) + enc.shape, BF16), ((1, passage_map.shape[1]), jnp.int32)]
        + [((n_mem,) + small.shape, BF16)]
        + [(full, BF16) for _, full in views]
    )
    kept = [
        ((rows, part), BF16),
        ((rows, part), BF16),
        ((rows, part), BF16),
        ((rows, part), BF16),
        ((pairs, 2, rows), F32),
        ((rows, width), BF16),
        ((own, width), F32),
        ((own, 2 * HD), F32),
        ((rows, part), BF16),
        ((passages, PLEN, part), BF16),
        ((passages, PLEN, part), BF16),
    ]
    scratch = [
        ((rows, width), BF16),
        (views[0][1], BF16),
        (views[1][1][1:], BF16),
        (views[2][1][1:], BF16),
        ((n_mem,) + small.shape, BF16),
    ] + kept + [
        ((2 * HD, rows), BF16),
        ((2 * HD, rows), F32),
        ((own, width), BF16),
        ((own, width), BF16),
        ((2,) + views[2][1][1:], BF16),
        ((4,) + enc.shape, BF16),
        (passage_map.shape, jnp.int32),
    ]
    scratch[2] = (views[1][1], BF16)
    outs = pl.pallas_call(
        functools.partial(front_kernel, n_mem, plane, kinds, places),
        in_specs=[VMEM] * (4 + len(params)),
        out_specs=[ANY, ANY, VMEM] + [ANY] * (len(shapes) + len(kept) - 3),
        out_shape=[jax.ShapeDtypeStruct(*item) for item in shapes + kept],
        scratch_shapes=[pltpu.VMEM(*item) for item in scratch]
        + [pltpu.SemaphoreType.DMA((90 + GATHER_SEMS * len(params),))],
        compiler_params=pltpu.CompilerParams(
            collective_id=0, has_side_effects=True, vmem_limit_bytes=60 * 2**20
        ),
        cost_estimate=pl.CostEstimate(
            flops=rows * width * part * 10, bytes_accessed=40 * 2**20, transcendentals=rows * rows * 8
        ),
        name="front",
    )(hidden_in, enc, passage_map, small, *[view for view, _ in views])
    count = 4 + len(params)
    return outs[:4], outs[4:count], outs[count:]


class PlaneSum:
    def __init__(self, place, sems, grad, own, bufs, rows, lanes=None):
        self.own = own
        self.from_near, self.via, self.add = bufs
        quarter = place.quarter
        first, count = rows
        half = count // 2
        self.lead, self.n_mem = own.shape[:2]
        lanes = pl.ds(*(lanes or (0, grad.shape[-1])))

        def piece(t, lo, size):
            return grad.at[:, :, flip(quarter, t), pl.ds(first + lo, size), lanes]

        loads = sems.take(3)
        self.loads = [pltpu.make_async_copy(piece(0, 0, count), own, loads[0])]
        send, recv = sems.take(6), sems.take(6)
        self.onward, self.direct, self.summed = [], [], []
        for t in (1, 2):
            lo = (t - 1) * half
            self.onward.append(
                remote(piece(3, lo, half), self.via.at[t - 1], send[t - 1], recv[t - 1], place.near(t))
            )
            self.direct.append(
                remote(
                    piece(t, lo, half),
                    self.from_near.at[t - 1, :, :, pl.ds(lo, half)],
                    send[t + 1],
                    recv[t + 1],
                    place.near(t),
                )
            )
            other = half - lo
            self.loads.append(
                pltpu.make_async_copy(piece(t, other, half), self.add.at[t - 1], loads[t])
            )
            self.summed.append(
                remote(
                    self.add.at[t - 1],
                    self.from_near.at[t - 1, :, :, pl.ds(other, half)],
                    send[t + 3],
                    recv[t + 3],
                    place.near(t),
                )
            )

    def start(self):
        for copy in self.onward + self.loads + self.direct:
            copy.start()

    def each(self, step):
        def run(i, carry):
            step(lax.div(i, jnp.int32(self.n_mem)), lax.rem(i, jnp.int32(self.n_mem)))
            return carry

        lax.fori_loop(0, self.lead * self.n_mem, run, 0)

    def middle(self):
        for copy in self.loads:
            copy.wait()
        for t in (1, 2):
            self.onward[2 - t].wait_recv()

            def add(l, m, t=t):
                total = self.add[t - 1, l, m].astype(F32) + self.via[2 - t, l, m].astype(F32)
                self.add[t - 1, l, m] = total.astype(BF16)

            self.each(add)
            self.summed[t - 1].start()

    def end(self):
        for copy in self.direct + self.summed:
            copy.wait_recv()

        def add(l, m):
            total = self.own[l, m].astype(F32)
            for t in range(2):
                total += self.from_near[t, l, m].astype(F32)
            self.own[l, m] = total.astype(BF16)

        self.each(add)

    def wait_send(self):
        for copy in self.onward + self.direct + self.summed:
            copy.wait_send()


class Settle:
    def __init__(self, place, sems, own, out, bufs, columns, n_mem, rows, lane=0):
        self.place, self.n_mem, self.columns, self.rows = place, n_mem, columns, rows
        self.lane = lane
        self.own, self.out = own, out
        self.line_in, self.far_in, self.slots = bufs
        quarter, mem, core = place.quarter, place.mem, place.core
        slots = self.slots

        def slot(t):
            return slots.at[flip(quarter, t), core]

        self.line = Line(
            place, sems, lambda s: own.at[:, flip(mem, s)], lambda s: self.line_in.at[s - 1], n_mem
        )
        others = place.planes - 1
        far_send, far_recv = sems.take(others), sems.take(others)
        self.far = [
            remote(slot(0), self.far_in.at[r - 1], far_send[r - 1], far_recv[r - 1], place.far(r))
            for r in range(1, place.planes)
        ]
        self.share = Share(place, sems, slot(0), slot)
        twin_send, twin_recv = sems.take(place.plane), sems.take(place.plane)
        self.twin = [
            remote(slot(t), slot(t), twin_send[t], twin_recv[t], place.twin())
            for t in range(place.plane)
        ]

    def start(self):
        self.line.start()

    def middle(self):
        for s in range(1, self.n_mem):
            self.line.wait_recv(s)
        quarter, core, mem = self.place.quarter, self.place.core, self.place.mem
        lead = self.own.shape[0]
        for l in range(lead):
            total = self.own[l, mem].astype(F32)
            for s in range(self.n_mem - 1):
                total += self.line_in[s, l].astype(F32)
            self.slots[quarter, core, l] = total.astype(BF16)
        if self.far:
            for copy in self.far:
                copy.start()
            for copy in self.far:
                copy.wait()
            for l in range(lead):
                total = self.slots[quarter, core, l].astype(F32)
                for r in range(len(self.far)):
                    total += self.far_in[r, l].astype(F32)
                self.slots[quarter, core, l] = total.astype(BF16)
        self.share.start()
        self.twin[0].start()

    def forward(self):
        self.share.forward()
        self.twin[1].start()
        self.twin[2].start()

    def end(self):
        self.share.wait()
        self.twin[3].start()
        for copy in self.twin:
            copy.wait()
        self.line.wait_send()
        lead = self.own.shape[0]
        wide = self.slots.shape[-1]
        first, count = self.rows
        for q in range(self.place.plane):
            for c in range(2):
                for l in range(lead):
                    if self.columns:
                        unit = self.out.shape[-1] // (2 * self.n_mem)
                        for b in range(wide // unit):
                            start = unit * (2 * (self.lane // unit + b) + c)
                            self.out[l, q, first : first + count, start : start + unit] = self.slots[
                                q, c, l, :, b * unit : (b + 1) * unit
                            ]
                    else:
                        self.out[c, q, first : first + count] = self.slots[q, c, l]


PLANE_SUM_SEMS = 15


def settle_sems(n_mem, plane, planes):
    return 2 * (n_mem - 1) + 2 * (planes - 1) + 8 + 2 * plane


def plane_sum_scratch(grad_shape, n_mem, count, cols=None):
    lead, cols = grad_shape[0], cols or grad_shape[-1]
    return [
        pltpu.VMEM((2, lead, n_mem, count, cols), BF16),
        pltpu.VMEM((2, lead, n_mem, count // 2, cols), BF16),
        pltpu.VMEM((2, lead, n_mem, count // 2, cols), BF16),
    ]


def settle_scratch(grad_shape, n_mem, plane, planes, count, cols=None):
    lead, cols = grad_shape[0], cols or grad_shape[-1]
    return [
        pltpu.VMEM((n_mem - 1, lead, count, cols), BF16),
        pltpu.VMEM((max(planes - 1, 1), lead, count, cols), BF16),
        pltpu.VMEM((plane, 2, lead, count, cols), BF16),
    ]


def sum_shape(grad_shape):
    lead, n_mem, _, rows, cols = grad_shape
    return jax.ShapeDtypeStruct((lead, n_mem, rows, cols), BF16)


def reduce_out(grad_shape, columns, plane):
    lead, _, _, rows, cols = grad_shape
    shape = (lead, plane, rows, 2 * cols) if columns else (2, plane, rows, cols)
    return jax.ShapeDtypeStruct(shape, BF16)


def reduce_peers(n_mem, plane, planes):
    return (
        [(1, 0)]
        + [(0, s) for s in range(1, n_mem)]
        + plane_peers(plane)
        + [(2 * plane * r, 0) for r in range(1, planes)]
    )


def whole(shape):
    return pl.BlockSpec(shape, lambda *grid: (0,) * len(shape))


class Fetch:
    def __init__(self, sems, src, dst):
        self.copy = pltpu.make_async_copy(src, dst, sems.take(1)[0])
        self.dst = dst
        self.here = False

    def start(self):
        self.copy.start()

    def get(self):
        if not self.here:
            self.copy.wait()
            self.here = True
        return self.dst


def unit_norm(values):
    centre = values - jnp.mean(values, axis=-1, keepdims=True)
    scale = lax.rsqrt(jnp.mean(centre * centre, axis=-1, keepdims=True) + 1e-05)
    return centre * scale, scale


def unit_norm_back(grad, unit, scale, gain):
    inner = grad * gain
    return (
        inner
        - jnp.mean(inner, axis=-1, keepdims=True)
        - unit * jnp.mean(inner * unit, axis=-1, keepdims=True)
    ) * scale


def feed_kernel(n_mem, plane, cot_ref, rows_ref, bias_ref, *refs):
    refs = Walk(refs)
    fetched = refs.take(4)
    out_part = refs.one()
    final_out, dca_ref, dz2_ref, sums_ref, bias_sum, own_out, dw_in, dw_co, dw_out = refs.take(9)
    kept = refs.take(4)
    out_w = refs.one()
    cot_vm, h2_vm, unit_vm, scale_vm, act_vm, slope_vm, p_vm, part_vm, twin_vm = refs.take(9)
    final_vm, df_vm, dco_vm = refs.take(3)
    bufs = refs.take(3)
    sems = Sems(refs.one())
    place = Place(plane)
    ca, unit1, w_co, w_in = [Fetch(sems, src, dst) for src, dst in zip(fetched, kept)]
    mem, quarter = place.mem, place.quarter
    own_piece = Fetch(sems, out_part.at[0, mem], out_w.at[0, mem])
    pieces = []
    for d in range(1, n_mem):
        source = lax.rem(mem + jnp.int32(n_mem - d), jnp.int32(n_mem))

        def place_of(t, source=source):
            return out_w.at[:, source, flip(quarter, t)]

        (sem,) = sems.take(1)
        pieces.append(
            (
                mem < d if d == 1 else mem >= (d if d == n_mem - 1 else 0),
                pltpu.make_async_copy(out_part.at[0, source], out_w.at[0, source], sem),
                pltpu.make_async_copy(out_part.at[:, source, quarter], place_of(0), sem),
                Share(place, sems, place_of(0), place_of),
            )
        )

    def each_piece(whole_step, part_step):
        for part, whole_copy, part_copy, share in pieces:
            if whole_step is not None:

                @pl.when(jnp.logical_not(part))
                def _():
                    whole_step(whole_copy)

            @pl.when(part)
            def _():
                part_step(part_copy, share)

    rows = h2_vm.shape[0]
    own = rows // 2
    seg = own // 2
    hidden = act_vm.shape[1]
    block = hidden // n_mem
    out_sum = PlaneSum(place, sems, dw_out, own_out, bufs, (0, own_out.shape[2]))
    spread_cot = Spread(
        place,
        sems,
        lambda k: cot_ref.at[flip(place.parity, k)],
        lambda k: cot_vm.at[pl.ds(seg * k, seg)],
    )
    spread_final = Spread(
        place,
        sems,
        lambda k: final_vm.at[pl.ds(seg * k, seg)],
        lambda k: final_out.at[place.parity],
    )

    def swap(src, dst):
        send, recv = sems.take(2)
        return remote(src, dst, send, recv, place.twin())

    def half_lanes(ref, i):
        wide = ref.shape[1] // 2
        return ref.at[:, pl.ds(i * wide, wide)]

    swap_co = swap(part_vm, twin_vm)
    swap_h2 = swap(h2_vm.at[pl.ds(0, own)], h2_vm.at[pl.ds(own, own)])
    swap_ffn = [swap(half_lanes(part_vm, i), half_lanes(twin_vm, i)) for i in range(2)]
    swap_df = swap(df_vm.at[pl.ds(0, own)], df_vm.at[pl.ds(own, own)])
    swap_dh2 = [swap(half_lanes(part_vm, i), half_lanes(twin_vm, i)) for i in range(2)]
    swap_dco = swap(dco_vm.at[pl.ds(0, own)], dco_vm.at[pl.ds(own, own)])

    for item in (ca, w_co, own_piece):
        item.start()
    each_piece(lambda copy: copy.start(), lambda copy, share: copy.start())
    for item in (unit1, w_in):
        item.start()
    place.meet(column_peers(n_mem) + plane_peers(plane))
    spread_cot.start()

    def share_start(copy, share):
        copy.wait()
        share.start()

    each_piece(None, share_start)
    row = {name: rows_ref[i : i + 1, :] for i, name in enumerate(("g0", "b6", "b5", "g1", "b7", "b9", "g2", "b8"))}
    sums_ref[...] = jnp.zeros_like(sums_ref)
    bias_sum[...] = jnp.zeros_like(bias_sum)

    def after(span):
        return pl.ds(pl.multiple_of(span.start + own, BLK), BLK)

    ca, w_co = ca.get(), w_co.get()

    def co_other(span):
        part_vm[span, :] = mm(ca[after(span), :], w_co[...]).astype(BF16)

    tiles(own, co_other)
    swap_co.start()
    unit1 = unit1.get()

    def co_own(span):
        p_vm[span, :] = unit1[span, :] * row["g0"] + row["b6"] + mm(ca[span, :], w_co[...])

    tiles(own, co_own)
    swap_co.wait()

    def second_norm(span):
        values = p_vm[span, :] + twin_vm[span, :].astype(F32) + row["b5"]
        unit, scale = unit_norm(values)
        unit_vm[span, :] = unit
        scale_vm[span, :] = jnp.broadcast_to(scale, (BLK, scale_vm.shape[1]))
        h2_vm[span, :] = (unit * row["g1"] + row["b7"]).astype(BF16)

    tiles(own, second_norm)
    swap_h2.start()
    w_in = w_in.get()

    def forward(span):
        def part(i, carry):
            lanes = pl.ds(pl.multiple_of(i * block, block), block)
            pre = mm(h2_vm[span, :], w_in[:, lanes]) + bias_ref[:, lanes]
            cdf = 0.5 * (1.0 + lax.erf(pre * 0.7071067811865476))
            act_vm[span, lanes] = (pre * cdf).astype(BF16)
            density = jnp.exp(-0.5 * pre * pre) * 0.3989422804014327
            slope_vm[span, lanes] = (cdf + pre * density).astype(BF16)
            return carry

        lax.fori_loop(0, n_mem, part, 0)

    ours, others = pl.ds(0, own), pl.ds(own, own)
    width = h2_vm.shape[1]
    column = width // 2
    each_piece(None, lambda copy, share: share.forward())
    forward(ours)
    swap_h2.wait()
    forward(others)
    own_piece.get()
    each_piece(lambda copy: copy.wait(), lambda copy, share: share.wait())
    for i in range(2):
        lanes = slice(i * column, (i + 1) * column)
        weights = out_w[0, :, :, :, lanes].reshape(hidden, column)
        part_vm[:, lanes] = mm(act_vm[others, :], weights).astype(BF16)
        swap_ffn[i].start()
    p_vm[...] = mm(act_vm[ours, :], out_w[0].reshape(hidden, width))
    for k in range(2):
        spread_cot.wait_recv(k)
    for copy in swap_ffn:
        copy.wait()

    def third_norm(span):
        values = (
            unit_vm[span, :] * row["g1"]
            + row["b7"]
            + p_vm[span, :]
            + twin_vm[span, :].astype(F32)
            + row["b9"]
        )
        unit, scale = unit_norm(values)
        final_vm[span, :] = (unit * row["g2"] + row["b8"]).astype(BF16)
        grad = cot_vm[span, :].astype(F32)
        out = unit_norm_back(grad, unit, scale, row["g2"])
        dz2_ref[span, :] = out
        low = out.astype(BF16)
        df_vm[span, :] = low
        sums_ref[0:1, :] += jnp.sum(grad * unit, axis=0, keepdims=True)
        sums_ref[1:2, :] += jnp.sum(grad, axis=0, keepdims=True)
        sums_ref[2:3, :] += jnp.sum(low.astype(F32), axis=0, keepdims=True)

    tiles(own, third_norm)
    swap_df.start()
    spread_final.start()
    swap_df.wait()

    def out_weights(m, carry):
        lanes = pl.ds(pl.multiple_of(m * block, block), block)
        dw_out[0, m] = mm(act_vm[:, lanes].T, df_vm[...]).astype(BF16).reshape(dw_out.shape[2:])
        return carry

    lax.fori_loop(0, n_mem, out_weights, 0)
    out_sum.start()

    def hidden_grad(i, carry):
        lanes = pl.ds(pl.multiple_of(i * block, block), block)
        weights = out_w[0, i].reshape(block, width)
        grad = mm(df_vm[...], weights, NT) * slope_vm[:, lanes].astype(F32)
        low = grad.astype(BF16)
        slope_vm[:, lanes] = low
        bias_sum[:, lanes] = jnp.sum(low.astype(F32), axis=0, keepdims=True)
        return carry

    lax.fori_loop(0, n_mem, hidden_grad, 0)
    narrow = width // 4
    for i in range(2):
        for j in (2 * i, 2 * i + 1):
            lanes = slice(j * narrow, (j + 1) * narrow)
            grad = mm(slope_vm[...], w_in[lanes, :], NT)
            part_vm[:, lanes] = grad[own:].astype(BF16)
            dz2_ref[:, lanes] += grad[:own]
        swap_dh2[i].start()
    out_sum.middle()
    for copy in swap_dh2:
        copy.wait()

    def second_back(span):
        grad = dz2_ref[span, :] + twin_vm[span, :].astype(F32)
        unit = unit_vm[span, :]
        out = unit_norm_back(grad, unit, scale_vm[span, :1], row["g1"])
        dz2_ref[span, :] = out
        low = out.astype(BF16)
        dco_vm[span, :] = low
        sums_ref[3:4, :] += jnp.sum(grad * unit, axis=0, keepdims=True)
        sums_ref[4:5, :] += jnp.sum(grad, axis=0, keepdims=True)
        sums_ref[5:6, :] += jnp.sum(low.astype(F32), axis=0, keepdims=True)

    tiles(own, second_back)
    swap_dco.start()
    depth = h2_vm.shape[1] // n_mem

    def in_weights(m, carry):
        lanes = pl.ds(pl.multiple_of(m * depth, depth), depth)
        dw_in[0, m] = mm(h2_vm[:, lanes].T, slope_vm[...]).astype(BF16).reshape(dw_in.shape[2:])
        return carry

    lax.fori_loop(0, n_mem, in_weights, 0)
    swap_dco.wait()

    dca_ref[...] = mm(dco_vm[...], w_co[...], NT).astype(BF16)
    heads = ca.shape[1] // n_mem

    def co_weights(m, carry):
        lanes = pl.ds(pl.multiple_of(m * heads, heads), heads)
        dw_co[0, m] = mm(ca[:, lanes].T, dco_vm[...]).astype(BF16).reshape(dw_co.shape[2:])
        return carry

    lax.fori_loop(0, n_mem, co_weights, 0)
    out_sum.end()
    out_sum.wait_send()
    spread_cot.wait_send()
    for k in range(2):
        spread_final.wait_recv(k)
    spread_final.wait_send()


def feed(n_mem, plane, cotangent, vectors, bias, ca, unit1, w_co, w_in, w_out):
    rows, part = ca.shape
    width, hidden = w_in.shape
    own = rows // 2

    def grad_shape(depth, cols):
        return (1, n_mem, plane, depth // (n_mem * plane), cols)

    out_shape, in_shape = grad_shape(hidden, width), grad_shape(width, hidden)
    shapes = [
        jax.ShapeDtypeStruct((2, own // 2, width), BF16),
        jax.ShapeDtypeStruct((rows, part), BF16),
        jax.ShapeDtypeStruct((own, width), F32),
        jax.ShapeDtypeStruct((8, width), F32),
        jax.ShapeDtypeStruct((1, hidden), F32),
        jax.ShapeDtypeStruct((1, n_mem, out_shape[3] // 2, width), BF16),
        jax.ShapeDtypeStruct(in_shape, BF16),
        jax.ShapeDtypeStruct(grad_shape(part, width), BF16),
        jax.ShapeDtypeStruct(out_shape, BF16),
    ]
    fetched = [ca, unit1, w_co, w_in, w_out]
    scratch = [pltpu.VMEM(item.shape, item.dtype) for item in fetched] + [
        pltpu.VMEM((own, width), BF16),
        pltpu.VMEM((rows, width), BF16),
        pltpu.VMEM((own, width), F32),
        pltpu.VMEM((own, 2 * HD), F32),
        pltpu.VMEM((rows, hidden), BF16),
        pltpu.VMEM((rows, hidden), BF16),
        pltpu.VMEM((own, width), F32),
        pltpu.VMEM((own, width), BF16),
        pltpu.VMEM((own, width), BF16),
        pltpu.VMEM((own, width), BF16),
        pltpu.VMEM((rows, width), BF16),
        pltpu.VMEM((rows, width), BF16),
    ]
    scratch += plane_sum_scratch(out_shape, n_mem, out_shape[3] // 2)
    scratch += [pltpu.SemaphoreType.DMA((PLANE_SUM_SEMS + 60,))]
    return pl.pallas_call(
        functools.partial(feed_kernel, n_mem, plane),
        in_specs=[VMEM] * 3 + [ANY] * len(fetched),
        out_specs=[ANY] + [VMEM] * (len(shapes) - 1),
        out_shape=shapes,
        scratch_shapes=scratch,
        compiler_params=pltpu.CompilerParams(
            vmem_limit_bytes=60 * 2**20, collective_id=1, has_side_effects=True
        ),
        cost_estimate=pl.CostEstimate(
            flops=rows * width * hidden * 12, bytes_accessed=40 * 2**20, transcendentals=rows * hidden * 2
        ),
        name="feed",
    )(cotangent, vectors, bias, *fetched)


def middle_kernel(n_mem, plane, planes, settled, slot_ref, member_ref, index_ref, *refs):
    refs = Walk(refs)
    dq_ref, dk_ref, dv_ref, wc_ref, scale_ref, gain_ref = refs.take(6)
    fetched = refs.take(6)
    ready = refs.take(len(settled))
    dsa_ref, dz1_ref, sums_ref, enc_out, own_cross, own_so = refs.take(6)
    outs = refs.take(len(settled))
    kept = refs.take(6)
    wk_t, wv_t, named_ref = refs.take(3)
    theirs, mine, twin_in, pair_in, dw_cross, dw_so, part_vm, twin_vm, dso_vm = refs.take(9)
    cross_bufs, so_bufs = refs.take(3), refs.take(3)
    settle_bufs = [refs.take(3) for _ in settled]
    sems = Sems(refs.one())
    place = Place(plane, planes)
    fetches = [Fetch(sems, src, dst) for src, dst in zip(fetched, kept)]
    h1_ref, enc_ref, dz2_ref, unit_ref, so_ref, sa_ref = kept
    settles = [
        Settle(
            place, sems, ready[i], outs[i], settle_bufs[i], columns, n_mem, (0, ready[i].shape[2])
        )
        for i, columns in enumerate(settled)
    ]
    cross_sum = PlaneSum(place, sems, dw_cross, own_cross, cross_bufs, (0, dw_cross.shape[3]))
    so_sum = PlaneSum(place, sems, dw_so, own_so, so_bufs, (0, dw_so.shape[3]))
    passages = mine.shape[0]
    units = passages // 2
    twin_sems = sems.take(2 * passages)
    twins = [
        remote(theirs.at[u], twin_in.at[u], twin_sems[2 * u], twin_sems[2 * u + 1], place.twin())
        for u in range(passages)
    ]
    pair_sems = sems.take(2 * units)
    pairs = [
        remote(
            mine.at[units + u], pair_in.at[u], pair_sems[2 * u], pair_sems[2 * u + 1], place.pair()
        )
        for u in range(units)
    ]
    homes = [
        Spread(place, sems, lambda k, u=u: mine.at[u], lambda k, u=u: enc_out.at[u], kinds=(0,))
        for u in range(units)
    ]
    swap_sems = sems.take(4)
    own = dz2_ref.shape[0]
    swap_part = remote(part_vm, twin_vm, swap_sems[0], swap_sems[1], place.twin())
    swap_dso = remote(
        dso_vm.at[pl.ds(0, own)], dso_vm.at[pl.ds(own, own)], swap_sems[2], swap_sems[3], place.twin()
    )

    for item in fetches:
        item.start()
    wk_t[...] = wc_ref[1].T
    wv_t[...] = wc_ref[2].T
    place.meet(
        column_peers(n_mem) + plane_peers(plane) + [(2 * plane * r, 0) for r in range(1, planes)]
    )
    for item in settles:
        item.start()

    def passage_grad(u):
        slot = slot_ref[u]
        value = mm(dk_ref[slot], wk_t[...]) + mm(dv_ref[slot], wv_t[...])
        return (value * member_ref[u]).astype(BF16)

    def add_twin(u):
        twins[u].wait_recv()

        def add(i, carry):
            span = pl.ds(pl.multiple_of(i * 64, 64), 64)
            total = mine[u, span, :].astype(F32) + twin_in[u, span, :].astype(F32)
            mine[u, span, :] = total.astype(BF16)
            return carry

        lax.fori_loop(0, PLEN // 64, add, 0)

    def send_home(u):
        add_twin(u)
        pairs[u].wait_recv()

        def add(i, carry):
            span = pl.ds(pl.multiple_of(i * 64, 64), 64)
            total = mine[u, span, :].astype(F32) + pair_in[u, span, :].astype(F32)
            mine[u, span, :] = total.astype(BF16)
            return carry

        lax.fori_loop(0, PLEN // 64, add, 0)
        homes[u].start()

    for group in (range(units, passages), range(units)):
        for u in group:
            theirs[u] = passage_grad(passages + u)
            twins[u].start()
        for u in group:
            mine[u] = passage_grad(u)
        if group.start:
            for u in group:
                add_twin(u)
                pairs[u - units].start()

    for item in fetches:
        item.get()
    for j in range(index_ref.shape[0]):
        named_ref[j * PLEN : (j + 1) * PLEN, :] = enc_ref[index_ref[j]]

    part = dw_cross.shape[-1]
    depth = h1_ref.shape[1] // n_mem

    def stacked(ref):
        return ref[...].reshape(-1, ref.shape[-1])

    def cross_weights(m, carry):
        lanes = pl.ds(pl.multiple_of(m * depth, depth), depth)
        split = dw_cross.shape[2:]
        dw_cross[0, m] = (
            (mm(h1_ref[:, lanes].T, dq_ref[...]) * 0.125).astype(BF16).reshape(split)
        )
        named_t = named_ref[:, lanes].T
        dw_cross[1, m] = mm(named_t, stacked(dk_ref)).astype(BF16).reshape(split)
        dw_cross[2, m] = mm(named_t, stacked(dv_ref)).astype(BF16).reshape(split)
        return carry

    lax.fori_loop(0, n_mem // 2, cross_weights, 0)
    send_home(0)
    lax.fori_loop(n_mem // 2, n_mem, cross_weights, 0)
    cross_sum.start()

    part_vm[...] = (mm(dq_ref[own:, :], wc_ref[0], NT) * 0.125).astype(BF16)
    swap_part.start()
    dz1_ref[...] = dz2_ref[...] + mm(dq_ref[:own, :], wc_ref[0], NT) * 0.125
    sums_ref[...] = jnp.zeros_like(sums_ref)
    sums_ref[3:4, :part] = 0.125 * jnp.sum(dq_ref[...].astype(F32), axis=0, keepdims=True)
    sums_ref[4:5, :part] = jnp.sum(stacked(dv_ref).astype(F32), axis=0, keepdims=True)
    send_home(1)
    swap_part.wait()
    gain = gain_ref[...]

    def norm(span):
        grad = dz1_ref[span, :] + twin_vm[span, :].astype(F32)
        unit = unit_ref[span, :]
        inner = grad * gain
        out = (
            inner
            - jnp.mean(inner, axis=-1, keepdims=True)
            - unit * jnp.mean(inner * unit, axis=-1, keepdims=True)
        ) * scale_ref[span, :1]
        dz1_ref[span, :] = out
        low = out.astype(BF16)
        dso_vm[span, :] = low
        sums_ref[0:1, :] += jnp.sum(grad * unit, axis=0, keepdims=True)
        sums_ref[1:2, :] += jnp.sum(grad, axis=0, keepdims=True)
        sums_ref[2:3, :] += jnp.sum(low.astype(F32), axis=0, keepdims=True)

    tiles(own, norm)
    swap_dso.start()
    cross_sum.middle()

    dsa_ref[:own, :] = mm(dso_vm[:own, :], so_ref[...], NT).astype(BF16)
    for u in range(2, units):
        send_home(u)
    swap_dso.wait()
    dsa_ref[own:, :] = mm(dso_vm[own:, :], so_ref[...], NT).astype(BF16)
    block = sa_ref.shape[1] // n_mem

    def so_weights(m, carry):
        lanes = pl.ds(pl.multiple_of(m * block, block), block)
        dw_so[0, m] = (
            mm(sa_ref[:, lanes].T, dso_vm[...]).astype(BF16).reshape(dw_so.shape[2:])
        )
        return carry

    lax.fori_loop(0, n_mem, so_weights, 0)
    so_sum.start()
    for item in settles:
        item.middle()
    cross_sum.end()
    for item in settles:
        item.forward()
    so_sum.middle()
    for item in settles:
        item.end()
    so_sum.end()
    cross_sum.wait_send()
    so_sum.wait_send()
    for copy in twins + pairs:
        copy.wait_send()
    for item in homes:
        item.wait_recv(0)
        item.wait_send()


def middle(
    n_mem, plane, planes, slot, member, index, dq, dk, dv, wc, so, sa, h1, enc, dz2, unit, scale, gain, ready
):
    rows, part = dq.shape
    width = h1.shape[1]
    own = rows // 2
    passages = slot.shape[0] // 2
    settled = tuple(columns for _, columns in ready)
    settled_shapes = [item.shape[:2] + (plane,) + item.shape[2:] for item, _ in ready]
    cross_shape = (3, n_mem, plane, width // (n_mem * plane), part)
    so_shape = (1, n_mem, plane, part // (n_mem * plane), width)
    shapes = [
        jax.ShapeDtypeStruct((rows, part), BF16),
        jax.ShapeDtypeStruct((own, width), F32),
        jax.ShapeDtypeStruct((8, width), F32),
        jax.ShapeDtypeStruct((passages // 2, PLEN, width), BF16),
        sum_shape(cross_shape),
        sum_shape(so_shape),
    ] + [reduce_out(shape, columns, plane) for shape, columns in zip(settled_shapes, settled)]
    fetched = [h1, enc, dz2, unit, so, sa]
    scratch = [pltpu.VMEM(item.shape, item.dtype) for item in fetched] + [
        pltpu.VMEM((part, width), BF16),
        pltpu.VMEM((part, width), BF16),
        pltpu.VMEM(dk.shape[:1] + (width,), BF16),
        pltpu.VMEM((passages, PLEN, width), BF16),
        pltpu.VMEM((passages, PLEN, width), BF16),
        pltpu.VMEM((passages, PLEN, width), BF16),
        pltpu.VMEM((passages // 2, PLEN, width), BF16),
        pltpu.VMEM(cross_shape, BF16),
        pltpu.VMEM(so_shape, BF16),
        pltpu.VMEM((own, width), BF16),
        pltpu.VMEM((own, width), BF16),
        pltpu.VMEM((rows, width), BF16),
    ]
    scratch += plane_sum_scratch(cross_shape, n_mem, cross_shape[3])
    scratch += plane_sum_scratch(so_shape, n_mem, so_shape[3])
    for shape in settled_shapes:
        scratch += settle_scratch(shape, n_mem, plane, planes, shape[3])
    count = (
        len(ready) * settle_sems(n_mem, plane, planes) + 2 * PLANE_SUM_SEMS + 2 * passages
        + passages + 4 * passages // 2 + 4 + 6
    )
    smem = pl.BlockSpec(memory_space=pltpu.SMEM)
    outs = pl.pallas_call(
        functools.partial(middle_kernel, n_mem, plane, planes, settled),
        in_specs=[smem, smem, smem] + [VMEM] * 6 + [ANY] * 6 + [VMEM] * len(ready),
        out_specs=[VMEM] * 3 + [ANY] + [VMEM] * (2 + len(ready)),
        out_shape=shapes,
        scratch_shapes=scratch + [pltpu.SemaphoreType.DMA((count,))],
        compiler_params=pltpu.CompilerParams(
            vmem_limit_bytes=60 * 2**20, collective_id=3, has_side_effects=True
        ),
        cost_estimate=pl.CostEstimate(
            flops=rows * part * width * 30, bytes_accessed=40 * 2**20, transcendentals=0
        ),
        name="middle",
    )(
        slot,
        member,
        index,
        dq,
        dk.reshape(-1, PLEN, part),
        dv.reshape(-1, PLEN, part),
        wc,
        scale,
        gain,
        *fetched,
        *[item for item, _ in ready],
    )
    return outs[:4], outs[4:6], outs[6:]


def self_attend_back(place, pair, q_vm, k_vm, v_vm, o_vm, do_vm, lse_vm, outs, scratch):
    dq_vm, dk_vm, dv_vm = outs
    q_a, do_a, k_t, q_h, do_h, p_vm, ds_vm = scratch
    base = 2 * place.core + place.parity
    count = q_vm.shape[0] // BLK
    lanes = pl.ds(pl.multiple_of(pair * 2 * HD, 2 * HD), 2 * HD)

    def rows(i):
        return pl.ds(pl.multiple_of(flip(base, i) * BLK, BLK), BLK)

    for i in range(count):
        span = slice(i * BLK, (i + 1) * BLK)
        q_a[span, :] = q_vm[rows(i), lanes]
        do_a[span, :] = do_vm[rows(i), lanes]
        k_t[:, span] = k_vm[rows(i), lanes].T
        q_t = q_a[span, :].T
        do_t = do_a[span, :].T
        prod = (do_a[span, :].astype(F32) * o_vm[rows(i), lanes].astype(F32)).T
        for head in range(2):
            delta = jnp.sum(prod[head * HD : (head + 1) * HD, :], axis=0, keepdims=True)
            q_h[head, :, span] = head_rows(q_t, head, lse_vm[pair, head : head + 1, span])
            do_h[head, :, span] = head_rows(do_t, head, delta)
    key_pos = lax.broadcasted_iota(jnp.int32, (BLK, BLK), 0)
    query_pos = lax.broadcasted_iota(jnp.int32, (BLK, BLK), 1)
    units = [(j, i, head) for j in range(count) for head in range(2) for i in range(j, count)]

    def products(unit):
        j, i, head = unit
        span = slice(i * BLK, (i + 1) * BLK)
        return (
            mm(ones_in(k_vm[rows(j), lanes], head), q_h[head, :, span]),
            mm(ones_in(v_vm[rows(j), lanes], head), do_h[head, :, span]),
        )

    ready = products(units[0])
    halves = {}
    for n, (j, i, head) in enumerate(units):
        coming = products(units[n + 1]) if n + 1 < len(units) else None
        scores, dprobs = ready
        probs = jnp.exp(scores)
        if i == j:
            probs = jnp.where(key_pos <= query_pos, probs, 0.0)
        keys, span = slice(j * BLK, (j + 1) * BLK), slice(i * BLK, (i + 1) * BLK)
        p_vm[head, keys, span] = probs.astype(BF16)
        ds_vm[head, keys, span] = (probs * dprobs).astype(BF16)
        if i == count - 1:
            late = slice(j * BLK, count * BLK)
            halves[head] = (
                mm(p_vm[head, keys, late], do_a[late, :]),
                mm(ds_vm[head, keys, late], q_a[late, :]),
            )
            if head == 1:
                dv_vm[rows(j), lanes] = pick_heads(halves[0][0], halves[1][0]).astype(BF16)
                dk_vm[rows(j), lanes] = pick_heads(halves[0][1], halves[1][1]).astype(BF16)
        ready = coming
    for i in range(count):
        span, keys = slice(i * BLK, (i + 1) * BLK), slice(0, (i + 1) * BLK)
        dq_t = jnp.concatenate(
            [
                mm(k_t[head * HD : (head + 1) * HD, keys], ds_vm[head, keys, span])
                for head in range(2)
            ],
            axis=0,
        )
        dq_vm[rows(i), lanes] = dq_t.T.astype(BF16) * BF16(0.125)


def last_kernel(n_mem, plane, planes, settled, chunks, *refs):
    refs = Walk(refs)
    q_ref, k_ref, v_ref, o_ref, do_ref, lse_ref, feed_ref, hidden_ref, middle_ref = refs.take(9)
    fetched = refs.take(3)
    ready = refs.take(len(settled))
    small_out, dx_out, self_out = refs.take(3)
    outs = refs.take(len(settled))
    x_ref, w_ref, dz1_ref = kept = refs.take(3)
    dq_vm, dk_vm, dv_vm = refs.take(3)
    attend_scratch = refs.take(7)
    x_t, dw_vm = refs.take(2)
    part_vm, twin_vm, dx_vm = refs.take(3)
    chunk_own = [refs.one() for _ in range(chunks)]
    chunk_bufs = [refs.take(3) for _ in range(chunks)]
    chunk_settle = [refs.take(3) for _ in range(chunks)]
    settle_bufs = [refs.take(3) for _ in settled]
    small_near, small_line, small_twin, small_far, small_sum, sem_ref = refs.take(6)
    sems = Sems(sem_ref)
    place = Place(plane, planes)
    fetches = [Fetch(sems, src, dst) for src, dst in zip(fetched, kept)]
    settles = [
        Settle(
            place, sems, ready[i], outs[i], settle_bufs[i], columns, n_mem, (0, ready[i].shape[2])
        )
        for i, columns in enumerate(settled)
    ]
    rows, part = q_ref.shape
    lanes = part // chunks
    depth = dw_vm.shape[3]
    sums = [
        PlaneSum(
            place, sems, dw_vm, chunk_own[c], chunk_bufs[c], (0, depth), (c * lanes, lanes)
        )
        for c in range(chunks)
    ]
    ends = [
        Settle(
            place, sems, chunk_own[c], self_out, chunk_settle[c], True, n_mem, (0, depth), c * lanes
        )
        for c in range(chunks)
    ]
    near_sems = sems.take(6)
    near = [
        remote(
            small_sum, small_near.at[t - 1], near_sems[2 * t - 2], near_sems[2 * t - 1], place.near(t)
        )
        for t in range(1, plane)
    ]
    line = Line(
        place, sems, lambda s: small_sum.at[flip(place.mem, s)], lambda s: small_line.at[s - 1], n_mem
    )
    twin_sems = sems.take(2)
    twin = remote(small_sum.at[place.mem], small_twin, twin_sems[0], twin_sems[1], place.twin())
    far_sems = sems.take(2 * (planes - 1))
    far = [
        remote(
            small_sum.at[place.mem],
            small_far.at[r - 1],
            far_sems[2 * r - 2],
            far_sems[2 * r - 1],
            place.far(r),
        )
        for r in range(1, planes)
    ]
    seg = dx_out.shape[1]
    own = 2 * seg
    spread = Spread(
        place,
        sems,
        lambda k: dx_vm.at[pl.ds(seg * k, seg)],
        lambda k: dx_out.at[place.parity],
    )
    swap_sems = sems.take(2)
    swap_part = remote(part_vm, twin_vm, swap_sems[0], swap_sems[1], place.twin())

    for item in fetches:
        item.start()
    place.meet(
        column_peers(n_mem) + plane_peers(plane) + [(2 * plane * r, 0) for r in range(1, planes)]
    )
    for item in settles:
        item.start()
    block = x_ref.shape[1] // n_mem

    def input_part(span):
        return (
            mm(dq_vm[span, :], w_ref[0], NT)
            + mm(dk_vm[span, :], w_ref[1], NT)
            + mm(dv_vm[span, :], w_ref[2], NT)
        )

    pairs = part // (2 * HD)
    late = []
    for c in range(chunks):
        for pair in range(c * pairs // chunks, (c + 1) * pairs // chunks):
            self_attend_back(
                place,
                pair,
                q_ref,
                k_ref,
                v_ref,
                o_ref,
                do_ref,
                lse_ref,
                (dq_vm, dk_vm, dv_vm),
                attend_scratch,
            )
        if c == 0:
            for item in fetches:
                item.get()
            for m in range(n_mem):
                x_t[m] = x_ref[:, m * block : (m + 1) * block].T
        span = slice(c * lanes, (c + 1) * lanes)

        def weights(m, carry, span=span):
            for i, grad in enumerate((dq_vm, dk_vm, dv_vm)):
                dw_vm[i, m, :, :, span] = (
                    mm(x_t[m], grad[:, span]).astype(BF16).reshape(plane, depth, lanes)
                )
            return carry

        if c < chunks - 2:
            lax.fori_loop(0, n_mem, weights, 0)
            sums[c].start()
        if c == 1:
            sums[0].middle()
        if c == 2:
            for item in settles:
                item.middle()
            sums[0].end()
            ends[0].start()
            sums[1].middle()
        late.append(weights)
    part_vm[...] = input_part(slice(own, 2 * own)).astype(BF16)
    swap_part.start()
    lax.fori_loop(0, n_mem, late[-2], 0)
    sums[-2].start()
    swap_part.wait()
    total = dz1_ref[...] + input_part(slice(0, own)) + twin_vm[...].astype(F32)
    dx_vm[...] = total.astype(BF16)
    spread.start()
    lax.fori_loop(0, n_mem, late[-1], 0)
    sums[-1].start()
    sums[1].end()
    ends[1].start()
    for item in settles:
        item.forward()
    sums[-2].middle()

    small_sum[...] = jnp.zeros_like(small_sum)
    wide = small_sum.shape[2]
    unit = wide // 2
    first = place.core == 0
    for row, ref, at in (
        (2, middle_ref, 2),
        (5, feed_ref, 5),
        (6, middle_ref, 1),
        (7, feed_ref, 4),
        (8, feed_ref, 1),
        (9, feed_ref, 2),
        (10, middle_ref, 0),
        (11, feed_ref, 3),
        (12, feed_ref, 0),
    ):
        for b in range(n_mem):
            small_sum[b, row : row + 1, :] = ref[at : at + 1, b * wide : (b + 1) * wide]
    for row, value in (
        (0, jnp.sum(dq_vm[...].astype(F32), axis=0, keepdims=True)),
        (1, jnp.sum(dv_vm[...].astype(F32), axis=0, keepdims=True)),
        (3, middle_ref[3:4, :part]),
        (4, middle_ref[4:5, :part]),
    ):
        for b in range(n_mem):
            side = value[:, b * unit : (b + 1) * unit]
            none = jnp.zeros_like(side)
            small_sum[b, row : row + 1, :unit] = jnp.where(first, side, none)
            small_sum[b, row : row + 1, unit:] = jnp.where(first, none, side)
    count = hidden_ref.shape[1] // (n_mem * wide)
    for b in range(n_mem):
        for i in range(count):
            at = (b * count + i) * wide
            side = hidden_ref[:, at : at + wide]
            none = jnp.zeros_like(side)
            row = 13 + i
            small_sum[b, row : row + 1, :] = jnp.where(first, side, none)
            small_sum[b, row + count : row + count + 1, :] = jnp.where(first, none, side)
    for copy in near:
        copy.start()
    sums[-1].middle()
    sums[-2].end()
    ends[-2].start()
    ends[0].middle()
    for copy in near:
        copy.wait()
    total = small_sum[...]
    for t in range(plane - 1):
        total += small_near[t]
    small_sum[...] = total
    line.start()
    sums[-1].end()
    ends[-1].start()
    ends[1].middle()
    ends[0].forward()
    for item in settles:
        item.end()
    ends[-2].middle()
    ends[1].forward()
    for s in range(1, n_mem):
        line.wait_recv(s)
    line.wait_send()
    value = small_sum[place.mem]
    for s in range(n_mem - 1):
        value += small_line[s]
    small_sum[place.mem] = value
    twin.start()
    ends[-1].middle()
    ends[-2].forward()
    for item in ends[:-2]:
        item.end()
    twin.wait()
    value = small_sum[place.mem] + small_twin[...]
    if far:
        small_sum[place.mem] = value
        for copy in far:
            copy.start()
        for copy in far:
            copy.wait()
        for r in range(planes - 1):
            value += small_far[r]
    small_out[...] = value
    ends[-1].forward()
    ends[-2].end()
    ends[-1].end()
    for item in sums:
        item.wait_send()
    for k in range(2):
        spread.wait_recv(k)
    spread.wait_send()


def last(n_mem, plane, planes, q, k, v, o, do, lse, x, w, dz1, sums, small_shape, ready):
    rows, part = q.shape
    chunks = part // (2 * HD)
    width = x.shape[1]
    own = rows // 2
    settled = tuple(columns for _, columns in ready)
    settled_shapes = [item.shape[:2] + (plane,) + item.shape[2:] for item, _ in ready]
    grad_shape = (3, n_mem, plane, width // (n_mem * plane), part)
    depth, lanes = grad_shape[3], part // chunks
    small_part = small_shape[1:]
    shapes = [
        jax.ShapeDtypeStruct(small_part, F32),
        jax.ShapeDtypeStruct((2, own // 2, width), BF16),
        reduce_out(grad_shape, True, plane),
    ] + [reduce_out(shape, columns, plane) for shape, columns in zip(settled_shapes, settled)]
    fetched = [x, w, dz1]
    scratch = (
        [pltpu.VMEM(item.shape, item.dtype) for item in fetched]
        + [pltpu.VMEM((rows, part), BF16)] * 3
        + [
            pltpu.VMEM((rows, 2 * HD), BF16),
            pltpu.VMEM((rows, 2 * HD), BF16),
            pltpu.VMEM((2 * HD, rows), BF16),
            pltpu.VMEM((2, 2 * HD, rows), BF16),
            pltpu.VMEM((2, 2 * HD, rows), BF16),
            pltpu.VMEM((2, rows, rows), BF16),
            pltpu.VMEM((2, rows, rows), BF16),
            pltpu.VMEM((n_mem, width // n_mem, rows), BF16),
            pltpu.VMEM(grad_shape, BF16),
        ]
        + [pltpu.VMEM((own, width), BF16)] * 3
        + [pltpu.VMEM((3, n_mem, depth, lanes), BF16)] * chunks
    )
    for _ in range(chunks):
        scratch += plane_sum_scratch(grad_shape, n_mem, depth, lanes)
    for _ in range(chunks):
        scratch += settle_scratch(grad_shape, n_mem, plane, planes, depth, lanes)
    for shape in settled_shapes:
        scratch += settle_scratch(shape, n_mem, plane, planes, shape[3])
    scratch += [
        pltpu.VMEM((plane - 1,) + small_shape, F32),
        pltpu.VMEM((n_mem - 1,) + small_part, F32),
        pltpu.VMEM(small_part, F32),
        pltpu.VMEM((max(planes - 1, 1),) + small_part, F32),
        pltpu.VMEM(small_shape, F32),
        pltpu.SemaphoreType.DMA(
            (
                (len(ready) + chunks) * settle_sems(n_mem, plane, planes)
                + chunks * PLANE_SUM_SEMS
                + 24
                + 2 * planes,
            )
        ),
    ]
    outs = pl.pallas_call(
        functools.partial(last_kernel, n_mem, plane, planes, settled, chunks),
        in_specs=[VMEM] * 9 + [ANY] * 3 + [VMEM] * len(ready),
        out_specs=[VMEM, ANY, VMEM] + [VMEM] * len(ready),
        out_shape=shapes,
        scratch_shapes=scratch,
        compiler_params=pltpu.CompilerParams(
            vmem_limit_bytes=60 * 2**20, collective_id=4, has_side_effects=True
        ),
        cost_estimate=pl.CostEstimate(
            flops=rows * rows * width * 40, bytes_accessed=40 * 2**20, transcendentals=rows * rows * 8
        ),
        name="last",
    )(q, k, v, o, do, lse, *sums, *fetched, *[item for item, _ in ready])
    return outs[0], outs[1], outs[2:]


def cross_forward_kernel(n_mem, plane, kinds, index_ref, q_ref, k_ref, v_ref, *refs):
    refs = Walk(refs)
    count_w = len(kinds)
    shards = refs.take(count_w)
    o_ref, lse_ref = refs.take(2)
    halves = refs.take(count_w)
    v_t, o_t, sem_ref = refs.take(3)
    sems = Sems(sem_ref)
    place = Place(plane)
    step = pl.program_id(0) * pl.num_programs(1) + pl.program_id(1)
    last = pl.num_programs(0) * pl.num_programs(1) - 1
    gathers = [
        Gather(place, sems, shard, half, columns, n_mem, (1,) if i == 1 else None)
        for i, (shard, half, columns) in enumerate(zip(shards, halves, kinds))
    ]
    @pl.when(step == 0)
    def _():
        for gather in gathers:
            gather.own.start()
        place.meet(column_peers(n_mem) + plane_peers(plane))
        for gather in gathers:
            gather.begin()

    rows = q_ref.shape[0]
    count = index_ref.shape[0]

    @pl.when(pl.program_id(1) == 0)
    def _():
        for j in range(count):
            v_t[:, j * BLK : (j + 1) * BLK] = v_ref[index_ref[j]].T

    units = []
    for i in range(rows // BLK):
        q_t = q_ref[i * BLK : (i + 1) * BLK, :].T
        for head in range(2):
            q_head = head_rows(q_t, head)

            def score(j, q_head=q_head):
                return mm(k_ref[index_ref[j]], q_head)

            def value(j, head=head):
                return v_t[head * HD : (head + 1) * HD, j * BLK : (j + 1) * BLK]

            units.append(
                (
                    [functools.partial(score, j) for j in range(count)],
                    [functools.partial(value, j) for j in range(count)],
                    (i, head),
                )
            )

    def finish(tag, mixed, lse):
        i, head = tag
        span = slice(i * BLK, (i + 1) * BLK)
        o_t[head * HD : (head + 1) * HD, span] = mixed
        lse_ref[0, head : head + 1, span] = lse

    whole_one, line_one = gathers
    plan = {
        4: [(whole_one.share, 1)],
        6: [(line_one.share, 1)],
        10: [(whole_one.share, 2)],
        12: [(line_one.share, 2), (whole_one.forward, 1)],
        14: [(line_one.forward, 1)],
        17: [(whole_one.share, 3)],
        19: [(line_one.share, 3), (whole_one.forward, 2)],
        24: [(whole_one.forward, 3)],
    }

    def serve(n):
        for when, calls in plan.items():
            if when % len(units) == n:

                @pl.when(step == when // len(units))
                def _():
                    for call, hops in calls:
                        call(hops)

    softmax_units(units, finish, serve)
    o_ref[...] = o_t[...].T.astype(BF16)

    @pl.when(step == last)
    def _():
        for gather in gathers:
            gather.finish()


def cross_forward(n_mem, plane, index, q, k, v, params):
    rows, width = q.shape
    pairs = width // (2 * HD)
    keys = index.shape[0] * PLEN
    block = 2 * BLK
    question = pl.BlockSpec((block, 2 * HD), lambda h, i: (i, h))
    memory = pl.BlockSpec(k.shape[:2] + (2 * HD,), lambda h, i: (0, 0, h))
    kinds = tuple(columns for _, columns in params)
    views = [half_views(shard, columns, n_mem, plane) for shard, columns in params]
    outs = pl.pallas_call(
        functools.partial(cross_forward_kernel, n_mem, plane, kinds),
        grid=(pairs, rows // block),
        in_specs=[pl.BlockSpec(memory_space=pltpu.SMEM), question, memory, memory]
        + [whole(view.shape) for view, _ in views],
        out_specs=[question, pl.BlockSpec((1, 2, block), lambda h, i: (h, 0, i))]
        + [ANY] * len(params),
        out_shape=[
            jax.ShapeDtypeStruct((rows, width), BF16),
            jax.ShapeDtypeStruct((pairs, 2, rows), F32),
        ]
        + [jax.ShapeDtypeStruct(full, BF16) for _, full in views],
        scratch_shapes=[
            pltpu.VMEM((2 * HD, keys), BF16),
            pltpu.VMEM((2 * HD, block), F32),
            pltpu.SemaphoreType.DMA((4 + GATHER_SEMS * len(params),)),
        ],
        compiler_params=pltpu.CompilerParams(
            vmem_limit_bytes=60 * 2**20, collective_id=2, has_side_effects=True
        ),
        cost_estimate=pl.CostEstimate(
            flops=rows * keys * width * 16,
            bytes_accessed=rows * width * 4 + k.size * 4,
            transcendentals=rows * keys * pairs * 2,
        ),
        name="cross_forward",
    )(index, q, k, v, *[view for view, _ in views])
    return outs[:2], outs[2:]


def cross_backward_kernel(
    n_mem, plane, planes, chunks, settled, index_ref, q_ref, k_ref, v_ref, o_ref, do_ref, lse_ref, *refs
):
    refs = Walk(refs)
    kinds = {which: columns for which, columns, _ in chunks}
    grads = refs.take(len(kinds))
    ready = refs.take(len(settled))
    dq_ref, dk_ref, dv_ref = refs.take(3)
    outs = refs.take(len(kinds))
    q_h, do_h, dq_t, p_vm, ds_vm = refs.take(5)
    sems = Sems(refs.refs[-1])
    place = Place(plane, planes)
    sums, settles = [], []
    for which, columns, rows_of in chunks:
        own = refs.one()
        sums.append(PlaneSum(place, sems, grads[which], own, refs.take(3), rows_of))
        settles.append(
            Settle(place, sems, own, outs[which], refs.take(3), columns, n_mem, rows_of)
        )
    first = [
        Settle(
            place, sems, ready[i], outs[which], refs.take(3), columns, n_mem, (0, ready[i].shape[2])
        )
        for i, (which, columns) in enumerate(settled)
    ]
    passage = pl.program_id(1)
    step = pl.program_id(0) * pl.num_programs(1) + passage
    steps = pl.num_programs(0) * pl.num_programs(1)
    rows = q_ref.shape[0]
    count = rows // BLK

    @pl.when(step == 0)
    def _():
        place.meet(
            column_peers(n_mem) + plane_peers(plane) + [(2 * plane * r, 0) for r in range(1, planes)]
        )
        for item in first:
            item.start()

    def at(when, *calls):
        @pl.when(step == when)
        def _():
            for call in calls:
                call()

    plan = ((0, 2, 5, 9, 10), (3, 5, 8, 12, 13), (6, 8, 11, 14, 15), (9, 10, 12, 15, 15))
    for i, (plane_sum, settle) in enumerate(zip(sums, settles)):
        start, middle, end, line, near = plan[i]
        at(start, plane_sum.start)
        at(middle, plane_sum.middle)
        at(end, plane_sum.end, settle.start)
        at(line, settle.middle)
        at(near, settle.forward)
    for item in first:
        at(6, item.middle)
        at(8, item.forward)

    @pl.when(passage == 0)
    def _():
        for i in range(count):
            span = slice(i * BLK, (i + 1) * BLK)
            q_t = q_ref[span, :].T
            grads_t = do_ref[span, :].T
            prod = (do_ref[span, :].astype(F32) * o_ref[span, :].astype(F32)).T
            for head in range(2):
                delta = jnp.sum(prod[head * HD : (head + 1) * HD, :], axis=0, keepdims=True)
                q_h[head, :, span] = head_rows(q_t, head, lse_ref[0, head : head + 1, span])
                do_h[head, :, span] = head_rows(grads_t, head, delta)
        dq_t[...] = jnp.zeros_like(dq_t)

    keys = dk_ref.shape[0] // BLK
    slots = [index_ref[passage * keys + j] for j in range(keys)]
    k_t = jnp.concatenate([k_ref[slot].T for slot in slots], axis=1)
    units = [(head, j, i) for head in range(2) for j in range(keys) for i in range(count)]

    def products(unit):
        head, j, i = unit
        span = slice(i * BLK, (i + 1) * BLK)
        return (
            mm(ones_in(k_ref[slots[j]], head), q_h[head, :, span]),
            mm(ones_in(v_ref[slots[j]], head), do_h[head, :, span]),
        )

    coming = products(units[0])
    halves = []
    for n, (head, j, i) in enumerate(units):
        scores, dprobs = coming
        if n + 1 < len(units):
            coming = products(units[n + 1])
        tile, span = slice(j * BLK, (j + 1) * BLK), slice(i * BLK, (i + 1) * BLK)
        probs = jnp.exp(scores)
        p_vm[head, tile, span] = probs.astype(BF16)
        ds_vm[head, tile, span] = (probs * dprobs).astype(BF16)
        if (j, i) == (keys - 1, count - 1):
            half = slice(head * HD, (head + 1) * HD)
            halves.append((mm(p_vm[head], do_ref[...]), mm(ds_vm[head], q_ref[...])))
            dq_t[half, :] += mm(k_t[half, :], ds_vm[head])
    dv_ref[...] = pick_heads(halves[0][0], halves[1][0]).astype(BF16)
    dk_ref[...] = pick_heads(halves[0][1], halves[1][1]).astype(BF16)

    @pl.when(passage == pl.num_programs(1) - 1)
    def _():
        dq_ref[...] = dq_t[...].T.astype(BF16)

    @pl.when(step == steps - 1)
    def _():
        for settle in first + settles:
            settle.end()
        for item in sums:
            item.wait_send()


def cross_backward(n_mem, plane, planes, index, q, k, v, o, do, lse, grads, ready):
    rows, width = q.shape
    pairs = width // (2 * HD)
    block = 2 * PLEN
    keys = index.shape[0] * PLEN
    passages = keys // block
    question = pl.BlockSpec((rows, 2 * HD), lambda h, u: (0, h))
    memory = pl.BlockSpec(k.shape[:2] + (2 * HD,), lambda h, u: (0, 0, h))
    grads_of = pl.BlockSpec((block, 2 * HD), lambda h, u: (u, h))
    shapes, chunks, scratch = [], [], []
    for which, (grad, columns, pieces, begin) in enumerate(grads):
        lead, _, _, depth, cols = grad.shape
        count = depth // pieces
        shapes.append(reduce_out(grad.shape, columns, plane))
        for i in range(begin, pieces):
            chunks.append((which, columns, (i * count, count)))
            scratch.append(pltpu.VMEM((lead, n_mem, count, cols), BF16))
            scratch += plane_sum_scratch(grad.shape, n_mem, count)
            scratch += settle_scratch(grad.shape, n_mem, plane, planes, count)
    settled = tuple((which, grads[which][1]) for _, which in ready)
    for item, _ in ready:
        shape = item.shape[:2] + (plane,) + item.shape[2:]
        scratch += settle_scratch(shape, n_mem, plane, planes, shape[3])
    outs = pl.pallas_call(
        functools.partial(cross_backward_kernel, n_mem, plane, planes, tuple(chunks), settled),
        grid=(pairs, passages),
        in_specs=[
            pl.BlockSpec(memory_space=pltpu.SMEM),
            question,
            memory,
            memory,
            question,
            question,
            pl.BlockSpec((1, 2, rows), lambda h, u: (h, 0, 0)),
        ]
        + [ANY] * len(grads)
        + [whole(item.shape) for item, _ in ready],
        out_specs=[question, grads_of, grads_of]
        + [whole(item.shape) for item in shapes],
        out_shape=[
            jax.ShapeDtypeStruct((rows, width), BF16),
            jax.ShapeDtypeStruct((keys, width), BF16),
            jax.ShapeDtypeStruct((keys, width), BF16),
        ]
        + shapes,
        scratch_shapes=[
            pltpu.VMEM((2, 2 * HD, rows), BF16),
            pltpu.VMEM((2, 2 * HD, rows), BF16),
            pltpu.VMEM((2 * HD, rows), F32),
            pltpu.VMEM((2, block, rows), BF16),
            pltpu.VMEM((2, block, rows), BF16),
        ]
        + scratch
        + [
            pltpu.SemaphoreType.DMA(
                (
                    len(chunks) * PLANE_SUM_SEMS
                    + (len(chunks) + len(ready)) * settle_sems(n_mem, plane, planes),
                )
            )
        ],
        compiler_params=pltpu.CompilerParams(
            vmem_limit_bytes=56 * 2**20, collective_id=5, has_side_effects=True
        ),
        cost_estimate=pl.CostEstimate(
            flops=rows * keys * width * 40,
            bytes_accessed=rows * width * 10 + k.size * 8,
            transcendentals=rows * keys * pairs * 2,
        ),
        name="cross_backward",
    )(index, q, k, v, o, do, lse, *[item[0] for item in grads], *[item for item, _ in ready])
    return outs[:3], outs[3:]


def widen_kernel(*refs):
    count = len(refs) // 2
    for src, dst in zip(refs[:count], refs[count:]):
        dst[...] = src[...].astype(F32)


def widen(pairs):
    steps = 8
    flats = [value.reshape(-1, like.shape[-1]) for value, like in pairs]
    blocks = [
        pl.BlockSpec((item.shape[0] // steps, item.shape[1]), lambda i: (i, 0)) for item in flats
    ]
    outs = pl.pallas_call(
        widen_kernel,
        grid=(steps,),
        in_specs=blocks,
        out_specs=blocks,
        out_shape=[jax.ShapeDtypeStruct(item.shape, F32) for item in flats],
        compiler_params=pltpu.CompilerParams(vmem_limit_bytes=60 * 2**20),
        cost_estimate=pl.CostEstimate(
            flops=0, bytes_accessed=6 * sum(item.size for item in flats), transcendentals=0
        ),
        name="widen",
    )(*flats)
    return [out.reshape(like.shape) for out, (_, like) in zip(outs, pairs)]


def body(
    hidden_in,
    encoder_rows,
    passage_map,
    self_qkv,
    self_out,
    cross_qkv,
    cross_out,
    ffn_in,
    ffn_out,
    ffn_in_bias,
    biases,
    gains,
    cotangent,
):
    n_pb = lax.axis_size("pb")
    n_mem = lax.axis_size("mem")
    columns = n_pb // 2
    plane = min(columns, 4)
    pb = lax.axis_index("pb")
    core = pb % 2
    width = hidden_in.shape[2]
    planes = columns // plane

    enc_local = encoder_rows.reshape(-1, PLEN, width)
    n_bias, n_gain = biases.shape[0], gains.shape[0]
    small = jnp.concatenate([biases, gains, ffn_in_bias.reshape(-1, biases.shape[1])], axis=0)
    n_small = small.shape[0]
    small_rows = -(-n_small // 16) * 16
    small = jnp.pad(small, ((0, small_rows - n_small), (0, 0)))
    rows_out, halves, kept = front(
        n_mem,
        plane,
        (n_bias, n_gain),
        hidden_in,
        enc_local,
        passage_map,
        small,
        [(self_qkv, True), (self_out, False), (cross_qkv, True), (cross_out, False)],
    )
    x_full, enc_full, index, small = rows_out
    sq, sk, sv, sa, self_lse, h1_full, unit1, scale1, cq, ck, cv = kept
    index = index.reshape(-1)

    def flat(half):
        lead, _, _, _, cols = half.shape
        return half.reshape(lead, -1, cols)

    w_self, w_cross = flat(halves[0]), flat(halves[2])
    w_self_out, w_cross_out = flat(halves[1])[0], flat(halves[3])[0]
    small = small.astype(F32)
    vectors = small[:, : n_bias + n_gain].transpose(1, 0, 2).reshape(n_bias + n_gain, width)
    bias, gain = vectors[:n_bias], vectors[n_bias:]
    ffn_bias = small[:, n_bias + n_gain : n_small].reshape(-1)

    def half_of(vector):
        parts = vector.reshape(n_mem, 2, -1)
        return jnp.where(core == 0, parts[:, 0], parts[:, 1]).reshape(-1)

    order = jnp.arange(encoder_rows.shape[1] * n_mem, dtype=jnp.int32)
    hits = index[None, :] == order[:, None]
    member = jnp.any(hits, axis=1).astype(F32)
    slot = jnp.sum(jnp.where(hits, jnp.arange(index.shape[0], dtype=jnp.int32)[None], 0), axis=1)
    (ca, cross_lse), halves = cross_forward(
        n_mem,
        plane,
        index,
        cq,
        ck,
        cv,
        [(ffn_in[None], True), (ffn_out, False)],
    )
    w_ffn_in, w_ffn_out = flat(halves[0])[0], halves[1]

    rows_of = jnp.stack(
        [gain[0], bias[6], bias[5], gain[1], bias[7], bias[9], gain[2], bias[8]]
    )
    layer_out, dca, dz2, feed_sums, hidden_sums, own_ffn_out, dw_ffn_in, dw_cross_out, dw_ffn_out = feed(
        n_mem,
        plane,
        cotangent,
        rows_of,
        half_of(ffn_bias)[None],
        ca,
        unit1,
        w_cross_out,
        w_ffn_in,
        w_ffn_out,
    )
    (dcq, dck, dcv), ffn_sums = cross_backward(
        n_mem,
        plane,
        planes,
        index,
        cq,
        ck,
        cv,
        ca,
        dca,
        cross_lse,
        [(dw_ffn_out, False, 2, 1), (dw_ffn_in, True, 2, 0), (dw_cross_out, False, 1, 0)],
        [(own_ffn_out, 0)],
    )
    (dsa, dz1, middle_sums, enc_sum), (own_cross, own_so), _ = middle(
        n_mem,
        plane,
        planes,
        slot,
        member,
        index,
        dcq,
        dck,
        dcv,
        w_cross,
        w_self_out,
        sa,
        h1_full,
        enc_full.reshape(-1, PLEN, width),
        dz2,
        unit1,
        scale1,
        gain[0][None],
        [],
    )

    vec, dx, sums = last(
        n_mem,
        plane,
        planes,
        sq,
        sk,
        sv,
        sa,
        dsa,
        self_lse,
        x_full,
        w_self,
        dz1,
        [feed_sums, hidden_sums, middle_sums],
        small.shape,
        [(own_so, False), (own_cross, True)],
    )
    (
        grad_in,
        grad_encoder,
        out_self_qkv,
        out_self_out,
        out_cross_qkv,
        out_cross_out,
        out_ffn_in,
        out_ffn_out,
    ) = widen(
        [
            (dx, hidden_in),
            (enc_sum, encoder_rows),
            (sums[0], self_qkv),
            (sums[1], self_out),
            (sums[2], cross_qkv),
            (ffn_sums[2], cross_out),
            (ffn_sums[1], ffn_in),
            (ffn_sums[0], ffn_out),
        ]
    )
    out_ffn_bias = vec[n_bias + n_gain : n_small].reshape(-1)
    return (
        layer_out,
        grad_in,
        grad_encoder,
        out_self_qkv,
        out_self_out,
        out_cross_qkv,
        out_cross_out,
        out_ffn_in,
        out_ffn_out,
        out_ffn_bias,
        vec[:n_bias],
        vec[n_bias : n_bias + n_gain],
    )


def solution(mesh):
    placed = (
        P("pb", "mem", None),
        P("pb", "mem", None, None),
        P("pb", None),
        P(None, "mem", None),
        P("mem", None),
        P(None, "mem", None),
        P("mem", None),
        P("mem", None),
        P("mem", None),
        P("mem"),
        P(None, "mem"),
        P(None, "mem"),
        P("pb", "mem", None),
    )
    return jax.shard_map(
        body,
        mesh=mesh,
        in_specs=placed,
        out_specs=(
            P("pb", "mem", None),
            P("pb", "mem", None),
            P("pb", "mem", None, None),
            P(None, "mem", None),
            P("mem", None),
            P(None, "mem", None),
            P("mem", None),
            P("mem", None),
            P("mem", None),
            P("mem"),
            P(None, "mem"),
            P(None, "mem"),
        ),
        check_vma=False,
    )
```

```python
import functools

import jax
import jax.numpy as jnp
from jax import lax
from jax.experimental import pallas as pl
from jax.experimental.pallas import tpu as pltpu
from jax.sharding import PartitionSpec as P

HD = 64
PLEN = 256
BLK = 256
F32 = jnp.float32
BF16 = jnp.bfloat16

NN = (((1,), (0,)), ((), ()))
NT = (((1,), (1,)), ((), ()))


def mm(a, b, dims=NN):
    return lax.dot_general(a, b, dims, preferred_element_type=F32)


def head_mask_rows(block, head):
    rows = lax.broadcasted_iota(jnp.int32, block.shape, 0)
    return jnp.where((rows // HD) == head, block, jnp.zeros_like(block))


def head_rows(block, head, extra=None):
    block = block.astype(F32)
    rows = lax.broadcasted_iota(jnp.int32, block.shape, 0)
    out = jnp.where((rows // HD) == head, block, 0.0)
    if extra is not None:
        rest = -extra
        for i in range(3):
            term = rest.astype(BF16).astype(F32)
            rest = rest - term
            out = jnp.where(rows == (1 - head) * HD + i, term, out)
    return out.astype(BF16)


def ones_in(block, head):
    lanes = lax.broadcasted_iota(jnp.int32, block.shape, 1)
    first = (1 - head) * HD
    return jnp.where((lanes >= first) & (lanes < first + 3), jnp.ones_like(block), block)


def pick_heads(first, second):
    lanes = lax.broadcasted_iota(jnp.int32, first.shape, 1)
    return jnp.where(lanes < HD, first, second)


MESH = pl.DeviceIdType.MESH
ANY = pl.BlockSpec(memory_space=pl.ANY)
VMEM = pl.BlockSpec(memory_space=pltpu.VMEM)
PLANE = 4


def flip(index, bits):
    bit = 1
    while bit <= bits:
        if bits & bit:
            unit = jnp.int32(bit)
            index = index + unit - 2 * unit * lax.rem(lax.div(index, unit), jnp.int32(2))
        bit *= 2
    return index


class Place:
    def __init__(self, plane, planes=1):
        self.pb = lax.axis_index("pb")
        self.mem = lax.axis_index("mem")
        two = jnp.int32(2)
        self.core = lax.rem(self.pb, two)
        self.quarter = lax.rem(lax.div(self.pb, two), jnp.int32(plane))
        self.parity = lax.rem(self.mem, two)
        self.half = lax.div(self.mem, two)
        self.plane = plane
        self.planes = planes

    def near(self, t):
        return (flip(self.pb, 2 * t), self.mem)

    def far(self, r):
        return (flip(self.pb, 2 * self.plane * r), self.mem)

    def line(self, s):
        return (self.pb, flip(self.mem, s))

    def twin(self):
        return (flip(self.pb, 1), self.mem)

    def pair(self):
        return (self.pb, flip(self.mem, 1))

    def worker(self, k):
        return (self.pb - self.core + self.half, 2 * self.core + flip(self.parity, k))

    def at_home(self):
        return self.half == self.core

    def meet(self, peers):
        barrier = pltpu.get_barrier_semaphore()
        for pb_bits, mem_bits in peers:
            pl.semaphore_signal(
                barrier,
                inc=1,
                device_id=(flip(self.pb, pb_bits), flip(self.mem, mem_bits)),
                device_id_type=MESH,
            )
        pl.semaphore_wait(barrier, len(peers))


def column_peers(n_mem):
    return [(a, b) for a in range(2) for b in range(n_mem) if (a, b) != (0, 0)]


def plane_peers(plane):
    return [(2 * t, 0) for t in range(1, plane)]


class Sems:
    def __init__(self, ref):
        self.ref = ref
        self.used = 0

    def take(self, count):
        first = self.used
        self.used += count
        return [self.ref.at[first + i] for i in range(count)]


def remote(src, dst, send_sem, recv_sem, device):
    return pltpu.make_async_remote_copy(
        src_ref=src,
        dst_ref=dst,
        send_sem=send_sem,
        recv_sem=recv_sem,
        device_id=device,
        device_id_type=MESH,
    )


class Spread:
    def __init__(self, place, sems, src, dst, kinds=(0, 1)):
        self.place, self.src, self.dst, self.kinds = place, src, dst, kinds
        self.send = sems.take(2)
        self.recv = sems.take(2)

    def copy(self, k):
        return remote(self.src(k), self.dst(k), self.send[k], self.recv[k], self.place.worker(k))

    def start(self):
        for k in self.kinds:
            if k == 0:
                home = self.place.at_home()

                @pl.when(home)
                def _():
                    pltpu.make_async_copy(self.src(0), self.dst(0), self.recv[0]).start()

                @pl.when(jnp.logical_not(home))
                def _():
                    self.copy(0).start()
            else:
                self.copy(k).start()

    def wait_recv(self, k):
        if k == 0:
            home = self.place.at_home()

            @pl.when(home)
            def _():
                pltpu.make_async_copy(self.src(0), self.dst(0), self.recv[0]).wait()

            @pl.when(jnp.logical_not(home))
            def _():
                self.copy(0).wait_recv()
        else:
            self.copy(k).wait_recv()

    def wait_send(self):
        for k in self.kinds:
            if k == 0:

                @pl.when(jnp.logical_not(self.place.at_home()))
                def _():
                    self.copy(0).wait_send()
            else:
                self.copy(k).wait_send()


class Own:
    def __init__(self, place, sems, shard, full, columns, n_mem):
        self.copies = []
        mem, core = place.mem, place.core
        if columns:
            unit = full.shape[-1] // n_mem
            for b, sem in zip(range(n_mem), sems.take(n_mem)):
                start = pl.multiple_of(2 * unit * b + unit * core, unit)
                src = shard.at[:, :, :, pl.ds(start, unit)]
                dst = full.at[:, mem, :, :, pl.ds(unit * b, unit)]
                self.copies.append(pltpu.make_async_copy(src, dst, sem))
        else:
            (sem,) = sems.take(1)
            self.copies.append(pltpu.make_async_copy(shard.at[core], full.at[0, mem], sem))

    def start(self):
        for copy in self.copies:
            copy.start()

    def wait(self):
        for copy in self.copies:
            copy.wait()


class Line:
    def __init__(self, place, sems, src, dst, n_mem):
        send, recv = sems.take(n_mem - 1), sems.take(n_mem - 1)
        self.copies = [
            remote(src(s), dst(s), send[s - 1], recv[s - 1], place.line(s)) for s in range(1, n_mem)
        ]

    def start(self):
        for copy in self.copies:
            copy.start()

    def wait_recv(self, s):
        self.copies[s - 1].wait_recv()

    def wait_send(self):
        for copy in self.copies:
            copy.wait_send()


class Share:
    def __init__(self, place, sems, src, block):
        send, recv = sems.take(4), sems.take(4)
        rows = src.shape[-2]
        half = rows // 2

        def part(ref, i):
            return ref.at[:, pl.ds(i * half, half)]

        self.first = [
            remote(src, block(0), send[t - 1], recv[t - 1], place.near(t)) for t in (1, 2)
        ]
        self.second = [
            remote(part(block(t), t - 1), part(block(t), t - 1), send[t + 1], recv[t + 1], place.near(3 - t))
            for t in (1, 2)
        ]

    def start(self):
        for copy in self.first:
            copy.start()

    def forward(self):
        for direct, onward in zip(self.first, self.second):
            direct.wait_recv()
            onward.start()

    def wait(self):
        for copy in self.first:
            copy.wait_send()
        for copy in self.second:
            copy.wait()


class Chain:
    def __init__(self, place, sems, block, n_mem):
        self.place, self.block, self.n = place, block, n_mem
        self.sems = {way: (sems.take(n_mem - 1), sems.take(n_mem - 1)) for way in (1, -1)}

    def copy(self, way, hops):
        mem = self.place.mem
        source = lax.rem(mem + jnp.int32(self.n - way * hops), jnp.int32(self.n))
        target = lax.rem(mem + jnp.int32(self.n + way), jnp.int32(self.n))
        send, recv = self.sems[way]
        piece = self.block(source)
        return remote(piece, piece, send[hops], recv[hops], (self.place.pb, target))

    def comes(self, way, hops):
        mem = self.place.mem
        return mem >= hops if way == 1 else mem + hops < self.n

    def goes(self, way, hops):
        mem = self.place.mem
        ahead = mem + 1 < self.n if way == 1 else mem >= 1
        return jnp.logical_and(ahead, self.comes(way, hops))

    def start(self):
        for way in (1, -1):

            @pl.when(self.goes(way, 0))
            def _():
                self.copy(way, 0).start()

    def relay(self, hops, arrived):
        for way in (1, -1):

            @pl.when(self.comes(way, hops))
            def _():
                self.copy(way, hops - 1).wait_recv()
                if hops < self.n - 1:

                    @pl.when(self.goes(way, hops))
                    def _():
                        self.copy(way, hops).start()

                arrived(hops if way == 1 else self.n - hops)

    def wait_send(self):
        for hops in range(self.n - 1):
            for way in (1, -1):

                @pl.when(self.goes(way, hops))
                def _():
                    self.copy(way, hops).wait_send()


class Gather:
    def __init__(self, place, sems, shard, full, columns, n_mem, in_plane=None):
        mem, quarter = place.mem, place.quarter
        self.n_mem = n_mem
        self.in_plane = tuple(range(1, n_mem)) if in_plane is None else in_plane
        self.own = Own(place, sems, shard, full, columns, n_mem)
        self.chain = Chain(place, sems, lambda i: full.at[:, i, quarter], n_mem)
        self.shares = {}
        for d in range(1, n_mem):
            if d not in self.in_plane and n_mem - d not in self.in_plane:
                continue
            source = lax.rem(mem + jnp.int32(n_mem - d), jnp.int32(n_mem))

            def block(t, source=source):
                return full.at[:, source, flip(quarter, t)]

            self.shares[d] = Share(place, sems, block(0), block)

    def begin(self):
        self.own.wait()
        self.chain.start()

    def share(self, hops):
        self.chain.relay(
            hops, lambda d: self.shares[d].start() if hops in self.in_plane else None
        )

    def forward(self, hops):
        for way, d in ((1, hops), (-1, self.n_mem - hops)):

            @pl.when(self.chain.comes(way, hops))
            def _():
                self.shares[d].forward()

    def finish(self):
        self.chain.wait_send()
        for hops in self.in_plane:
            for way, d in ((1, hops), (-1, self.n_mem - hops)):

                @pl.when(self.chain.comes(way, hops))
                def _():
                    self.shares[d].wait()


GATHER_SEMS = 44


def half_views(shard, columns, n_mem, plane):
    if columns:
        lead, depth, hidden = shard.shape
        part = depth // plane
        return shard.reshape(lead, plane, part, hidden), (lead, n_mem, plane, part, hidden // 2)
    depth, width = shard.shape
    part = depth // 2 // plane
    return shard.reshape(2, plane, part, width), (1, n_mem, plane, part, width)


class Walk:
    def __init__(self, refs):
        self.refs = list(refs)

    def take(self, count):
        out, self.refs = self.refs[:count], self.refs[count:]
        return out

    def one(self):
        return self.take(1)[0]


def softmax_units(units, finish, serve=None):
    def scores_of(unit, j):
        return unit[0][j]()

    ready = [scores_of(units[0], j) for j in range(len(units[0][0]))]
    for n, (_, values, tag) in enumerate(units):
        if serve is not None:
            serve(n)
        coming = list(range(len(units[n + 1][0]))) if n + 1 < len(units) else []
        following = []
        top = functools.reduce(
            jnp.maximum, [jnp.max(tile, axis=0, keepdims=True) for tile in ready]
        )
        total = jnp.zeros_like(top)
        acc = None
        share = -(-len(coming) // len(ready))
        for j, tile in enumerate(ready):
            for i in coming[j * share : (j + 1) * share]:
                following.append(scores_of(units[n + 1], i))
            probs = jnp.exp(tile - top)
            total += jnp.sum(probs, axis=0, keepdims=True)
            part = mm(values[j](), probs.astype(BF16))
            acc = part if acc is None else acc + part
        finish(tag, acc / total, top + jnp.log(total))
        ready = following


def self_attend(place, pair, q_vm, k_vm, v_vm, o_vm, lse_vm, v_t, o_t):
    base = 2 * place.core + place.parity
    count = q_vm.shape[0] // BLK
    lanes = pl.ds(pl.multiple_of(pair * 2 * HD, 2 * HD), 2 * HD)

    def rows(i):
        return pl.ds(pl.multiple_of(flip(base, i) * BLK, BLK), BLK)

    for j in range(count):
        v_t[:, j * BLK : (j + 1) * BLK] = v_vm[rows(j), lanes].T
    key_pos = lax.broadcasted_iota(jnp.int32, (BLK, BLK), 0)
    query_pos = lax.broadcasted_iota(jnp.int32, (BLK, BLK), 1)
    units = []
    for i in range(count):
        q_t = q_vm[rows(i), lanes].T
        for head in range(2):
            q_head = head_rows(q_t, head)

            def score(j, i=i, q_head=q_head):
                tile = mm(k_vm[rows(j), lanes], q_head)
                return jnp.where(key_pos <= query_pos, tile, -1000000000.0) if j == i else tile

            def value(j, head=head):
                return v_t[head * HD : (head + 1) * HD, j * BLK : (j + 1) * BLK]

            units.append(
                (
                    [functools.partial(score, j) for j in range(i + 1)],
                    [functools.partial(value, j) for j in range(i + 1)],
                    (i, head),
                )
            )

    def finish(tag, mixed, lse):
        i, head = tag
        span = slice(i * BLK, (i + 1) * BLK)
        o_t[head * HD : (head + 1) * HD, span] = mixed
        lse_vm[pair, head : head + 1, span] = lse

    softmax_units(units, finish)
    for i in range(count):
        o_vm[rows(i), lanes] = o_t[:, i * BLK : (i + 1) * BLK].T.astype(BF16)


def tiles(rows, step):
    def run(i, carry):
        step(pl.ds(pl.multiple_of(i * BLK, BLK), BLK))
        return carry

    lax.fori_loop(0, rows // BLK, run, 0)


def front_kernel(n_mem, plane, kinds, places, x_ref, enc_ref, map_ref, small_ref, *refs):
    refs = Walk(refs)
    count = len(kinds)
    shards = refs.take(count)
    x_out, enc_out, index_out, small_out = refs.take(4)
    halves = refs.take(count)
    kept = refs.take(11)
    x_vm, w_vm, so_vm, cq_w, small_vm = refs.take(5)
    q_vm, k_vm, v_vm, sa_vm, lse_vm, h1_vm, unit_vm, scale_vm, cq_vm = refs.take(9)
    k_all, v_all, v_t, o_t, part_vm, twin_vm, kv_w, enc_vm, map_in = refs.take(9)
    sems = Sems(refs.one())
    place = Place(plane)
    n_bias, n_gain = places
    rows = x_ref.shape[1]
    gathers = [
        Gather(place, sems, shard, half, columns, n_mem)
        for shard, half, columns in zip(shards, halves, kinds)
    ]
    spread = Spread(
        place,
        sems,
        lambda k: x_ref.at[flip(place.parity, k)],
        lambda k: x_out.at[pl.ds(rows * k, rows)],
    )
    twin_send, twin_recv = sems.take(2), sems.take(2)
    twin = [
        remote(
            x_out.at[pl.ds(rows * k, rows)],
            x_out.at[pl.ds(rows * (k + 2), rows)],
            twin_send[k],
            twin_recv[k],
            place.twin(),
        )
        for k in range(2)
    ]
    map_sems = sems.take(2)
    map_copy = remote(map_ref, map_in, map_sems[0], map_sems[1], place.twin())
    (small_sem,) = sems.take(1)
    small_own = pltpu.make_async_copy(small_ref, small_out.at[place.mem], small_sem)
    small_line = Line(
        place, sems, lambda s: small_ref, lambda s: small_out.at[place.mem], n_mem
    )
    units = enc_vm.shape[1]
    encs, enc_twins, enc_pairs, enc_onwards, enc_ends = [], [], [], [], []
    for u in range(units):
        encs.append(
            Spread(
                place, sems, lambda k, u=u: enc_ref.at[u], lambda k, u=u: enc_vm.at[0, u], kinds=(0,)
            )
        )
        pair_sems, twin_sems, end_sems = sems.take(2), sems.take(2), sems.take(2)
        enc_pairs.append(remote(enc_ref.at[u], enc_vm.at[1, u], *pair_sems, place.pair()))
        enc_onwards.append(remote(enc_vm.at[0, u], enc_vm.at[1, u], *pair_sems, place.pair()))
        enc_twins.append(remote(enc_vm.at[0, u], enc_vm.at[2, u], *twin_sems, place.twin()))
        enc_ends.append(remote(enc_vm.at[1, u], enc_vm.at[3, u], *end_sems, place.twin()))
    enc_keeps = [
        pltpu.make_async_copy(enc_vm.at[i], enc_out.at[i], sem) for i, sem in enumerate(sems.take(4))
    ]
    home = place.at_home()
    away = jnp.logical_not(home)
    loads = [
        pltpu.make_async_copy(src, dst, sem)
        for src, dst, sem in zip(
            (x_out, halves[0], halves[1], halves[2].at[0], small_out, halves[2].at[pl.ds(1, 2)]),
            (x_vm, w_vm, so_vm, cq_w, small_vm, kv_w),
            sems.take(6),
        )
    ]
    keeps = [
        pltpu.make_async_copy(src, dst, sem)
        for src, dst, sem in zip(
            (q_vm, k_vm, v_vm, sa_vm, lse_vm, h1_vm, unit_vm, scale_vm, cq_vm, k_all, v_all),
            kept,
            sems.take(11),
        )
    ]
    swap_sems = sems.take(4)
    own = 2 * rows
    swap_part = remote(part_vm, twin_vm, swap_sems[0], swap_sems[1], place.twin())
    swap_h1 = remote(
        h1_vm.at[pl.ds(0, own)], h1_vm.at[pl.ds(own, own)], swap_sems[2], swap_sems[3], place.twin()
    )

    for gather in gathers:
        gather.own.start()
    small_own.start()
    place.meet(column_peers(n_mem) + plane_peers(plane))
    for gather in gathers:
        gather.begin()
    small_line.start()
    map_copy.start()
    spread.start()
    for gather in gathers:
        gather.share(1)
    for gather in gathers:
        gather.share(2)
    gathers[0].forward(1)
    for k in range(2):
        spread.wait_recv(k)
        twin[k].start()
    for gather in gathers:
        gather.share(3)
    for u in range(units):
        encs[u].start()

        @pl.when(home)
        def _():
            enc_pairs[u].start()

    def first_arrival(u):
        encs[u].wait_recv(0)

        @pl.when(away)
        def _():
            enc_onwards[u].start()

        enc_twins[u].start()

    def second_arrival(u):
        @pl.when(home)
        def _():
            enc_pairs[u].wait()

        @pl.when(away)
        def _():
            enc_onwards[u].wait()

        enc_ends[u].start()

    for hops in (2, 3):
        gathers[0].forward(hops)
    for hops in (1, 2, 3):
        for gather in gathers[1:]:
            gather.forward(hops)
    for copy in twin:
        copy.wait_recv()
    small_own.wait()
    for s in range(1, n_mem):
        small_line.wait_recv(s)
    gathers[0].finish()
    for copy in (loads[0], loads[1], loads[4]):
        copy.start()
    for copy in (loads[0], loads[1], loads[4]):
        copy.wait()

    def half_row(row):
        lanes = pl.ds(pl.multiple_of(place.core * 2 * HD, 2 * HD), 2 * HD)
        return jnp.concatenate(
            [small_vm[b, :, lanes].astype(F32)[row : row + 1] for b in range(n_mem)], axis=1
        )

    def full_row(row):
        return jnp.concatenate(
            [small_vm[b].astype(F32)[row : row + 1] for b in range(n_mem)], axis=1
        )

    bias_q, bias_v = half_row(0), half_row(1)
    depth = x_vm.shape[1]

    def weight(ref):
        return ref[...].reshape(-1, ref.shape[-1])

    def project(span):
        x_tile = x_vm[span, :]
        q_vm[span, :] = ((mm(x_tile, weight(w_vm.at[0])) + bias_q) * 0.125).astype(BF16)
        k_vm[span, :] = mm(x_tile, weight(w_vm.at[1])).astype(BF16)
        v_vm[span, :] = (mm(x_tile, weight(w_vm.at[2])) + bias_v).astype(BF16)

    tiles(x_vm.shape[0], project)
    for copy in keeps[:3]:
        copy.start()
    pairs = q_vm.shape[1] // (2 * HD)
    for pair in range(pairs):
        self_attend(place, pair, q_vm, k_vm, v_vm, sa_vm, lse_vm, v_t, o_t)
        if pair in (0, pairs // 2):
            first_arrival(min(pair, 1))
    for copy in keeps[3:5]:
        copy.start()
    for gather in gathers[1:]:
        gather.finish()
    for copy in (loads[2], loads[3], loads[5]):
        copy.start()
    for copy in (loads[2], loads[3], loads[5]):
        copy.wait()

    def other_part(span):
        part_vm[span, :] = mm(
            sa_vm[pl.ds(pl.multiple_of(span.start + own, BLK), BLK), :], weight(so_vm)
        ).astype(BF16)

    tiles(own, other_part)
    swap_part.start()

    def own_part(span):
        unit_vm[span, :] = mm(sa_vm[span, :], weight(so_vm)) + x_vm[span, :].astype(F32)

    tiles(own, own_part)
    for u in range(2, units):
        first_arrival(u)
    bias_out = full_row(2)
    gain, shift = full_row(n_bias), full_row(6)
    swap_part.wait()

    def normalise(span):
        values = unit_vm[span, :] + twin_vm[span, :].astype(F32) + bias_out
        centre = values - jnp.mean(values, axis=-1, keepdims=True)
        scale = lax.rsqrt(jnp.mean(centre * centre, axis=-1, keepdims=True) + 1e-05)
        unit = centre * scale
        unit_vm[span, :] = unit
        scale_vm[span, :] = jnp.broadcast_to(scale, (BLK, scale_vm.shape[1]))
        h1_vm[span, :] = (unit * gain + shift).astype(BF16)

    tiles(own, normalise)
    swap_h1.start()
    for copy in keeps[6:8]:
        copy.start()
    bias_cq = half_row(3)

    def queries(span):
        cq_vm[span, :] = ((mm(h1_vm[span, :], weight(cq_w)) + bias_cq) * 0.125).astype(BF16)

    tiles(own, queries)
    swap_h1.wait()
    keeps[5].start()

    def other_queries(span):
        queries(pl.ds(pl.multiple_of(span.start + own, BLK), BLK))

    tiles(own, other_queries)
    keeps[8].start()

    map_copy.wait()
    near_map, far_map = map_ref[...], map_in[...]
    both_maps = jnp.where(home, near_map, far_map)
    mine = jnp.where(place.parity == 0, both_maps[:1], both_maps[1:])
    group = lax.div(mine, jnp.full_like(mine, units))
    index_out[...] = (group ^ (2 * place.core + place.parity)) * units + lax.rem(
        mine, jnp.full_like(mine, units)
    )

    bias_cv = half_row(4)

    def memory(block, u):
        rows_here = enc_vm[block, u]
        k_all[block * units + u] = mm(rows_here, weight(kv_w.at[0])).astype(BF16)
        v_all[block * units + u] = (mm(rows_here, weight(kv_w.at[1])) + bias_cv).astype(BF16)

    for u in range(units):
        second_arrival(u)
        memory(0, u)
    enc_keeps[0].start()
    enc_keeps[1].start()
    for block, copies in ((2, enc_twins), (1, None), (3, enc_ends)):
        for u in range(units):
            if copies is not None:
                copies[u].wait_recv()
            memory(block, u)
    enc_keeps[2].start()
    enc_keeps[3].start()
    for copy in keeps[9:]:
        copy.start()
    spread.wait_send()
    for copy in twin:
        copy.wait_send()
    small_line.wait_send()
    for item in encs:
        item.wait_send()
    for copy in enc_twins + enc_ends:
        copy.wait_send()
    for copy in keeps + enc_keeps:
        copy.wait()


def front(n_mem, plane, places, hidden_in, enc, passage_map, small, params):
    kinds = tuple(columns for _, columns in params)
    views = [half_views(shard, columns, n_mem, plane) for shard, columns in params]
    seg, width = hidden_in.shape[1:]
    rows, own = 4 * seg, 2 * seg
    part = width // 2
    pairs = part // (2 * HD)
    passages = 4 * enc.shape[0]
    shapes = (
        [((rows, width), BF16), ((4,) + enc.shape, BF16), ((1, passage_map.shape[1]), jnp.int32)]
        + [((n_mem,) + small.shape, BF16)]
        + [(full, BF16) for _, full in views]
    )
    kept = [
        ((rows, part), BF16),
        ((rows, part), BF16),
        ((rows, part), BF16),
        ((rows, part), BF16),
        ((pairs, 2, rows), F32),
        ((rows, width), BF16),
        ((own, width), F32),
        ((own, 2 * HD), F32),
        ((rows, part), BF16),
        ((passages, PLEN, part), BF16),
        ((passages, PLEN, part), BF16),
    ]
    scratch = [
        ((rows, width), BF16),
        (views[0][1], BF16),
        (views[1][1][1:], BF16),
        (views[2][1][1:], BF16),
        ((n_mem,) + small.shape, BF16),
    ] + kept + [
        ((2 * HD, rows), BF16),
        ((2 * HD, rows), F32),
        ((own, width), BF16),
        ((own, width), BF16),
        ((2,) + views[2][1][1:], BF16),
        ((4,) + enc.shape, BF16),
        (passage_map.shape, jnp.int32),
    ]
    scratch[2] = (views[1][1], BF16)
    outs = pl.pallas_call(
        functools.partial(front_kernel, n_mem, plane, kinds, places),
        in_specs=[VMEM] * (4 + len(params)),
        out_specs=[ANY, ANY, VMEM] + [ANY] * (len(shapes) + len(kept) - 3),
        out_shape=[jax.ShapeDtypeStruct(*item) for item in shapes + kept],
        scratch_shapes=[pltpu.VMEM(*item) for item in scratch]
        + [pltpu.SemaphoreType.DMA((90 + GATHER_SEMS * len(params),))],
        compiler_params=pltpu.CompilerParams(
            collective_id=0, has_side_effects=True, vmem_limit_bytes=60 * 2**20
        ),
        cost_estimate=pl.CostEstimate(
            flops=rows * width * part * 10, bytes_accessed=40 * 2**20, transcendentals=rows * rows * 8
        ),
        name="front",
    )(hidden_in, enc, passage_map, small, *[view for view, _ in views])
    count = 4 + len(params)
    return outs[:4], outs[4:count], outs[count:]


class PlaneSum:
    def __init__(self, place, sems, grad, own, bufs, rows, lanes=None):
        self.own = own
        self.from_near, self.via, self.add = bufs
        quarter = place.quarter
        first, count = rows
        half = count // 2
        self.lead, self.n_mem = own.shape[:2]
        lanes = pl.ds(*(lanes or (0, grad.shape[-1])))

        def piece(t, lo, size):
            return grad.at[:, :, flip(quarter, t), pl.ds(first + lo, size), lanes]

        loads = sems.take(3)
        self.loads = [pltpu.make_async_copy(piece(0, 0, count), own, loads[0])]
        send, recv = sems.take(6), sems.take(6)
        self.onward, self.direct, self.summed = [], [], []
        for t in (1, 2):
            lo = (t - 1) * half
            self.onward.append(
                remote(piece(3, lo, half), self.via.at[t - 1], send[t - 1], recv[t - 1], place.near(t))
            )
            self.direct.append(
                remote(
                    piece(t, lo, half),
                    self.from_near.at[t - 1, :, :, pl.ds(lo, half)],
                    send[t + 1],
                    recv[t + 1],
                    place.near(t),
                )
            )
            other = half - lo
            self.loads.append(
                pltpu.make_async_copy(piece(t, other, half), self.add.at[t - 1], loads[t])
            )
            self.summed.append(
                remote(
                    self.add.at[t - 1],
                    self.from_near.at[t - 1, :, :, pl.ds(other, half)],
                    send[t + 3],
                    recv[t + 3],
                    place.near(t),
                )
            )

    def start(self):
        for copy in self.onward + self.loads + self.direct:
            copy.start()

    def each(self, step):
        def run(i, carry):
            step(lax.div(i, jnp.int32(self.n_mem)), lax.rem(i, jnp.int32(self.n_mem)))
            return carry

        lax.fori_loop(0, self.lead * self.n_mem, run, 0)

    def middle(self):
        for copy in self.loads:
            copy.wait()
        for t in (1, 2):
            self.onward[2 - t].wait_recv()

            def add(l, m, t=t):
                total = self.add[t - 1, l, m].astype(F32) + self.via[2 - t, l, m].astype(F32)
                self.add[t - 1, l, m] = total.astype(BF16)

            self.each(add)
            self.summed[t - 1].start()

    def end(self):
        for copy in self.direct + self.summed:
            copy.wait_recv()

        def add(l, m):
            total = self.own[l, m].astype(F32)
            for t in range(2):
                total += self.from_near[t, l, m].astype(F32)
            self.own[l, m] = total.astype(BF16)

        self.each(add)

    def wait_send(self):
        for copy in self.onward + self.direct + self.summed:
            copy.wait_send()


class Settle:
    def __init__(self, place, sems, own, out, bufs, columns, n_mem, rows, lane=0):
        self.place, self.n_mem, self.columns, self.rows = place, n_mem, columns, rows
        self.lane = lane
        self.own, self.out = own, out
        self.line_in, self.far_in, self.slots = bufs
        quarter, mem, core = place.quarter, place.mem, place.core
        slots = self.slots

        def slot(t):
            return slots.at[flip(quarter, t), core]

        self.line = Line(
            place, sems, lambda s: own.at[:, flip(mem, s)], lambda s: self.line_in.at[s - 1], n_mem
        )
        others = place.planes - 1
        far_send, far_recv = sems.take(others), sems.take(others)
        self.far = [
            remote(slot(0), self.far_in.at[r - 1], far_send[r - 1], far_recv[r - 1], place.far(r))
            for r in range(1, place.planes)
        ]
        self.share = Share(place, sems, slot(0), slot)
        twin_send, twin_recv = sems.take(place.plane), sems.take(place.plane)
        self.twin = [
            remote(slot(t), slot(t), twin_send[t], twin_recv[t], place.twin())
            for t in range(place.plane)
        ]

    def start(self):
        self.line.start()

    def middle(self):
        for s in range(1, self.n_mem):
            self.line.wait_recv(s)
        quarter, core, mem = self.place.quarter, self.place.core, self.place.mem
        lead = self.own.shape[0]
        for l in range(lead):
            total = self.own[l, mem].astype(F32)
            for s in range(self.n_mem - 1):
                total += self.line_in[s, l].astype(F32)
            self.slots[quarter, core, l] = total.astype(BF16)
        if self.far:
            for copy in self.far:
                copy.start()
            for copy in self.far:
                copy.wait()
            for l in range(lead):
                total = self.slots[quarter, core, l].astype(F32)
                for r in range(len(self.far)):
                    total += self.far_in[r, l].astype(F32)
                self.slots[quarter, core, l] = total.astype(BF16)
        self.share.start()
        self.twin[0].start()

    def forward(self):
        self.share.forward()
        self.twin[1].start()
        self.twin[2].start()

    def end(self):
        self.share.wait()
        self.twin[3].start()
        for copy in self.twin:
            copy.wait()
        self.line.wait_send()
        lead = self.own.shape[0]
        wide = self.slots.shape[-1]
        first, count = self.rows
        for q in range(self.place.plane):
            for c in range(2):
                for l in range(lead):
                    if self.columns:
                        unit = self.out.shape[-1] // (2 * self.n_mem)
                        for b in range(wide // unit):
                            start = unit * (2 * (self.lane // unit + b) + c)
                            self.out[l, q, first : first + count, start : start + unit] = self.slots[
                                q, c, l, :, b * unit : (b + 1) * unit
                            ]
                    else:
                        self.out[c, q, first : first + count] = self.slots[q, c, l]


PLANE_SUM_SEMS = 15


def settle_sems(n_mem, plane, planes):
    return 2 * (n_mem - 1) + 2 * (planes - 1) + 8 + 2 * plane


def plane_sum_scratch(grad_shape, n_mem, count, cols=None):
    lead, cols = grad_shape[0], cols or grad_shape[-1]
    return [
        pltpu.VMEM((2, lead, n_mem, count, cols), BF16),
        pltpu.VMEM((2, lead, n_mem, count // 2, cols), BF16),
        pltpu.VMEM((2, lead, n_mem, count // 2, cols), BF16),
    ]


def settle_scratch(grad_shape, n_mem, plane, planes, count, cols=None):
    lead, cols = grad_shape[0], cols or grad_shape[-1]
    return [
        pltpu.VMEM((n_mem - 1, lead, count, cols), BF16),
        pltpu.VMEM((max(planes - 1, 1), lead, count, cols), BF16),
        pltpu.VMEM((plane, 2, lead, count, cols), BF16),
    ]


def sum_shape(grad_shape):
    lead, n_mem, _, rows, cols = grad_shape
    return jax.ShapeDtypeStruct((lead, n_mem, rows, cols), BF16)


def reduce_out(grad_shape, columns, plane):
    lead, _, _, rows, cols = grad_shape
    shape = (lead, plane, rows, 2 * cols) if columns else (2, plane, rows, cols)
    return jax.ShapeDtypeStruct(shape, BF16)


def reduce_peers(n_mem, plane, planes):
    return (
        [(1, 0)]
        + [(0, s) for s in range(1, n_mem)]
        + plane_peers(plane)
        + [(2 * plane * r, 0) for r in range(1, planes)]
    )


def whole(shape):
    return pl.BlockSpec(shape, lambda *grid: (0,) * len(shape))


class Fetch:
    def __init__(self, sems, src, dst):
        self.copy = pltpu.make_async_copy(src, dst, sems.take(1)[0])
        self.dst = dst
        self.here = False

    def start(self):
        self.copy.start()

    def get(self):
        if not self.here:
            self.copy.wait()
            self.here = True
        return self.dst


def unit_norm(values):
    centre = values - jnp.mean(values, axis=-1, keepdims=True)
    scale = lax.rsqrt(jnp.mean(centre * centre, axis=-1, keepdims=True) + 1e-05)
    return centre * scale, scale


def unit_norm_back(grad, unit, scale, gain):
    inner = grad * gain
    return (
        inner
        - jnp.mean(inner, axis=-1, keepdims=True)
        - unit * jnp.mean(inner * unit, axis=-1, keepdims=True)
    ) * scale


def feed_kernel(n_mem, plane, cot_ref, rows_ref, bias_ref, *refs):
    refs = Walk(refs)
    fetched = refs.take(4)
    out_part = refs.one()
    final_out, dca_ref, dz2_ref, sums_ref, bias_sum, own_out, dw_in, dw_co = refs.take(8)
    kept = refs.take(4)
    out_w = refs.one()
    cot_vm, h2_vm, unit_vm, scale_vm, act_vm, slope_vm, p_vm, part_vm, twin_vm = refs.take(9)
    final_vm, df_vm, dco_vm, dw_out = refs.take(4)
    bufs = refs.take(3)
    sems = Sems(refs.one())
    place = Place(plane)
    ca, unit1, w_co, w_in = [Fetch(sems, src, dst) for src, dst in zip(fetched, kept)]
    mem, quarter = place.mem, place.quarter
    own_piece = Fetch(sems, out_part.at[0, mem], out_w.at[0, mem])
    pieces = []
    for d in range(1, n_mem):
        source = lax.rem(mem + jnp.int32(n_mem - d), jnp.int32(n_mem))

        def place_of(t, source=source):
            return out_w.at[:, source, flip(quarter, t)]

        (sem,) = sems.take(1)
        pieces.append(
            (
                mem < d if d == 1 else mem >= (d if d == n_mem - 1 else 0),
                pltpu.make_async_copy(out_part.at[0, source], out_w.at[0, source], sem),
                pltpu.make_async_copy(out_part.at[:, source, quarter], place_of(0), sem),
                Share(place, sems, place_of(0), place_of),
            )
        )

    def each_piece(whole_step, part_step):
        for part, whole_copy, part_copy, share in pieces:
            if whole_step is not None:

                @pl.when(jnp.logical_not(part))
                def _():
                    whole_step(whole_copy)

            @pl.when(part)
            def _():
                part_step(part_copy, share)

    rows = h2_vm.shape[0]
    own = rows // 2
    seg = own // 2
    hidden = act_vm.shape[1]
    block = hidden // n_mem
    out_sum = PlaneSum(place, sems, dw_out, own_out, bufs, (0, own_out.shape[2]))
    spread_cot = Spread(
        place,
        sems,
        lambda k: cot_ref.at[flip(place.parity, k)],
        lambda k: cot_vm.at[pl.ds(seg * k, seg)],
    )
    spread_final = Spread(
        place,
        sems,
        lambda k: final_vm.at[pl.ds(seg * k, seg)],
        lambda k: final_out.at[place.parity],
    )

    def swap(src, dst):
        send, recv = sems.take(2)
        return remote(src, dst, send, recv, place.twin())

    def half_lanes(ref, i):
        wide = ref.shape[1] // 2
        return ref.at[:, pl.ds(i * wide, wide)]

    swap_co = swap(part_vm, twin_vm)
    swap_h2 = swap(h2_vm.at[pl.ds(0, own)], h2_vm.at[pl.ds(own, own)])
    swap_ffn = [swap(half_lanes(part_vm, i), half_lanes(twin_vm, i)) for i in range(2)]
    swap_df = swap(df_vm.at[pl.ds(0, own)], df_vm.at[pl.ds(own, own)])
    swap_dh2 = [swap(half_lanes(part_vm, i), half_lanes(twin_vm, i)) for i in range(2)]
    swap_dco = swap(dco_vm.at[pl.ds(0, own)], dco_vm.at[pl.ds(own, own)])

    for item in (ca, w_co, own_piece):
        item.start()
    each_piece(lambda copy: copy.start(), lambda copy, share: copy.start())
    for item in (unit1, w_in):
        item.start()
    place.meet(column_peers(n_mem) + plane_peers(plane))
    spread_cot.start()

    def share_start(copy, share):
        copy.wait()
        share.start()

    each_piece(None, share_start)
    row = {name: rows_ref[i : i + 1, :] for i, name in enumerate(("g0", "b6", "b5", "g1", "b7", "b9", "g2", "b8"))}
    sums_ref[...] = jnp.zeros_like(sums_ref)
    bias_sum[...] = jnp.zeros_like(bias_sum)

    def after(span):
        return pl.ds(pl.multiple_of(span.start + own, BLK), BLK)

    ca, w_co = ca.get(), w_co.get()

    def co_other(span):
        part_vm[span, :] = mm(ca[after(span), :], w_co[...]).astype(BF16)

    tiles(own, co_other)
    swap_co.start()
    unit1 = unit1.get()

    def co_own(span):
        p_vm[span, :] = unit1[span, :] * row["g0"] + row["b6"] + mm(ca[span, :], w_co[...])

    tiles(own, co_own)
    swap_co.wait()

    def second_norm(span):
        values = p_vm[span, :] + twin_vm[span, :].astype(F32) + row["b5"]
        unit, scale = unit_norm(values)
        unit_vm[span, :] = unit
        scale_vm[span, :] = jnp.broadcast_to(scale, (BLK, scale_vm.shape[1]))
        h2_vm[span, :] = (unit * row["g1"] + row["b7"]).astype(BF16)

    tiles(own, second_norm)
    swap_h2.start()
    w_in = w_in.get()

    def forward(span):
        def part(i, carry):
            lanes = pl.ds(pl.multiple_of(i * block, block), block)
            pre = mm(h2_vm[span, :], w_in[:, lanes]) + bias_ref[:, lanes]
            cdf = 0.5 * (1.0 + lax.erf(pre * 0.7071067811865476))
            act_vm[span, lanes] = (pre * cdf).astype(BF16)
            density = jnp.exp(-0.5 * pre * pre) * 0.3989422804014327
            slope_vm[span, lanes] = (cdf + pre * density).astype(BF16)
            return carry

        lax.fori_loop(0, n_mem, part, 0)

    ours, others = pl.ds(0, own), pl.ds(own, own)
    width = h2_vm.shape[1]
    column = width // 2
    each_piece(None, lambda copy, share: share.forward())
    forward(ours)
    swap_h2.wait()
    forward(others)
    own_piece.get()
    each_piece(lambda copy: copy.wait(), lambda copy, share: share.wait())
    for i in range(2):
        lanes = slice(i * column, (i + 1) * column)
        weights = out_w[0, :, :, :, lanes].reshape(hidden, column)
        part_vm[:, lanes] = mm(act_vm[others, :], weights).astype(BF16)
        swap_ffn[i].start()
    p_vm[...] = mm(act_vm[ours, :], out_w[0].reshape(hidden, width))
    for k in range(2):
        spread_cot.wait_recv(k)
    for copy in swap_ffn:
        copy.wait()

    def third_norm(span):
        values = (
            unit_vm[span, :] * row["g1"]
            + row["b7"]
            + p_vm[span, :]
            + twin_vm[span, :].astype(F32)
            + row["b9"]
        )
        unit, scale = unit_norm(values)
        final_vm[span, :] = (unit * row["g2"] + row["b8"]).astype(BF16)
        grad = cot_vm[span, :].astype(F32)
        out = unit_norm_back(grad, unit, scale, row["g2"])
        dz2_ref[span, :] = out
        low = out.astype(BF16)
        df_vm[span, :] = low
        sums_ref[0:1, :] += jnp.sum(grad * unit, axis=0, keepdims=True)
        sums_ref[1:2, :] += jnp.sum(grad, axis=0, keepdims=True)
        sums_ref[2:3, :] += jnp.sum(low.astype(F32), axis=0, keepdims=True)

    tiles(own, third_norm)
    swap_df.start()
    spread_final.start()
    swap_df.wait()

    def out_weights(m, carry):
        lanes = pl.ds(pl.multiple_of(m * block, block), block)
        dw_out[0, m] = mm(act_vm[:, lanes].T, df_vm[...]).astype(BF16).reshape(dw_out.shape[2:])
        return carry

    lax.fori_loop(0, n_mem, out_weights, 0)
    out_sum.start()

    def hidden_grad(i, carry):
        lanes = pl.ds(pl.multiple_of(i * block, block), block)
        weights = out_w[0, i].reshape(block, width)
        grad = mm(df_vm[...], weights, NT) * slope_vm[:, lanes].astype(F32)
        low = grad.astype(BF16)
        slope_vm[:, lanes] = low
        bias_sum[:, lanes] = jnp.sum(low.astype(F32), axis=0, keepdims=True)
        return carry

    lax.fori_loop(0, n_mem, hidden_grad, 0)
    narrow = width // 4
    for i in range(2):
        for j in (2 * i, 2 * i + 1):
            lanes = slice(j * narrow, (j + 1) * narrow)
            grad = mm(slope_vm[...], w_in[lanes, :], NT)
            part_vm[:, lanes] = grad[own:].astype(BF16)
            dz2_ref[:, lanes] += grad[:own]
        swap_dh2[i].start()
        if i == 0:
            out_sum.middle()
    for copy in swap_dh2:
        copy.wait()

    def second_back(span):
        grad = dz2_ref[span, :] + twin_vm[span, :].astype(F32)
        unit = unit_vm[span, :]
        out = unit_norm_back(grad, unit, scale_vm[span, :1], row["g1"])
        dz2_ref[span, :] = out
        low = out.astype(BF16)
        dco_vm[span, :] = low
        sums_ref[3:4, :] += jnp.sum(grad * unit, axis=0, keepdims=True)
        sums_ref[4:5, :] += jnp.sum(grad, axis=0, keepdims=True)
        sums_ref[5:6, :] += jnp.sum(low.astype(F32), axis=0, keepdims=True)

    tiles(own, second_back)
    swap_dco.start()
    depth = h2_vm.shape[1] // n_mem

    def in_weights(m, carry):
        lanes = pl.ds(pl.multiple_of(m * depth, depth), depth)
        dw_in[0, m] = mm(h2_vm[:, lanes].T, slope_vm[...]).astype(BF16).reshape(dw_in.shape[2:])
        return carry

    lax.fori_loop(0, n_mem, in_weights, 0)
    swap_dco.wait()

    dca_ref[...] = mm(dco_vm[...], w_co[...], NT).astype(BF16)
    heads = ca.shape[1] // n_mem

    def co_weights(m, carry):
        lanes = pl.ds(pl.multiple_of(m * heads, heads), heads)
        dw_co[0, m] = mm(ca[:, lanes].T, dco_vm[...]).astype(BF16).reshape(dw_co.shape[2:])
        return carry

    lax.fori_loop(0, n_mem, co_weights, 0)
    out_sum.end()
    out_sum.wait_send()
    spread_cot.wait_send()
    for k in range(2):
        spread_final.wait_recv(k)
    spread_final.wait_send()


def feed(n_mem, plane, cotangent, vectors, bias, ca, unit1, w_co, w_in, w_out):
    rows, part = ca.shape
    width, hidden = w_in.shape
    own = rows // 2

    def grad_shape(depth, cols):
        return (1, n_mem, plane, depth // (n_mem * plane), cols)

    out_shape, in_shape = grad_shape(hidden, width), grad_shape(width, hidden)
    shapes = [
        jax.ShapeDtypeStruct((2, own // 2, width), BF16),
        jax.ShapeDtypeStruct((rows, part), BF16),
        jax.ShapeDtypeStruct((own, width), F32),
        jax.ShapeDtypeStruct((8, width), F32),
        jax.ShapeDtypeStruct((1, hidden), F32),
        sum_shape(out_shape),
        jax.ShapeDtypeStruct(in_shape, BF16),
        jax.ShapeDtypeStruct(grad_shape(part, width), BF16),
    ]
    fetched = [ca, unit1, w_co, w_in, w_out]
    scratch = [pltpu.VMEM(item.shape, item.dtype) for item in fetched] + [
        pltpu.VMEM((own, width), BF16),
        pltpu.VMEM((rows, width), BF16),
        pltpu.VMEM((own, width), F32),
        pltpu.VMEM((own, 2 * HD), F32),
        pltpu.VMEM((rows, hidden), BF16),
        pltpu.VMEM((rows, hidden), BF16),
        pltpu.VMEM((own, width), F32),
        pltpu.VMEM((own, width), BF16),
        pltpu.VMEM((own, width), BF16),
        pltpu.VMEM((own, width), BF16),
        pltpu.VMEM((rows, width), BF16),
        pltpu.VMEM((rows, width), BF16),
        pltpu.VMEM(out_shape, BF16),
    ]
    scratch += plane_sum_scratch(out_shape, n_mem, out_shape[3])
    scratch += [pltpu.SemaphoreType.DMA((PLANE_SUM_SEMS + 60,))]
    return pl.pallas_call(
        functools.partial(feed_kernel, n_mem, plane),
        in_specs=[VMEM] * 3 + [ANY] * len(fetched),
        out_specs=[ANY] + [VMEM] * (len(shapes) - 1),
        out_shape=shapes,
        scratch_shapes=scratch,
        compiler_params=pltpu.CompilerParams(
            vmem_limit_bytes=60 * 2**20, collective_id=1, has_side_effects=True
        ),
        cost_estimate=pl.CostEstimate(
            flops=rows * width * hidden * 12, bytes_accessed=40 * 2**20, transcendentals=rows * hidden * 2
        ),
        name="feed",
    )(cotangent, vectors, bias, *fetched)


def middle_kernel(n_mem, plane, planes, settled, slot_ref, member_ref, index_ref, *refs):
    refs = Walk(refs)
    dq_ref, dk_ref, dv_ref, wc_ref, scale_ref, gain_ref = refs.take(6)
    fetched = refs.take(6)
    ready = refs.take(len(settled))
    dsa_ref, dz1_ref, sums_ref, enc_out, own_cross, own_so = refs.take(6)
    outs = refs.take(len(settled))
    kept = refs.take(6)
    wk_t, wv_t, named_ref = refs.take(3)
    theirs, mine, twin_in, pair_in, dw_cross, dw_so, part_vm, twin_vm, dso_vm = refs.take(9)
    cross_bufs, so_bufs = refs.take(3), refs.take(3)
    settle_bufs = [refs.take(3) for _ in settled]
    sems = Sems(refs.one())
    place = Place(plane, planes)
    fetches = [Fetch(sems, src, dst) for src, dst in zip(fetched, kept)]
    h1_ref, enc_ref, dz2_ref, unit_ref, so_ref, sa_ref = kept
    settles = [
        Settle(
            place, sems, ready[i], outs[i], settle_bufs[i], columns, n_mem, (0, ready[i].shape[2])
        )
        for i, columns in enumerate(settled)
    ]
    cross_sum = PlaneSum(place, sems, dw_cross, own_cross, cross_bufs, (0, dw_cross.shape[3]))
    so_sum = PlaneSum(place, sems, dw_so, own_so, so_bufs, (0, dw_so.shape[3]))
    passages = mine.shape[0]
    units = passages // 2
    twin_sems = sems.take(2 * passages)
    twins = [
        remote(theirs.at[u], twin_in.at[u], twin_sems[2 * u], twin_sems[2 * u + 1], place.twin())
        for u in range(passages)
    ]
    pair_sems = sems.take(2 * units)
    pairs = [
        remote(
            mine.at[units + u], pair_in.at[u], pair_sems[2 * u], pair_sems[2 * u + 1], place.pair()
        )
        for u in range(units)
    ]
    homes = [
        Spread(place, sems, lambda k, u=u: mine.at[u], lambda k, u=u: enc_out.at[u], kinds=(0,))
        for u in range(units)
    ]
    swap_sems = sems.take(4)
    own = dz2_ref.shape[0]
    swap_part = remote(part_vm, twin_vm, swap_sems[0], swap_sems[1], place.twin())
    swap_dso = remote(
        dso_vm.at[pl.ds(0, own)], dso_vm.at[pl.ds(own, own)], swap_sems[2], swap_sems[3], place.twin()
    )

    for item in fetches:
        item.start()
    wk_t[...] = wc_ref[1].T
    wv_t[...] = wc_ref[2].T
    place.meet(
        column_peers(n_mem) + plane_peers(plane) + [(2 * plane * r, 0) for r in range(1, planes)]
    )
    for item in settles:
        item.start()

    def passage_grad(u):
        slot = slot_ref[u]
        value = mm(dk_ref[slot], wk_t[...]) + mm(dv_ref[slot], wv_t[...])
        return (value * member_ref[u]).astype(BF16)

    def add_twin(u):
        twins[u].wait_recv()

        def add(i, carry):
            span = pl.ds(pl.multiple_of(i * 64, 64), 64)
            total = mine[u, span, :].astype(F32) + twin_in[u, span, :].astype(F32)
            mine[u, span, :] = total.astype(BF16)
            return carry

        lax.fori_loop(0, PLEN // 64, add, 0)

    def send_home(u):
        add_twin(u)
        pairs[u].wait_recv()

        def add(i, carry):
            span = pl.ds(pl.multiple_of(i * 64, 64), 64)
            total = mine[u, span, :].astype(F32) + pair_in[u, span, :].astype(F32)
            mine[u, span, :] = total.astype(BF16)
            return carry

        lax.fori_loop(0, PLEN // 64, add, 0)
        homes[u].start()

    for group in (range(units, passages), range(units)):
        for u in group:
            theirs[u] = passage_grad(passages + u)
            twins[u].start()
        for u in group:
            mine[u] = passage_grad(u)
        if group.start:
            for u in group:
                add_twin(u)
                pairs[u - units].start()

    for item in fetches:
        item.get()
    for j in range(index_ref.shape[0]):
        named_ref[j * PLEN : (j + 1) * PLEN, :] = enc_ref[index_ref[j]]

    part = dw_cross.shape[-1]
    depth = h1_ref.shape[1] // n_mem

    def stacked(ref):
        return ref[...].reshape(-1, ref.shape[-1])

    def cross_weights(m, carry):
        lanes = pl.ds(pl.multiple_of(m * depth, depth), depth)
        split = dw_cross.shape[2:]
        dw_cross[0, m] = (
            (mm(h1_ref[:, lanes].T, dq_ref[...]) * 0.125).astype(BF16).reshape(split)
        )
        named_t = named_ref[:, lanes].T
        dw_cross[1, m] = mm(named_t, stacked(dk_ref)).astype(BF16).reshape(split)
        dw_cross[2, m] = mm(named_t, stacked(dv_ref)).astype(BF16).reshape(split)
        return carry

    lax.fori_loop(0, n_mem // 2, cross_weights, 0)
    send_home(0)
    lax.fori_loop(n_mem // 2, n_mem, cross_weights, 0)
    cross_sum.start()

    part_vm[...] = (mm(dq_ref[own:, :], wc_ref[0], NT) * 0.125).astype(BF16)
    swap_part.start()
    dz1_ref[...] = dz2_ref[...] + mm(dq_ref[:own, :], wc_ref[0], NT) * 0.125
    sums_ref[...] = jnp.zeros_like(sums_ref)
    sums_ref[3:4, :part] = 0.125 * jnp.sum(dq_ref[...].astype(F32), axis=0, keepdims=True)
    sums_ref[4:5, :part] = jnp.sum(stacked(dv_ref).astype(F32), axis=0, keepdims=True)
    send_home(1)
    swap_part.wait()
    gain = gain_ref[...]

    def norm(span):
        grad = dz1_ref[span, :] + twin_vm[span, :].astype(F32)
        unit = unit_ref[span, :]
        inner = grad * gain
        out = (
            inner
            - jnp.mean(inner, axis=-1, keepdims=True)
            - unit * jnp.mean(inner * unit, axis=-1, keepdims=True)
        ) * scale_ref[span, :1]
        dz1_ref[span, :] = out
        low = out.astype(BF16)
        dso_vm[span, :] = low
        sums_ref[0:1, :] += jnp.sum(grad * unit, axis=0, keepdims=True)
        sums_ref[1:2, :] += jnp.sum(grad, axis=0, keepdims=True)
        sums_ref[2:3, :] += jnp.sum(low.astype(F32), axis=0, keepdims=True)

    tiles(own, norm)
    swap_dso.start()
    cross_sum.middle()

    dsa_ref[:own, :] = mm(dso_vm[:own, :], so_ref[...], NT).astype(BF16)
    for u in range(2, units):
        send_home(u)
    swap_dso.wait()
    dsa_ref[own:, :] = mm(dso_vm[own:, :], so_ref[...], NT).astype(BF16)
    block = sa_ref.shape[1] // n_mem

    def so_weights(m, carry):
        lanes = pl.ds(pl.multiple_of(m * block, block), block)
        dw_so[0, m] = (
            mm(sa_ref[:, lanes].T, dso_vm[...]).astype(BF16).reshape(dw_so.shape[2:])
        )
        return carry

    lax.fori_loop(0, n_mem, so_weights, 0)
    so_sum.start()
    for item in settles:
        item.middle()
    cross_sum.end()
    for item in settles:
        item.forward()
    so_sum.middle()
    for item in settles:
        item.end()
    so_sum.end()
    cross_sum.wait_send()
    so_sum.wait_send()
    for copy in twins + pairs:
        copy.wait_send()
    for item in homes:
        item.wait_recv(0)
        item.wait_send()


def middle(
    n_mem, plane, planes, slot, member, index, dq, dk, dv, wc, so, sa, h1, enc, dz2, unit, scale, gain, ready
):
    rows, part = dq.shape
    width = h1.shape[1]
    own = rows // 2
    passages = slot.shape[0] // 2
    settled = tuple(columns for _, columns in ready)
    settled_shapes = [item.shape[:2] + (plane,) + item.shape[2:] for item, _ in ready]
    cross_shape = (3, n_mem, plane, width // (n_mem * plane), part)
    so_shape = (1, n_mem, plane, part // (n_mem * plane), width)
    shapes = [
        jax.ShapeDtypeStruct((rows, part), BF16),
        jax.ShapeDtypeStruct((own, width), F32),
        jax.ShapeDtypeStruct((8, width), F32),
        jax.ShapeDtypeStruct((passages // 2, PLEN, width), BF16),
        sum_shape(cross_shape),
        sum_shape(so_shape),
    ] + [reduce_out(shape, columns, plane) for shape, columns in zip(settled_shapes, settled)]
    fetched = [h1, enc, dz2, unit, so, sa]
    scratch = [pltpu.VMEM(item.shape, item.dtype) for item in fetched] + [
        pltpu.VMEM((part, width), BF16),
        pltpu.VMEM((part, width), BF16),
        pltpu.VMEM(dk.shape[:1] + (width,), BF16),
        pltpu.VMEM((passages, PLEN, width), BF16),
        pltpu.VMEM((passages, PLEN, width), BF16),
        pltpu.VMEM((passages, PLEN, width), BF16),
        pltpu.VMEM((passages // 2, PLEN, width), BF16),
        pltpu.VMEM(cross_shape, BF16),
        pltpu.VMEM(so_shape, BF16),
        pltpu.VMEM((own, width), BF16),
        pltpu.VMEM((own, width), BF16),
        pltpu.VMEM((rows, width), BF16),
    ]
    scratch += plane_sum_scratch(cross_shape, n_mem, cross_shape[3])
    scratch += plane_sum_scratch(so_shape, n_mem, so_shape[3])
    for shape in settled_shapes:
        scratch += settle_scratch(shape, n_mem, plane, planes, shape[3])
    count = (
        len(ready) * settle_sems(n_mem, plane, planes) + 2 * PLANE_SUM_SEMS + 2 * passages
        + passages + 4 * passages // 2 + 4 + 6
    )
    smem = pl.BlockSpec(memory_space=pltpu.SMEM)
    outs = pl.pallas_call(
        functools.partial(middle_kernel, n_mem, plane, planes, settled),
        in_specs=[smem, smem, smem] + [VMEM] * 6 + [ANY] * 6 + [VMEM] * len(ready),
        out_specs=[VMEM] * 3 + [ANY] + [VMEM] * (2 + len(ready)),
        out_shape=shapes,
        scratch_shapes=scratch + [pltpu.SemaphoreType.DMA((count,))],
        compiler_params=pltpu.CompilerParams(
            vmem_limit_bytes=60 * 2**20, collective_id=3, has_side_effects=True
        ),
        cost_estimate=pl.CostEstimate(
            flops=rows * part * width * 30, bytes_accessed=40 * 2**20, transcendentals=0
        ),
        name="middle",
    )(
        slot,
        member,
        index,
        dq,
        dk.reshape(-1, PLEN, part),
        dv.reshape(-1, PLEN, part),
        wc,
        scale,
        gain,
        *fetched,
        *[item for item, _ in ready],
    )
    return outs[:4], outs[4:6], outs[6:]


def self_attend_back(place, pair, q_vm, k_vm, v_vm, o_vm, do_vm, lse_vm, outs, scratch):
    dq_vm, dk_vm, dv_vm = outs
    q_a, do_a, k_t, q_h, do_h, p_vm, ds_vm = scratch
    base = 2 * place.core + place.parity
    count = q_vm.shape[0] // BLK
    lanes = pl.ds(pl.multiple_of(pair * 2 * HD, 2 * HD), 2 * HD)

    def rows(i):
        return pl.ds(pl.multiple_of(flip(base, i) * BLK, BLK), BLK)

    for i in range(count):
        span = slice(i * BLK, (i + 1) * BLK)
        q_a[span, :] = q_vm[rows(i), lanes]
        do_a[span, :] = do_vm[rows(i), lanes]
        k_t[:, span] = k_vm[rows(i), lanes].T
        q_t = q_a[span, :].T
        do_t = do_a[span, :].T
        prod = (do_a[span, :].astype(F32) * o_vm[rows(i), lanes].astype(F32)).T
        for head in range(2):
            delta = jnp.sum(prod[head * HD : (head + 1) * HD, :], axis=0, keepdims=True)
            q_h[head, :, span] = head_rows(q_t, head, lse_vm[pair, head : head + 1, span])
            do_h[head, :, span] = head_rows(do_t, head, delta)
    key_pos = lax.broadcasted_iota(jnp.int32, (BLK, BLK), 0)
    query_pos = lax.broadcasted_iota(jnp.int32, (BLK, BLK), 1)
    units = [(j, i, head) for j in range(count) for head in range(2) for i in range(j, count)]

    def products(unit):
        j, i, head = unit
        span = slice(i * BLK, (i + 1) * BLK)
        return (
            mm(ones_in(k_vm[rows(j), lanes], head), q_h[head, :, span]),
            mm(ones_in(v_vm[rows(j), lanes], head), do_h[head, :, span]),
        )

    ready = products(units[0])
    halves = {}
    for n, (j, i, head) in enumerate(units):
        coming = products(units[n + 1]) if n + 1 < len(units) else None
        scores, dprobs = ready
        probs = jnp.exp(scores)
        if i == j:
            probs = jnp.where(key_pos <= query_pos, probs, 0.0)
        keys, span = slice(j * BLK, (j + 1) * BLK), slice(i * BLK, (i + 1) * BLK)
        p_vm[head, keys, span] = probs.astype(BF16)
        ds_vm[head, keys, span] = (probs * dprobs).astype(BF16)
        if i == count - 1:
            late = slice(j * BLK, count * BLK)
            halves[head] = (
                mm(p_vm[head, keys, late], do_a[late, :]),
                mm(ds_vm[head, keys, late], q_a[late, :]),
            )
            if head == 1:
                dv_vm[rows(j), lanes] = pick_heads(halves[0][0], halves[1][0]).astype(BF16)
                dk_vm[rows(j), lanes] = pick_heads(halves[0][1], halves[1][1]).astype(BF16)
        ready = coming
    for i in range(count):
        span, keys = slice(i * BLK, (i + 1) * BLK), slice(0, (i + 1) * BLK)
        dq_t = jnp.concatenate(
            [
                mm(k_t[head * HD : (head + 1) * HD, keys], ds_vm[head, keys, span])
                for head in range(2)
            ],
            axis=0,
        )
        dq_vm[rows(i), lanes] = dq_t.T.astype(BF16) * BF16(0.125)


def last_kernel(n_mem, plane, planes, settled, chunks, *refs):
    refs = Walk(refs)
    q_ref, k_ref, v_ref, o_ref, do_ref, lse_ref, feed_ref, hidden_ref, middle_ref = refs.take(9)
    fetched = refs.take(3)
    ready = refs.take(len(settled))
    small_out, dx_out, self_out = refs.take(3)
    outs = refs.take(len(settled))
    x_ref, w_ref, dz1_ref = kept = refs.take(3)
    dq_vm, dk_vm, dv_vm = refs.take(3)
    attend_scratch = refs.take(7)
    x_t, dw_vm = refs.take(2)
    part_vm, twin_vm, dx_vm = refs.take(3)
    chunk_own = [refs.one() for _ in range(chunks)]
    chunk_bufs = [refs.take(3) for _ in range(chunks)]
    chunk_settle = [refs.take(3) for _ in range(chunks)]
    settle_bufs = [refs.take(3) for _ in settled]
    small_near, small_line, small_twin, small_far, small_sum, sem_ref = refs.take(6)
    sems = Sems(sem_ref)
    place = Place(plane, planes)
    fetches = [Fetch(sems, src, dst) for src, dst in zip(fetched, kept)]
    settles = [
        Settle(
            place, sems, ready[i], outs[i], settle_bufs[i], columns, n_mem, (0, ready[i].shape[2])
        )
        for i, columns in enumerate(settled)
    ]
    rows, part = q_ref.shape
    lanes = part // chunks
    depth = dw_vm.shape[3]
    sums = [
        PlaneSum(
            place, sems, dw_vm, chunk_own[c], chunk_bufs[c], (0, depth), (c * lanes, lanes)
        )
        for c in range(chunks)
    ]
    ends = [
        Settle(
            place, sems, chunk_own[c], self_out, chunk_settle[c], True, n_mem, (0, depth), c * lanes
        )
        for c in range(chunks)
    ]
    near_sems = sems.take(6)
    near = [
        remote(
            small_sum, small_near.at[t - 1], near_sems[2 * t - 2], near_sems[2 * t - 1], place.near(t)
        )
        for t in range(1, plane)
    ]
    line = Line(
        place, sems, lambda s: small_sum.at[flip(place.mem, s)], lambda s: small_line.at[s - 1], n_mem
    )
    twin_sems = sems.take(2)
    twin = remote(small_sum.at[place.mem], small_twin, twin_sems[0], twin_sems[1], place.twin())
    far_sems = sems.take(2 * (planes - 1))
    far = [
        remote(
            small_sum.at[place.mem],
            small_far.at[r - 1],
            far_sems[2 * r - 2],
            far_sems[2 * r - 1],
            place.far(r),
        )
        for r in range(1, planes)
    ]
    seg = dx_out.shape[1]
    own = 2 * seg
    spread = Spread(
        place,
        sems,
        lambda k: dx_vm.at[pl.ds(seg * k, seg)],
        lambda k: dx_out.at[place.parity],
    )
    swap_sems = sems.take(2)
    swap_part = remote(part_vm, twin_vm, swap_sems[0], swap_sems[1], place.twin())

    for item in fetches:
        item.start()
    place.meet(
        column_peers(n_mem) + plane_peers(plane) + [(2 * plane * r, 0) for r in range(1, planes)]
    )
    for item in settles:
        item.start()
    block = x_ref.shape[1] // n_mem

    def input_part(span):
        return (
            mm(dq_vm[span, :], w_ref[0], NT)
            + mm(dk_vm[span, :], w_ref[1], NT)
            + mm(dv_vm[span, :], w_ref[2], NT)
        )

    pairs = part // (2 * HD)
    late = []
    for c in range(chunks):
        for pair in range(c * pairs // chunks, (c + 1) * pairs // chunks):
            self_attend_back(
                place,
                pair,
                q_ref,
                k_ref,
                v_ref,
                o_ref,
                do_ref,
                lse_ref,
                (dq_vm, dk_vm, dv_vm),
                attend_scratch,
            )
        if c == 0:
            for item in fetches:
                item.get()
            for m in range(n_mem):
                x_t[m] = x_ref[:, m * block : (m + 1) * block].T
        span = slice(c * lanes, (c + 1) * lanes)

        def weights(m, carry, span=span):
            for i, grad in enumerate((dq_vm, dk_vm, dv_vm)):
                dw_vm[i, m, :, :, span] = (
                    mm(x_t[m], grad[:, span]).astype(BF16).reshape(plane, depth, lanes)
                )
            return carry

        if c < chunks - 2:
            lax.fori_loop(0, n_mem, weights, 0)
            sums[c].start()
        if c == 1:
            sums[0].middle()
        if c == 2:
            for item in settles:
                item.middle()
            sums[0].end()
            ends[0].start()
            sums[1].middle()
        late.append(weights)
    part_vm[...] = input_part(slice(own, 2 * own)).astype(BF16)
    swap_part.start()
    lax.fori_loop(0, n_mem, late[-2], 0)
    sums[-2].start()
    swap_part.wait()
    total = dz1_ref[...] + input_part(slice(0, own)) + twin_vm[...].astype(F32)
    dx_vm[...] = total.astype(BF16)
    spread.start()
    lax.fori_loop(0, n_mem, late[-1], 0)
    sums[-1].start()
    sums[1].end()
    ends[1].start()
    for item in settles:
        item.forward()
    sums[-2].middle()

    small_sum[...] = jnp.zeros_like(small_sum)
    wide = small_sum.shape[2]
    unit = wide // 2
    first = place.core == 0
    for row, ref, at in (
        (2, middle_ref, 2),
        (5, feed_ref, 5),
        (6, middle_ref, 1),
        (7, feed_ref, 4),
        (8, feed_ref, 1),
        (9, feed_ref, 2),
        (10, middle_ref, 0),
        (11, feed_ref, 3),
        (12, feed_ref, 0),
    ):
        for b in range(n_mem):
            small_sum[b, row : row + 1, :] = ref[at : at + 1, b * wide : (b + 1) * wide]
    for row, value in (
        (0, jnp.sum(dq_vm[...].astype(F32), axis=0, keepdims=True)),
        (1, jnp.sum(dv_vm[...].astype(F32), axis=0, keepdims=True)),
        (3, middle_ref[3:4, :part]),
        (4, middle_ref[4:5, :part]),
    ):
        for b in range(n_mem):
            side = value[:, b * unit : (b + 1) * unit]
            none = jnp.zeros_like(side)
            small_sum[b, row : row + 1, :unit] = jnp.where(first, side, none)
            small_sum[b, row : row + 1, unit:] = jnp.where(first, none, side)
    count = hidden_ref.shape[1] // (n_mem * wide)
    for b in range(n_mem):
        for i in range(count):
            at = (b * count + i) * wide
            side = hidden_ref[:, at : at + wide]
            none = jnp.zeros_like(side)
            row = 13 + i
            small_sum[b, row : row + 1, :] = jnp.where(first, side, none)
            small_sum[b, row + count : row + count + 1, :] = jnp.where(first, none, side)
    for copy in near:
        copy.start()
    sums[-1].middle()
    sums[-2].end()
    ends[-2].start()
    ends[0].middle()
    for copy in near:
        copy.wait()
    total = small_sum[...]
    for t in range(plane - 1):
        total += small_near[t]
    small_sum[...] = total
    line.start()
    sums[-1].end()
    ends[-1].start()
    ends[1].middle()
    ends[0].forward()
    for item in settles:
        item.end()
    ends[-2].middle()
    ends[1].forward()
    for s in range(1, n_mem):
        line.wait_recv(s)
    line.wait_send()
    value = small_sum[place.mem]
    for s in range(n_mem - 1):
        value += small_line[s]
    small_sum[place.mem] = value
    twin.start()
    ends[-1].middle()
    ends[-2].forward()
    for item in ends[:-2]:
        item.end()
    twin.wait()
    value = small_sum[place.mem] + small_twin[...]
    if far:
        small_sum[place.mem] = value
        for copy in far:
            copy.start()
        for copy in far:
            copy.wait()
        for r in range(planes - 1):
            value += small_far[r]
    small_out[...] = value
    ends[-1].forward()
    ends[-2].end()
    ends[-1].end()
    for item in sums:
        item.wait_send()
    for k in range(2):
        spread.wait_recv(k)
    spread.wait_send()


def last(n_mem, plane, planes, q, k, v, o, do, lse, x, w, dz1, sums, small_shape, ready):
    rows, part = q.shape
    chunks = part // (2 * HD)
    width = x.shape[1]
    own = rows // 2
    settled = tuple(columns for _, columns in ready)
    settled_shapes = [item.shape[:2] + (plane,) + item.shape[2:] for item, _ in ready]
    grad_shape = (3, n_mem, plane, width // (n_mem * plane), part)
    depth, lanes = grad_shape[3], part // chunks
    small_part = small_shape[1:]
    shapes = [
        jax.ShapeDtypeStruct(small_part, F32),
        jax.ShapeDtypeStruct((2, own // 2, width), BF16),
        reduce_out(grad_shape, True, plane),
    ] + [reduce_out(shape, columns, plane) for shape, columns in zip(settled_shapes, settled)]
    fetched = [x, w, dz1]
    scratch = (
        [pltpu.VMEM(item.shape, item.dtype) for item in fetched]
        + [pltpu.VMEM((rows, part), BF16)] * 3
        + [
            pltpu.VMEM((rows, 2 * HD), BF16),
            pltpu.VMEM((rows, 2 * HD), BF16),
            pltpu.VMEM((2 * HD, rows), BF16),
            pltpu.VMEM((2, 2 * HD, rows), BF16),
            pltpu.VMEM((2, 2 * HD, rows), BF16),
            pltpu.VMEM((2, rows, rows), BF16),
            pltpu.VMEM((2, rows, rows), BF16),
            pltpu.VMEM((n_mem, width // n_mem, rows), BF16),
            pltpu.VMEM(grad_shape, BF16),
        ]
        + [pltpu.VMEM((own, width), BF16)] * 3
        + [pltpu.VMEM((3, n_mem, depth, lanes), BF16)] * chunks
    )
    for _ in range(chunks):
        scratch += plane_sum_scratch(grad_shape, n_mem, depth, lanes)
    for _ in range(chunks):
        scratch += settle_scratch(grad_shape, n_mem, plane, planes, depth, lanes)
    for shape in settled_shapes:
        scratch += settle_scratch(shape, n_mem, plane, planes, shape[3])
    scratch += [
        pltpu.VMEM((plane - 1,) + small_shape, F32),
        pltpu.VMEM((n_mem - 1,) + small_part, F32),
        pltpu.VMEM(small_part, F32),
        pltpu.VMEM((max(planes - 1, 1),) + small_part, F32),
        pltpu.VMEM(small_shape, F32),
        pltpu.SemaphoreType.DMA(
            (
                (len(ready) + chunks) * settle_sems(n_mem, plane, planes)
                + chunks * PLANE_SUM_SEMS
                + 24
                + 2 * planes,
            )
        ),
    ]
    outs = pl.pallas_call(
        functools.partial(last_kernel, n_mem, plane, planes, settled, chunks),
        in_specs=[VMEM] * 9 + [ANY] * 3 + [VMEM] * len(ready),
        out_specs=[VMEM, ANY, VMEM] + [VMEM] * len(ready),
        out_shape=shapes,
        scratch_shapes=scratch,
        compiler_params=pltpu.CompilerParams(
            vmem_limit_bytes=60 * 2**20, collective_id=4, has_side_effects=True
        ),
        cost_estimate=pl.CostEstimate(
            flops=rows * rows * width * 40, bytes_accessed=40 * 2**20, transcendentals=rows * rows * 8
        ),
        name="last",
    )(q, k, v, o, do, lse, *sums, *fetched, *[item for item, _ in ready])
    return outs[0], outs[1], outs[2:]


def cross_forward_kernel(n_mem, plane, kinds, index_ref, q_ref, k_ref, v_ref, *refs):
    refs = Walk(refs)
    count_w = len(kinds)
    shards = refs.take(count_w)
    o_ref, lse_ref = refs.take(2)
    halves = refs.take(count_w)
    v_t, o_t, sem_ref = refs.take(3)
    sems = Sems(sem_ref)
    place = Place(plane)
    step = pl.program_id(0) * pl.num_programs(1) + pl.program_id(1)
    last = pl.num_programs(0) * pl.num_programs(1) - 1
    gathers = [
        Gather(place, sems, shard, half, columns, n_mem, (1,) if i == 1 else None)
        for i, (shard, half, columns) in enumerate(zip(shards, halves, kinds))
    ]
    @pl.when(step == 0)
    def _():
        for gather in gathers:
            gather.own.start()
        place.meet(column_peers(n_mem) + plane_peers(plane))
        for gather in gathers:
            gather.begin()

    rows = q_ref.shape[0]
    count = index_ref.shape[0]

    @pl.when(pl.program_id(1) == 0)
    def _():
        for j in range(count):
            v_t[:, j * BLK : (j + 1) * BLK] = v_ref[index_ref[j]].T

    units = []
    for i in range(rows // BLK):
        q_t = q_ref[i * BLK : (i + 1) * BLK, :].T
        for head in range(2):
            q_head = head_rows(q_t, head)

            def score(j, q_head=q_head):
                return mm(k_ref[index_ref[j]], q_head)

            def value(j, head=head):
                return v_t[head * HD : (head + 1) * HD, j * BLK : (j + 1) * BLK]

            units.append(
                (
                    [functools.partial(score, j) for j in range(count)],
                    [functools.partial(value, j) for j in range(count)],
                    (i, head),
                )
            )

    def finish(tag, mixed, lse):
        i, head = tag
        span = slice(i * BLK, (i + 1) * BLK)
        o_t[head * HD : (head + 1) * HD, span] = mixed
        lse_ref[0, head : head + 1, span] = lse

    whole_one, line_one = gathers
    plan = {
        4: [(whole_one.share, 1)],
        6: [(line_one.share, 1)],
        10: [(whole_one.share, 2)],
        12: [(line_one.share, 2), (whole_one.forward, 1)],
        14: [(line_one.forward, 1)],
        17: [(whole_one.share, 3)],
        19: [(line_one.share, 3), (whole_one.forward, 2)],
        24: [(whole_one.forward, 3)],
    }

    def serve(n):
        for when, calls in plan.items():
            if when % len(units) == n:

                @pl.when(step == when // len(units))
                def _():
                    for call, hops in calls:
                        call(hops)

    softmax_units(units, finish, serve)
    o_ref[...] = o_t[...].T.astype(BF16)

    @pl.when(step == last)
    def _():
        for gather in gathers:
            gather.finish()


def cross_forward(n_mem, plane, index, q, k, v, params):
    rows, width = q.shape
    pairs = width // (2 * HD)
    keys = index.shape[0] * PLEN
    block = 2 * BLK
    question = pl.BlockSpec((block, 2 * HD), lambda h, i: (i, h))
    memory = pl.BlockSpec(k.shape[:2] + (2 * HD,), lambda h, i: (0, 0, h))
    kinds = tuple(columns for _, columns in params)
    views = [half_views(shard, columns, n_mem, plane) for shard, columns in params]
    outs = pl.pallas_call(
        functools.partial(cross_forward_kernel, n_mem, plane, kinds),
        grid=(pairs, rows // block),
        in_specs=[pl.BlockSpec(memory_space=pltpu.SMEM), question, memory, memory]
        + [whole(view.shape) for view, _ in views],
        out_specs=[question, pl.BlockSpec((1, 2, block), lambda h, i: (h, 0, i))]
        + [ANY] * len(params),
        out_shape=[
            jax.ShapeDtypeStruct((rows, width), BF16),
            jax.ShapeDtypeStruct((pairs, 2, rows), F32),
        ]
        + [jax.ShapeDtypeStruct(full, BF16) for _, full in views],
        scratch_shapes=[
            pltpu.VMEM((2 * HD, keys), BF16),
            pltpu.VMEM((2 * HD, block), F32),
            pltpu.SemaphoreType.DMA((4 + GATHER_SEMS * len(params),)),
        ],
        compiler_params=pltpu.CompilerParams(
            vmem_limit_bytes=60 * 2**20, collective_id=2, has_side_effects=True
        ),
        cost_estimate=pl.CostEstimate(
            flops=rows * keys * width * 16,
            bytes_accessed=rows * width * 4 + k.size * 4,
            transcendentals=rows * keys * pairs * 2,
        ),
        name="cross_forward",
    )(index, q, k, v, *[view for view, _ in views])
    return outs[:2], outs[2:]


def cross_backward_kernel(
    n_mem, plane, planes, chunks, settled, index_ref, q_ref, k_ref, v_ref, o_ref, do_ref, lse_ref, *refs
):
    refs = Walk(refs)
    kinds = {which: columns for which, columns, _ in chunks}
    grads = refs.take(len(kinds))
    ready = refs.take(len(settled))
    dq_ref, dk_ref, dv_ref = refs.take(3)
    outs = refs.take(len(kinds))
    ready_outs = refs.take(len(settled))
    q_h, do_h, dq_t, p_vm, ds_vm = refs.take(5)
    sems = Sems(refs.refs[-1])
    place = Place(plane, planes)
    sums, settles = [], []
    for which, columns, rows_of in chunks:
        own = refs.one()
        sums.append(PlaneSum(place, sems, grads[which], own, refs.take(3), rows_of))
        settles.append(
            Settle(place, sems, own, outs[which], refs.take(3), columns, n_mem, rows_of)
        )
    first = [
        Settle(
            place, sems, ready[i], ready_outs[i], refs.take(3), columns, n_mem, (0, ready[i].shape[2])
        )
        for i, columns in enumerate(settled)
    ]
    passage = pl.program_id(1)
    step = pl.program_id(0) * pl.num_programs(1) + passage
    steps = pl.num_programs(0) * pl.num_programs(1)
    rows = q_ref.shape[0]
    count = rows // BLK

    @pl.when(step == 0)
    def _():
        place.meet(
            column_peers(n_mem) + plane_peers(plane) + [(2 * plane * r, 0) for r in range(1, planes)]
        )
        for item in first:
            item.start()

    def at(when, *calls):
        @pl.when(step == when)
        def _():
            for call in calls:
                call()

    plan = ((0, 2, 5, 9, 10), (4, 6, 9, 13, 14), (8, 9, 11, 14, 15))
    for i, (plane_sum, settle) in enumerate(zip(sums, settles)):
        start, middle, end, line, near = plan[i]
        at(start, plane_sum.start)
        at(middle, plane_sum.middle)
        at(end, plane_sum.end, settle.start)
        at(line, settle.middle)
        at(near, settle.forward)
    for item in first:
        at(7, item.middle)
        at(9, item.forward)

    @pl.when(passage == 0)
    def _():
        for i in range(count):
            span = slice(i * BLK, (i + 1) * BLK)
            q_t = q_ref[span, :].T
            grads_t = do_ref[span, :].T
            prod = (do_ref[span, :].astype(F32) * o_ref[span, :].astype(F32)).T
            for head in range(2):
                delta = jnp.sum(prod[head * HD : (head + 1) * HD, :], axis=0, keepdims=True)
                q_h[head, :, span] = head_rows(q_t, head, lse_ref[0, head : head + 1, span])
                do_h[head, :, span] = head_rows(grads_t, head, delta)
        dq_t[...] = jnp.zeros_like(dq_t)

    keys = dk_ref.shape[0] // BLK
    slots = [index_ref[passage * keys + j] for j in range(keys)]
    k_t = jnp.concatenate([k_ref[slot].T for slot in slots], axis=1)
    units = [(head, j, i) for head in range(2) for j in range(keys) for i in range(count)]

    def products(unit):
        head, j, i = unit
        span = slice(i * BLK, (i + 1) * BLK)
        return (
            mm(ones_in(k_ref[slots[j]], head), q_h[head, :, span]),
            mm(ones_in(v_ref[slots[j]], head), do_h[head, :, span]),
        )

    coming = products(units[0])
    halves = []
    for n, (head, j, i) in enumerate(units):
        scores, dprobs = coming
        if n + 1 < len(units):
            coming = products(units[n + 1])
        tile, span = slice(j * BLK, (j + 1) * BLK), slice(i * BLK, (i + 1) * BLK)
        probs = jnp.exp(scores)
        p_vm[head, tile, span] = probs.astype(BF16)
        ds_vm[head, tile, span] = (probs * dprobs).astype(BF16)
        if (j, i) == (keys - 1, count - 1):
            half = slice(head * HD, (head + 1) * HD)
            halves.append((mm(p_vm[head], do_ref[...]), mm(ds_vm[head], q_ref[...])))
            dq_t[half, :] += mm(k_t[half, :], ds_vm[head])
    dv_ref[...] = pick_heads(halves[0][0], halves[1][0]).astype(BF16)
    dk_ref[...] = pick_heads(halves[0][1], halves[1][1]).astype(BF16)

    @pl.when(passage == pl.num_programs(1) - 1)
    def _():
        dq_ref[...] = dq_t[...].T.astype(BF16)

    @pl.when(step == steps - 1)
    def _():
        for settle in first + settles:
            settle.end()
        for item in sums:
            item.wait_send()


def cross_backward(n_mem, plane, planes, index, q, k, v, o, do, lse, grads, ready):
    rows, width = q.shape
    pairs = width // (2 * HD)
    block = 2 * PLEN
    keys = index.shape[0] * PLEN
    passages = keys // block
    question = pl.BlockSpec((rows, 2 * HD), lambda h, u: (0, h))
    memory = pl.BlockSpec(k.shape[:2] + (2 * HD,), lambda h, u: (0, 0, h))
    grads_of = pl.BlockSpec((block, 2 * HD), lambda h, u: (u, h))
    shapes, chunks, scratch = [], [], []
    for which, (grad, columns, pieces) in enumerate(grads):
        lead, _, _, depth, cols = grad.shape
        count = depth // pieces
        shapes.append(reduce_out(grad.shape, columns, plane))
        for i in range(pieces):
            chunks.append((which, columns, (i * count, count)))
            scratch.append(pltpu.VMEM((lead, n_mem, count, cols), BF16))
            scratch += plane_sum_scratch(grad.shape, n_mem, count)
            scratch += settle_scratch(grad.shape, n_mem, plane, planes, count)
    settled = tuple(columns for _, columns in ready)
    for item, columns in ready:
        shape = item.shape[:2] + (plane,) + item.shape[2:]
        shapes.append(reduce_out(shape, columns, plane))
        scratch += settle_scratch(shape, n_mem, plane, planes, shape[3])
    outs = pl.pallas_call(
        functools.partial(cross_backward_kernel, n_mem, plane, planes, tuple(chunks), settled),
        grid=(pairs, passages),
        in_specs=[
            pl.BlockSpec(memory_space=pltpu.SMEM),
            question,
            memory,
            memory,
            question,
            question,
            pl.BlockSpec((1, 2, rows), lambda h, u: (h, 0, 0)),
        ]
        + [ANY] * len(grads)
        + [whole(item.shape) for item, _ in ready],
        out_specs=[question, grads_of, grads_of]
        + [whole(item.shape) for item in shapes],
        out_shape=[
            jax.ShapeDtypeStruct((rows, width), BF16),
            jax.ShapeDtypeStruct((keys, width), BF16),
            jax.ShapeDtypeStruct((keys, width), BF16),
        ]
        + shapes,
        scratch_shapes=[
            pltpu.VMEM((2, 2 * HD, rows), BF16),
            pltpu.VMEM((2, 2 * HD, rows), BF16),
            pltpu.VMEM((2 * HD, rows), F32),
            pltpu.VMEM((2, block, rows), BF16),
            pltpu.VMEM((2, block, rows), BF16),
        ]
        + scratch
        + [
            pltpu.SemaphoreType.DMA(
                (
                    len(chunks) * PLANE_SUM_SEMS
                    + (len(chunks) + len(ready)) * settle_sems(n_mem, plane, planes),
                )
            )
        ],
        compiler_params=pltpu.CompilerParams(
            vmem_limit_bytes=56 * 2**20, collective_id=5, has_side_effects=True
        ),
        cost_estimate=pl.CostEstimate(
            flops=rows * keys * width * 40,
            bytes_accessed=rows * width * 10 + k.size * 8,
            transcendentals=rows * keys * pairs * 2,
        ),
        name="cross_backward",
    )(index, q, k, v, o, do, lse, *[item[0] for item in grads], *[item for item, _ in ready])
    return outs[:3], outs[3:]


def widen_kernel(*refs):
    count = len(refs) // 2
    for src, dst in zip(refs[:count], refs[count:]):
        dst[...] = src[...].astype(F32)


def widen(pairs):
    steps = 8
    flats = [value.reshape(-1, like.shape[-1]) for value, like in pairs]
    blocks = [
        pl.BlockSpec((item.shape[0] // steps, item.shape[1]), lambda i: (i, 0)) for item in flats
    ]
    outs = pl.pallas_call(
        widen_kernel,
        grid=(steps,),
        in_specs=blocks,
        out_specs=blocks,
        out_shape=[jax.ShapeDtypeStruct(item.shape, F32) for item in flats],
        compiler_params=pltpu.CompilerParams(vmem_limit_bytes=60 * 2**20),
        cost_estimate=pl.CostEstimate(
            flops=0, bytes_accessed=6 * sum(item.size for item in flats), transcendentals=0
        ),
        name="widen",
    )(*flats)
    return [out.reshape(like.shape) for out, (_, like) in zip(outs, pairs)]


def body(
    hidden_in,
    encoder_rows,
    passage_map,
    self_qkv,
    self_out,
    cross_qkv,
    cross_out,
    ffn_in,
    ffn_out,
    ffn_in_bias,
    biases,
    gains,
    cotangent,
):
    n_pb = lax.axis_size("pb")
    n_mem = lax.axis_size("mem")
    columns = n_pb // 2
    plane = min(columns, 4)
    pb = lax.axis_index("pb")
    core = pb % 2
    width = hidden_in.shape[2]
    planes = columns // plane

    enc_local = encoder_rows.reshape(-1, PLEN, width)
    n_bias, n_gain = biases.shape[0], gains.shape[0]
    small = jnp.concatenate([biases, gains, ffn_in_bias.reshape(-1, biases.shape[1])], axis=0)
    n_small = small.shape[0]
    small_rows = -(-n_small // 16) * 16
    small = jnp.pad(small, ((0, small_rows - n_small), (0, 0)))
    rows_out, halves, kept = front(
        n_mem,
        plane,
        (n_bias, n_gain),
        hidden_in,
        enc_local,
        passage_map,
        small,
        [(self_qkv, True), (self_out, False), (cross_qkv, True), (cross_out, False)],
    )
    x_full, enc_full, index, small = rows_out
    sq, sk, sv, sa, self_lse, h1_full, unit1, scale1, cq, ck, cv = kept
    index = index.reshape(-1)

    def flat(half):
        lead, _, _, _, cols = half.shape
        return half.reshape(lead, -1, cols)

    w_self, w_cross = flat(halves[0]), flat(halves[2])
    w_self_out, w_cross_out = flat(halves[1])[0], flat(halves[3])[0]
    small = small.astype(F32)
    vectors = small[:, : n_bias + n_gain].transpose(1, 0, 2).reshape(n_bias + n_gain, width)
    bias, gain = vectors[:n_bias], vectors[n_bias:]
    ffn_bias = small[:, n_bias + n_gain : n_small].reshape(-1)

    def half_of(vector):
        parts = vector.reshape(n_mem, 2, -1)
        return jnp.where(core == 0, parts[:, 0], parts[:, 1]).reshape(-1)

    order = jnp.arange(encoder_rows.shape[1] * n_mem, dtype=jnp.int32)
    hits = index[None, :] == order[:, None]
    member = jnp.any(hits, axis=1).astype(F32)
    slot = jnp.sum(jnp.where(hits, jnp.arange(index.shape[0], dtype=jnp.int32)[None], 0), axis=1)
    (ca, cross_lse), halves = cross_forward(
        n_mem,
        plane,
        index,
        cq,
        ck,
        cv,
        [(ffn_in[None], True), (ffn_out, False)],
    )
    w_ffn_in, w_ffn_out = flat(halves[0])[0], halves[1]

    rows_of = jnp.stack(
        [gain[0], bias[6], bias[5], gain[1], bias[7], bias[9], gain[2], bias[8]]
    )
    layer_out, dca, dz2, feed_sums, hidden_sums, own_ffn_out, dw_ffn_in, dw_cross_out = feed(
        n_mem,
        plane,
        cotangent,
        rows_of,
        half_of(ffn_bias)[None],
        ca,
        unit1,
        w_cross_out,
        w_ffn_in,
        w_ffn_out,
    )
    (dcq, dck, dcv), ffn_sums = cross_backward(
        n_mem,
        plane,
        planes,
        index,
        cq,
        ck,
        cv,
        ca,
        dca,
        cross_lse,
        [(dw_ffn_in, True, 2), (dw_cross_out, False, 1)],
        [(own_ffn_out, False)],
    )
    (dsa, dz1, middle_sums, enc_sum), (own_cross, own_so), _ = middle(
        n_mem,
        plane,
        planes,
        slot,
        member,
        index,
        dcq,
        dck,
        dcv,
        w_cross,
        w_self_out,
        sa,
        h1_full,
        enc_full.reshape(-1, PLEN, width),
        dz2,
        unit1,
        scale1,
        gain[0][None],
        [],
    )

    vec, dx, sums = last(
        n_mem,
        plane,
        planes,
        sq,
        sk,
        sv,
        sa,
        dsa,
        self_lse,
        x_full,
        w_self,
        dz1,
        [feed_sums, hidden_sums, middle_sums],
        small.shape,
        [(own_so, False), (own_cross, True)],
    )
    (
        grad_in,
        grad_encoder,
        out_self_qkv,
        out_self_out,
        out_cross_qkv,
        out_cross_out,
        out_ffn_in,
        out_ffn_out,
    ) = widen(
        [
            (dx, hidden_in),
            (enc_sum, encoder_rows),
            (sums[0], self_qkv),
            (sums[1], self_out),
            (sums[2], cross_qkv),
            (ffn_sums[1], cross_out),
            (ffn_sums[0], ffn_in),
            (ffn_sums[2], ffn_out),
        ]
    )
    out_ffn_bias = vec[n_bias + n_gain : n_small].reshape(-1)
    return (
        layer_out,
        grad_in,
        grad_encoder,
        out_self_qkv,
        out_self_out,
        out_cross_qkv,
        out_cross_out,
        out_ffn_in,
        out_ffn_out,
        out_ffn_bias,
        vec[:n_bias],
        vec[n_bias : n_bias + n_gain],
    )


def solution(mesh):
    placed = (
        P("pb", "mem", None),
        P("pb", "mem", None, None),
        P("pb", None),
        P(None, "mem", None),
        P("mem", None),
        P(None, "mem", None),
        P("mem", None),
        P("mem", None),
        P("mem", None),
        P("mem"),
        P(None, "mem"),
        P(None, "mem"),
        P("pb", "mem", None),
    )
    return jax.shard_map(
        body,
        mesh=mesh,
        in_specs=placed,
        out_specs=(
            P("pb", "mem", None),
            P("pb", "mem", None),
            P("pb", "mem", None, None),
            P(None, "mem", None),
            P("mem", None),
            P(None, "mem", None),
            P("mem", None),
            P("mem", None),
            P("mem", None),
            P("mem"),
            P(None, "mem"),
            P(None, "mem"),
        ),
        check_vma=False,
    )
```
